32 devices in a mesh: probe: 4 (over y, core), ex: 8 (over z, x).
Axes of the slice: x: 2, y: 2, z: 4, core: 2. Of those that a mesh axis runs over, the one named last changes fastest.
Arguments:
- tokens: bfloat16 [2048, 768], P('ex'), may hold values from -6 to 6
- segment_ids: int32 [2048], replicated, may hold values from 0 to 6, as said below
- qkv_weight: bfloat16 [768, 2304], replicated, may hold values from -0.21875 to 0.21875
- qkv_bias: bfloat16 [2304], replicated, may hold values from -4 to 4
- out_weight: bfloat16 [768, 768], replicated, may hold values from -1.75 to 1.75
- out_bias: bfloat16 [768], replicated, may hold values from -6 to 6
- up_weight: bfloat16 [768, 3072], replicated, may hold values from -0.21875 to 0.21875
- up_bias: bfloat16 [3072], replicated, may hold values from -4 to 4
- down_weight: bfloat16 [3072, 768], replicated, may hold values from -0.109375 to 0.109375
- down_bias: bfloat16 [768], replicated, may hold values from -6 to 6
- norm1_gain: float32 [768], replicated, may hold values from 0.1 to 1.9
- norm1_bias: float32 [768], replicated, may hold values from -4 to 4
- norm2_gain: float32 [768], replicated, may hold values from 0.1 to 1.9
- norm2_bias: float32 [768], replicated, may hold values from -4 to 4
- probe_dirs: bfloat16 [16, 768, 3072], P('probe', 'ex'), may hold values from -0.21875 to 0.21875
- out_grad: bfloat16 [2048, 768], P('ex'), may hold values from -6 to 6
Outputs:
- layer_out: bfloat16 [2048, 768], P('ex')
- input_grad: bfloat16 [2048, 768], P('ex')
- grad_qkv_weight: float32 [768, 2304], P('ex')
- grad_qkv_bias: float32 [2304], replicated
- grad_out_weight: float32 [768, 768], P('ex')
- grad_out_bias: float32 [768], replicated
- grad_up_weight: float32 [768, 3072], P('ex')
- grad_up_bias: float32 [3072], replicated
- grad_down_weight: float32 [3072, 768], P('ex')
- grad_down_bias: float32 [768], replicated
- grad_norm1_gain: float32 [768], replicated
- grad_norm1_bias: float32 [768], replicated
- grad_norm2_gain: float32 [768], replicated
- grad_norm2_bias: float32 [768], replicated
- curvature: float32 [16, 768, 3072], P('probe', 'ex')
- probe_scores: float32 [16, 1], P('probe')
The draws below stay inside these ranges and needn't reach their ends.
Inputs may be any that keep to these rules, and one draw needn't show every extreme that they name: `segment_ids`: along each row of 2048 tokens the ids never fall; no id occurs in two rows.
All inputs are finite; a program needn't handle non-finite values.
Results may differ from the reference program's by a relative error of at most 0.012.
Values may be sent and summed in bfloat16 or wider, within the bound.
No kernel may reach another device: no remote copies, remote signals or barrier semaphores. Data moves between devices by JAX's collectives and lax.ppermute only.
A program may use at most 256 MiB of HBM per device.

```python
import jax
import jax.numpy as jnp
from jax import lax

D = 768
HEADS = 12
HEAD_DIM = 64
ROT = 16
FF = 3072
SEQ = 2048
TOK_DEV = 256
TOKENS = 2048
ROWS = 1
PROBES = 16


def draw_segment_ids(key, part):
    key = jax.random.fold_in(key, 11)
    row_count = TOKENS // SEQ
    first_key, second_key = jax.random.split(key)
    early = jax.random.randint(first_key, (row_count, 3), 1, TOK_DEV)
    late = jax.random.randint(second_key, (row_count, 3), SEQ - TOK_DEV + 1, SEQ)
    cuts = jnp.concatenate([early, late], axis=1)
    token_place = jnp.arange(SEQ)
    within = jnp.sum((cuts[:, :, None] <= token_place[None, None, :]).astype(jnp.int32), axis=1)
    row_base = 8 * jnp.arange(row_count)[:, None]
    return (within + row_base).reshape(row_count * SEQ).astype(jnp.int32)


def block_scale(key, dims, cuts, low, high):
    factor_of = 1.0
    for dim, shards_of in cuts:
        steps = jax.random.uniform(jax.random.fold_in(jax.random.fold_in(key, 6), dim), (shards_of,), jnp.float32, low / len(cuts), high / len(cuts))
        factor_of = factor_of * jnp.repeat(jnp.exp(steps), dims[dim] // shards_of).reshape((-1,) + (1,) * (len(dims) - 1 - dim))
    return factor_of


def scatter_about(stream_key, shape, width, reach, shards=(), kind=jnp.bfloat16):
    loudness = block_scale(stream_key, shape, shards, -0.22, 0.18) if shards else 1.0
    entries = jax.random.normal(stream_key, shape, jnp.float32) * width * loudness
    return jnp.minimum(jnp.maximum(entries, -reach), reach).astype(kind)


def setup_inputs(seed: int = 0) -> dict:
    streams_of = jax.random.split(jax.random.key(seed), 17)
    return {
        "tokens": scatter_about(streams_of[0], (TOKENS, D), 1.0, 6.0, ((0, 8),)),
        "segment_ids": draw_segment_ids(jax.random.fold_in(streams_of[16], 71), 0),
        "qkv_weight": scatter_about(streams_of[2], (D, 3 * D), D ** -0.5, 0.21875),
        "qkv_bias": scatter_about(streams_of[3], (3 * D,), 0.3, 4.0),
        "out_weight": scatter_about(streams_of[4], (D, D), (D // 64) ** -0.5, 1.75),
        "out_bias": scatter_about(streams_of[5], (D,), 0.5, 6.0),
        "up_weight": scatter_about(streams_of[6], (D, FF), D ** -0.5, 0.21875),
        "up_bias": scatter_about(streams_of[7], (FF,), 0.3, 4.0),
        "down_weight": scatter_about(streams_of[8], (FF, D), FF ** -0.5, 0.109375),
        "down_bias": scatter_about(streams_of[9], (D,), 0.5, 6.0),
        "norm1_gain": jnp.clip(1.0 + 0.18 * jax.random.normal(streams_of[10], (D,), jnp.float32), 0.1, 1.9),
        "norm1_bias": scatter_about(streams_of[11], (D,), 0.3, 4.0, (), jnp.float32),
        "norm2_gain": jnp.clip(1.0 + 0.18 * jax.random.normal(streams_of[12], (D,), jnp.float32), 0.1, 1.9),
        "norm2_bias": scatter_about(streams_of[13], (D,), 0.3, 4.0, (), jnp.float32),
        "probe_dirs": scatter_about(streams_of[14], (PROBES, D, FF), D ** -0.5, 0.21875, ((0, 4), (1, 8))),
        "out_grad": scatter_about(streams_of[15], (TOKENS, D), 1.0, 6.0, ((0, 8),)),
    }


@jax.custom_vjp
def low(v):
    return lax.optimization_barrier(v.astype(jnp.bfloat16)).astype(jnp.float32)

@jax.custom_vjp
def low_back(v):
    return v

def low_keep(v):
    return (low(v), None)

def low_pass(kept, grad):
    return (grad,)

def back_keep(v):
    return (v, None)

def back_low(kept, grad):
    return (low(grad),)
low.defvjp(low_keep, low_pass)
low_back.defvjp(back_keep, back_low)
highest = lax.Precision.HIGHEST
eps_norm = 1e-05
masked_score = -1e+30

def layer_norm(features, gain_vec, shift_vec):
    center = lax.optimization_barrier(jnp.mean(features, axis=-1, keepdims=True))
    centred = features - center
    spread = lax.optimization_barrier(jnp.mean(centred * centred, axis=-1, keepdims=True))
    return centred * lax.rsqrt(spread + eps_norm) * gain_vec + shift_vec

def gelu_exact(features):
    return jax.nn.gelu(features, approximate=False)

def rotary_tables(positions):
    steps = jnp.arange(ROT // 2, dtype=jnp.float32) * (2.0 / ROT)
    inverse = jnp.power(10000.0, -steps)
    angles = positions.astype(jnp.float32)[:, None] * inverse[None, :]
    angles = jnp.concatenate([angles, angles], axis=1)
    return (jnp.cos(angles), jnp.sin(angles))

def rotate(features, cosine, sine_part):
    turned = features[..., :ROT]
    rest_dims = features[..., ROT:]
    first_half = turned[..., :ROT // 2]
    second_half = turned[..., ROT // 2:]
    half_turn = jnp.concatenate([-second_half, first_half], axis=-1)
    turned = turned * cosine[:, None, :] + half_turn * sine_part[:, None, :]
    return jnp.concatenate([turned, rest_dims], axis=-1)

def row_attention(queries, key_rows, value_rows, row_segments):
    scores_now = jnp.einsum('qhd,khd->hqk', queries, key_rows, precision=highest) * HEAD_DIM ** (-0.5)
    scores_now = low_back(scores_now)
    token_place = jnp.arange(SEQ)
    allowed = (token_place[None, :] <= token_place[:, None]) & (row_segments[None, :] == row_segments[:, None])
    scores_now = jnp.where(allowed[None], scores_now, masked_score)
    prob_rows = low(jax.nn.softmax(scores_now, axis=-1))
    return jnp.einsum('hqk,khd->qhd', prob_rows, value_rows, precision=highest)

def attend_row(items):
    return jax.checkpoint(row_attention)(*items)

def layer_forward(inputs, qkv_w, qkv_b, out_w, out_b, up_w, up_b, down_w, down_b, gain_one, shift_one, gain_two, shift_two, tap_hidden, tap_active, segment_ids):
    tok_count = inputs.shape[0]
    row_count = tok_count // SEQ
    positions = jnp.arange(tok_count) % SEQ
    cosine, sine_part = rotary_tables(positions)
    normed_one = low(layer_norm(inputs, gain_one, shift_one))
    mixed_proj = low_back(jnp.dot(normed_one, qkv_w, precision=highest) + qkv_b)
    mixed_proj = mixed_proj.reshape(tok_count, HEADS, 3 * HEAD_DIM)
    queries = low(rotate(mixed_proj[..., :HEAD_DIM], cosine, sine_part))
    key_rows = low(rotate(mixed_proj[..., HEAD_DIM:2 * HEAD_DIM], cosine, sine_part))
    value_rows = low(mixed_proj[..., 2 * HEAD_DIM:])
    shape_rows = (row_count, SEQ, HEADS, HEAD_DIM)
    attended = lax.map(attend_row, (queries.reshape(shape_rows), key_rows.reshape(shape_rows), value_rows.reshape(shape_rows), segment_ids.reshape(row_count, SEQ)))
    attended = low_back(low(attended.reshape(tok_count, HEADS * HEAD_DIM)))
    attn_branch = jnp.dot(attended, out_w, precision=highest) + out_b
    normed_two = low(layer_norm(inputs, gain_two, shift_two))
    hidden = low_back(jnp.dot(normed_two, up_w, precision=highest) + up_b + tap_hidden)
    active = low(gelu_exact(hidden)) + tap_active
    mlp_branch = jnp.dot(active, down_w, precision=highest) + down_b
    return (inputs + attn_branch + mlp_branch, normed_two)

def reference(tokens, segment_ids, qkv_weight, qkv_bias, out_weight, out_bias, up_weight, up_bias, down_weight, down_bias, norm1_gain, norm1_bias, norm2_gain, norm2_bias, probe_dirs, out_grad):
    floats = [member.astype(jnp.float32) for member in (tokens, qkv_weight, qkv_bias, out_weight, out_bias, up_weight, up_bias, down_weight, down_bias, norm1_gain, norm1_bias, norm2_gain, norm2_bias)]
    tap_hidden = jnp.zeros((TOKENS, FF), jnp.float32)
    tap_active = jnp.zeros((TOKENS, FF), jnp.float32)

    def forward(*params):
        return layer_forward(*params, segment_ids)
    output, pullback, normed_two = jax.vjp(forward, *floats, tap_hidden, tap_active, has_aux=True)
    cotangent = out_grad.astype(jnp.float32)
    grads = pullback(cotangent)
    input_grad = grads[0]
    hidden_grad = grads[13]
    upstream = grads[14]
    up_float = floats[5]
    up_bias_float = floats[6]

    def slope(weight):
        hidden = low_back(jnp.dot(normed_two, weight, precision=highest) + up_bias_float)
        return jax.vjp(gelu_exact, hidden)[1](upstream)[0]

    def probe_terms(direction):
        along = jnp.dot(normed_two, direction, precision=highest)

        def contract(weight):
            return jnp.sum(along * slope(weight))
        curvature = jax.grad(contract)(up_float)
        per_token = lax.optimization_barrier(jnp.sum(along * hidden_grad, axis=1))
        return (curvature, lax.optimization_barrier(jnp.sum(per_token.reshape(ROWS, SEQ), axis=1)))
    curvature, probe_scores = lax.map(probe_terms, probe_dirs.astype(jnp.float32))
    return (output.astype(jnp.bfloat16), input_grad.astype(jnp.bfloat16), grads[1], grads[2], grads[3], grads[4], grads[5], grads[6], grads[7], grads[8], grads[9], grads[10], grads[11], grads[12], curvature, probe_scores)
```

```python
import functools

import jax
import jax.numpy as jnp
import numpy as np
from jax import lax
from jax.experimental import pallas as pl
from jax.experimental.pallas import tpu as pltpu
from jax.sharding import PartitionSpec as P

HEADS = 12
HEAD_DIM = 64
ROT = 16
SEQ = 2048

BF = jnp.bfloat16
F32 = jnp.float32
eps_norm = 1e-05
masked_score = -1e30
half_root = 0.7071067811865476
gauss_peak = 0.3989422804014327
MB = 1024 * 1024
LANES = 128
LIGHT = pl.CostEstimate(flops=1000, bytes_accessed=1000, transcendentals=0)
BIG = 58


def dot(a, b):
    return jnp.dot(a, b, preferred_element_type=F32)


def dot_nt(a, b):
    return lax.dot_general(a, b, (((1,), (1,)), ((), ())), preferred_element_type=F32)


def dot_tn(a, b):
    return lax.dot_general(a, b, (((0,), (0,)), ((), ())), preferred_element_type=F32)


def spread_of(features):
    center = jnp.mean(features, axis=-1, keepdims=True)
    centred = features - center
    spread = jnp.mean(centred * centred, axis=-1, keepdims=True)
    return centred, lax.rsqrt(spread + eps_norm)


def standardize(features):
    centred, factor = spread_of(features)
    return centred * factor


def norm_input_term(grad, gain_row, unit, factor):
    unit_grad = grad * gain_row
    inner = unit_grad - jnp.mean(unit_grad, -1, keepdims=True)
    return (inner - unit * jnp.mean(unit_grad * unit, -1, keepdims=True)) * factor


def gelu_parts(pre_act):
    below = 0.5 + 0.5 * lax.erf(pre_act * half_root)
    density = gauss_peak * jnp.exp(-0.5 * pre_act * pre_act)
    return below, density


def rotary_tables(count):
    steps = np.arange(ROT // 2, dtype=np.float32) * np.float32(2.0 / ROT)
    inverse = np.power(np.float32(10000.0), -steps).astype(np.float32)
    angles = np.arange(count, dtype=np.float32)[:, None] * inverse[None, :]
    angles = np.concatenate([angles, angles], axis=1)
    cosine = np.ones((count, HEAD_DIM), np.float32)
    sine = np.zeros((count, HEAD_DIM), np.float32)
    cosine[:, :ROT], sine[:, :ROT] = np.cos(angles), np.sin(angles)
    return np.concatenate([cosine, cosine], axis=1), np.concatenate([sine, sine], axis=1)


def params(limit_mb, **more):
    return pltpu.CompilerParams(vmem_limit_bytes=limit_mb * MB, **more)


def shaped(shape, dtype):
    return jax.ShapeDtypeStruct(shape, dtype)


def whole(*shape):
    return pl.BlockSpec(shape, lambda i: (0,) * len(shape))


VMEM = pl.BlockSpec(memory_space=pltpu.VMEM)
SMEM = pl.BlockSpec(memory_space=pltpu.SMEM)
ANY = pl.BlockSpec(memory_space=pl.ANY)


def call(kernel, *, inputs, in_specs, after=(), aliases=None, **more):
    spare = len(after)

    def body(*refs):
        kernel(*refs[: len(inputs)], *refs[len(inputs) + spare :])

    return pl.pallas_call(
        body, in_specs=list(in_specs) + [ANY] * spare, input_output_aliases=aliases or {},
        cost_estimate=LIGHT, **more,
    )(*inputs, *after)


def tie(value, after):
    return call(
        lambda value_ref, out_ref: None,
        inputs=[value],
        after=after,
        aliases={0: 0},
        in_specs=[ANY],
        out_specs=ANY,
        out_shape=shaped(value.shape, value.dtype),
        name="tie",
    )


def pack_kernel(dirs_ref, packed_ref, sems):
    probes = dirs_ref.shape[0]
    blocks, _, width = packed_ref.shape
    part_width = width // probes
    copies = []
    for block in range(blocks):
        for k in range(probes):
            source = dirs_ref.at[k, :, block * part_width : (block + 1) * part_width]
            target = packed_ref.at[block, :, k * part_width : (k + 1) * part_width]
            copies.append(pltpu.make_async_copy(source, target, sems.at[len(copies)]))
    for copy in copies:
        copy.start()
    for copy in copies:
        copy.wait()


def pack(dirs, blocks, rows, after):
    probes, local_rows, hidden_width = dirs.shape
    part_width = hidden_width // blocks
    if rows > 1:
        split = dirs.reshape(probes, local_rows, rows, blocks, part_width // rows)
        return split.transpose(3, 1, 0, 2, 4).reshape(blocks, local_rows, probes * part_width)
    return call(
        pack_kernel,
        inputs=[dirs],
        after=after,
        in_specs=[ANY],
        out_specs=ANY,
        out_shape=shaped((blocks, local_rows, probes * part_width), dirs.dtype),
        scratch_shapes=[pltpu.SemaphoreType.DMA((blocks * probes,))],
        compiler_params=params(8),
        name="pack",
    )


def stack_kernel(plan, *refs):
    sources, targets = refs[: -len(plan)], refs[-len(plan) :]
    for parts, target in zip(plan, targets):
        number = 0
        for part in parts:
            count = sources[part].shape[0]
            target[number : number + count] = sources[part][...]
            number += count


def stack(sources, plan, after):
    heights = [sum(sources[part].shape[0] for part in parts) for parts in plan]
    return call(
        functools.partial(stack_kernel, plan),
        inputs=sources,
        after=after,
        in_specs=[VMEM] * len(sources),
        out_specs=[VMEM] * len(plan),
        out_shape=[shaped((n,) + sources[parts[0]].shape[1:], BF) for n, parts in zip(heights, plan)],
        compiler_params=params(8),
        name="stack",
    )


def vectors_kernel(*refs):
    *sources, first_bias, second_bias, vectors_ref = refs
    vectors_ref[...] = jnp.zeros_like(vectors_ref)
    for number, source in enumerate(sources):
        vectors_ref[number : number + 1, :] = source[...].reshape(1, -1)
    total = first_bias[...].astype(F32) + second_bias[...].astype(F32)
    vectors_ref[len(sources) : len(sources) + 1, :] = total.reshape(1, -1)


def vectors_of(*sources):
    return call(
        vectors_kernel,
        inputs=list(sources),
        in_specs=[VMEM] * len(sources),
        out_specs=VMEM,
        out_shape=shaped((8, sources[0].shape[0]), F32),
        compiler_params=params(4),
        name="vectors",
    )


def local_kernel(
    tokens_ref, grads_ref, up_ref, up_bias_ref, down_ref, vectors_ref,
    base_ref, rest_ref, small_ref, normed_s, branch_s, back_s,
):
    step = pl.program_id(0)
    gain, shift, out_bias = vectors_ref[2:3, :], vectors_ref[3:4, :], vectors_ref[4:5, :]

    @pl.when(step == 0)
    def _():
        unit = standardize(tokens_ref[...].astype(F32))
        normed_s[...] = (unit * gain + shift).astype(BF)
        branch_s[...] = jnp.zeros_like(branch_s)
        back_s[...] = jnp.zeros_like(back_s)

    bias = up_bias_ref[pl.ds(pl.multiple_of(step * up_ref.shape[1], LANES), up_ref.shape[1])]
    hidden = dot(normed_s[...], up_ref[...]) + bias.astype(F32).reshape(1, -1)
    upstream = dot_nt(grads_ref[...], down_ref[...])
    below, density = gelu_parts(hidden)
    branch_s[...] += dot((hidden * below).astype(BF), down_ref[...])
    hidden_grad = (upstream * (below + hidden * density)).astype(BF)
    back_s[...] += dot_nt(hidden_grad, up_ref[...])

    @pl.when(step == pl.num_programs(0) - 1)
    def _():
        inputs = tokens_ref[...].astype(F32)
        cot = grads_ref[...].astype(F32)
        centred, factor = spread_of(inputs)
        unit = centred * factor
        back = back_s[...]
        base_ref[...] = inputs + branch_s[...] + out_bias
        rest_ref[...] = cot + norm_input_term(back, gain, unit, factor)
        small_ref[...] = jnp.zeros_like(small_ref)
        small_ref[0:1, :] = jnp.sum(cot, axis=0, keepdims=True)
        small_ref[1:2, :] = jnp.sum(back * unit, axis=0, keepdims=True)
        small_ref[2:3, :] = jnp.sum(back, axis=0, keepdims=True)


def local_part(tokens, grads, up_weight, up_bias, down_weight, vectors):
    tok_count, feature_width = tokens.shape
    hidden_width = up_weight.shape[1]
    step = 512
    own = whole(tok_count, feature_width)
    return call(
        local_kernel,
        inputs=[tokens, grads, up_weight, up_bias, down_weight, vectors],
        grid=(hidden_width // step,),
        in_specs=[
            own, own,
            pl.BlockSpec((feature_width, step), lambda i: (0, i)),
            whole(hidden_width),
            pl.BlockSpec((step, feature_width), lambda i: (i, 0)),
            whole(8, feature_width),
        ],
        out_specs=[own, own, whole(8, feature_width)],
        out_shape=[
            shaped((tok_count, feature_width), F32),
            shaped((tok_count, feature_width), F32),
            shaped((8, feature_width), F32),
        ],
        scratch_shapes=[
            pltpu.VMEM((tok_count, feature_width), BF),
            pltpu.VMEM((tok_count, feature_width), F32),
            pltpu.VMEM((tok_count, feature_width), F32),
        ],
        compiler_params=params(BIG),
        name="local",
    )


def lanes(rows):
    return lax.broadcasted_iota(jnp.int32, (rows, 2 * HEAD_DIM), 1)


def flipped(tile):
    return pltpu.roll(tile, HEAD_DIM, 1)


def joined(left, right):
    return jnp.where(lanes(left.shape[0]) < HEAD_DIM, left, flipped(right))


def half_turned(tile):
    place_in = lanes(tile.shape[0]) % HEAD_DIM
    low = pltpu.roll(tile, 2 * HEAD_DIM - ROT // 2, 1)
    high = pltpu.roll(tile, ROT // 2, 1)
    return jnp.where(place_in < ROT // 2, -low, jnp.where(place_in < ROT, high, 0.0))


def with_column(tile, lane, column):
    first = column.astype(BF).astype(F32)
    number = lanes(tile.shape[0])
    return jnp.where(number == lane, first, jnp.where(number == lane + 1, column - first, tile))


def heads_joined(values):
    heads = len(values)
    values = [joined(values[k], values[k + 1]) if k + 1 < heads else values[k] for k in range(0, heads, 2)]
    if heads % 2:
        values[-1] = jnp.where(lanes(values[-1].shape[0]) < HEAD_DIM, values[-1], 0.0)
    return jnp.concatenate(values, axis=1)


def attention_kernel(heads, blocks, plan, *refs):
    count = sum(len(sides) for sides, _ in plan)
    piece_refs, refs = list(refs[:count]), refs[count:]
    groups = [(sides, distances, [piece_refs.pop(0) for _ in sides]) for sides, distances in plan]
    (
        place_ref, tokens_ref, weight_ref, bias_ref, vectors_ref, out_weight_ref, cos_ref, sin_ref, seg_ref,
        local_ref, up_bias_ref, shared_ref, keep_ref, send_ref,
        weight_s, bias_s, out_weight_s, attended_s, query_s, key_s, value_s, back_s,
        query_grad_s, key_grad_s, value_grad_s, grad_s, grad_out_s, small_s,
    ) = refs
    place = place_ref[0]
    block, feature_width = tokens_ref.shape
    pair = 2 * HEAD_DIM
    scale = HEAD_DIM ** (-0.5)
    gain, shift = vectors_ref[0:1, :], vectors_ref[1:2, :]
    own_rows = pl.ds(pl.multiple_of(place * block, block), block)

    def rows_of(number):
        return pl.ds(pl.multiple_of(number * block, block), block)

    def side_rows(distance, side, count):
        own = place_ref[1] % (block // count)
        first = jnp.bitwise_xor(place, distance) * block + jnp.bitwise_xor(own, side) * count
        return pl.ds(pl.multiple_of(first, count), count)

    def together(refs, slot, part):
        return jnp.concatenate([ref[slot, part] for ref in refs], axis=0)

    def arrange(source, target):
        for head in range(heads):
            start = head * 3 * HEAD_DIM
            tile = source[:, start : start + pair].astype(F32)
            target[:, head * pair : (head + 1) * pair] = tile.astype(target.dtype)
            target[:, (heads + head) * pair : (heads + head + 1) * pair] = half_turned(tile).astype(target.dtype)
        values = [source[:, (3 * head + 2) * HEAD_DIM : (3 * head + 3) * HEAD_DIM] for head in range(heads)]
        values.append(jnp.zeros((source.shape[0], -heads * HEAD_DIM % pair), source.dtype))
        target[:, 2 * heads * pair :] = jnp.concatenate(values, axis=1).astype(target.dtype)

    arrange(weight_ref, weight_s)
    arrange(bias_ref, bias_s)
    out_weight_s[...] = jnp.zeros_like(out_weight_s)
    out_weight_s[: heads * HEAD_DIM, :] = out_weight_ref[...]

    def project(sides, refs, slot, distance):
        unit = standardize(together(refs, slot, 0).astype(F32))
        normed = (unit * gain + shift).astype(BF)
        whole_part = dot(normed, weight_s[...]) + bias_s[:1, :]
        whole_back = dot_nt(together(refs, slot, 1), out_weight_s[...])
        count = block // len(sides)
        for number, side in enumerate(sides):
            here = slice(number * count, (number + 1) * count)
            place_heads(side_rows(distance, side, count), whole_part[here], whole_back[here])

    def place_heads(rows, part, back_part):
        cosine, sine = cos_ref[rows, :], sin_ref[rows, :]
        number = lanes(part.shape[0])
        segment = seg_ref[rows, :]
        match = (number == HEAD_DIM + segment // 8) | (number == HEAD_DIM + 8 + segment % 8)
        coded = (number >= HEAD_DIM) & (number < HEAD_DIM + 16)
        query_code = jnp.where(coded & ~match, masked_score, 0.0)
        ones = (number >= HEAD_DIM + 16) & (number < HEAD_DIM + 18)
        key_code = jnp.where(match | ones, 1.0, 0.0)
        value_code = jnp.where((number >= HEAD_DIM) & (number < HEAD_DIM + 2), 1.0, 0.0)
        first = number < HEAD_DIM
        for head in range(heads):
            plain = part[:, head * pair : (head + 1) * pair]
            turned = part[:, (heads + head) * pair : (heads + head + 1) * pair]
            both = plain * cosine + turned * sine
            query_s[head, rows, :] = jnp.where(first, both * scale, query_code).astype(BF)
            key_s[head, rows, :] = jnp.where(first, flipped(both), key_code).astype(BF)
            start = 2 * heads * pair + head // 2 * pair
            tile = part[:, start : start + pair]
            back_tile = back_part[:, head // 2 * pair : head // 2 * pair + pair]
            if head % 2:
                tile, back_tile = flipped(tile), flipped(back_tile)
            value_s[head, rows, :] = jnp.where(first, tile, value_code).astype(BF)
            back_s[head, rows, :] = jnp.where(first, back_tile, 0.0).astype(BF)

    for sides, distances, refs in groups:
        for slot, distance in enumerate(distances):
            project(sides, refs, slot, distance)

    square = (block, block)
    lower = lax.broadcasted_iota(jnp.int32, square, 1) <= lax.broadcasted_iota(jnp.int32, square, 0)

    def attend(head, carry):
        def scores_of(number):
            start, stop = number * block, (number + 1) * block
            query = query_s[head, start:stop, :]
            near = jnp.where(lower, dot_nt(query, key_s[head, start:stop, :]), masked_score)
            return near, dot_nt(query, key_s[head, :start, :]) if number else None

        ahead = scores_of(0)
        for number in range(blocks):
            start, stop = number * block, (number + 1) * block
            near, far = ahead
            if number + 1 < blocks:
                ahead = scores_of(number + 1)
            top = jnp.max(near, axis=-1, keepdims=True)
            if number:
                top = jnp.maximum(top, jnp.max(far, axis=-1, keepdims=True))
            got = dot(jnp.exp(near - top).astype(BF), value_s[head, start:stop, :])
            if number:
                got = got + dot(jnp.exp(far - top).astype(BF), value_s[head, :start, :])
            total = got[:, HEAD_DIM : HEAD_DIM + 1]
            attended = got / total
            attended_s[head, start:stop, :] = attended.astype(BF)
            back = back_s[head, start:stop, :].astype(F32)
            delta = jnp.sum(attended * back, axis=-1, keepdims=True)
            log_total = top + jnp.log(total)
            query = query_s[head, start:stop, :].astype(F32)
            query_s[head, start:stop, :] = with_column(query, HEAD_DIM + 16, -log_total).astype(BF)
            back_s[head, start:stop, :] = with_column(back, HEAD_DIM, -delta).astype(BF)
        return carry

    lax.fori_loop(0, heads, attend, 0)

    def joined_rows(rows):
        return heads_joined([attended_s[head, rows, :].astype(F32) for head in range(heads)]).astype(BF)

    shared_ref[:block, feature_width:] = joined_rows(own_rows)[:, : heads * HEAD_DIM]

    total = jnp.zeros((out_weight_s.shape[0], feature_width), F32)
    for sides, distances, refs in groups:
        for slot, distance in enumerate(distances):
            rows = [joined_rows(side_rows(distance, side, block // len(sides))) for side in sides]
            total = total + dot_tn(jnp.concatenate(rows, axis=0), together(refs, slot, 1))
    grad_out_s[...] = total

    square = (block, block)
    lower = lax.broadcasted_iota(jnp.int32, square, 1) <= lax.broadcasted_iota(jnp.int32, square, 0)
    upper = lax.broadcasted_iota(jnp.int32, square, 0) <= lax.broadcasted_iota(jnp.int32, square, 1)

    def to_keys(rows, head, mask):
        query, back = query_s[head, rows, :], back_s[head, rows, :]
        scores = dot_nt(key_s[head, own_rows, :], query)
        if mask is not None:
            scores = jnp.where(mask, scores, masked_score)
        probs = jnp.exp(scores)
        score_grad = probs * dot_nt(value_s[head, own_rows, :], back)
        return dot(probs.astype(BF), back), dot(score_grad.astype(BF), query)

    def to_queries(rows, head, mask):
        key, value = key_s[head, rows, :], value_s[head, rows, :]
        scores = dot_nt(query_s[head, own_rows, :], key)
        if mask is not None:
            scores = jnp.where(mask, scores, masked_score)
        score_grad = jnp.exp(scores) * dot_nt(back_s[head, own_rows, :], value)
        return dot(score_grad.astype(BF), key)

    for head in range(heads):
        value_grad_s[head], key_grad_s[head] = to_keys(own_rows, head, upper)
        query_grad_s[head] = to_queries(own_rows, head, lower)

    def later(number, carry):
        rows = rows_of(number)
        for head in range(heads):
            value_grad, key_grad = to_keys(rows, head, None)
            value_grad_s[head] += value_grad
            key_grad_s[head] += key_grad
        return carry

    def earlier(number, carry):
        rows = rows_of(number)
        for head in range(heads):
            query_grad_s[head] += to_queries(rows, head, None)
        return carry

    lax.fori_loop(place + 1, blocks, later, 0)
    lax.fori_loop(0, place, earlier, 0)

    cosine, sine = cos_ref[own_rows, :], sin_ref[own_rows, :]
    tiles = []
    for head in range(heads):
        both = joined(query_grad_s[head] * scale, key_grad_s[head])
        both = both * cosine - half_turned(both * sine)
        value = value_grad_s[head]
        if head % 2 == 0:
            tiles += [both, value]
        else:
            tiles[-1] = joined(tiles[-1], both)
            tiles.append(joined(flipped(both), value))
    if heads % 2:
        tiles[-1] = jnp.where(lanes(block) < HEAD_DIM, tiles[-1], 0.0)
    mixed_grad = jnp.concatenate(tiles, axis=1).astype(BF)[:, : 3 * heads * HEAD_DIM]
    unit = standardize(tokens_ref[...].astype(F32))
    normed = (unit * gain + shift).astype(BF)
    normed_back = dot_nt(mixed_grad, weight_ref[...])
    shared_ref[:block, :feature_width] = normed_back.astype(BF)

    local_rows = feature_width // blocks
    holds, first = place_ref[2] == 1, pl.multiple_of(place_ref[3], local_rows)
    rows = jnp.where(holds, grad_out_s[pl.ds(first, local_rows), :], 0.0)
    shared_ref[block:, :feature_width] = rows.astype(BF)
    shared_ref[block:, feature_width:] = jnp.zeros((local_rows, heads * HEAD_DIM), BF)

    width = keep_ref.shape[2]
    grad_qkv = dot_tn(normed, mixed_grad).astype(BF)
    fill = jnp.zeros((feature_width, width - grad_qkv.shape[1]), BF)
    grad_s[...] = jnp.concatenate([grad_qkv, fill], axis=1).reshape(grad_s.shape)
    bit = place % 2
    for number in range(blocks // 2):
        keep_ref[number] = grad_s[2 * number + bit]
        send_ref[number * local_rows : (number + 1) * local_rows, :] = grad_s[2 * number + 1 - bit]

    piece = feature_width // 2
    probe_place = place_ref[1]
    sole = probe_place == 0
    small_s[...] = jnp.zeros_like(small_s)

    def put(row, values):
        small_s[row : row + 1, :piece] = values[:, :piece]
        small_s[row + 1 : row + 2, :piece] = values[:, piece:]

    for number in range(3):
        put(2 * number, jnp.where(sole, local_ref[number : number + 1, :], 0.0))
    put(6, jnp.sum(normed_back * unit, axis=0, keepdims=True))
    put(8, jnp.sum(normed_back, axis=0, keepdims=True))
    bias_grad = jnp.sum(mixed_grad.astype(F32), axis=0, keepdims=True)
    small_s[pl.ds(10 + 2 * probe_place, 1), :piece] = bias_grad[:, :piece]
    rest = bias_grad.shape[1] - piece
    small_s[pl.ds(11 + 2 * probe_place, 1), :rest] = bias_grad[:, piece:]
    small_s[pl.ds(10 + 2 * place_ref[4] + place, 1), :piece] = jnp.where(sole, up_bias_ref[...], 0.0)
    put_small(send_ref, blocks // 2 * local_rows, small_s[...])


def put_small(target, first, small):
    count = small.shape[0]
    high = small.astype(BF)
    target[first : first + count, : small.shape[1]] = high
    target[first + count : first + 2 * count, : small.shape[1]] = (small - high.astype(F32)).astype(BF)


def get_small(source, first, width):
    count = (source.shape[0] - first) // 2
    high = source[first : first + count, :width].astype(F32)
    return high + source[first + count :, :width].astype(F32)


def fold_kernel(place_ref, keep_ref, mine_ref, got_ref, *refs):
    count, local_rows, width = keep_ref.shape
    send_ref, total_s = refs[-2:]
    for number in range(count):
        got = got_ref[number * local_rows : (number + 1) * local_rows, :].astype(F32)
        total_s[number] = (keep_ref[number].astype(F32) + got).astype(BF)
    bit = place_ref[0]
    for number in range(count // 2):
        refs[0][number] = total_s[2 * number + bit]
        send_ref[number * local_rows : (number + 1) * local_rows, :] = total_s[2 * number + 1 - bit]
    if count == 1:
        send_ref[:local_rows, :] = total_s[0]
    small = get_small(mine_ref, count * local_rows, width) + get_small(got_ref, count * local_rows, width)
    put_small(send_ref, max(count // 2, 1) * local_rows, small)


def fold(bit, keep, mine, got, after):
    count, local_rows, width = keep.shape
    left = max(count // 2, 1) * local_rows + mine.shape[0] - count * local_rows
    halves = [shaped((count // 2, local_rows, width), BF)] if count > 1 else []
    return call(
        fold_kernel,
        inputs=[bit[None].astype(jnp.int32), keep, mine, got],
        after=after,
        in_specs=[SMEM] + [VMEM] * 3,
        out_specs=[VMEM] * (len(halves) + 1),
        out_shape=halves + [shaped((left, width), BF)],
        scratch_shapes=[pltpu.VMEM(keep.shape, BF)],
        compiler_params=params(8),
        name="fold",
    )


def pair_kernel(local_rows, place_ref, mine_ref, got_ref, out_ref):
    width = mine_ref.shape[1]
    odd = place_ref[0] == 1
    mine, got = mine_ref[:local_rows, :], got_ref[:local_rows, :]
    out_ref[:local_rows, :width] = jnp.where(odd, got, mine)
    out_ref[:local_rows, width:] = jnp.where(odd, mine, got)
    put_small(out_ref, local_rows, get_small(mine_ref, local_rows, width) + get_small(got_ref, local_rows, width))
    out_ref[local_rows:, width:] = jnp.zeros((out_ref.shape[0] - local_rows, width), BF)


def pair(core, mine, got, local_rows, after):
    return call(
        functools.partial(pair_kernel, local_rows),
        inputs=[core[None].astype(jnp.int32), mine, got],
        after=after,
        in_specs=[SMEM, VMEM, VMEM],
        out_specs=VMEM,
        out_shape=shaped((mine.shape[0], 2 * mine.shape[1]), BF),
        compiler_params=params(8),
        name="pair",
    )


def join_kernel(local_rows, mixed_width, blocks, place_ref, mine_ref, got_ref, qkv_ref, *vector_refs):
    *sum_refs, qkv_bias_ref, up_bias_ref = vector_refs
    width = mine_ref.shape[1] // 2
    upper = place_ref[0] == 1
    mine, got = mine_ref[:local_rows, :], got_ref[:local_rows, :]
    parts = []
    for side in (jnp.where(upper, got, mine), jnp.where(upper, mine, got)):
        parts += [side[:, :mixed_width], side[:, width : width + mixed_width]]
    qkv_ref[...] = jnp.concatenate([part.astype(F32) for part in parts], axis=1)
    small = get_small(mine_ref, local_rows, width) + get_small(got_ref, local_rows, width)
    piece = sum_refs[0].shape[0] // 2

    def rows(first, count, total):
        parts = [small[number : number + 1, :piece] for number in range(first, first + count)]
        return jnp.concatenate(parts, axis=1)[:, :total]

    for number, ref in enumerate(sum_refs):
        ref[...] = rows(2 * number, 2, 2 * piece).reshape(ref.shape)
    groups = qkv_bias_ref.shape[0] // mixed_width
    first = 2 * len(sum_refs)
    bias = [rows(first + 2 * number, 2, mixed_width) for number in range(groups)]
    qkv_bias_ref[...] = jnp.concatenate(bias, axis=1).reshape(qkv_bias_ref.shape)
    up_bias_ref[...] = rows(first + 2 * groups, blocks, blocks * piece).reshape(up_bias_ref.shape)


def join(upper, mine, got, local_rows, mixed_width, blocks, feature_width, after):
    vector = shaped((feature_width,), F32)
    return call(
        functools.partial(join_kernel, local_rows, mixed_width, blocks),
        inputs=[upper[None].astype(jnp.int32), mine, got],
        after=after,
        in_specs=[SMEM, VMEM, VMEM],
        out_specs=[VMEM] * 8,
        out_shape=[shaped((local_rows, 4 * mixed_width), F32)]
        + [vector] * 5
        + [shaped((4 * mixed_width,), F32), shaped((blocks * (feature_width // 2),), F32)],
        compiler_params=params(12),
        name="join",
    )


def attention(
    heads, blocks, numbers, pieces, tokens, weight, bias, vectors, out_weight, segments, local_small, up_bias, after
):
    tok_count, feature_width = tokens.shape
    pair = 2 * HEAD_DIM
    head_width = heads * HEAD_DIM
    mixed_width = 3 * head_width
    value_tiles = -(-heads // 2) * pair
    cos_table, sin_table = rotary_tables(SEQ)
    local_rows = feature_width // blocks
    width = -(-mixed_width // LANES) * LANES
    small_rows = -(-(10 + 2 * HEADS // heads + blocks) // 16) * 16
    return call(
        functools.partial(attention_kernel, heads, blocks, [plan for _, plan in pieces]),
        inputs=[array for arrays, _ in pieces for array in arrays] + [
            numbers, tokens, weight,
            jnp.broadcast_to(bias.astype(F32)[None], (8, bias.shape[0])), vectors,
            out_weight, cos_table, sin_table, segments[:, None], local_small, up_bias,
        ],
        after=after,
        in_specs=[VMEM] * sum(len(arrays) for arrays, _ in pieces) + [SMEM] + [VMEM] * 10,
        out_specs=[VMEM] * 3,
        out_shape=[
            shaped((tok_count + local_rows, feature_width + head_width), BF),
            shaped((blocks // 2, local_rows, width), BF),
            shaped((blocks // 2 * local_rows + 2 * small_rows, width), BF),
        ],
        scratch_shapes=[
            pltpu.VMEM((feature_width, 2 * heads * pair + value_tiles), BF),
            pltpu.VMEM((8, 2 * heads * pair + value_tiles), F32),
            pltpu.VMEM((value_tiles, feature_width), BF),
        ]
        + [pltpu.VMEM((heads, SEQ, pair), BF)] * 5
        + [pltpu.VMEM((heads, tok_count, pair), F32)] * 3
        + [
            pltpu.VMEM((blocks, local_rows, width), BF),
            pltpu.VMEM((value_tiles, feature_width), F32),
            pltpu.VMEM((small_rows, width), F32),
        ],
        compiler_params=params(50),
        name="attention",
    )


def hidden_kernel(first_call, *refs):
    if first_call:
        grad_down_in, grad_up_in, bias_grad_in = (None, None, None)
    else:
        grad_down_in, grad_up_in, bias_grad_in = refs[-9:-6]
        refs = refs[:-9] + refs[-6:]
    piece_refs, (up_ref, up_bias_ref, down_ref, vectors_ref) = refs[1:-10], refs[-10:-6]
    normed_ref, turned_ref, curve_ref, grad_down_ref, grad_up_ref, bias_grad_ref = refs[-6:]
    cot = jnp.concatenate([ref[0, 1] for ref in piece_refs], axis=0)
    unit = standardize(jnp.concatenate([ref[0, 0] for ref in piece_refs], axis=0).astype(F32))
    normed = (unit * vectors_ref[2:3, :] + vectors_ref[3:4, :]).astype(BF)
    normed_ref[...] = normed
    turned = normed.T
    turned_ref[...] = turned
    hidden = dot(normed, up_ref[...]) + up_bias_ref[...]
    upstream = dot_nt(cot, down_ref[...])
    below, density = gelu_parts(hidden)
    active = (hidden * below).astype(BF)
    hidden_grad = (upstream * (below + hidden * density)).astype(BF)
    curve_ref[...] = upstream * density * (2.0 - hidden * hidden)

    @pl.when(pl.program_id(0) == 0)
    def _():
        for before, target in (
            (grad_down_in, grad_down_ref), (grad_up_in, grad_up_ref), (bias_grad_in, bias_grad_ref),
        ):
            target[...] = jnp.zeros_like(target) if first_call else before[...]

    grad_down_ref[...] += dot_tn(active, cot)
    grad_up_ref[...] += dot(turned, hidden_grad)
    bias_grad_ref[...] += jnp.sum(hidden_grad.astype(F32), axis=0, keepdims=True)


def hidden_units(place, pieces, up_part, up_bias_part, down_part, vectors, before):
    arrays = [array for arrays, _ in pieces for array in arrays]
    slots, _, side_rows, feature_width = arrays[0].shape
    part_width = up_bias_part.shape[1]
    tok_count = len(arrays) * side_rows
    count = slots * tok_count

    def fixed(*shape):
        return pl.BlockSpec(shape, lambda i, place_ref: (0,) * len(shape))

    piece = pl.BlockSpec((1, 2, side_rows, feature_width), lambda i, place_ref: (i, 0, 0, 0))
    sums = [fixed(part_width, feature_width), fixed(feature_width, part_width), fixed(1, part_width)]
    return pl.pallas_call(
        functools.partial(hidden_kernel, before is None),
        grid_spec=pltpu.PrefetchScalarGridSpec(
            num_scalar_prefetch=1,
            grid=(slots,),
            in_specs=[piece] * len(arrays) + [
                pl.BlockSpec((feature_width, part_width), lambda i, place_ref: (0, place_ref[0])),
                fixed(1, part_width),
                pl.BlockSpec((part_width, feature_width), lambda i, place_ref: (place_ref[0], 0)),
                fixed(8, feature_width),
            ] + (sums if before else []),
            out_specs=[
                pl.BlockSpec((tok_count, feature_width), lambda i, place_ref: (i, 0)),
                pl.BlockSpec((feature_width, tok_count), lambda i, place_ref: (0, i)),
                pl.BlockSpec((tok_count, part_width), lambda i, place_ref: (i, 0)),
            ] + sums,
        ),
        out_shape=[
            shaped((count, feature_width), BF),
            shaped((feature_width, count), BF),
            shaped((count, part_width), F32),
            shaped((part_width, feature_width), F32),
            shaped((feature_width, part_width), F32),
            shaped((1, part_width), F32),
        ],
        compiler_params=params(BIG),
        name="hidden_units",
        cost_estimate=LIGHT,
    )(
        jnp.where(up_part.shape[1] > part_width, place, 0)[None].astype(jnp.int32),
        *arrays, up_part, up_bias_part, down_part, vectors, *(before[3:] if before else []),
    )


def share_kernel(probes, place_ref, dirs_ref, grad_up_ref, share_ref):
    blocks, local_rows, width = share_ref.shape
    part_width = grad_up_ref.shape[1]
    half = part_width // 2
    grad_up = grad_up_ref[...]
    own = jnp.where(place_ref[0] == 1, grad_up[:, half:], grad_up[:, :half]).astype(BF)
    row = lax.broadcasted_iota(jnp.int32, (1, width - half), 1)
    scores = jnp.zeros((1, width - half), F32)
    for number in range(probes):
        part = dirs_ref[:, number * part_width : (number + 1) * part_width].astype(F32)
        score = jnp.sum(jnp.sum(part * grad_up, axis=0, keepdims=True), axis=1, keepdims=True)
        high = score.astype(BF).astype(F32)
        scores = jnp.where(row == number, high, scores)
        scores = jnp.where(row == probes + number, score - high, scores)
    scores = jnp.broadcast_to(scores, (own.shape[0], width - half)).astype(BF)
    share_ref[...] = jnp.concatenate([own, scores], axis=1).reshape(share_ref.shape)


def share_of(core, dirs, grad_up, blocks, probes):
    feature_width, part_width = grad_up.shape
    width = -(-(part_width // 2 + 2 * probes) // LANES) * LANES
    return call(
        functools.partial(share_kernel, probes),
        inputs=[core[None].astype(jnp.int32), dirs, grad_up],
        in_specs=[SMEM, VMEM, VMEM],
        out_specs=VMEM,
        out_shape=shaped((blocks, feature_width // blocks, width), BF),
        compiler_params=params(16),
        name="share",
    )


def curvature_kernel(probes, halves, dirs_ref, *refs):
    token_refs, share_ref, (curvature_ref, total_s) = refs[: 3 * halves], refs[3 * halves], refs[-2:]
    step = pl.program_id(0)
    width = dirs_ref.shape[1]
    part_width = width // probes

    @pl.when(step == 0)
    def _():
        total_s[...] = jnp.zeros_like(total_s)

    for number in range(halves):
        normed_ref, turned_ref, curve_ref = token_refs[3 * number : 3 * number + 3]
        along = dot(normed_ref[...], dirs_ref[...])
        curve = curve_ref[...]
        weighted = []
        for k in range(probes):
            part = along[:, k * part_width : (k + 1) * part_width]
            weighted.append((part * curve).astype(BF))
        total_s[...] += dot(turned_ref[...], jnp.concatenate(weighted, axis=1))

    @pl.when(step == pl.num_programs(0) - 1)
    def _():
        curvature_ref[:, :, :width] = total_s[...].astype(BF).reshape(curvature_ref.shape[:2] + (width,))
        if curvature_ref.shape[2] > width:
            curvature_ref[:, :, width:] = share_ref[...]


def curvature_part(blocks, number, probes, halves, dirs, share, after):
    normed, _, curve = halves[0]
    (count, feature_width), part_width = normed.shape, curve.shape[1]
    width = probes * part_width
    steps = 2
    tok_count = count // steps
    more = ([], [], 0) if share is None else ([whole(*share.shape)], [share], share.shape[2])
    out = (blocks, feature_width // blocks, width + more[2])
    return call(
        functools.partial(curvature_kernel, probes, len(halves)),
        inputs=[dirs] + [array for half in halves for array in half] + more[1],
        after=after,
        grid=(steps,),
        in_specs=[pl.BlockSpec((feature_width, width), lambda i: (0, number))]
        + [
            pl.BlockSpec((tok_count, feature_width), lambda i: (i, 0)),
            pl.BlockSpec((feature_width, tok_count), lambda i: (0, i)),
            pl.BlockSpec((tok_count, part_width), lambda i: (i, 0)),
        ] * len(halves)
        + more[0],
        out_specs=whole(*out),
        out_shape=shaped(out, BF),
        scratch_shapes=[pltpu.VMEM((feature_width, width), F32)],
        compiler_params=params(BIG),
        name="curvature",
    )


def unpack_kernel(probes, share, got_ref, *refs):
    blocks, _, width = got_ref.shape
    part_width = (width - share) // probes
    curvature_ref = refs[-3] if share else refs[-1]
    number = pl.program_id(0)
    for block in range(blocks):
        here = slice(block * part_width, (block + 1) * part_width)
        for k in range(probes):
            @pl.when(number == k)
            def _(k=k):
                part = got_ref[block, :, k * part_width : (k + 1) * part_width]
                curvature_ref[0, :, here] = part.astype(F32)
    if share:
        up_ref, score_ref = refs[-2:]

        @pl.when(number == 0)
        def _():
            total = jnp.zeros(score_ref.shape, F32)
            for block in range(blocks):
                part = got_ref[block, :, width - share :]
                up_ref[:, block * share : (block + 1) * share] = part
                total = total + part[: total.shape[0], share - LANES :].astype(F32)
            score_ref[...] = total


def unpack(got, number, probes, share, probe_count, before, after):
    blocks, local_rows, width = got.shape
    part_width = (width - share) // probes
    out_specs = [pl.BlockSpec((1, local_rows, blocks * part_width), lambda i: (number * probes + i, 0, 0))]
    out_shape = [shaped((probe_count, local_rows, blocks * part_width), F32)]
    if share:
        out_specs += [whole(local_rows, blocks * share), whole(16, LANES)]
        out_shape += [shaped((local_rows, blocks * share), BF), shaped((16, LANES), F32)]
    return call(
        functools.partial(unpack_kernel, probes, share),
        inputs=[got],
        after=[*([] if before is None else [before]), *after],
        aliases={1: 0} if before is not None else {},
        grid=(probes,),
        in_specs=[whole(*got.shape)],
        out_specs=out_specs,
        out_shape=out_shape,
        compiler_params=params(BIG),
        name="unpack",
    )


def spread_kernel(blocks, half, place_ref, mine_ref, got_ref, out_ref):
    odd = place_ref[0] == 1
    stride = mine_ref.shape[1] // blocks
    for block in range(blocks):
        here = slice(block * stride, block * stride + half)
        mine, got = mine_ref[:, here], got_ref[:, here]
        both = jnp.concatenate([jnp.where(odd, got, mine), jnp.where(odd, mine, got)], axis=1)
        out_ref[:, block * 2 * half : (block + 1) * 2 * half] = both.astype(F32)


def spread(core, mine, got, blocks, half):
    return call(
        functools.partial(spread_kernel, blocks, half),
        inputs=[core[None].astype(jnp.int32), mine, got],
        in_specs=[SMEM, VMEM, VMEM],
        out_specs=VMEM,
        out_shape=shaped((mine.shape[0], blocks * 2 * half), F32),
        compiler_params=params(12),
        name="spread",
    )


def merge_kernel(tok_count, feature_width, place_ref, mine_ref, got_ref, merged_ref):
    odd = place_ref[0] == 1
    total = mine_ref[:, :feature_width].astype(F32) + got_ref[:, :feature_width].astype(F32)
    merged_ref[:, :feature_width] = total.astype(BF)
    mine, got = mine_ref[:, feature_width:], got_ref[:, feature_width:]
    merged_ref[:, feature_width:] = jnp.concatenate(
        [jnp.where(odd, got, mine), jnp.where(odd, mine, got)], axis=1
    )


def merge(core, mine, got, tok_count, feature_width):
    count, width = mine.shape
    return call(
        functools.partial(merge_kernel, tok_count, feature_width),
        inputs=[core[None].astype(jnp.int32), mine, got],
        in_specs=[SMEM, VMEM, VMEM],
        out_specs=VMEM,
        out_shape=shaped((count, 2 * width - feature_width), BF),
        compiler_params=params(12),
        name="merge",
    )


def finish_kernel(
    place_ref, mine_ref, got_ref, tokens_ref, base_ref, rest_ref, vectors_ref, out_weight_ref,
    layer_out_ref, input_grad_ref, grad_out_ref,
):
    tok_count, feature_width = tokens_ref.shape
    upper = place_ref[0] == 1
    mine, got = mine_ref[:tok_count, feature_width:], got_ref[:tok_count, feature_width:]
    attended = jnp.concatenate([jnp.where(upper, got, mine), jnp.where(upper, mine, got)], axis=1)
    layer_out_ref[...] = (base_ref[...] + dot(attended, out_weight_ref[...])).astype(BF)
    total = mine_ref[:, :feature_width].astype(F32) + got_ref[:, :feature_width].astype(F32)
    centred, factor = spread_of(tokens_ref[...].astype(F32))
    term = norm_input_term(total[:tok_count], vectors_ref[0:1, :], centred * factor, factor)
    input_grad_ref[...] = (rest_ref[...] + term).astype(BF)
    grad_out_ref[...] = total[tok_count:]


def finish(upper, mine, got, tokens, base, rest, vectors, out_weight, after):
    tok_count, feature_width = tokens.shape
    return call(
        finish_kernel,
        inputs=[upper[None].astype(jnp.int32), mine, got, tokens, base, rest, vectors, out_weight],
        after=after,
        in_specs=[SMEM] + [VMEM] * 7,
        out_specs=[VMEM] * 3,
        out_shape=[
            shaped(tokens.shape, BF),
            shaped(tokens.shape, BF),
            shaped((mine.shape[0] - tok_count, feature_width), F32),
        ],
        compiler_params=params(20),
        name="finish",
    )


def on_device(
    tokens,
    segment_ids,
    qkv_weight,
    qkv_bias,
    out_weight,
    out_bias,
    up_weight,
    up_bias,
    down_weight,
    down_bias,
    norm1_gain,
    norm1_bias,
    norm2_gain,
    norm2_bias,
    probe_dirs,
    out_grad,
):
    tok_count, feature_width = tokens.shape
    hidden_width = up_weight.shape[1]
    probe_count, local_rows = probe_dirs.shape[:2]
    groups = lax.axis_size("ex")
    probe_groups = lax.axis_size("probe")
    blocks = SEQ // tok_count
    rows = groups // blocks
    ex_place = lax.axis_index("ex")
    place = ex_place % blocks
    row_place = ex_place // blocks
    probe_place = lax.axis_index("probe")
    core, upper = probe_place % 2, probe_place // 2
    heads = HEADS // probe_groups
    head_width = heads * HEAD_DIM
    part_width = hidden_width // blocks
    fine = part_width // rows
    row_groups = None
    if rows > 1:
        row_groups = [[r * blocks + b for b in range(blocks)] for r in range(rows)]
    across = [[r * blocks + b for r in range(rows)] for b in range(blocks)]

    def swap(value, distance):
        return lax.ppermute(value, "ex", [(i, i ^ distance) for i in range(groups)])

    def swap_probe(value, distance):
        return lax.ppermute(value, "probe", [(i, i ^ distance) for i in range(probe_groups)])

    def over_rows(value):
        if rows > 1:
            return lax.psum_scatter(value, "ex", axis_index_groups=across, scatter_dimension=0, tiled=True)
        return value

    def my_part(value, axis):
        shape = value.shape
        split = shape[:axis] + (rows, blocks, fine) + shape[axis + 1 :]
        part = lax.dynamic_index_in_dim(value.reshape(split), place, axis + 1, keepdims=False)
        return part.reshape(shape[:axis] + (part_width,) + shape[axis + 1 :])

    half, quarter = tok_count // 2, tok_count // 4
    both = jnp.stack([tokens, out_grad])[None]
    mine = lax.dynamic_slice_in_dim(both, core * half, half, axis=2)
    share = lax.dynamic_slice_in_dim(both, probe_place * quarter, quarter, axis=2)
    near, aside, diagonal = swap(mine, 2), swap(mine, 1), swap(mine, 3)
    far, farthest = swap(share, 4), swap(share, 6)

    vectors = vectors_of(norm1_gain, norm1_bias, norm2_gain, norm2_bias, out_bias, down_bias)
    base, rest, local_small = local_part(tokens, out_grad, up_weight, up_bias, down_weight, vectors)

    first, second, third = stack(
        [mine, aside, near, diagonal, far, farthest], [(0, 1), (2, 3), (4, 5)], [local_small]
    )
    first_other, second_other = swap_probe(first, 1), swap_probe(second, 1)
    third_aside, third_over = swap(third, 1), swap_probe(third, 2)
    up_bias_part = my_part(up_bias, 0).astype(F32)[None]
    up_part, down_part = up_weight, down_weight
    if rows > 1:
        up_part, down_part = my_part(up_weight, 1), my_part(down_weight, 0)
    pieces = [
        ((first, first_other), ((0, 1), (0, 1))),
        ((second, second_other), ((0, 1), (2, 3))),
    ]
    units = hidden_units(place, pieces, up_part, up_bias_part, down_part, vectors, None)
    third_across = swap_probe(third_aside, 2)

    dirs = pack(probe_dirs, blocks, rows, [third_aside])
    dirs = lax.all_to_all(dirs, "ex", 0, 0, axis_index_groups=row_groups, tiled=True)
    dirs = dirs.reshape(blocks * local_rows, probe_count * part_width)
    if rows > 1:
        dirs = lax.all_gather(dirs, "ex", axis_index_groups=across, tiled=True)

    quarters = [third, third_over, third_aside, third_across]
    (quarters_all,) = stack(quarters, [(0, 1, 2, 3)], [units[5]])
    swapped = swap_probe(quarters_all, 1)
    swapped = [swapped[2 * k : 2 * k + 2] for k in range(4)]
    sides = (0, 2, 1, 3)
    pieces += [
        ((third, third_over, swapped[0], swapped[1]), (sides, (4, 6))),
        ((third_aside, third_across, swapped[2], swapped[3]), (sides, (5, 7))),
    ]
    halves = [units[:3]]
    units = hidden_units(place, pieces[2:], up_part, up_bias_part, down_part, vectors, units)
    halves.append(units[:3])
    grad_down, grad_up, grad_up_bias = units[3:]

    first_unit = probe_place * 3 * head_width
    block_rows = feature_width // blocks
    offset = place * block_rows - probe_place * head_width
    holds = (offset >= 0) & (offset < head_width)
    numbers = jnp.stack([place, probe_place, holds, jnp.where(holds, offset, 0), probe_groups])
    shared, keep, send = attention(
        heads, blocks, numbers.astype(jnp.int32), pieces, tokens,
        lax.dynamic_slice_in_dim(qkv_weight, first_unit, 3 * head_width, 1),
        lax.dynamic_slice_in_dim(qkv_bias, first_unit, 3 * head_width, 0), vectors,
        lax.dynamic_slice_in_dim(out_weight, probe_place * head_width, head_width, 0),
        lax.dynamic_slice_in_dim(segment_ids, row_place * SEQ, SEQ), local_small, grad_up_bias, [],
    )
    got = swap(send, 1)
    close = swap_probe(shared, 1)

    def to_owners(part):
        part = over_rows(part.reshape(feature_width, -1)).reshape(blocks, local_rows, -1)
        return lax.all_to_all(part, "ex", 0, 0, axis_index_groups=row_groups, tiled=True)

    chunk = probe_count // 2
    part = curvature_part(blocks, 0, chunk, halves, dirs, None, [shared])
    shared = merge(core, shared, close, tok_count, feature_width)
    close = swap_probe(shared, 2)
    keep, send = fold((place // 2) % 2, keep, send, got, [part])
    got = swap(send, 2)
    outgoing = [to_owners(tie(part, [send, shared]))]
    share = share_of(core, dirs, grad_up, blocks, probe_count)
    part = curvature_part(blocks, 1, chunk, halves, dirs, share, [send])
    layer_out, input_grad, grad_out_weight = finish(
        upper, shared, close, tokens, base, rest, vectors, out_weight, [part]
    )
    keep, send = fold((place // 4) % 2, keep, send, got, [part])
    (send,) = fold(place * 0, keep, send, swap(send, 4), [])
    outgoing.append(to_owners(tie(part, [send])))
    curvature = None
    if rows == 1:
        (curvature,) = unpack(outgoing[0], 0, chunk, 0, probe_count, None, [])
    send = pair(core, send, swap_probe(send, 1), block_rows, [])
    grad_qkv_weight, *small = join(
        upper, send, swap_probe(send, 2), block_rows, 3 * head_width, blocks, feature_width, [layer_out]
    )

    share_width = share.shape[2]
    half_width = part_width // 2
    if rows == 1:
        curvature, up_half, scores = unpack(outgoing[1], 1, chunk, share_width, probe_count, curvature, small[6:])
        grad_up_weight = spread(core, up_half, swap_probe(up_half, 1), blocks, half_width)
        scores = scores[0]
    else:
        whole_units = jnp.concatenate([got[:, :, : chunk * part_width] for got in outgoing], axis=2)
        whole_units = whole_units.reshape(blocks, local_rows, probe_count, rows, fine)
        curvature = whole_units.transpose(2, 1, 3, 0, 4).reshape(probe_count, local_rows, hidden_width)
        curvature = curvature.astype(F32)
        up_half = outgoing[1][:, :, chunk * part_width : chunk * part_width + half_width]
        both = lax.all_gather(up_half, "probe", axis_index_groups=[[0, 1], [2, 3]])
        both = both.transpose(2, 1, 0, 3).reshape(local_rows, blocks, rows, fine)
        grad_up_weight = both.transpose(0, 2, 1, 3).reshape(local_rows, hidden_width).astype(F32)
        scores = lax.psum(share[0, 0, -LANES:].astype(F32), "ex", axis_index_groups=row_groups)
    start = half_width % LANES
    scores = scores[start : start + probe_count] + scores[start + probe_count : start + 2 * probe_count]
    scores = scores[:, None]

    def over_groups(value):
        value = lax.all_gather(value, "ex", axis_index_groups=row_groups, tiled=True)
        return lax.dynamic_slice_in_dim(over_rows(value), place * local_rows, local_rows, 0)

    if rows > 1:
        grad_down = over_rows(grad_down)
        grad_qkv_weight, grad_out_weight = over_groups(grad_qkv_weight), over_groups(grad_out_weight)
        small = lax.psum(small, "ex", axis_index_groups=across)
        scores = lax.all_gather(scores, "ex", axis_index_groups=across, axis=1, tiled=True)
    sums, grad_qkv_bias, grad_up_bias = small[:5], small[5], small[6]
    if rows > 1:
        grad_up_bias = grad_up_bias.reshape(blocks, rows, fine).transpose(1, 0, 2).reshape(-1)
    return (
        layer_out,
        input_grad,
        grad_qkv_weight,
        grad_qkv_bias,
        grad_out_weight,
        sums[0],
        grad_up_weight,
        grad_up_bias,
        grad_down,
        sums[0],
        sums[3],
        sums[4],
        sums[1],
        sums[2],
        curvature,
        scores,
    )


def solution(mesh):
    in_specs = (
        P("ex", None),
        P(),
        P(),
        P(),
        P(),
        P(),
        P(),
        P(),
        P(),
        P(),
        P(),
        P(),
        P(),
        P(),
        P("probe", "ex", None),
        P("ex", None),
    )
    out_specs = (
        P("ex", None),
        P("ex", None),
        P("ex", None),
        P(),
        P("ex", None),
        P(),
        P("ex", None),
        P(),
        P("ex", None),
        P(),
        P(),
        P(),
        P(),
        P(),
        P("probe", "ex", None),
        P("probe", None),
    )
    return jax.shard_map(
        on_device, mesh=mesh, in_specs=in_specs, out_specs=out_specs, check_vma=False
    )
```

```python
import functools

import jax
import jax.numpy as jnp
import numpy as np
from jax import lax
from jax.experimental import pallas as pl
from jax.experimental.pallas import tpu as pltpu
from jax.sharding import PartitionSpec as P

HEADS = 12
HEAD_DIM = 64
ROT = 16
SEQ = 2048

BF = jnp.bfloat16
F32 = jnp.float32
eps_norm = 1e-05
masked_score = -1e30
half_root = 0.7071067811865476
gauss_peak = 0.3989422804014327
MB = 1024 * 1024
LANES = 128
LIGHT = pl.CostEstimate(flops=1000, bytes_accessed=1000, transcendentals=0)
BIG = 58


def dot(a, b):
    return jnp.dot(a, b, preferred_element_type=F32)


def dot_nt(a, b):
    return lax.dot_general(a, b, (((1,), (1,)), ((), ())), preferred_element_type=F32)


def dot_tn(a, b):
    return lax.dot_general(a, b, (((0,), (0,)), ((), ())), preferred_element_type=F32)


def spread_of(features):
    center = jnp.mean(features, axis=-1, keepdims=True)
    centred = features - center
    spread = jnp.mean(centred * centred, axis=-1, keepdims=True)
    return centred, lax.rsqrt(spread + eps_norm)


def standardize(features):
    centred, factor = spread_of(features)
    return centred * factor


def norm_input_term(grad, gain_row, unit, factor):
    unit_grad = grad * gain_row
    inner = unit_grad - jnp.mean(unit_grad, -1, keepdims=True)
    return (inner - unit * jnp.mean(unit_grad * unit, -1, keepdims=True)) * factor


def gelu_parts(pre_act):
    below = 0.5 + 0.5 * lax.erf(pre_act * half_root)
    density = gauss_peak * jnp.exp(-0.5 * pre_act * pre_act)
    return below, density


def rotary_tables(count):
    steps = np.arange(ROT // 2, dtype=np.float32) * np.float32(2.0 / ROT)
    inverse = np.power(np.float32(10000.0), -steps).astype(np.float32)
    angles = np.arange(count, dtype=np.float32)[:, None] * inverse[None, :]
    angles = np.concatenate([angles, angles], axis=1)
    cosine = np.ones((count, HEAD_DIM), np.float32)
    sine = np.zeros((count, HEAD_DIM), np.float32)
    cosine[:, :ROT], sine[:, :ROT] = np.cos(angles), np.sin(angles)
    return np.concatenate([cosine, cosine], axis=1), np.concatenate([sine, sine], axis=1)


def params(limit_mb, **more):
    return pltpu.CompilerParams(vmem_limit_bytes=limit_mb * MB, **more)


def shaped(shape, dtype):
    return jax.ShapeDtypeStruct(shape, dtype)


def whole(*shape):
    return pl.BlockSpec(shape, lambda i: (0,) * len(shape))


VMEM = pl.BlockSpec(memory_space=pltpu.VMEM)
SMEM = pl.BlockSpec(memory_space=pltpu.SMEM)
ANY = pl.BlockSpec(memory_space=pl.ANY)


def call(kernel, *, inputs, in_specs, after=(), aliases=None, **more):
    spare = len(after)

    def body(*refs):
        kernel(*refs[: len(inputs)], *refs[len(inputs) + spare :])

    return pl.pallas_call(
        body, in_specs=list(in_specs) + [ANY] * spare, input_output_aliases=aliases or {},
        cost_estimate=LIGHT, **more,
    )(*inputs, *after)


def tie(value, after):
    return call(
        lambda value_ref, out_ref: None,
        inputs=[value],
        after=after,
        aliases={0: 0},
        in_specs=[ANY],
        out_specs=ANY,
        out_shape=shaped(value.shape, value.dtype),
        name="tie",
    )


def pack_kernel(dirs_ref, packed_ref, sems):
    probes = dirs_ref.shape[0]
    blocks, _, width = packed_ref.shape
    part_width = width // probes
    copies = []
    for block in range(blocks):
        for k in range(probes):
            source = dirs_ref.at[k, :, block * part_width : (block + 1) * part_width]
            target = packed_ref.at[block, :, k * part_width : (k + 1) * part_width]
            copies.append(pltpu.make_async_copy(source, target, sems.at[len(copies)]))
    for copy in copies:
        copy.start()
    for copy in copies:
        copy.wait()


def pack(dirs, blocks, rows, after):
    probes, local_rows, hidden_width = dirs.shape
    part_width = hidden_width // blocks
    if rows > 1:
        split = dirs.reshape(probes, local_rows, rows, blocks, part_width // rows)
        return split.transpose(3, 1, 0, 2, 4).reshape(blocks, local_rows, probes * part_width)
    return call(
        pack_kernel,
        inputs=[dirs],
        after=after,
        in_specs=[ANY],
        out_specs=ANY,
        out_shape=shaped((blocks, local_rows, probes * part_width), dirs.dtype),
        scratch_shapes=[pltpu.SemaphoreType.DMA((blocks * probes,))],
        compiler_params=params(8),
        name="pack",
    )


def slices_kernel(place_ref, tokens_ref, grads_ref, half_ref, quarter_ref):
    for part, source in enumerate((tokens_ref, grads_ref)):
        for target, number in ((half_ref, place_ref[0]), (quarter_ref, place_ref[1])):
            count = target.shape[2]
            target[0, part] = source[pl.ds(pl.multiple_of(number * count, count), count), :]


def slices_of(core, probe_place, probe_groups, tokens, grads):
    tok_count, feature_width = tokens.shape
    sizes = (tok_count // 2, tok_count // probe_groups)
    return call(
        slices_kernel,
        inputs=[jnp.stack([core, probe_place]).astype(jnp.int32), tokens, grads],
        in_specs=[SMEM, VMEM, VMEM],
        out_specs=[VMEM] * 2,
        out_shape=[shaped((1, 2, size, feature_width), BF) for size in sizes],
        compiler_params=params(8),
        name="slices",
    )


def stack_kernel(plan, *refs):
    sources, targets = refs[: -len(plan)], refs[-len(plan) :]
    for parts, target in zip(plan, targets):
        number = 0
        for part in parts:
            count = sources[part].shape[0]
            target[number : number + count] = sources[part][...]
            number += count


def stack(sources, plan, after):
    heights = [sum(sources[part].shape[0] for part in parts) for parts in plan]
    return call(
        functools.partial(stack_kernel, plan),
        inputs=sources,
        after=after,
        in_specs=[VMEM] * len(sources),
        out_specs=[VMEM] * len(plan),
        out_shape=[shaped((n,) + sources[parts[0]].shape[1:], BF) for n, parts in zip(heights, plan)],
        compiler_params=params(8),
        name="stack",
    )


def vectors_kernel(groups, blocks, *refs):
    *sources, first_bias, second_bias, qkv_bias_ref, segment_ref, vectors_ref = refs
    vectors_ref[...] = jnp.zeros_like(vectors_ref)
    for number, source in enumerate(sources):
        vectors_ref[number : number + 1, :] = source[...].reshape(1, -1)
    total = first_bias[...].astype(F32) + second_bias[...].astype(F32)
    vectors_ref[len(sources) : len(sources) + 1, :] = total.reshape(1, -1)
    width = qkv_bias_ref.shape[0] // groups
    bias = qkv_bias_ref[...].astype(F32).reshape(1, -1)
    for number in range(groups):
        vectors_ref[8 + number : 9 + number, :width] = bias[:, number * width : (number + 1) * width]
    block = segment_ref.shape[0] // blocks
    for number in range(blocks):
        row = segment_ref[number * block : (number + 1) * block].astype(F32).reshape(1, -1)
        vectors_ref[16 + number : 17 + number, :block] = row


def vectors_of(groups, blocks, *sources):
    return call(
        functools.partial(vectors_kernel, groups, blocks),
        inputs=list(sources),
        in_specs=[VMEM] * len(sources),
        out_specs=VMEM,
        out_shape=shaped((16 + blocks, sources[0].shape[0]), F32),
        compiler_params=params(4),
        name="vectors",
    )


def local_kernel(
    tokens_ref, grads_ref, up_ref, up_bias_ref, down_ref, vectors_ref,
    base_ref, rest_ref, small_ref, normed_s, branch_s, back_s,
):
    step = pl.program_id(0)
    gain, shift, out_bias = vectors_ref[2:3, :], vectors_ref[3:4, :], vectors_ref[4:5, :]

    @pl.when(step == 0)
    def _():
        unit = standardize(tokens_ref[...].astype(F32))
        normed_s[...] = (unit * gain + shift).astype(BF)
        branch_s[...] = jnp.zeros_like(branch_s)
        back_s[...] = jnp.zeros_like(back_s)

    bias = up_bias_ref[pl.ds(pl.multiple_of(step * up_ref.shape[1], LANES), up_ref.shape[1])]
    hidden = dot(normed_s[...], up_ref[...]) + bias.astype(F32).reshape(1, -1)
    upstream = dot_nt(grads_ref[...], down_ref[...])
    below, density = gelu_parts(hidden)
    branch_s[...] += dot((hidden * below).astype(BF), down_ref[...])
    hidden_grad = (upstream * (below + hidden * density)).astype(BF)
    back_s[...] += dot_nt(hidden_grad, up_ref[...])

    @pl.when(step == pl.num_programs(0) - 1)
    def _():
        inputs = tokens_ref[...].astype(F32)
        cot = grads_ref[...].astype(F32)
        centred, factor = spread_of(inputs)
        unit = centred * factor
        back = back_s[...]
        base_ref[...] = inputs + branch_s[...] + out_bias
        rest_ref[...] = cot + norm_input_term(back, gain, unit, factor)
        small_ref[...] = jnp.zeros_like(small_ref)
        small_ref[0:1, :] = jnp.sum(cot, axis=0, keepdims=True)
        small_ref[1:2, :] = jnp.sum(back * unit, axis=0, keepdims=True)
        small_ref[2:3, :] = jnp.sum(back, axis=0, keepdims=True)


def local_part(tokens, grads, up_weight, up_bias, down_weight, vectors):
    tok_count, feature_width = tokens.shape
    hidden_width = up_weight.shape[1]
    step = 512
    own = whole(tok_count, feature_width)
    return call(
        local_kernel,
        inputs=[tokens, grads, up_weight, up_bias, down_weight, vectors],
        grid=(hidden_width // step,),
        in_specs=[
            own, own,
            pl.BlockSpec((feature_width, step), lambda i: (0, i)),
            whole(hidden_width),
            pl.BlockSpec((step, feature_width), lambda i: (i, 0)),
            whole(8, feature_width),
        ],
        out_specs=[own, own, whole(8, feature_width)],
        out_shape=[
            shaped((tok_count, feature_width), F32),
            shaped((tok_count, feature_width), F32),
            shaped((8, feature_width), F32),
        ],
        scratch_shapes=[
            pltpu.VMEM((tok_count, feature_width), BF),
            pltpu.VMEM((tok_count, feature_width), F32),
            pltpu.VMEM((tok_count, feature_width), F32),
        ],
        compiler_params=params(BIG),
        name="local",
    )


def lanes(rows):
    return lax.broadcasted_iota(jnp.int32, (rows, 2 * HEAD_DIM), 1)


def flipped(tile):
    return pltpu.roll(tile, HEAD_DIM, 1)


def joined(left, right):
    return jnp.where(lanes(left.shape[0]) < HEAD_DIM, left, flipped(right))


def half_turned(tile):
    place_in = lanes(tile.shape[0]) % HEAD_DIM
    low = pltpu.roll(tile, 2 * HEAD_DIM - ROT // 2, 1)
    high = pltpu.roll(tile, ROT // 2, 1)
    return jnp.where(place_in < ROT // 2, -low, jnp.where(place_in < ROT, high, 0.0))


def with_column(tile, lane, column):
    first = column.astype(BF).astype(F32)
    number = lanes(tile.shape[0])
    return jnp.where(number == lane, first, jnp.where(number == lane + 1, column - first, tile))


def heads_joined(values):
    heads = len(values)
    values = [joined(values[k], values[k + 1]) if k + 1 < heads else values[k] for k in range(0, heads, 2)]
    if heads % 2:
        values[-1] = jnp.where(lanes(values[-1].shape[0]) < HEAD_DIM, values[-1], 0.0)
    return jnp.concatenate(values, axis=1)


def attention_kernel(heads, blocks, count, plan, *refs):
    array_refs, refs = refs[:count], refs[count:]
    (
        place_ref, tokens_ref, weight_ref, vectors_ref, out_weight_ref, cos_ref, sin_ref,
        query_s, key_s, value_s, back_s, unit_s, attended_ref, grad_out_ref,
        window_s, weight_s, bias_s, out_weight_s, attended_s, query_code_s, key_code_s, grad_out_s, sems,
    ) = refs
    place, probe_place = place_ref[0], place_ref[1]
    block, feature_width = tokens_ref.shape
    pair = 2 * HEAD_DIM
    scale = HEAD_DIM ** (-0.5)
    gain, shift = vectors_ref[0:1, :], vectors_ref[1:2, :]
    own_rows = pl.ds(pl.multiple_of(place * block, block), block)
    head_width = heads * HEAD_DIM
    mixed_width = 3 * head_width

    first = probe_place * mixed_width // LANES * LANES
    columns = pl.ds(pl.multiple_of(first, LANES), window_s.shape[1])
    rows = pl.ds(pl.multiple_of(probe_place * head_width, HEAD_DIM), head_width)
    copies = [
        pltpu.make_async_copy(weight_ref.at[:, columns], window_s, sems.at[0]),
        pltpu.make_async_copy(out_weight_ref.at[rows, :], out_weight_s.at[:head_width, :], sems.at[1]),
    ]
    for copy in copies:
        copy.start()

    def rows_of(number):
        return pl.ds(pl.multiple_of(number * block, block), block)

    def side_rows(distance, side, count):
        own = place_ref[1] % (block // count)
        first = jnp.bitwise_xor(place, distance) * block + jnp.bitwise_xor(own, side) * count
        return pl.ds(pl.multiple_of(first, count), count)

    def together(refs, slot, part):
        return jnp.concatenate([array_refs[ref][base + slot, part] for ref, base in refs], axis=0)

    def arrange(source, target):
        for head in range(heads):
            start = head * 3 * HEAD_DIM
            tile = source[:, start : start + pair].astype(F32)
            target[:, head * pair : (head + 1) * pair] = tile.astype(target.dtype)
            target[:, (heads + head) * pair : (heads + head + 1) * pair] = half_turned(tile).astype(target.dtype)
        values = [source[:, (3 * head + 2) * HEAD_DIM : (3 * head + 3) * HEAD_DIM] for head in range(heads)]
        values.append(jnp.zeros((source.shape[0], -heads * HEAD_DIM % pair), source.dtype))
        target[:, 2 * heads * pair :] = jnp.concatenate(values, axis=1).astype(target.dtype)

    number = lanes(block)
    ones = (number >= HEAD_DIM + 16) & (number < HEAD_DIM + 18)
    coded = (number >= HEAD_DIM) & (number < HEAD_DIM + 16)
    for index in range(blocks):
        segment = jnp.broadcast_to(vectors_ref[16 + index : 17 + index, :block], (pair, block)).T
        segment = segment.astype(jnp.int32)
        match = (number == HEAD_DIM + segment // 8) | (number == HEAD_DIM + 8 + segment % 8)
        here = slice(index * block, (index + 1) * block)
        query_code_s[here, :] = jnp.where(coded & ~match, masked_score, 0.0)
        key_code_s[here, :] = jnp.where(match | ones, 1.0, 0.0)

    out_weight_s[head_width:, :] = jnp.zeros((out_weight_s.shape[0] - head_width, feature_width), BF)
    copies[0].wait()
    odd = probe_place * mixed_width % LANES != 0
    window = window_s[...]
    weight = jnp.where(odd, window[:, HEAD_DIM : HEAD_DIM + mixed_width], window[:, :mixed_width])
    arrange(weight, weight_s)
    bias = vectors_ref[pl.ds(8 + probe_place, 1), :mixed_width]
    arrange(jnp.broadcast_to(bias, (8, mixed_width)), bias_s)
    copies[1].wait()

    def project(sides, refs, slot, distance):
        unit = standardize(together(refs, slot, 0).astype(F32))
        normed = (unit * gain + shift).astype(BF)
        low = unit.astype(BF)
        whole_part = dot(normed, weight_s[...]) + bias_s[:1, :]
        whole_back = dot_nt(together(refs, slot, 1), out_weight_s[...])
        count = block // len(sides)
        for number, side in enumerate(sides):
            here = slice(number * count, (number + 1) * count)
            rows = side_rows(distance, side, count)
            unit_s[rows, :] = low[here]
            place_heads(rows, whole_part[here], whole_back[here])

    def place_heads(rows, part, back_part):
        cosine, sine = cos_ref[rows, :], sin_ref[rows, :]
        number = lanes(part.shape[0])
        query_code, key_code = query_code_s[rows, :], key_code_s[rows, :]
        value_code = jnp.where((number >= HEAD_DIM) & (number < HEAD_DIM + 2), 1.0, 0.0)
        first = number < HEAD_DIM
        for head in range(heads):
            plain = part[:, head * pair : (head + 1) * pair]
            turned = part[:, (heads + head) * pair : (heads + head + 1) * pair]
            both = plain * cosine + turned * sine
            query_s[head, rows, :] = jnp.where(first, both * scale, query_code).astype(BF)
            key_s[head, rows, :] = jnp.where(first, flipped(both), key_code).astype(BF)
            start = 2 * heads * pair + head // 2 * pair
            tile = part[:, start : start + pair]
            back_tile = back_part[:, head // 2 * pair : head // 2 * pair + pair]
            if head % 2:
                tile, back_tile = flipped(tile), flipped(back_tile)
            value_s[head, rows, :] = jnp.where(first, tile, value_code).astype(BF)
            back_s[head, rows, :] = jnp.where(first, back_tile, 0.0).astype(BF)

    for sides, distances, refs in plan:
        for slot, distance in enumerate(distances):
            project(sides, refs, slot, distance)

    square = (block, block)
    lower = lax.broadcasted_iota(jnp.int32, square, 1) <= lax.broadcasted_iota(jnp.int32, square, 0)

    def attend(head, carry):
        def scores_of(number):
            start, stop = number * block, (number + 1) * block
            query = query_s[head, start:stop, :]
            near = jnp.where(lower, dot_nt(query, key_s[head, start:stop, :]), masked_score)
            return near, dot_nt(query, key_s[head, :start, :]) if number else None

        ahead = scores_of(0)
        for number in range(blocks):
            start, stop = number * block, (number + 1) * block
            near, far = ahead
            if number + 1 < blocks:
                ahead = scores_of(number + 1)
            top = jnp.max(near, axis=-1, keepdims=True)
            if number:
                top = jnp.maximum(top, jnp.max(far, axis=-1, keepdims=True))
            got = dot(jnp.exp(near - top).astype(BF), value_s[head, start:stop, :])
            if number:
                got = got + dot(jnp.exp(far - top).astype(BF), value_s[head, :start, :])
            total = got[:, HEAD_DIM : HEAD_DIM + 1]
            attended = got / total
            attended_s[head, start:stop, :] = attended.astype(BF)
            back = back_s[head, start:stop, :].astype(F32)
            delta = jnp.sum(attended * back, axis=-1, keepdims=True)
            log_total = top + jnp.log(total)
            query = query_s[head, start:stop, :].astype(F32)
            query_s[head, start:stop, :] = with_column(query, HEAD_DIM + 16, -log_total).astype(BF)
            back_s[head, start:stop, :] = with_column(back, HEAD_DIM, -delta).astype(BF)
        return carry

    lax.fori_loop(0, heads, attend, 0)

    def joined_rows(rows):
        return heads_joined([attended_s[head, rows, :].astype(F32) for head in range(heads)]).astype(BF)

    attended_ref[...] = joined_rows(own_rows)[:, : heads * HEAD_DIM]

    total = jnp.zeros((out_weight_s.shape[0], feature_width), F32)
    for sides, distances, refs in plan:
        for slot, distance in enumerate(distances):
            rows = [joined_rows(side_rows(distance, side, block // len(sides))) for side in sides]
            total = total + dot_tn(jnp.concatenate(rows, axis=0), together(refs, slot, 1))
    grad_out_s[...] = total
    holds, first = place_ref[2] == 1, pl.multiple_of(place_ref[3], grad_out_ref.shape[0])
    rows = jnp.where(holds, grad_out_s[pl.ds(first, grad_out_ref.shape[0]), :], 0.0)
    grad_out_ref[...] = rows.astype(BF)


def attention_back_kernel(
    heads, blocks, place_ref, query_s, key_s, value_s, back_s, unit_ref, attended_ref, grad_out_ref, weight_ref,
    vectors_ref, cos_ref, sin_ref,
    keep_ref, send_ref,
    query_grad_s, key_grad_s, both_s, value_grad_s, mixed_s, total_s, small_s, window_s, sems,
):
    place, probe_place = place_ref[0], place_ref[1]
    block, head_width = attended_ref.shape
    feature_width = unit_ref.shape[1]
    mixed_width = 3 * head_width
    scale = HEAD_DIM ** (-0.5)
    first = probe_place * mixed_width // LANES * LANES
    columns = pl.ds(pl.multiple_of(first, LANES), window_s.shape[1])
    copy = pltpu.make_async_copy(weight_ref.at[:, columns], window_s, sems.at[0])
    copy.start()
    square = (block, block)
    upper = lax.broadcasted_iota(jnp.int32, square, 0) <= lax.broadcasted_iota(jnp.int32, square, 1)

    def through(head, carry):
        query_grad_s[...] = jnp.zeros_like(query_grad_s)
        for number in range(blocks):
            start, stop = number * block, (number + 1) * block
            key, value = key_s[head, start:stop, :], value_s[head, start:stop, :]
            key_grad = value_grad = None
            for rows, mask in ((slice(start, stop), upper), (slice(stop, blocks * block), None)):
                if rows.start == rows.stop:
                    continue
                query, back = query_s[head, rows, :], back_s[head, rows, :]
                scores = dot_nt(key, query)
                if mask is not None:
                    scores = jnp.where(mask, scores, masked_score)
                probs = jnp.exp(scores)
                score_grad = (probs * dot_nt(value, back)).astype(BF)
                value_term, key_term = dot(probs.astype(BF), back), dot(score_grad, query)
                value_grad = value_term if value_grad is None else value_grad + value_term
                key_grad = key_term if key_grad is None else key_grad + key_term
                query_grad_s[rows, :] += dot_tn(score_grad, key)
            key_grad_s[start:stop, :] = key_grad
            value_grad_s[head, start:stop, :] = value_grad.astype(BF)
        for number in range(blocks):
            rows = slice(number * block, (number + 1) * block)
            both = joined(query_grad_s[rows, :] * scale, key_grad_s[rows, :])
            both = both * cos_ref[rows, :] - half_turned(both * sin_ref[rows, :])
            both_s[head, rows, :] = both.astype(BF)
        return carry

    lax.fori_loop(0, heads, through, 0)

    for number in range(blocks):
        rows = slice(number * block, (number + 1) * block)
        tiles = []
        for head in range(heads):
            both, value = both_s[head, rows, :].astype(F32), value_grad_s[head, rows, :].astype(F32)
            if head % 2 == 0:
                tiles += [both, value]
            else:
                tiles[-1] = joined(tiles[-1], both)
                tiles.append(joined(flipped(both), value))
        if heads % 2:
            tiles[-1] = jnp.where(lanes(block) < HEAD_DIM, tiles[-1], 0.0)
        mixed_s[rows, :] = jnp.concatenate(tiles, axis=1).astype(BF)

    total_s[...] = dot_tn(unit_ref[...], mixed_s[...])
    sums = jnp.sum(mixed_s[...].astype(F32), axis=0, keepdims=True)
    copy.wait()
    odd = probe_place * mixed_width % LANES != 0
    window = window_s[...]
    weight = jnp.where(odd, window[:, HEAD_DIM : HEAD_DIM + mixed_width], window[:, :mixed_width])

    own_rows = pl.ds(pl.multiple_of(place * block, block), block)
    mixed_own = mixed_s[own_rows, :][:, :mixed_width]
    normed_back = dot_nt(mixed_own, weight).astype(BF)

    local_rows = grad_out_ref.shape[0]
    first = pl.multiple_of(place * local_rows, local_rows)
    pick = lax.broadcasted_iota(jnp.int32, (local_rows, feature_width), 1) == first + lax.broadcasted_iota(
        jnp.int32, (local_rows, feature_width), 0
    )
    gain, shift = [
        jnp.sum(jnp.where(pick, vectors_ref[k : k + 1, :], 0.0), axis=1, keepdims=True) for k in range(2)
    ]
    grad_qkv = (total_s[pl.ds(first, local_rows), :] * gain + sums * shift).astype(BF)

    wide = weight.astype(F32)
    columns = [
        jnp.sum(wide * total_s[:, :mixed_width], axis=1, keepdims=True),
        jnp.sum(wide * sums[:, :mixed_width], axis=1, keepdims=True),
    ]
    number = lax.broadcasted_iota(jnp.int32, (feature_width, LANES), 1)
    columns = jnp.where(number == 0, columns[0], jnp.where(number == 1, columns[1], 0.0)).T
    piece = feature_width // 2
    small_s[...] = jnp.zeros_like(small_s)
    for k in range(2):
        for part in range(2):
            here = slice(part * piece, (part + 1) * piece)
            small_s[2 * k + part : 2 * k + part + 1, :piece] = columns[k : k + 1, here]
    small_s[pl.ds(4 + 2 * probe_place, 1), :piece] = sums[:, :piece]
    small_s[pl.ds(5 + 2 * probe_place, 1), : mixed_width - piece] = sums[:, piece:mixed_width]
    half, few = block // 2, local_rows // 2
    third = head_width
    odd = probe_place % 2 == 1

    def halves(value):
        low, high = value[: value.shape[0] // 2], value[value.shape[0] // 2 :]
        return jnp.where(odd, high, low), jnp.where(odd, low, high)

    attended, grad_out = attended_ref[...], grad_out_ref[...]
    for number, target in enumerate((keep_ref, send_ref)):
        target[...] = jnp.zeros_like(target)
        target[:half, :feature_width] = halves(normed_back)[number]
        target[:half, feature_width:] = halves(attended)[number]
        target[half : half + few, :feature_width] = halves(grad_out)[number]
        part = halves(grad_qkv)[number]
        target[half : half + few, feature_width:] = part[:, :third]
        target[half + few : half + 2 * few, : 2 * third] = part[:, third : 3 * third]
        put_small(target, half + 2 * few, small_s[...])


def put_small(target, first, small):
    width = small.shape[1]
    high = small.astype(BF)
    target[first:, :width] = high
    target[first:, width : 2 * width] = (small - high.astype(F32)).astype(BF)


def get_small(source, first, width):
    return source[first:, :width].astype(F32) + source[first:, width : 2 * width].astype(F32)


def attention(heads, blocks, numbers, pieces, tokens, qkv_weight, vectors, out_weight, after):
    tok_count, feature_width = tokens.shape
    pair = 2 * HEAD_DIM
    head_width = heads * HEAD_DIM
    value_tiles = -(-heads // 2) * pair
    arrays, plan = [], []
    for refs, (sides, distances) in pieces:
        numbered = []
        for array, base in refs:
            if not any(array is other for other in arrays):
                arrays.append(array)
            numbered.append(([array is other for other in arrays].index(True), base))
        plan.append((sides, distances, numbered))
    cos_table, sin_table = rotary_tables(SEQ)
    per_head = shaped((heads, SEQ, pair), BF)
    window = -(-(3 * head_width) // LANES) * LANES
    return call(
        functools.partial(attention_kernel, heads, blocks, len(arrays), plan),
        inputs=arrays + [numbers, tokens, qkv_weight, vectors, out_weight, cos_table, sin_table],
        after=after,
        in_specs=[VMEM] * len(arrays) + [SMEM, VMEM, ANY, VMEM, ANY, VMEM, VMEM],
        out_specs=[VMEM] * 7,
        out_shape=[per_head] * 4
        + [
            shaped((SEQ, feature_width), BF),
            shaped((tok_count, head_width), BF),
            shaped((feature_width // blocks, feature_width), BF),
        ],
        scratch_shapes=[
            pltpu.VMEM((feature_width, window), BF),
            pltpu.VMEM((feature_width, 2 * heads * pair + value_tiles), BF),
            pltpu.VMEM((8, 2 * heads * pair + value_tiles), F32),
            pltpu.VMEM((value_tiles, feature_width), BF),
            pltpu.VMEM((heads, SEQ, pair), BF),
            pltpu.VMEM((SEQ, pair), F32),
            pltpu.VMEM((SEQ, pair), F32),
            pltpu.VMEM((value_tiles, feature_width), F32),
            pltpu.SemaphoreType.DMA((2,)),
        ],
        compiler_params=params(52),
        name="attention",
    )


def attention_back(heads, blocks, numbers, parts, qkv_weight, vectors, after):
    *_, unit, attended, grad_out = parts
    (tok_count, head_width), (local_rows, feature_width) = attended.shape, grad_out.shape
    pair = 2 * HEAD_DIM
    width = -(-(3 * head_width) // LANES) * LANES
    small_rows = -(-(4 + 2 * HEADS // heads) // 16) * 16
    cos_table, sin_table = rotary_tables(SEQ)
    return call(
        functools.partial(attention_back_kernel, heads, blocks),
        inputs=[numbers, *parts, qkv_weight, vectors, cos_table, sin_table],
        after=after,
        in_specs=[SMEM] + [VMEM] * 7 + [ANY] + [VMEM] * 3,
        out_specs=[VMEM] * 2,
        out_shape=[
            shaped((tok_count // 2 + local_rows + small_rows, feature_width + head_width), BF),
        ] * 2,
        scratch_shapes=[
            pltpu.VMEM((SEQ, pair), F32),
            pltpu.VMEM((SEQ, pair), F32),
            pltpu.VMEM((heads, SEQ, pair), BF),
            pltpu.VMEM((heads, SEQ, pair), BF),
            pltpu.VMEM((SEQ, width), BF),
            pltpu.VMEM((feature_width, width), F32),
            pltpu.VMEM((small_rows, feature_width // 2), F32),
            pltpu.VMEM((feature_width, width), BF),
            pltpu.SemaphoreType.DMA((1,)),
        ],
        compiler_params=params(52),
        name="attention_back",
    )


def hidden_kernel(first_call, *refs):
    if first_call:
        before_refs = [None] * 4
    else:
        before_refs = refs[-11:-7]
        refs = refs[:-11] + refs[-7:]
    piece_refs, (up_ref, up_bias_ref, down_ref, vectors_ref) = refs[1:-11], refs[-11:-7]
    normed_ref, turned_ref, curve_ref, grad_down_ref, grad_up_ref, bias_grad_ref, cot_sum_ref = refs[-7:]
    cot = jnp.concatenate([ref[0, 1] for ref in piece_refs], axis=0)
    unit = standardize(jnp.concatenate([ref[0, 0] for ref in piece_refs], axis=0).astype(F32))
    normed = (unit * vectors_ref[2:3, :] + vectors_ref[3:4, :]).astype(BF)
    normed_ref[...] = normed
    turned = normed.T
    turned_ref[...] = turned
    hidden = dot(normed, up_ref[...]) + up_bias_ref[...]
    upstream = dot_nt(cot, down_ref[...])
    below, density = gelu_parts(hidden)
    active = (hidden * below).astype(BF)
    hidden_grad = (upstream * (below + hidden * density)).astype(BF)
    curve_ref[...] = upstream * density * (2.0 - hidden * hidden)

    @pl.when(pl.program_id(0) == 0)
    def _():
        for before, target in zip(before_refs, (grad_down_ref, grad_up_ref, bias_grad_ref, cot_sum_ref)):
            target[...] = jnp.zeros_like(target) if first_call else before[...]

    grad_down_ref[...] += dot_tn(active, cot)
    grad_up_ref[...] += dot(turned, hidden_grad)
    bias_grad_ref[...] += jnp.sum(hidden_grad.astype(F32), axis=0, keepdims=True)
    cot_sum_ref[...] += jnp.sum(cot.astype(F32), axis=0, keepdims=True)


def hidden_units(place, pieces, up_part, up_bias_part, down_part, vectors, before):
    refs = [ref for refs, _ in pieces for ref in refs]
    arrays, slots = [array for array, _ in refs], len(pieces[0][1][1])
    _, _, side_rows, feature_width = arrays[0].shape
    part_width = up_bias_part.shape[1]
    tok_count = len(arrays) * side_rows
    count = slots * tok_count

    def fixed(*shape):
        return pl.BlockSpec(shape, lambda i, place_ref: (0,) * len(shape))

    def piece(base):
        return pl.BlockSpec((1, 2, side_rows, feature_width), lambda i, place_ref: (base + i, 0, 0, 0))

    sums = [
        fixed(part_width, feature_width), fixed(feature_width, part_width),
        fixed(1, part_width), fixed(1, feature_width),
    ]
    return pl.pallas_call(
        functools.partial(hidden_kernel, before is None),
        grid_spec=pltpu.PrefetchScalarGridSpec(
            num_scalar_prefetch=1,
            grid=(slots,),
            in_specs=[piece(base) for _, base in refs] + [
                pl.BlockSpec((feature_width, part_width), lambda i, place_ref: (0, place_ref[0])),
                fixed(1, part_width),
                pl.BlockSpec((part_width, feature_width), lambda i, place_ref: (place_ref[0], 0)),
                fixed(8, feature_width),
            ] + (sums if before else []),
            out_specs=[
                pl.BlockSpec((tok_count, feature_width), lambda i, place_ref: (i, 0)),
                pl.BlockSpec((feature_width, tok_count), lambda i, place_ref: (0, i)),
                pl.BlockSpec((tok_count, part_width), lambda i, place_ref: (i, 0)),
            ] + sums,
        ),
        out_shape=[
            shaped((count, feature_width), BF),
            shaped((feature_width, count), BF),
            shaped((count, part_width), F32),
            shaped((part_width, feature_width), F32),
            shaped((feature_width, part_width), F32),
            shaped((1, part_width), F32),
            shaped((1, feature_width), F32),
        ],
        compiler_params=params(BIG),
        name="hidden_units",
        cost_estimate=LIGHT,
    )(
        jnp.where(up_part.shape[1] > part_width, place, 0)[None].astype(jnp.int32),
        *arrays, up_part, up_bias_part, down_part, vectors, *(before[3:] if before else []),
    )


def curvature_kernel(probes, halves, place_ref, dirs_ref, grad_up_ref, local_ref, up_bias_ref, *refs):
    token_refs, (curvature_ref, score_ref, total_s, score_s, spare_s) = refs[: 3 * halves], refs[3 * halves :]
    step, steps = pl.program_id(0), pl.num_programs(0)
    feature_width, width = dirs_ref.shape
    part_width = width // probes
    half = part_width // 2

    @pl.when(step == 0)
    def _():
        total_s[...] = jnp.zeros_like(total_s)
        score_s[...] = jnp.zeros_like(score_s)

    count = feature_width // steps
    rows = pl.ds(pl.multiple_of(step * count, count), count)
    grad_up = grad_up_ref[rows, :]
    for k in range(probes):
        part = dirs_ref[rows, k * part_width : (k + 1) * part_width].astype(F32)
        score_s[k : k + 1, :] += jnp.sum(part * grad_up, axis=0, keepdims=True)

    for number in range(halves):
        normed_ref, turned_ref, curve_ref = token_refs[3 * number : 3 * number + 3]
        along = dot(normed_ref[...], dirs_ref[...])
        curve = curve_ref[...]
        weighted = []
        for k in range(probes):
            part = along[:, k * part_width : (k + 1) * part_width]
            weighted.append((part * curve).astype(BF))
        total_s[...] += dot(turned_ref[...], jnp.concatenate(weighted, axis=1))

    @pl.when(step == steps - 1)
    def _():
        shape = curvature_ref.shape[:2]
        curvature_ref[:, :, :width] = total_s[...].astype(BF).reshape(shape + (width,))
        grad_up = grad_up_ref[...]
        own = jnp.where(place_ref[0] == 1, grad_up[:, half:], grad_up[:, :half]).astype(BF)
        scores = jnp.sum(score_s[...], axis=1, keepdims=True)
        score_ref[...] = jnp.broadcast_to(scores, score_ref.shape)

        spare_s[...] = jnp.zeros_like(spare_s)
        row = 0
        for values in (local_ref[1:2, :], local_ref[2:3, :], up_bias_ref[...]):
            high = values.astype(BF).astype(F32)
            for part in (high, values - high):
                for start in range(0, values.shape[1], HEAD_DIM):
                    spare_s[row : row + 1, HEAD_DIM:] = part[:, start : start + HEAD_DIM]
                    row += 1
        high = scores.astype(BF).astype(F32)
        for part in (high, scores - high):
            for k in range(probes):
                spare_s[row : row + 1, HEAD_DIM + k : HEAD_DIM + k + 1] = part[k : k + 1, :]
            row += 1
        tail = jnp.concatenate([own[:, LANES:], jnp.zeros((feature_width, HEAD_DIM), BF)], axis=1)
        tail = tail.reshape(shape + (LANES,)) + spare_s[...].astype(BF)[None]
        curvature_ref[:, :, width : width + LANES] = own[:, :LANES].reshape(shape + (LANES,))
        curvature_ref[:, :, width + LANES :] = tail


def curvature_of(blocks, core, probes, halves, dirs, grad_up, local_small, up_bias_grad, after):
    normed, _, curve = halves[0]
    (count, feature_width), part_width = normed.shape, curve.shape[1]
    width = probes * part_width
    steps = 2
    tok_count = count // steps
    local_rows = feature_width // blocks
    out = (blocks, local_rows, width + 2 * LANES)
    return call(
        functools.partial(curvature_kernel, probes, len(halves)),
        inputs=[core[None].astype(jnp.int32), dirs, grad_up, local_small, up_bias_grad]
        + [array for half in halves for array in half],
        after=after,
        grid=(steps,),
        in_specs=[
            SMEM, whole(feature_width, width), whole(feature_width, part_width), whole(8, feature_width),
            whole(1, part_width),
        ]
        + [
            pl.BlockSpec((tok_count, feature_width), lambda i: (i, 0)),
            pl.BlockSpec((feature_width, tok_count), lambda i: (0, i)),
            pl.BlockSpec((tok_count, part_width), lambda i: (i, 0)),
        ] * len(halves),
        out_specs=[whole(*out), whole(8, LANES)],
        out_shape=[shaped(out, BF), shaped((8, LANES), F32)],
        scratch_shapes=[
            pltpu.VMEM((feature_width, width), F32),
            pltpu.VMEM((8, part_width), F32),
            pltpu.VMEM((local_rows, LANES), F32),
        ],
        compiler_params=params(BIG),
        name="curvature",
    )


def unpack_kernel(probes, got_ref, curvature_ref):
    blocks = got_ref.shape[0]
    part_width = curvature_ref.shape[2] // blocks
    number = pl.program_id(0)
    for k in range(probes):

        @pl.when(number == k)
        def _(k=k):
            for block in range(blocks):
                part = got_ref[block, :, k * part_width : (k + 1) * part_width]
                curvature_ref[0, :, block * part_width : (block + 1) * part_width] = part.astype(F32)


def unpack(got, probes, part_width, after):
    blocks, local_rows, _ = got.shape
    return call(
        functools.partial(unpack_kernel, probes),
        inputs=[got],
        after=after,
        grid=(probes,),
        in_specs=[whole(*got.shape)],
        out_specs=pl.BlockSpec((1, local_rows, blocks * part_width), lambda i: (i, 0, 0)),
        out_shape=shaped((probes, local_rows, blocks * part_width), F32),
        compiler_params=params(BIG),
        name="unpack",
    )


def peel_kernel(probes, got_ref, up_ref, gain_ref, shift_ref, up_bias_ref, score_ref):
    blocks, _, share = got_ref.shape
    part_width = up_bias_ref.shape[0] // blocks
    tails = []
    for block in range(blocks):
        up_ref[:, block * share : (block + 1) * share] = got_ref[block]
        tails.append(got_ref[block, :, share - LANES :].astype(F32))
    total = tails[0]
    for tail in tails[1:]:
        total = total + tail

    def vector(rows, first, length):
        count = length // HEAD_DIM
        parts = [
            rows[first + k : first + k + 1, HEAD_DIM:] + rows[first + count + k : first + count + k + 1, HEAD_DIM:]
            for k in range(count)
        ]
        return jnp.concatenate(parts, axis=1)

    length = gain_ref.shape[0]
    step = 2 * length // HEAD_DIM
    gain_ref[...] = vector(total, 0, length).reshape(gain_ref.shape)
    shift_ref[...] = vector(total, step, length).reshape(shift_ref.shape)
    biases = [vector(tail, 2 * step, part_width) for tail in tails]
    up_bias_ref[...] = jnp.concatenate(biases, axis=1).reshape(up_bias_ref.shape)
    row = 2 * step + 2 * part_width // HEAD_DIM
    for k in range(probes):
        lane = HEAD_DIM + k
        score_ref[k : k + 1, :] = total[row : row + 1, lane : lane + 1] + total[row + 1 : row + 2, lane : lane + 1]


def peel(got, probes, part_width, after):
    blocks, local_rows, width = got.shape
    share = width - probes * part_width
    feature_width = blocks * local_rows
    vector = shaped((feature_width,), F32)
    return call(
        functools.partial(peel_kernel, probes),
        inputs=[got],
        after=after,
        grid=(1,),
        in_specs=[pl.BlockSpec((blocks, local_rows, share), lambda i: (0, 0, width // share - 1))],
        out_specs=[
            whole(local_rows, blocks * share), whole(feature_width), whole(feature_width),
            whole(blocks * part_width), whole(probes, 1),
        ],
        out_shape=[
            shaped((local_rows, blocks * share), BF),
            vector, vector, shaped((blocks * part_width,), F32), shaped((probes, 1), F32),
        ],
        compiler_params=params(BIG),
        name="peel",
    )


def spread_kernel(blocks, half, place_ref, mine_ref, got_ref, out_ref):
    odd = place_ref[0] == 1
    stride = mine_ref.shape[1] // blocks
    for block in range(blocks):
        here = slice(block * stride, block * stride + half)
        mine, got = mine_ref[:, here], got_ref[:, here]
        both = jnp.concatenate([jnp.where(odd, got, mine), jnp.where(odd, mine, got)], axis=1)
        out_ref[:, block * 2 * half : (block + 1) * 2 * half] = both.astype(F32)


def spread(core, mine, got, blocks, half, after):
    return call(
        functools.partial(spread_kernel, blocks, half),
        inputs=[core[None].astype(jnp.int32), mine, got],
        after=after,
        in_specs=[SMEM, VMEM, VMEM],
        out_specs=VMEM,
        out_shape=shaped((mine.shape[0], blocks * 2 * half), F32),
        compiler_params=params(12),
        name="spread",
    )


def merge_kernel(feature_width, half, few, place_ref, mine_ref, got_ref, merged_ref):
    odd = place_ref[0] == 1
    third = mine_ref.shape[1] - feature_width

    def ordered(rows, columns):
        mine, got = mine_ref[rows, columns], got_ref[rows, columns]
        return jnp.concatenate([jnp.where(odd, got, mine), jnp.where(odd, mine, got)], axis=1)

    main = slice(0, half + few)
    total = mine_ref[main, :feature_width].astype(F32) + got_ref[main, :feature_width].astype(F32)
    merged_ref[...] = jnp.zeros_like(merged_ref)
    merged_ref[main, :feature_width] = total.astype(BF)
    merged_ref[main, feature_width:] = ordered(main, slice(feature_width, feature_width + third))
    rows = slice(half + few, half + 2 * few)
    merged_ref[rows, : 4 * third] = ordered(rows, slice(0, 2 * third))
    first, width = half + 2 * few, feature_width // 2
    put_small(merged_ref, first, get_small(mine_ref, first, width) + get_small(got_ref, first, width))


def merge(core, mine, got, feature_width, half, few):
    count, width = mine.shape
    return call(
        functools.partial(merge_kernel, feature_width, half, few),
        inputs=[core[None].astype(jnp.int32), mine, got],
        in_specs=[SMEM, VMEM, VMEM],
        out_specs=VMEM,
        out_shape=shaped((count, 2 * width - feature_width), BF),
        compiler_params=params(12),
        name="merge",
    )


def finish_kernel(
    few, place_ref, mine_ref, got_ref, tokens_ref, base_ref, rest_ref, vectors_ref, out_weight_ref,
    final_ref, small_ref,
):
    tok_count, feature_width = tokens_ref.shape
    half = tok_count // 2
    third = (mine_ref.shape[1] - feature_width) // 2
    upper = place_ref[1] == 1
    own = pl.ds(pl.multiple_of(place_ref[0] * half, half), half)

    def ordered(rows, columns):
        mine, got = mine_ref[rows, columns], got_ref[rows, columns]
        return jnp.where(upper, got, mine), jnp.where(upper, mine, got)

    attended = jnp.concatenate(ordered(slice(0, half), slice(feature_width, None)), axis=1)
    layer_out = base_ref[own, :] + dot(attended, out_weight_ref[...])
    main = slice(0, half + few)
    total = mine_ref[main, :feature_width].astype(F32) + got_ref[main, :feature_width].astype(F32)
    centred, factor = spread_of(tokens_ref[own, :].astype(F32))
    term = norm_input_term(total[:half], vectors_ref[0:1, :], centred * factor, factor)
    final_ref[:half, :feature_width] = layer_out.astype(BF)
    final_ref[:half, feature_width:] = (rest_ref[own, :] + term).astype(BF)
    parts = []
    firsts = ordered(slice(half, half + few), slice(feature_width, None))
    others = ordered(slice(half + few, half + 2 * few), slice(0, 4 * third))
    for first, other in zip(firsts, others):
        for core in range(2):
            parts += [first[:, core * third : (core + 1) * third], other[:, 2 * core * third : 2 * (core + 1) * third]]
    grad_qkv = jnp.concatenate(parts, axis=1)
    final_ref[half : half + few, :feature_width] = total[half:].astype(BF)
    final_ref[half : half + few, feature_width:] = grad_qkv[:, :feature_width]
    final_ref[half + few :, :] = grad_qkv[:, feature_width:]
    first, width = half + 2 * few, feature_width // 2
    small_ref[...] = get_small(mine_ref, first, width) + get_small(got_ref, first, width)


def finish(places, mine, got, tokens, base, rest, vectors, out_weight, few):
    tok_count, feature_width = tokens.shape
    half = tok_count // 2
    return call(
        functools.partial(finish_kernel, few),
        inputs=[places, mine, got, tokens, base, rest, vectors, out_weight],
        in_specs=[SMEM] + [VMEM] * 7,
        out_specs=[VMEM] * 2,
        out_shape=[
            shaped((half + 2 * few, 2 * feature_width), BF),
            shaped((mine.shape[0] - half - 2 * few, feature_width // 2), F32),
        ],
        compiler_params=params(20),
        name="finish",
    )


def join_kernel(
    few, mixed_width, place_ref, mine_ref, got_ref, small_ref, cot_ref,
    layer_out_ref, input_grad_ref, out_ref, qkv_ref, gain_ref, shift_ref, qkv_bias_ref, cot_sum_ref,
):
    half = layer_out_ref.shape[0] // 2
    feature_width = layer_out_ref.shape[1]
    odd = place_ref[0] == 1
    mine, got = mine_ref[...], got_ref[...]
    for core, side in enumerate((jnp.where(odd, got, mine), jnp.where(odd, mine, got))):
        rows = slice(core * half, (core + 1) * half)
        layer_out_ref[rows, :] = side[:half, :feature_width]
        input_grad_ref[rows, :] = side[:half, feature_width:]
        rows = slice(core * few, (core + 1) * few)
        out_ref[rows, :] = side[half : half + few, :feature_width].astype(F32)
        qkv_ref[rows, :feature_width] = side[half : half + few, feature_width:].astype(F32)
        qkv_ref[rows, feature_width:] = side[half + few :, :].astype(F32)
    small = small_ref[...]

    def rows_of(first, total):
        return jnp.concatenate([small[first : first + 1, :], small[first + 1 : first + 2, :]], axis=1)[:, :total]

    gain_ref[...] = rows_of(0, feature_width).reshape(gain_ref.shape)
    shift_ref[...] = rows_of(2, feature_width).reshape(shift_ref.shape)
    groups = qkv_bias_ref.shape[0] // mixed_width
    bias = [rows_of(4 + 2 * number, mixed_width) for number in range(groups)]
    qkv_bias_ref[...] = jnp.concatenate(bias, axis=1).reshape(qkv_bias_ref.shape)
    cot_sum_ref[...] = cot_ref[...].reshape(cot_sum_ref.shape)


def join(core, mine, got, small, cot, tok_count, few, mixed_width):
    feature_width = cot.shape[1]
    vector = shaped((feature_width,), F32)
    return call(
        functools.partial(join_kernel, few, mixed_width),
        inputs=[core[None].astype(jnp.int32), mine, got, small, cot],
        in_specs=[SMEM] + [VMEM] * 4,
        out_specs=[VMEM] * 8,
        out_shape=[shaped((tok_count, feature_width), BF)] * 2
        + [shaped((2 * few, feature_width), F32), shaped((2 * few, 3 * feature_width), F32), vector, vector]
        + [shaped((4 * mixed_width,), F32), vector],
        compiler_params=params(16),
        name="join",
    )


def on_device(
    tokens,
    segment_ids,
    qkv_weight,
    qkv_bias,
    out_weight,
    out_bias,
    up_weight,
    up_bias,
    down_weight,
    down_bias,
    norm1_gain,
    norm1_bias,
    norm2_gain,
    norm2_bias,
    probe_dirs,
    out_grad,
):
    tok_count, feature_width = tokens.shape
    hidden_width = up_weight.shape[1]
    probe_count, local_rows = probe_dirs.shape[:2]
    groups = lax.axis_size("ex")
    probe_groups = lax.axis_size("probe")
    blocks = SEQ // tok_count
    rows = groups // blocks
    ex_place = lax.axis_index("ex")
    place = ex_place % blocks
    row_place = ex_place // blocks
    probe_place = lax.axis_index("probe")
    core, upper = probe_place % 2, probe_place // 2
    heads = HEADS // probe_groups
    head_width = heads * HEAD_DIM
    part_width = hidden_width // blocks
    fine = part_width // rows
    row_groups = None
    if rows > 1:
        row_groups = [[r * blocks + b for b in range(blocks)] for r in range(rows)]
    across = [[r * blocks + b for r in range(rows)] for b in range(blocks)]

    def swap(value, distance):
        return lax.ppermute(value, "ex", [(i, i ^ distance) for i in range(groups)])

    def swap_probe(value, distance):
        return lax.ppermute(value, "probe", [(i, i ^ distance) for i in range(probe_groups)])

    def over_rows(value):
        if rows > 1:
            return lax.psum_scatter(value, "ex", axis_index_groups=across, scatter_dimension=0, tiled=True)
        return value

    def my_part(value, axis):
        shape = value.shape
        split = shape[:axis] + (rows, blocks, fine) + shape[axis + 1 :]
        part = lax.dynamic_index_in_dim(value.reshape(split), place, axis + 1, keepdims=False)
        return part.reshape(shape[:axis] + (part_width,) + shape[axis + 1 :])

    mine, share = slices_of(core, probe_place, probe_groups, tokens, out_grad)
    near, aside, diagonal = swap(mine, 2), swap(mine, 1), swap(mine, 3)
    far, farthest = swap(share, 4), swap(share, 6)

    segments = segment_ids
    if rows > 1:
        segments = lax.dynamic_slice_in_dim(segment_ids, row_place * SEQ, SEQ)
    vectors = vectors_of(
        probe_groups, blocks, norm1_gain, norm1_bias, norm2_gain, norm2_bias, out_bias, down_bias, qkv_bias, segments
    )
    base, rest, local_small = local_part(tokens, out_grad, up_weight, up_bias, down_weight, vectors)

    first, second, third = stack(
        [mine, aside, near, diagonal, far, farthest], [(0, 1), (2, 3), (4, 5)], [local_small]
    )
    first_other, second_other = swap_probe(first, 1), swap_probe(second, 1)
    third_aside, third_over = swap(third, 1), swap_probe(third, 2)
    up_bias_part = my_part(up_bias, 0).astype(F32)[None]
    up_part, down_part = up_weight, down_weight
    if rows > 1:
        up_part, down_part = my_part(up_weight, 1), my_part(down_weight, 0)
    pieces = [
        ([(first, 0), (first_other, 0)], ((0, 1), (0, 1))),
        ([(second, 0), (second_other, 0)], ((0, 1), (2, 3))),
    ]
    units = hidden_units(place, pieces, up_part, up_bias_part, down_part, vectors, None)
    third_across = swap_probe(third_aside, 2)

    dirs = tie(pack(probe_dirs, blocks, rows, [local_small]), [third_aside, third_over])
    dirs = lax.all_to_all(dirs, "ex", 0, 0, axis_index_groups=row_groups, tiled=True)
    dirs = dirs.reshape(blocks * local_rows, probe_count * part_width)
    if rows > 1:
        dirs = lax.all_gather(dirs, "ex", axis_index_groups=across, tiled=True)

    (quarters,) = stack([third, third_over, third_aside, third_across], [(0, 1, 2, 3)], [units[5]])
    swapped = swap_probe(quarters, 1)
    for slot, distances in ((0, (4, 6)), (4, (5, 7))):
        refs = [(array, slot + 2 * k) for array in (quarters, swapped) for k in range(2)]
        pieces.append((refs, ((0, 2, 1, 3), distances)))
    halves = [units[:3]]
    units = hidden_units(place, pieces[2:], up_part, up_bias_part, down_part, vectors, units)
    halves.append(units[:3])
    grad_down, grad_up, grad_up_bias, cot_sum = units[3:]

    block_rows = feature_width // blocks
    offset = place * block_rows - probe_place * head_width
    holds = (offset >= 0) & (offset < head_width)
    numbers = jnp.stack([place, probe_place, holds, jnp.where(holds, offset, 0)]).astype(jnp.int32)
    parts = attention(heads, blocks, numbers, pieces, tokens, qkv_weight, vectors, out_weight, [cot_sum])

    part, scores = curvature_of(
        blocks, core, probe_count, halves, dirs, grad_up, local_small, grad_up_bias, parts[-1:]
    )
    part = over_rows(part.reshape(feature_width, -1)).reshape(blocks, local_rows, -1)
    got = lax.all_to_all(part, "ex", 0, 0, axis_index_groups=row_groups, tiled=True)

    keep, send = attention_back(heads, blocks, numbers, parts, qkv_weight, vectors, [scores])
    half, few = tok_count // 2, block_rows // 2
    merged = merge(core, keep, swap_probe(send, 1), feature_width, half, few)
    final, small = finish(
        jnp.stack([core, upper]).astype(jnp.int32), merged, swap_probe(merged, 2), tokens, base, rest, vectors,
        out_weight, few,
    )
    (
        layer_out, input_grad, grad_out_weight, grad_qkv_weight,
        grad_gain_one, grad_shift_one, grad_qkv_bias, cot_sum,
    ) = join(core, final, swap_probe(final, 1), small, cot_sum, tok_count, few, 3 * head_width)

    if rows == 1:
        up_half, grad_gain_two, grad_shift_two, grad_up_bias, scores = peel(
            got, probe_count, part_width, [layer_out]
        )
        other_half = swap_probe(up_half, 1)
        curvature = unpack(got, probe_count, part_width, [up_half])
        grad_up_weight = spread(core, up_half, other_half, blocks, part_width // 2, [curvature])
    else:
        start = probe_count * part_width
        units = got[:, :, :start].reshape(blocks, local_rows, probe_count, rows, fine)
        curvature = units.transpose(2, 1, 3, 0, 4).reshape(probe_count, local_rows, hidden_width)
        curvature = curvature.astype(F32)
        up_half = got[:, :, start : start + part_width // 2]
        both = lax.all_gather(up_half, "probe", axis_index_groups=[[0, 1], [2, 3]])
        both = both.transpose(2, 1, 0, 3).reshape(local_rows, blocks, rows, fine)
        grad_up_weight = both.transpose(0, 2, 1, 3).reshape(local_rows, hidden_width).astype(F32)
        grad_down = over_rows(grad_down)

        def over_groups(value):
            value = lax.all_gather(value, "ex", axis_index_groups=row_groups, tiled=True)
            return lax.dynamic_slice_in_dim(over_rows(value), place * local_rows, local_rows, 0)

        grad_qkv_weight, grad_out_weight = over_groups(grad_qkv_weight), over_groups(grad_out_weight)
        grad_gain_one, grad_shift_one, grad_qkv_bias, cot_sum, grad_up_bias = lax.psum(
            (grad_gain_one, grad_shift_one, grad_qkv_bias, cot_sum, grad_up_bias[0]),
            "ex",
            axis_index_groups=across,
        )
        grad_up_bias = lax.all_gather(grad_up_bias, "ex", axis_index_groups=row_groups)
        grad_up_bias = grad_up_bias.reshape(blocks, rows, fine).transpose(1, 0, 2).reshape(-1)
        grad_gain_two, grad_shift_two = lax.psum((local_small[1], local_small[2]), "ex")
        scores = lax.psum(scores[:probe_count, :1], "ex", axis_index_groups=row_groups)
        scores = lax.all_gather(scores, "ex", axis_index_groups=across, axis=1, tiled=True)
    return (
        layer_out,
        input_grad,
        grad_qkv_weight,
        grad_qkv_bias,
        grad_out_weight,
        cot_sum,
        grad_up_weight,
        grad_up_bias,
        grad_down,
        cot_sum,
        grad_gain_one,
        grad_shift_one,
        grad_gain_two,
        grad_shift_two,
        curvature,
        scores,
    )


def solution(mesh):
    in_specs = (
        P("ex", None),
        P(),
        P(),
        P(),
        P(),
        P(),
        P(),
        P(),
        P(),
        P(),
        P(),
        P(),
        P(),
        P(),
        P("probe", "ex", None),
        P("ex", None),
    )
    out_specs = (
        P("ex", None),
        P("ex", None),
        P("ex", None),
        P(),
        P("ex", None),
        P(),
        P("ex", None),
        P(),
        P("ex", None),
        P(),
        P(),
        P(),
        P(),
        P(),
        P("probe", "ex", None),
        P("probe", None),
    )
    return jax.shard_map(
        on_device, mesh=mesh, in_specs=in_specs, out_specs=out_specs, check_vma=False
    )
```

```python
import functools

import jax
import jax.numpy as jnp
import numpy as np
from jax import lax
from jax.experimental import pallas as pl
from jax.experimental.pallas import tpu as pltpu
from jax.sharding import PartitionSpec as P

HEADS = 12
HEAD_DIM = 64
ROT = 16
SEQ = 2048

BF = jnp.bfloat16
F32 = jnp.float32
eps_norm = 1e-05
masked_score = -1e30
half_root = 0.7071067811865476
gauss_peak = 0.3989422804014327
MB = 1024 * 1024
LANES = 128
STEPS = 4
LIGHT = pl.CostEstimate(flops=1000, bytes_accessed=1000, transcendentals=0)
BIG = 58


def dot(a, b):
    return jnp.dot(a, b, preferred_element_type=F32)


def dot_nt(a, b):
    return lax.dot_general(a, b, (((1,), (1,)), ((), ())), preferred_element_type=F32)


def dot_tn(a, b):
    return lax.dot_general(a, b, (((0,), (0,)), ((), ())), preferred_element_type=F32)


def spread_of(features):
    center = jnp.mean(features, axis=-1, keepdims=True)
    centred = features - center
    spread = jnp.mean(centred * centred, axis=-1, keepdims=True)
    return centred, lax.rsqrt(spread + eps_norm)


def standardize(features):
    centred, factor = spread_of(features)
    return centred * factor


def norm_input_term(grad, gain_row, unit, factor):
    unit_grad = grad * gain_row
    inner = unit_grad - jnp.mean(unit_grad, -1, keepdims=True)
    return (inner - unit * jnp.mean(unit_grad * unit, -1, keepdims=True)) * factor


def gelu_parts(pre_act):
    below = 0.5 + 0.5 * lax.erf(pre_act * half_root)
    density = gauss_peak * jnp.exp(-0.5 * pre_act * pre_act)
    return below, density


def rotary_tables(count):
    steps = np.arange(ROT // 2, dtype=np.float32) * np.float32(2.0 / ROT)
    inverse = np.power(np.float32(10000.0), -steps).astype(np.float32)
    angles = np.arange(count, dtype=np.float32)[:, None] * inverse[None, :]
    angles = np.concatenate([angles, angles], axis=1)
    cosine = np.ones((count, HEAD_DIM), np.float32)
    sine = np.zeros((count, HEAD_DIM), np.float32)
    cosine[:, :ROT], sine[:, :ROT] = np.cos(angles), np.sin(angles)
    return np.concatenate([cosine, cosine], axis=1), np.concatenate([sine, sine], axis=1)


def params(limit_mb, **more):
    return pltpu.CompilerParams(vmem_limit_bytes=limit_mb * MB, **more)


def shaped(shape, dtype):
    return jax.ShapeDtypeStruct(shape, dtype)


def whole(*shape):
    return pl.BlockSpec(shape, lambda i: (0,) * len(shape))


VMEM = pl.BlockSpec(memory_space=pltpu.VMEM)
SMEM = pl.BlockSpec(memory_space=pltpu.SMEM)
ANY = pl.BlockSpec(memory_space=pl.ANY)


def far(array):
    return pltpu.with_memory_space_constraint(array, pltpu.HBM)


def call(kernel, *, inputs, in_specs, after=(), aliases=None, **more):
    spare = len(after)

    def body(*refs):
        kernel(*refs[: len(inputs)], *refs[len(inputs) + spare :])

    return pl.pallas_call(
        body, in_specs=list(in_specs) + [ANY] * spare, input_output_aliases=aliases or {},
        cost_estimate=LIGHT, **more,
    )(*inputs, *after)


def tie(value, after):
    return call(
        lambda value_ref, out_ref: None,
        inputs=[value],
        after=after,
        aliases={0: 0},
        in_specs=[ANY],
        out_specs=ANY,
        out_shape=shaped(value.shape, value.dtype),
        name="tie",
    )


def pack_kernel(dirs_ref, packed_ref, sems):
    probes = dirs_ref.shape[0]
    blocks, _, width = packed_ref.shape
    part_width = width // probes
    copies = []
    for block in range(blocks):
        for k in range(probes):
            source = dirs_ref.at[k, :, block * part_width : (block + 1) * part_width]
            target = packed_ref.at[block, :, k * part_width : (k + 1) * part_width]
            copies.append(pltpu.make_async_copy(source, target, sems.at[len(copies)]))
    for copy in copies:
        copy.start()
    for copy in copies:
        copy.wait()


def pack(dirs, blocks, rows, after):
    probes, local_rows, hidden_width = dirs.shape
    part_width = hidden_width // blocks
    if rows > 1:
        split = dirs.reshape(probes, local_rows, rows, blocks, part_width // rows)
        return split.transpose(3, 1, 0, 2, 4).reshape(blocks, local_rows, probes * part_width)
    return call(
        pack_kernel,
        inputs=[dirs],
        after=after,
        in_specs=[VMEM],
        out_specs=ANY,
        out_shape=pltpu.HBM((blocks, local_rows, probes * part_width), dirs.dtype),
        scratch_shapes=[pltpu.SemaphoreType.DMA((blocks * probes,))],
        compiler_params=params(8),
        name="pack",
    )


def slices_kernel(place_ref, tokens_ref, grads_ref, both_ref, first_ref, sems):
    count = both_ref.shape[2]
    copies = []
    for part, source in enumerate((tokens_ref, grads_ref)):
        for target, slot, side in ((both_ref, 0, 0), (both_ref, 1, 2), (first_ref, 0, 0)):
            first = jnp.bitwise_xor(place_ref[0], side) * count
            rows = pl.ds(pl.multiple_of(first, count), count)
            copies.append(pltpu.make_async_copy(source.at[rows, :], target.at[slot, part], sems.at[len(copies)]))
    for copy in copies:
        copy.start()
    for copy in copies:
        copy.wait()


def slices_of(probe_place, probe_groups, tokens, grads):
    tok_count, feature_width = tokens.shape
    size = tok_count // probe_groups
    return call(
        slices_kernel,
        inputs=[probe_place[None].astype(jnp.int32), far(tokens), far(grads)],
        in_specs=[SMEM, ANY, ANY],
        out_specs=[VMEM] * 2,
        out_shape=[shaped((count, 2, size, feature_width), BF) for count in (2, 1)],
        scratch_shapes=[pltpu.SemaphoreType.DMA((6,))],
        compiler_params=params(8),
        name="slices",
    )


def stack_kernel(plan, *refs):
    sources, targets = refs[: -len(plan)], refs[-len(plan) :]
    for parts, target in zip(plan, targets):
        number = 0
        for part in parts:
            count = sources[part].shape[0]
            target[number : number + count] = sources[part][...]
            number += count


def stack(sources, plan, after):
    heights = [sum(sources[part].shape[0] for part in parts) for parts in plan]
    return call(
        functools.partial(stack_kernel, plan),
        inputs=sources,
        after=after,
        in_specs=[VMEM] * len(sources),
        out_specs=[VMEM] * len(plan),
        out_shape=[shaped((n,) + sources[parts[0]].shape[1:], BF) for n, parts in zip(heights, plan)],
        compiler_params=params(8),
        name="stack",
    )


def vectors_kernel(groups, blocks, count, *refs):
    sources, vectors_ref, held, sems = refs[:count], refs[count], refs[count + 1 : -1], refs[-1]
    copies = [pltpu.make_async_copy(source, target, sems.at[k]) for k, (source, target) in enumerate(zip(sources, held))]
    for copy in copies:
        copy.start()
    vectors_ref[...] = jnp.zeros_like(vectors_ref)
    for copy in copies:
        copy.wait()
    *plain, first_bias, second_bias, qkv_bias, segments = held
    for number, source in enumerate(plain):
        vectors_ref[number : number + 1, :] = source[...].reshape(1, -1)
    total = first_bias[...].astype(F32) + second_bias[...].astype(F32)
    vectors_ref[len(plain) : len(plain) + 1, :] = total.reshape(1, -1)
    width = qkv_bias.shape[0] // groups
    bias = qkv_bias[...].astype(F32).reshape(1, -1)
    for number in range(groups):
        vectors_ref[8 + number : 9 + number, :width] = bias[:, number * width : (number + 1) * width]
    block = segments.shape[0] // blocks
    for number in range(blocks):
        row = segments[number * block : (number + 1) * block].astype(F32).reshape(1, -1)
        vectors_ref[16 + number : 17 + number, :block] = row


def vectors_of(groups, blocks, *sources):
    return call(
        functools.partial(vectors_kernel, groups, blocks, len(sources)),
        inputs=[far(source) for source in sources],
        in_specs=[ANY] * len(sources),
        out_specs=VMEM,
        out_shape=shaped((16 + blocks, sources[0].shape[0]), F32),
        scratch_shapes=[pltpu.VMEM(source.shape, source.dtype) for source in sources]
        + [pltpu.SemaphoreType.DMA((len(sources),))],
        compiler_params=params(4),
        name="vectors",
    )


def local_kernel(
    tokens_ref, grads_ref, up_ref, up_bias_ref, down_ref, vectors_ref,
    base_ref, rest_ref, small_ref, normed_s, branch_s, back_s,
):
    step = pl.program_id(0)
    gain, shift, out_bias = vectors_ref[2:3, :], vectors_ref[3:4, :], vectors_ref[4:5, :]

    @pl.when(step == 0)
    def _():
        unit = standardize(tokens_ref[...].astype(F32))
        normed_s[...] = (unit * gain + shift).astype(BF)
        branch_s[...] = jnp.zeros_like(branch_s)
        back_s[...] = jnp.zeros_like(back_s)

    bias = up_bias_ref[pl.ds(pl.multiple_of(step * up_ref.shape[1], LANES), up_ref.shape[1])]
    hidden = dot(normed_s[...], up_ref[...]) + bias.astype(F32).reshape(1, -1)
    upstream = dot_nt(grads_ref[...], down_ref[...])
    below, density = gelu_parts(hidden)
    branch_s[...] += dot((hidden * below).astype(BF), down_ref[...])
    hidden_grad = (upstream * (below + hidden * density)).astype(BF)
    back_s[...] += dot_nt(hidden_grad, up_ref[...])

    @pl.when(step == pl.num_programs(0) - 1)
    def _():
        inputs = tokens_ref[...].astype(F32)
        cot = grads_ref[...].astype(F32)
        centred, factor = spread_of(inputs)
        unit = centred * factor
        back = back_s[...]
        base_ref[...] = inputs + branch_s[...] + out_bias
        rest_ref[...] = cot + norm_input_term(back, gain, unit, factor)
        small_ref[...] = jnp.zeros_like(small_ref)
        small_ref[0:1, :] = jnp.sum(cot, axis=0, keepdims=True)
        small_ref[1:2, :] = jnp.sum(back * unit, axis=0, keepdims=True)
        small_ref[2:3, :] = jnp.sum(back, axis=0, keepdims=True)


def local_part(tokens, grads, up_weight, up_bias, down_weight, vectors):
    tok_count, feature_width = tokens.shape
    hidden_width = up_weight.shape[1]
    step = 512
    own = whole(tok_count, feature_width)
    return call(
        local_kernel,
        inputs=[tokens, grads, far(up_weight), up_bias, far(down_weight), vectors],
        grid=(hidden_width // step,),
        in_specs=[
            own, own,
            pl.BlockSpec((feature_width, step), lambda i: (0, i)),
            whole(hidden_width),
            pl.BlockSpec((step, feature_width), lambda i: (i, 0)),
            whole(8, feature_width),
        ],
        out_specs=[own, own, whole(8, feature_width)],
        out_shape=[
            shaped((tok_count, feature_width), F32),
            shaped((tok_count, feature_width), F32),
            shaped((8, feature_width), F32),
        ],
        scratch_shapes=[
            pltpu.VMEM((tok_count, feature_width), BF),
            pltpu.VMEM((tok_count, feature_width), F32),
            pltpu.VMEM((tok_count, feature_width), F32),
        ],
        compiler_params=params(24),
        name="local",
    )


def lanes(rows):
    return lax.broadcasted_iota(jnp.int32, (rows, 2 * HEAD_DIM), 1)


def flipped(tile):
    return pltpu.roll(tile, HEAD_DIM, 1)


def joined(left, right):
    return jnp.where(lanes(left.shape[0]) < HEAD_DIM, left, flipped(right))


def half_turned(tile):
    place_in = lanes(tile.shape[0]) % HEAD_DIM
    low = pltpu.roll(tile, 2 * HEAD_DIM - ROT // 2, 1)
    high = pltpu.roll(tile, ROT // 2, 1)
    return jnp.where(place_in < ROT // 2, -low, jnp.where(place_in < ROT, high, 0.0))


def with_column(tile, lane, column):
    first = column.astype(BF).astype(F32)
    number = lanes(tile.shape[0])
    return jnp.where(number == lane, first, jnp.where(number == lane + 1, column - first, tile))


def heads_joined(values):
    heads = len(values)
    values = [joined(values[k], values[k + 1]) if k + 1 < heads else values[k] for k in range(0, heads, 2)]
    if heads % 2:
        values[-1] = jnp.where(lanes(values[-1].shape[0]) < HEAD_DIM, values[-1], 0.0)
    return jnp.concatenate(values, axis=1)


def attention_kernel(heads, blocks, block, count, plan, *refs):
    sources, refs = refs[:count], refs[count:]
    (
        place_ref, weight_ref, vectors_ref, out_weight_ref, cos_in, sin_in,
        query_out, key_out, value_out, back_out, unit_out, cot_out, attended_out,
        cos_ref, sin_ref, query_s, key_s, value_s, back_s, unit_s, cot_s,
        window_s, weight_s, bias_s, out_weight_s, attended_s, query_code_s, key_code_s, sems,
        *array_refs,
    ) = refs
    place, probe_place = place_ref[0], place_ref[1]
    feature_width = unit_s.shape[1]
    pair = 2 * HEAD_DIM
    scale = HEAD_DIM ** (-0.5)
    gain, shift = vectors_ref[0:1, :], vectors_ref[1:2, :]
    own_rows = pl.ds(pl.multiple_of(place * block, block), block)
    head_width = heads * HEAD_DIM
    mixed_width = 3 * head_width

    first = probe_place * mixed_width // LANES * LANES
    columns = pl.ds(pl.multiple_of(first, LANES), window_s.shape[1])
    rows = pl.ds(pl.multiple_of(probe_place * head_width, HEAD_DIM), head_width)
    moves = [(weight_ref.at[:, columns], window_s), (out_weight_ref.at[rows, :], out_weight_s.at[:head_width, :])]
    moves += [(cos_in, cos_ref), (sin_in, sin_ref)] + list(zip(sources, array_refs))
    copies = [pltpu.make_async_copy(source, target, sems.at[k]) for k, (source, target) in enumerate(moves)]
    for copy in copies:
        copy.start()
    done = len(copies)

    def leave(number, source, target):
        return pltpu.make_async_copy(source, target, sems.at[done + number])

    def rows_of(number):
        return pl.ds(pl.multiple_of(number * block, block), block)

    def side_rows(distance, side, count):
        own = place_ref[1] % (block // count)
        first = jnp.bitwise_xor(place, distance) * block + jnp.bitwise_xor(own, side) * count
        return pl.ds(pl.multiple_of(first, count), count)

    def together(refs, slot, part):
        return jnp.concatenate([array_refs[ref][base + slot, part] for ref, base in refs], axis=0)

    def arrange(source, target):
        for head in range(heads):
            start = head * 3 * HEAD_DIM
            tile = source[:, start : start + pair].astype(F32)
            target[:, head * pair : (head + 1) * pair] = tile.astype(target.dtype)
            target[:, (heads + head) * pair : (heads + head + 1) * pair] = half_turned(tile).astype(target.dtype)
        values = [source[:, (3 * head + 2) * HEAD_DIM : (3 * head + 3) * HEAD_DIM] for head in range(heads)]
        values.append(jnp.zeros((source.shape[0], -heads * HEAD_DIM % pair), source.dtype))
        target[:, 2 * heads * pair :] = jnp.concatenate(values, axis=1).astype(target.dtype)

    number = lanes(block)
    ones = (number >= HEAD_DIM + 16) & (number < HEAD_DIM + 18)
    coded = (number >= HEAD_DIM) & (number < HEAD_DIM + 16)
    for index in range(blocks):
        segment = jnp.broadcast_to(vectors_ref[16 + index : 17 + index, :block], (pair, block)).T
        segment = segment.astype(jnp.int32)
        match = (number == HEAD_DIM + segment // 8) | (number == HEAD_DIM + 8 + segment % 8)
        here = slice(index * block, (index + 1) * block)
        query_code_s[here, :] = jnp.where(coded & ~match, masked_score, 0.0)
        key_code_s[here, :] = jnp.where(match | ones, 1.0, 0.0)

    out_weight_s[head_width:, :] = jnp.zeros((out_weight_s.shape[0] - head_width, feature_width), BF)
    copies[0].wait()
    odd = probe_place * mixed_width % LANES != 0
    window = window_s[...]
    weight = jnp.where(odd, window[:, HEAD_DIM : HEAD_DIM + mixed_width], window[:, :mixed_width])
    arrange(weight, weight_s)
    bias = vectors_ref[pl.ds(8 + probe_place, 1), :mixed_width]
    arrange(jnp.broadcast_to(bias, (8, mixed_width)), bias_s)
    for copy in copies[1:4]:
        copy.wait()

    def project(sides, refs, slot, distance):
        unit = standardize(together(refs, slot, 0).astype(F32))
        normed = (unit * gain + shift).astype(BF)
        low = unit.astype(BF)
        whole_part = dot(normed, weight_s[...]) + bias_s[:1, :]
        cot = together(refs, slot, 1)
        whole_back = dot_nt(cot, out_weight_s[...])
        count = block // len(sides)
        for number, side in enumerate(sides):
            here = slice(number * count, (number + 1) * count)
            rows = side_rows(distance, side, count)
            unit_s[rows, :] = low[here]
            cot_s[rows, :] = cot[here]
            place_heads(rows, whole_part[here], whole_back[here])

    def place_heads(rows, part, back_part):
        cosine, sine = cos_ref[rows, :], sin_ref[rows, :]
        number = lanes(part.shape[0])
        query_code, key_code = query_code_s[rows, :], key_code_s[rows, :]
        value_code = jnp.where((number >= HEAD_DIM) & (number < HEAD_DIM + 2), 1.0, 0.0)
        first = number < HEAD_DIM
        for head in range(heads):
            plain = part[:, head * pair : (head + 1) * pair]
            turned = part[:, (heads + head) * pair : (heads + head + 1) * pair]
            both = plain * cosine + turned * sine
            query_s[head, rows, :] = jnp.where(first, both * scale, query_code).astype(BF)
            key_s[head, rows, :] = jnp.where(first, flipped(both), key_code).astype(BF)
            start = 2 * heads * pair + head // 2 * pair
            tile = part[:, start : start + pair]
            back_tile = back_part[:, head // 2 * pair : head // 2 * pair + pair]
            if head % 2:
                tile, back_tile = flipped(tile), flipped(back_tile)
            value_s[head, rows, :] = jnp.where(first, tile, value_code).astype(BF)
            back_s[head, rows, :] = jnp.where(first, back_tile, 0.0).astype(BF)

    here = set()
    for sides, distances, refs in plan:
        for number in sorted({ref for ref, _ in refs} - here):
            copies[4 + number].wait()
            here.add(number)
        for slot, distance in enumerate(distances):
            project(sides, refs, slot, distance)
    leaving = [leave(0, key_s, key_out), leave(1, value_s, value_out), leave(2, unit_s, unit_out)]
    leaving.append(leave(3, cot_s, cot_out))
    for copy in leaving:
        copy.start()

    square = (block, block)
    lower = lax.broadcasted_iota(jnp.int32, square, 1) <= lax.broadcasted_iota(jnp.int32, square, 0)

    def head_leaving(head):
        pairs = ((query_s, query_out), (back_s, back_out), (attended_s, attended_out))
        return [leave(4 + 3 * head + k, source.at[head], target.at[head]) for k, (source, target) in enumerate(pairs)]

    def attend(head, carry):
        def scores_of(number):
            start, stop = number * block, (number + 1) * block
            query = query_s[head, start:stop, :]
            near = jnp.where(lower, dot_nt(query, key_s[head, start:stop, :]), masked_score)
            return near, dot_nt(query, key_s[head, :start, :]) if number else None

        ahead = scores_of(0)
        for number in range(blocks):
            start, stop = number * block, (number + 1) * block
            near, far = ahead
            if number + 1 < blocks:
                ahead = scores_of(number + 1)
            top = jnp.max(near, axis=-1, keepdims=True)
            if number:
                top = jnp.maximum(top, jnp.max(far, axis=-1, keepdims=True))
            got = dot(jnp.exp(near - top).astype(BF), value_s[head, start:stop, :])
            if number:
                got = got + dot(jnp.exp(far - top).astype(BF), value_s[head, :start, :])
            total = got[:, HEAD_DIM : HEAD_DIM + 1]
            attended = got / total
            attended_s[head, start:stop, :] = attended.astype(BF)
            back = back_s[head, start:stop, :].astype(F32)
            delta = jnp.sum(attended * back, axis=-1, keepdims=True)
            log_total = top + jnp.log(total)
            query = query_s[head, start:stop, :].astype(F32)
            query_s[head, start:stop, :] = with_column(query, HEAD_DIM + 16, -log_total).astype(BF)
            back_s[head, start:stop, :] = with_column(back, HEAD_DIM, -delta).astype(BF)
        for copy in head_leaving(head):
            copy.start()
        return carry

    lax.fori_loop(0, heads, attend, 0)

    for copy in leaving:
        copy.wait()
    for head in range(heads):
        for copy in head_leaving(head):
            copy.wait()


def attention_back_kernel(
    heads, blocks, place_ref, query_in, key_in, value_in, back_in, unit_in, attended_ref, grad_out_ref, weight_ref,
    vectors_ref, cos_in, sin_in,
    keep_ref, send_ref,
    query_s, key_s, value_s, back_s, unit_ref, cos_ref, sin_ref,
    query_grad_s, key_grad_s, both_s, value_grad_s, mixed_s, total_s, small_s, window_s, sems,
):
    place, probe_place = place_ref[0], place_ref[1]
    block, head_width = attended_ref.shape
    feature_width = unit_ref.shape[1]
    mixed_width = 3 * head_width
    scale = HEAD_DIM ** (-0.5)
    first = probe_place * mixed_width // LANES * LANES
    columns = pl.ds(pl.multiple_of(first, LANES), window_s.shape[1])
    others = [(cos_in, cos_ref), (sin_in, sin_ref), (unit_in, unit_ref), (weight_ref.at[:, columns], window_s)]
    others = [pltpu.make_async_copy(source, target, sems.at[k]) for k, (source, target) in enumerate(others)]

    def arriving(head):
        pairs = ((key_in, key_s), (query_in, query_s), (value_in, value_s), (back_in, back_s))
        return [
            pltpu.make_async_copy(source.at[head], target.at[head], sems.at[4 + len(pairs) * head + k])
            for k, (source, target) in enumerate(pairs)
        ]

    for copy in arriving(0) + others[:2]:
        copy.start()
    for head in range(1, heads):
        for copy in arriving(head):
            copy.start()
    for copy in others[2:]:
        copy.start()
    for copy in others[:2]:
        copy.wait()
    square = (block, block)
    upper = lax.broadcasted_iota(jnp.int32, square, 0) <= lax.broadcasted_iota(jnp.int32, square, 1)

    def through(head, carry):
        for copy in arriving(head):
            copy.wait()
        query_grad_s[...] = jnp.zeros_like(query_grad_s)
        for number in range(blocks):
            start, stop = number * block, (number + 1) * block
            key, value = key_s[head, start:stop, :], value_s[head, start:stop, :]
            key_t = key.T
            key_grad = value_grad = None
            for rows, mask in ((slice(start, stop), upper), (slice(stop, blocks * block), None)):
                if rows.start == rows.stop:
                    continue
                query, back = query_s[head, rows, :], back_s[head, rows, :]
                scores = dot_nt(key, query)
                if mask is not None:
                    scores = jnp.where(mask, scores, masked_score)
                probs = jnp.exp(scores)
                score_grad = (probs * dot_nt(value, back)).astype(BF)
                value_term, key_term = dot(probs.astype(BF), back), dot(score_grad, query)
                value_grad = value_term if value_grad is None else value_grad + value_term
                key_grad = key_term if key_grad is None else key_grad + key_term
                query_grad_s[:, rows] += dot(key_t, score_grad)
            key_grad_s[start:stop, :] = key_grad
            value_grad_s[head, start:stop, :] = value_grad.astype(BF)
        for number in range(blocks):
            rows = slice(number * block, (number + 1) * block)
            both = joined(query_grad_s[:, rows].T * scale, key_grad_s[rows, :])
            both = both * cos_ref[rows, :] - half_turned(both * sin_ref[rows, :])
            both_s[head, rows, :] = both.astype(BF)
        return carry

    lax.fori_loop(0, heads, through, 0)

    for number in range(blocks):
        rows = slice(number * block, (number + 1) * block)
        tiles = []
        for head in range(heads):
            both, value = both_s[head, rows, :].astype(F32), value_grad_s[head, rows, :].astype(F32)
            if head % 2 == 0:
                tiles += [both, value]
            else:
                tiles[-1] = joined(tiles[-1], both)
                tiles.append(joined(flipped(both), value))
        if heads % 2:
            tiles[-1] = jnp.where(lanes(block) < HEAD_DIM, tiles[-1], 0.0)
        mixed_s[rows, :] = jnp.concatenate(tiles, axis=1).astype(BF)

    others[2].wait()
    total_s[...] = dot_tn(unit_ref[...], mixed_s[...])
    sums = jnp.sum(mixed_s[...].astype(F32), axis=0, keepdims=True)
    others[3].wait()
    odd = probe_place * mixed_width % LANES != 0
    window = window_s[...]
    weight = jnp.where(odd, window[:, HEAD_DIM : HEAD_DIM + mixed_width], window[:, :mixed_width])

    own_rows = pl.ds(pl.multiple_of(place * block, block), block)
    mixed_own = mixed_s[own_rows, :][:, :mixed_width]
    normed_back = dot_nt(mixed_own, weight).astype(BF)

    local_rows = grad_out_ref.shape[0]
    first = pl.multiple_of(place * local_rows, local_rows)
    pick = lax.broadcasted_iota(jnp.int32, (local_rows, feature_width), 1) == first + lax.broadcasted_iota(
        jnp.int32, (local_rows, feature_width), 0
    )
    gain, shift = [
        jnp.sum(jnp.where(pick, vectors_ref[k : k + 1, :], 0.0), axis=1, keepdims=True) for k in range(2)
    ]
    grad_qkv = (total_s[pl.ds(first, local_rows), :] * gain + sums * shift).astype(BF)

    wide = weight.astype(F32)
    columns = [
        jnp.sum(wide * total_s[:, :mixed_width], axis=1, keepdims=True),
        jnp.sum(wide * sums[:, :mixed_width], axis=1, keepdims=True),
    ]
    number = lax.broadcasted_iota(jnp.int32, (feature_width, LANES), 1)
    columns = jnp.where(number == 0, columns[0], jnp.where(number == 1, columns[1], 0.0)).T
    piece = feature_width // 2
    small_s[...] = jnp.zeros_like(small_s)
    for k in range(2):
        for part in range(2):
            here = slice(part * piece, (part + 1) * piece)
            small_s[2 * k + part : 2 * k + part + 1, :piece] = columns[k : k + 1, here]
    small_s[pl.ds(4 + 2 * probe_place, 1), :piece] = sums[:, :piece]
    small_s[pl.ds(5 + 2 * probe_place, 1), : mixed_width - piece] = sums[:, piece:mixed_width]
    half, few = block // 2, local_rows // 2
    third = head_width
    odd = probe_place % 2 == 1

    def halves(value):
        low, high = value[: value.shape[0] // 2], value[value.shape[0] // 2 :]
        return jnp.where(odd, high, low), jnp.where(odd, low, high)

    attended, grad_out = attended_ref[...], grad_out_ref[...]
    for number, target in enumerate((keep_ref, send_ref)):
        target[...] = jnp.zeros_like(target)
        target[:half, :feature_width] = halves(normed_back)[number]
        target[:half, feature_width:] = halves(attended)[number]
        target[half : half + few, :feature_width] = halves(grad_out)[number]
        part = halves(grad_qkv)[number]
        target[half : half + few, feature_width:] = part[:, :third]
        target[half + few : half + 2 * few, : 2 * third] = part[:, third : 3 * third]
        put_small(target, half + 2 * few, small_s[...])


def put_small(target, first, small):
    width = small.shape[1]
    high = small.astype(BF)
    target[first:, :width] = high
    target[first:, width : 2 * width] = (small - high.astype(F32)).astype(BF)


def get_small(source, first, width):
    return source[first:, :width].astype(F32) + source[first:, width : 2 * width].astype(F32)


def attention(heads, blocks, numbers, pieces, tokens, qkv_weight, vectors, out_weight, after):
    tok_count, feature_width = tokens.shape
    pair = 2 * HEAD_DIM
    head_width = heads * HEAD_DIM
    value_tiles = -(-heads // 2) * pair
    arrays, plan = [], []
    for refs, (sides, distances) in pieces:
        numbered = []
        for array, base in refs:
            if not any(array is other for other in arrays):
                arrays.append(array)
            numbered.append(([array is other for other in arrays].index(True), base))
        plan.append((sides, distances, numbered))
    cos_table, sin_table = rotary_tables(SEQ)
    per_head = shaped((heads, SEQ, pair), BF)
    window = -(-(3 * head_width) // LANES) * LANES
    return call(
        functools.partial(attention_kernel, heads, blocks, tok_count, len(arrays), plan),
        inputs=arrays + [numbers, far(qkv_weight), vectors, far(out_weight), far(jnp.asarray(cos_table)), far(jnp.asarray(sin_table))],
        after=after,
        in_specs=[ANY] * len(arrays) + [SMEM, ANY, VMEM, ANY, ANY, ANY],
        out_specs=[ANY] * 7,
        out_shape=[pltpu.HBM(per_head.shape, BF)] * 4
        + [pltpu.HBM((SEQ, feature_width), BF)] * 2
        + [pltpu.HBM(per_head.shape, BF)],
        scratch_shapes=[pltpu.VMEM((SEQ, pair), F32)] * 2
        + [pltpu.VMEM((heads, SEQ, pair), BF)] * 4
        + [pltpu.VMEM((SEQ, feature_width), BF)] * 2
        + [
            pltpu.VMEM((feature_width, window), BF),
            pltpu.VMEM((feature_width, 2 * heads * pair + value_tiles), BF),
            pltpu.VMEM((8, 2 * heads * pair + value_tiles), F32),
            pltpu.VMEM((value_tiles, feature_width), BF),
            pltpu.VMEM((heads, SEQ, pair), BF),
            pltpu.VMEM((SEQ, pair), F32),
            pltpu.VMEM((SEQ, pair), F32),
            pltpu.SemaphoreType.DMA((4 + len(arrays) + 4 + 3 * heads,)),
        ]
        + [pltpu.VMEM(array.shape, array.dtype) for array in arrays],
        compiler_params=params(44),
        name="attention",
    )


def attention_back(heads, blocks, numbers, parts, qkv_weight, vectors, after):
    *_, unit, attended, grad_out = parts
    (tok_count, head_width), (local_rows, feature_width) = attended.shape, grad_out.shape
    pair = 2 * HEAD_DIM
    width = -(-(3 * head_width) // LANES) * LANES
    small_rows = -(-(4 + 2 * HEADS // heads) // 16) * 16
    cos_table, sin_table = rotary_tables(SEQ)
    return call(
        functools.partial(attention_back_kernel, heads, blocks),
        inputs=[numbers, *[far(part) for part in parts[:5]], *parts[5:], far(qkv_weight), vectors, far(jnp.asarray(cos_table)), far(jnp.asarray(sin_table))],
        after=after,
        in_specs=[SMEM] + [ANY] * 5 + [VMEM] * 2 + [ANY, VMEM, ANY, ANY],
        out_specs=[VMEM] * 2,
        out_shape=[
            shaped((tok_count // 2 + local_rows + small_rows, feature_width + head_width), BF),
        ] * 2,
        scratch_shapes=[pltpu.VMEM((heads, SEQ, pair), BF)] * 4
        + [pltpu.VMEM((SEQ, feature_width), BF)]
        + [pltpu.VMEM((SEQ, pair), F32)] * 2
        + [
            pltpu.VMEM((pair, SEQ), F32),
            pltpu.VMEM((SEQ, pair), F32),
            pltpu.VMEM((heads, SEQ, pair), BF),
            pltpu.VMEM((heads, SEQ, pair), BF),
            pltpu.VMEM((SEQ, width), BF),
            pltpu.VMEM((feature_width, width), F32),
            pltpu.VMEM((small_rows, feature_width // 2), F32),
            pltpu.VMEM((feature_width, width), BF),
            pltpu.SemaphoreType.DMA((4 + 4 * heads,)),
        ],
        compiler_params=params(42),
        name="attention_back",
    )


def hidden_kernel(sides, first_call, *refs):
    place_ref, count = refs[0], len(sides)
    piece_refs, (up_ref, up_bias_ref, down_ref, vectors_ref) = refs[1 : count + 1], refs[count + 1 : count + 5]
    before_refs = [None, None] if first_call else refs[count + 5 : count + 7]
    normed_ref, turned_ref, curve_ref, grad_ref, active_ref, bias_grad_ref, cot_sum_ref = refs[-7:]
    cot = jnp.concatenate([ref[0, 1] for ref in piece_refs], axis=0)
    unit = standardize(jnp.concatenate([ref[0, 0] for ref in piece_refs], axis=0).astype(F32))
    normed = (unit * vectors_ref[2:3, :] + vectors_ref[3:4, :]).astype(BF)
    normed_ref[...] = normed
    turned_ref[...] = normed.T
    hidden = dot(normed, up_ref[...]) + up_bias_ref[...]
    upstream = dot_nt(cot, down_ref[...])
    below, density = gelu_parts(hidden)
    active = (hidden * below).astype(BF)
    hidden_grad = (upstream * (below + hidden * density)).astype(BF)
    grad_ref[...] = hidden_grad
    curve_ref[...] = upstream * density * (2.0 - hidden * hidden)
    size = active.shape[0] // count
    for number, side in enumerate(sides):
        rows = pl.ds(pl.multiple_of(jnp.bitwise_xor(place_ref[2], side) * size, size), size)
        active_ref[rows, :] = active[number * size : (number + 1) * size]

    @pl.when(pl.program_id(0) == 0)
    def _():
        for before, target in zip(before_refs, (bias_grad_ref, cot_sum_ref)):
            target[...] = jnp.zeros_like(target) if first_call else before[...]

    bias_grad_ref[...] += jnp.sum(hidden_grad.astype(F32), axis=0, keepdims=True)
    cot_sum_ref[...] += jnp.sum(cot.astype(F32), axis=0, keepdims=True)


def hidden_units(places, pieces, sides, first, distances, count, up_part, up_bias_part, down_part, vectors, before):
    arrays = [array for array, _ in pieces]
    feature_width, part_width = arrays[0].shape[3], up_bias_part.shape[1]
    tok_count = sum(array.shape[2] for array in arrays)

    def fixed(*shape):
        return pl.BlockSpec(shape, lambda i, place_ref: (0,) * len(shape))

    def piece(array, slot_of):
        return pl.BlockSpec((1,) + array.shape[1:], lambda i, place_ref: (slot_of(i), 0, 0, 0))

    def block_of(i, place_ref):
        distance = distances[0]
        for number in range(1, len(distances)):
            distance = jnp.where(i == number, distances[number], distance)
        return (jnp.bitwise_xor(place_ref[1], distance), 0)

    units = pl.BlockSpec((tok_count, part_width), lambda i, place_ref: (first + i, 0))
    sums = [fixed(1, part_width), fixed(1, feature_width)]
    inputs = [places, *arrays, far(up_part), up_bias_part, far(down_part), vectors]
    aliases = {}
    if before:
        aliases = {len(inputs) + 2 + k: k for k in range(5)}
        inputs += list(before[5:]) + [far(array) for array in before[:5]]

    def body(*refs):
        spare = 5 if before else 0
        kept = len(refs) - 7 - spare
        hidden_kernel(sides, before is None, *refs[:kept], *refs[kept + spare :])

    return pl.pallas_call(
        body,
        grid_spec=pltpu.PrefetchScalarGridSpec(
            num_scalar_prefetch=1,
            grid=(len(distances),),
            in_specs=[piece(array, slot_of) for array, slot_of in pieces] + [
                pl.BlockSpec((feature_width, part_width), lambda i, place_ref: (0, place_ref[0])),
                fixed(1, part_width),
                pl.BlockSpec((part_width, feature_width), lambda i, place_ref: (place_ref[0], 0)),
                fixed(8, feature_width),
            ] + (sums + [ANY] * 5 if before else []),
            out_specs=[
                pl.BlockSpec((tok_count, feature_width), lambda i, place_ref: (first + i, 0)),
                pl.BlockSpec((feature_width, tok_count), lambda i, place_ref: (0, first + i)),
                units, units, pl.BlockSpec((tok_count, part_width), block_of),
            ] + sums,
        ),
        out_shape=[
            pltpu.HBM((count, feature_width), BF),
            pltpu.HBM((feature_width, count), BF),
            pltpu.HBM((count, part_width), F32),
            pltpu.HBM((count, part_width), BF),
            pltpu.HBM((count, part_width), BF),
            shaped((1, part_width), F32),
            shaped((1, feature_width), F32),
        ],
        input_output_aliases=aliases,
        compiler_params=params(30),
        name="hidden_units",
        cost_estimate=LIGHT,
    )(*inputs)


def curvature_kernel(
    probes, place_ref, dirs_ref, local_ref, up_bias_ref, normed_ref, turned_ref, curve_ref, grad_ref,
    curvature_ref, score_ref, total_s, score_s, spare_s, weighted_s,
):
    step, steps = pl.program_id(0), pl.num_programs(0)
    feature_width, width = dirs_ref.shape
    part_width = width // probes
    half = part_width // 2

    @pl.when(step == 0)
    def _():
        score_s[...] = jnp.zeros_like(score_s)

    along = dot(normed_ref[...], dirs_ref[...])
    curve, grad = curve_ref[...], grad_ref[...]
    wide = grad.astype(F32)
    for k in range(probes):
        part = along[:, k * part_width : (k + 1) * part_width]
        weighted_s[:, k * part_width : (k + 1) * part_width] = (part * curve).astype(BF)
        score_s[k : k + 1, :] += jnp.sum(part * wide, axis=0, keepdims=True)
    weighted_s[:, width:] = grad
    total = dot(turned_ref[...], weighted_s[...])

    @pl.when(step == 0)
    def _():
        total_s[...] = total

    @pl.when((step > 0) & (step < steps - 1))
    def _():
        total_s[...] += total

    @pl.when(step == steps - 1)
    def _():
        shape = curvature_ref.shape[:2]
        final = (total_s[...] + total).astype(BF)
        curvature_ref[:, :, :width] = final[:, :width].reshape(shape + (width,))
        own = jnp.where(place_ref[0] == 1, final[:, width + half :], final[:, width : width + half])
        scores = jnp.sum(score_s[...], axis=1, keepdims=True)
        score_ref[...] = jnp.broadcast_to(scores, score_ref.shape)

        spare_s[...] = jnp.zeros_like(spare_s)
        row = 0
        for values in (local_ref[1:2, :], local_ref[2:3, :], up_bias_ref[...]):
            high = values.astype(BF).astype(F32)
            for part in (high, values - high):
                for start in range(0, values.shape[1], HEAD_DIM):
                    spare_s[row : row + 1, HEAD_DIM:] = part[:, start : start + HEAD_DIM]
                    row += 1
        high = scores.astype(BF).astype(F32)
        for part in (high, scores - high):
            for k in range(probes):
                spare_s[row : row + 1, HEAD_DIM + k : HEAD_DIM + k + 1] = part[k : k + 1, :]
            row += 1
        tail = jnp.concatenate([own[:, LANES:], jnp.zeros((feature_width, HEAD_DIM), BF)], axis=1)
        tail = tail.reshape(shape + (LANES,)) + spare_s[...].astype(BF)[None]
        curvature_ref[:, :, width : width + LANES] = own[:, :LANES].reshape(shape + (LANES,))
        curvature_ref[:, :, width + LANES :] = tail


def curvature_of(blocks, core, probes, units, dirs, local_small, up_bias_grad, after):
    (count, feature_width), part_width = units[0].shape, units[2].shape[1]
    width = probes * part_width
    steps = STEPS
    size = count // steps
    local_rows = feature_width // blocks
    out = (blocks, local_rows, width + 2 * LANES)
    return call(
        functools.partial(curvature_kernel, probes),
        inputs=[core[None].astype(jnp.int32), far(dirs), local_small, up_bias_grad] + [far(array) for array in units],
        after=after,
        grid=(steps,),
        in_specs=[
            SMEM, whole(feature_width, width), whole(8, feature_width), whole(1, part_width),
            pl.BlockSpec((size, feature_width), lambda i: (i, 0)),
            pl.BlockSpec((feature_width, size), lambda i: (0, i)),
            pl.BlockSpec((size, part_width), lambda i: (i, 0)),
            pl.BlockSpec((size, part_width), lambda i: (i, 0)),
        ],
        out_specs=[whole(*out), whole(8, LANES)],
        out_shape=[shaped(out, BF), shaped((8, LANES), F32)],
        scratch_shapes=[
            pltpu.VMEM((feature_width, width + part_width), F32),
            pltpu.VMEM((8, part_width), F32),
            pltpu.VMEM((local_rows, LANES), F32),
            pltpu.VMEM((size, width + part_width), BF),
        ],
        compiler_params=params(52),
        name="curvature",
    )


def weights_kernel(heads, place_ref, active_in, cot_in, attended_in, down_ref, attended_ref, out_ref, *scratch):
    active_s, cot_s, attended_s, joined_s, total_s, sems = scratch
    moves = [(cot_in, cot_s), (active_in, active_s), (attended_in, attended_s)]
    copies = [pltpu.make_async_copy(source, target, sems.at[k]) for k, (source, target) in enumerate(moves)]
    for copy in copies:
        copy.start()
    for copy in copies[:2]:
        copy.wait()
    down_ref[...] = dot_tn(active_s[...], cot_s[...])
    copies[2].wait()
    block = attended_ref.shape[0]
    for number in range(cot_s.shape[0] // block):
        rows = slice(number * block, (number + 1) * block)
        values = [attended_s[head, rows, :].astype(F32) for head in range(heads)]
        joined_s[rows, :] = heads_joined(values).astype(BF)
    own = pl.ds(pl.multiple_of(place_ref[0] * block, block), block)
    attended_ref[...] = joined_s[own, :][:, : attended_ref.shape[1]]
    total_s[...] = dot_tn(joined_s[...], cot_s[...])
    local_rows = out_ref.shape[0]
    rows = pl.ds(pl.multiple_of(place_ref[3], local_rows), local_rows)
    out_ref[...] = jnp.where(place_ref[2] == 1, total_s[rows, :], 0.0).astype(BF)


def weights_back(heads, blocks, numbers, active, cot, attended, after):
    (count, feature_width), part_width, pair = cot.shape, active.shape[1], 2 * HEAD_DIM
    value_tiles = -(-heads // 2) * pair
    return call(
        functools.partial(weights_kernel, heads),
        inputs=[numbers, far(active), far(cot), far(attended)],
        after=after,
        in_specs=[SMEM, ANY, ANY, ANY],
        out_specs=[VMEM] * 3,
        out_shape=[
            shaped((part_width, feature_width), F32),
            shaped((count // blocks, heads * HEAD_DIM), BF),
            shaped((feature_width // blocks, feature_width), BF),
        ],
        scratch_shapes=[
            pltpu.VMEM(active.shape, BF),
            pltpu.VMEM(cot.shape, BF),
            pltpu.VMEM(attended.shape, BF),
            pltpu.VMEM((count, value_tiles), BF),
            pltpu.VMEM((value_tiles, feature_width), F32),
            pltpu.SemaphoreType.DMA((3,)),
        ],
        compiler_params=params(32),
        name="weights_back",
    )


def unpack_kernel(probes, got_ref, curvature_ref):
    blocks = got_ref.shape[0]
    part_width = curvature_ref.shape[2] // blocks
    number = pl.program_id(0)
    for k in range(probes):

        @pl.when(number == k)
        def _(k=k):
            for block in range(blocks):
                part = got_ref[block, :, k * part_width : (k + 1) * part_width]
                curvature_ref[0, :, block * part_width : (block + 1) * part_width] = part.astype(F32)


def unpack(got, probes, part_width, after):
    blocks, local_rows, _ = got.shape
    return call(
        functools.partial(unpack_kernel, probes),
        inputs=[far(got)],
        after=after,
        grid=(probes,),
        in_specs=[whole(*got.shape)],
        out_specs=pl.BlockSpec((1, local_rows, blocks * part_width), lambda i: (i, 0, 0)),
        out_shape=pltpu.HBM((probes, local_rows, blocks * part_width), F32),
        compiler_params=params(24),
        name="unpack",
    )


def peel_kernel(probes, got_ref, up_ref, gain_ref, shift_ref, up_bias_ref, score_ref):
    blocks, _, share = got_ref.shape
    part_width = up_bias_ref.shape[0] // blocks
    tails = []
    for block in range(blocks):
        up_ref[:, block * share : (block + 1) * share] = got_ref[block]
        tails.append(got_ref[block, :, share - LANES :].astype(F32))
    total = tails[0]
    for tail in tails[1:]:
        total = total + tail

    def vector(rows, first, length):
        count = length // HEAD_DIM
        parts = [
            rows[first + k : first + k + 1, HEAD_DIM:] + rows[first + count + k : first + count + k + 1, HEAD_DIM:]
            for k in range(count)
        ]
        return jnp.concatenate(parts, axis=1)

    length = gain_ref.shape[0]
    step = 2 * length // HEAD_DIM
    gain_ref[...] = vector(total, 0, length).reshape(gain_ref.shape)
    shift_ref[...] = vector(total, step, length).reshape(shift_ref.shape)
    biases = [vector(tail, 2 * step, part_width) for tail in tails]
    up_bias_ref[...] = jnp.concatenate(biases, axis=1).reshape(up_bias_ref.shape)
    row = 2 * step + 2 * part_width // HEAD_DIM
    for k in range(probes):
        lane = HEAD_DIM + k
        score_ref[k : k + 1, :] = total[row : row + 1, lane : lane + 1] + total[row + 1 : row + 2, lane : lane + 1]


def peel(got, probes, part_width, after):
    blocks, local_rows, width = got.shape
    share = width - probes * part_width
    feature_width = blocks * local_rows
    vector = shaped((feature_width,), F32)
    return call(
        functools.partial(peel_kernel, probes),
        inputs=[got],
        after=after,
        grid=(1,),
        in_specs=[pl.BlockSpec((blocks, local_rows, share), lambda i: (0, 0, width // share - 1))],
        out_specs=[
            whole(local_rows, blocks * share), whole(feature_width), whole(feature_width),
            whole(blocks * part_width), whole(probes, 1),
        ],
        out_shape=[
            shaped((local_rows, blocks * share), BF),
            vector, vector, shaped((blocks * part_width,), F32), shaped((probes, 1), F32),
        ],
        compiler_params=params(BIG),
        name="peel",
    )


def spread_kernel(blocks, half, place_ref, mine_ref, got_ref, out_ref):
    odd = place_ref[0] == 1
    stride = mine_ref.shape[1] // blocks
    for block in range(blocks):
        here = slice(block * stride, block * stride + half)
        mine, got = mine_ref[:, here], got_ref[:, here]
        both = jnp.concatenate([jnp.where(odd, got, mine), jnp.where(odd, mine, got)], axis=1)
        out_ref[:, block * 2 * half : (block + 1) * 2 * half] = both.astype(F32)


def spread(core, mine, got, blocks, half, after):
    return call(
        functools.partial(spread_kernel, blocks, half),
        inputs=[core[None].astype(jnp.int32), mine, got],
        after=after,
        in_specs=[SMEM, VMEM, VMEM],
        out_specs=VMEM,
        out_shape=shaped((mine.shape[0], blocks * 2 * half), F32),
        compiler_params=params(12),
        name="spread",
    )


def merge_kernel(feature_width, half, few, place_ref, mine_ref, got_ref, merged_ref):
    odd = place_ref[0] == 1
    third = mine_ref.shape[1] - feature_width

    def ordered(rows, columns):
        mine, got = mine_ref[rows, columns], got_ref[rows, columns]
        return jnp.concatenate([jnp.where(odd, got, mine), jnp.where(odd, mine, got)], axis=1)

    main = slice(0, half + few)
    total = mine_ref[main, :feature_width].astype(F32) + got_ref[main, :feature_width].astype(F32)
    merged_ref[...] = jnp.zeros_like(merged_ref)
    merged_ref[main, :feature_width] = total.astype(BF)
    merged_ref[main, feature_width:] = ordered(main, slice(feature_width, feature_width + third))
    rows = slice(half + few, half + 2 * few)
    merged_ref[rows, : 4 * third] = ordered(rows, slice(0, 2 * third))
    first, width = half + 2 * few, feature_width // 2
    put_small(merged_ref, first, get_small(mine_ref, first, width) + get_small(got_ref, first, width))


def merge(core, mine, got, feature_width, half, few):
    count, width = mine.shape
    return call(
        functools.partial(merge_kernel, feature_width, half, few),
        inputs=[core[None].astype(jnp.int32), mine, got],
        in_specs=[SMEM, VMEM, VMEM],
        out_specs=VMEM,
        out_shape=shaped((count, 2 * width - feature_width), BF),
        compiler_params=params(12),
        name="merge",
    )


def finish_kernel(
    few, place_ref, mine_ref, got_ref, tokens_ref, base_ref, rest_ref, vectors_ref, out_weight_ref,
    final_ref, small_ref,
):
    tok_count, feature_width = tokens_ref.shape
    half = tok_count // 2
    third = (mine_ref.shape[1] - feature_width) // 2
    upper = place_ref[1] == 1
    own = pl.ds(pl.multiple_of(place_ref[0] * half, half), half)

    def ordered(rows, columns):
        mine, got = mine_ref[rows, columns], got_ref[rows, columns]
        return jnp.where(upper, got, mine), jnp.where(upper, mine, got)

    attended = jnp.concatenate(ordered(slice(0, half), slice(feature_width, None)), axis=1)
    layer_out = base_ref[own, :] + dot(attended, out_weight_ref[...])
    main = slice(0, half + few)
    total = mine_ref[main, :feature_width].astype(F32) + got_ref[main, :feature_width].astype(F32)
    centred, factor = spread_of(tokens_ref[own, :].astype(F32))
    term = norm_input_term(total[:half], vectors_ref[0:1, :], centred * factor, factor)
    final_ref[:half, :feature_width] = layer_out.astype(BF)
    final_ref[:half, feature_width:] = (rest_ref[own, :] + term).astype(BF)
    parts = []
    firsts = ordered(slice(half, half + few), slice(feature_width, None))
    others = ordered(slice(half + few, half + 2 * few), slice(0, 4 * third))
    for first, other in zip(firsts, others):
        for core in range(2):
            parts += [first[:, core * third : (core + 1) * third], other[:, 2 * core * third : 2 * (core + 1) * third]]
    grad_qkv = jnp.concatenate(parts, axis=1)
    final_ref[half : half + few, :feature_width] = total[half:].astype(BF)
    final_ref[half : half + few, feature_width:] = grad_qkv[:, :feature_width]
    final_ref[half + few :, :] = grad_qkv[:, feature_width:]
    first, width = half + 2 * few, feature_width // 2
    small_ref[...] = get_small(mine_ref, first, width) + get_small(got_ref, first, width)


def finish(places, mine, got, tokens, base, rest, vectors, out_weight, few):
    tok_count, feature_width = tokens.shape
    half = tok_count // 2
    return call(
        functools.partial(finish_kernel, few),
        inputs=[places, mine, got, tokens, far(base), far(rest), vectors, far(out_weight)],
        in_specs=[SMEM] + [VMEM] * 7,
        out_specs=[VMEM] * 2,
        out_shape=[
            shaped((half + 2 * few, 2 * feature_width), BF),
            shaped((mine.shape[0] - half - 2 * few, feature_width // 2), F32),
        ],
        compiler_params=params(20),
        name="finish",
    )


def join_kernel(
    few, mixed_width, place_ref, mine_ref, got_ref, small_ref, cot_ref,
    layer_out_ref, input_grad_ref, out_ref, qkv_ref, gain_ref, shift_ref, qkv_bias_ref, cot_sum_ref,
):
    half = layer_out_ref.shape[0] // 2
    feature_width = layer_out_ref.shape[1]
    odd = place_ref[0] == 1
    mine, got = mine_ref[...], got_ref[...]
    for core, side in enumerate((jnp.where(odd, got, mine), jnp.where(odd, mine, got))):
        rows = slice(core * half, (core + 1) * half)
        layer_out_ref[rows, :] = side[:half, :feature_width]
        input_grad_ref[rows, :] = side[:half, feature_width:]
        rows = slice(core * few, (core + 1) * few)
        out_ref[rows, :] = side[half : half + few, :feature_width].astype(F32)
        qkv_ref[rows, :feature_width] = side[half : half + few, feature_width:].astype(F32)
        qkv_ref[rows, feature_width:] = side[half + few :, :].astype(F32)
    small = small_ref[...]

    def rows_of(first, total):
        return jnp.concatenate([small[first : first + 1, :], small[first + 1 : first + 2, :]], axis=1)[:, :total]

    gain_ref[...] = rows_of(0, feature_width).reshape(gain_ref.shape)
    shift_ref[...] = rows_of(2, feature_width).reshape(shift_ref.shape)
    groups = qkv_bias_ref.shape[0] // mixed_width
    bias = [rows_of(4 + 2 * number, mixed_width) for number in range(groups)]
    qkv_bias_ref[...] = jnp.concatenate(bias, axis=1).reshape(qkv_bias_ref.shape)
    cot_sum_ref[...] = cot_ref[...].reshape(cot_sum_ref.shape)


def join(core, mine, got, small, cot, tok_count, few, mixed_width):
    feature_width = cot.shape[1]
    vector = shaped((feature_width,), F32)
    return call(
        functools.partial(join_kernel, few, mixed_width),
        inputs=[core[None].astype(jnp.int32), mine, got, small, cot],
        in_specs=[SMEM] + [VMEM] * 4,
        out_specs=[VMEM] * 8,
        out_shape=[shaped((tok_count, feature_width), BF)] * 2
        + [shaped((2 * few, feature_width), F32), shaped((2 * few, 3 * feature_width), F32), vector, vector]
        + [shaped((4 * mixed_width,), F32), vector],
        compiler_params=params(16),
        name="join",
    )


def on_device(
    tokens,
    segment_ids,
    qkv_weight,
    qkv_bias,
    out_weight,
    out_bias,
    up_weight,
    up_bias,
    down_weight,
    down_bias,
    norm1_gain,
    norm1_bias,
    norm2_gain,
    norm2_bias,
    probe_dirs,
    out_grad,
):
    tok_count, feature_width = tokens.shape
    hidden_width = up_weight.shape[1]
    probe_count, local_rows = probe_dirs.shape[:2]
    groups = lax.axis_size("ex")
    probe_groups = lax.axis_size("probe")
    blocks = SEQ // tok_count
    rows = groups // blocks
    ex_place = lax.axis_index("ex")
    place = ex_place % blocks
    row_place = ex_place // blocks
    probe_place = lax.axis_index("probe")
    core, upper = probe_place % 2, probe_place // 2
    heads = HEADS // probe_groups
    head_width = heads * HEAD_DIM
    part_width = hidden_width // blocks
    fine = part_width // rows
    row_groups = None
    if rows > 1:
        row_groups = [[r * blocks + b for b in range(blocks)] for r in range(rows)]
    across = [[r * blocks + b for r in range(rows)] for b in range(blocks)]

    def swap(value, distance):
        return lax.ppermute(value, "ex", [(i, i ^ distance) for i in range(groups)])

    def swap_probe(value, distance):
        return lax.ppermute(value, "probe", [(i, i ^ distance) for i in range(probe_groups)])

    def over_rows(value):
        if rows > 1:
            return lax.psum_scatter(value, "ex", axis_index_groups=across, scatter_dimension=0, tiled=True)
        return value

    def my_part(value, axis):
        shape = value.shape
        split = shape[:axis] + (rows, blocks, fine) + shape[axis + 1 :]
        part = lax.dynamic_index_in_dim(value.reshape(split), place, axis + 1, keepdims=False)
        return part.reshape(shape[:axis] + (part_width,) + shape[axis + 1 :])

    mine, share = slices_of(probe_place, probe_groups, tokens, out_grad)
    aside = swap(mine, 1)
    near, diagonal, distant, farthest = [swap(share, distance) for distance in (2, 3, 4, 6)]

    segments = segment_ids
    if rows > 1:
        segments = lax.dynamic_slice_in_dim(segment_ids, row_place * SEQ, SEQ)
    vectors = vectors_of(
        probe_groups, blocks, norm1_gain, norm1_bias, norm2_gain, norm2_bias, out_bias, down_bias, qkv_bias, segments
    )
    base, rest, local_small = local_part(tokens, out_grad, up_weight, up_bias, down_weight, vectors)

    second, third = stack([near, diagonal, distant, farthest], [(0, 1), (2, 3)], [local_small])
    third_aside, third_over = swap(third, 1), swap_probe(third, 2)
    (quarters,) = stack([mine, aside, third, third_over], [(0, 1, 2, 3)], [])
    swapped = swap_probe(quarters, 1)
    up_bias_part = my_part(up_bias, 0).astype(F32)[None]
    up_part, down_part = up_weight, down_weight
    if rows > 1:
        up_part, down_part = my_part(up_weight, 1), my_part(down_weight, 0)

    def pieces_of(array, other, slots, distances):
        return [
            ([(side, slot) for side in (array, other) for slot in pair], ((0, 2, 1, 3), (distance,)))
            for pair, distance in zip(slots, distances)
        ]

    pieces = pieces_of(quarters, swapped, ((0, 1), (2, 3), (4, 6), (5, 7)), (0, 1, 4, 6))
    slots = [lambda i: jnp.where(i < 2, 2 * i, i + 2), lambda i: jnp.where(i < 2, 2 * i + 1, i + 4)]
    refs = [(array, slot_of) for array in (quarters, swapped) for slot_of in slots]
    unit_place = place if rows == 1 else place * 0
    places = jnp.stack([unit_place, place, probe_place]).astype(jnp.int32)
    fixed = (SEQ, up_part, up_bias_part, down_part, vectors)
    units = hidden_units(places, refs, (0, 2, 1, 3), 0, (0, 1, 4, 6), *fixed, None)
    second_over, third_across = swap_probe(second, 2), swap_probe(third_aside, 2)

    dirs = tie(pack(probe_dirs, blocks, rows, [local_small]), [third_aside, quarters])
    dirs = lax.all_to_all(dirs, "ex", 0, 0, axis_index_groups=row_groups, tiled=True)
    dirs = dirs.reshape(blocks * local_rows, probe_count * part_width)
    if rows > 1:
        dirs = lax.all_gather(dirs, "ex", axis_index_groups=across, tiled=True)

    last = ((second, second_over, (2, 3)), (third_aside, third_across, (5, 7)))
    for number, (array, over, distances) in enumerate(last):
        (quarters,) = stack([array, over], [(0, 1)], [units[5]])
        swapped = swap_probe(quarters, 1)
        pieces += pieces_of(quarters, swapped, ((0, 2), (1, 3)), distances)
        refs = [(side, lambda i, k=k: i + 2 * k) for side in (quarters, swapped) for k in range(2)]
        units = hidden_units(places, refs, (0, 2, 1, 3), 4 + 2 * number, distances, *fixed, units)
    *units, active, grad_up_bias, cot_sum = units

    block_rows = feature_width // blocks
    offset = place * block_rows - probe_place * head_width
    holds = (offset >= 0) & (offset < head_width)
    numbers = jnp.stack([place, probe_place, holds, jnp.where(holds, offset, 0)]).astype(jnp.int32)
    *parts, cot, attended = attention(heads, blocks, numbers, pieces, tokens, qkv_weight, vectors, out_weight, [cot_sum])

    part, scores = curvature_of(
        blocks, core, probe_count, units, dirs, local_small, grad_up_bias, [far(attended)]
    )
    part = over_rows(part.reshape(feature_width, -1)).reshape(blocks, local_rows, -1)
    got = lax.all_to_all(part, "ex", 0, 0, axis_index_groups=row_groups, tiled=True)

    grad_down, attended, grad_out = weights_back(heads, blocks, numbers, active, cot, attended, [scores])
    parts += [attended, grad_out]
    keep, send = attention_back(heads, blocks, numbers, parts, qkv_weight, vectors, [scores])
    half, few = tok_count // 2, block_rows // 2
    merged = merge(core, keep, swap_probe(send, 1), feature_width, half, few)
    final, small = finish(
        jnp.stack([core, upper]).astype(jnp.int32), merged, swap_probe(merged, 2), tokens, base, rest, vectors,
        out_weight, few,
    )
    (
        layer_out, input_grad, grad_out_weight, grad_qkv_weight,
        grad_gain_one, grad_shift_one, grad_qkv_bias, cot_sum,
    ) = join(core, final, swap_probe(final, 1), small, cot_sum, tok_count, few, 3 * head_width)

    if rows == 1:
        up_half, grad_gain_two, grad_shift_two, grad_up_bias, scores = peel(
            got, probe_count, part_width, [layer_out]
        )
        other_half = swap_probe(up_half, 1)
        curvature = unpack(got, probe_count, part_width, [scores])
        grad_up_weight = spread(core, up_half, other_half, blocks, part_width // 2, [])
    else:
        start = probe_count * part_width
        units = got[:, :, :start].reshape(blocks, local_rows, probe_count, rows, fine)
        curvature = units.transpose(2, 1, 3, 0, 4).reshape(probe_count, local_rows, hidden_width)
        curvature = curvature.astype(F32)
        up_half = got[:, :, start : start + part_width // 2]
        both = lax.all_gather(up_half, "probe", axis_index_groups=[[0, 1], [2, 3]])
        both = both.transpose(2, 1, 0, 3).reshape(local_rows, blocks, rows, fine)
        grad_up_weight = both.transpose(0, 2, 1, 3).reshape(local_rows, hidden_width).astype(F32)
        grad_down = over_rows(grad_down)

        def over_groups(value):
            value = lax.all_gather(value, "ex", axis_index_groups=row_groups, tiled=True)
            return lax.dynamic_slice_in_dim(over_rows(value), place * local_rows, local_rows, 0)

        grad_qkv_weight, grad_out_weight = over_groups(grad_qkv_weight), over_groups(grad_out_weight)
        grad_gain_one, grad_shift_one, grad_qkv_bias, cot_sum, grad_up_bias = lax.psum(
            (grad_gain_one, grad_shift_one, grad_qkv_bias, cot_sum, grad_up_bias[0]),
            "ex",
            axis_index_groups=across,
        )
        grad_up_bias = lax.all_gather(grad_up_bias, "ex", axis_index_groups=row_groups)
        grad_up_bias = grad_up_bias.reshape(blocks, rows, fine).transpose(1, 0, 2).reshape(-1)
        grad_gain_two, grad_shift_two = lax.psum((local_small[1], local_small[2]), "ex")
        scores = lax.psum(scores[:probe_count, :1], "ex", axis_index_groups=row_groups)
        scores = lax.all_gather(scores, "ex", axis_index_groups=across, axis=1, tiled=True)
    return (
        layer_out,
        input_grad,
        grad_qkv_weight,
        grad_qkv_bias,
        grad_out_weight,
        cot_sum,
        grad_up_weight,
        grad_up_bias,
        grad_down,
        cot_sum,
        grad_gain_one,
        grad_shift_one,
        grad_gain_two,
        grad_shift_two,
        curvature,
        scores,
    )


def solution(mesh):
    in_specs = (
        P("ex", None),
        P(),
        P(),
        P(),
        P(),
        P(),
        P(),
        P(),
        P(),
        P(),
        P(),
        P(),
        P(),
        P(),
        P("probe", "ex", None),
        P("ex", None),
    )
    out_specs = (
        P("ex", None),
        P("ex", None),
        P("ex", None),
        P(),
        P("ex", None),
        P(),
        P("ex", None),
        P(),
        P("ex", None),
        P(),
        P(),
        P(),
        P(),
        P(),
        P("probe", "ex", None),
        P("probe", None),
    )
    return jax.shard_map(
        on_device, mesh=mesh, in_specs=in_specs, out_specs=out_specs, check_vma=False
    )
```

```python
import functools

import jax
import jax.numpy as jnp
import numpy as np
from jax import lax
from jax.experimental import pallas as pl
from jax.experimental.pallas import tpu as pltpu
from jax.sharding import PartitionSpec as P

HEADS = 12
HEAD_DIM = 64
ROT = 16
SEQ = 2048

BF = jnp.bfloat16
F32 = jnp.float32
eps_norm = 1e-05
masked_score = -1e30
half_root = 0.7071067811865476
gauss_peak = 0.3989422804014327
MB = 1024 * 1024
LANES = 128
LIGHT = pl.CostEstimate(flops=1000, bytes_accessed=1000, transcendentals=0)
BIG = 58


def dot(a, b):
    return jnp.dot(a, b, preferred_element_type=F32)


def dot_nt(a, b):
    return lax.dot_general(a, b, (((1,), (1,)), ((), ())), preferred_element_type=F32)


def dot_tn(a, b):
    return lax.dot_general(a, b, (((0,), (0,)), ((), ())), preferred_element_type=F32)


def spread_of(features):
    center = jnp.mean(features, axis=-1, keepdims=True)
    centred = features - center
    spread = jnp.mean(centred * centred, axis=-1, keepdims=True)
    return centred, lax.rsqrt(spread + eps_norm)


def standardize(features):
    centred, factor = spread_of(features)
    return centred * factor


def norm_input_term(grad, gain_row, unit, factor):
    unit_grad = grad * gain_row
    inner = unit_grad - jnp.mean(unit_grad, -1, keepdims=True)
    return (inner - unit * jnp.mean(unit_grad * unit, -1, keepdims=True)) * factor


def gelu_parts(pre_act):
    below = 0.5 + 0.5 * lax.erf(pre_act * half_root)
    density = gauss_peak * jnp.exp(-0.5 * pre_act * pre_act)
    return below, density


def rotary_tables(count):
    steps = np.arange(ROT // 2, dtype=np.float32) * np.float32(2.0 / ROT)
    inverse = np.power(np.float32(10000.0), -steps).astype(np.float32)
    angles = np.arange(count, dtype=np.float32)[:, None] * inverse[None, :]
    angles = np.concatenate([angles, angles], axis=1)
    cosine = np.ones((count, HEAD_DIM), np.float32)
    sine = np.zeros((count, HEAD_DIM), np.float32)
    cosine[:, :ROT], sine[:, :ROT] = np.cos(angles), np.sin(angles)
    return np.concatenate([cosine, cosine], axis=1), np.concatenate([sine, sine], axis=1)


def params(limit_mb, **more):
    return pltpu.CompilerParams(vmem_limit_bytes=limit_mb * MB, **more)


def shaped(shape, dtype):
    return jax.ShapeDtypeStruct(shape, dtype)


def whole(*shape):
    return pl.BlockSpec(shape, lambda i: (0,) * len(shape))


VMEM = pl.BlockSpec(memory_space=pltpu.VMEM)
SMEM = pl.BlockSpec(memory_space=pltpu.SMEM)
ANY = pl.BlockSpec(memory_space=pl.ANY)


def far(array):
    return pltpu.with_memory_space_constraint(array, pltpu.HBM)


def call(kernel, *, inputs, in_specs, after=(), aliases=None, **more):
    spare = len(after)

    def body(*refs):
        kernel(*refs[: len(inputs)], *refs[len(inputs) + spare :])

    return pl.pallas_call(
        body, in_specs=list(in_specs) + [ANY] * spare, input_output_aliases=aliases or {},
        cost_estimate=LIGHT, **more,
    )(*inputs, *after)


def tie(value, after):
    return call(
        lambda value_ref, out_ref: None,
        inputs=[value],
        after=after,
        aliases={0: 0},
        in_specs=[ANY],
        out_specs=ANY,
        out_shape=shaped(value.shape, value.dtype),
        name="tie",
    )


def pack_kernel(dirs_ref, packed_ref, sems):
    probes = dirs_ref.shape[0]
    blocks, _, width = packed_ref.shape
    part_width = width // probes
    copies = []
    for block in range(blocks):
        for k in range(probes):
            source = dirs_ref.at[k, :, block * part_width : (block + 1) * part_width]
            target = packed_ref.at[block, :, k * part_width : (k + 1) * part_width]
            copies.append(pltpu.make_async_copy(source, target, sems.at[len(copies)]))
    for copy in copies:
        copy.start()
    for copy in copies:
        copy.wait()


def pack(dirs, blocks, rows, after):
    probes, local_rows, hidden_width = dirs.shape
    part_width = hidden_width // blocks
    if rows > 1:
        split = dirs.reshape(probes, local_rows, rows, blocks, part_width // rows)
        return split.transpose(3, 1, 0, 2, 4).reshape(blocks, local_rows, probes * part_width)
    return call(
        pack_kernel,
        inputs=[dirs],
        after=after,
        in_specs=[VMEM],
        out_specs=ANY,
        out_shape=pltpu.HBM((blocks, local_rows, probes * part_width), dirs.dtype),
        scratch_shapes=[pltpu.SemaphoreType.DMA((blocks * probes,))],
        compiler_params=params(8),
        name="pack",
    )


def slices_kernel(place_ref, tokens_ref, grads_ref, both_ref, first_ref, sems):
    count = both_ref.shape[2]
    copies = []
    for part, source in enumerate((tokens_ref, grads_ref)):
        for target, slot, side in ((both_ref, 0, 0), (both_ref, 1, 2), (first_ref, 0, 0)):
            first = jnp.bitwise_xor(place_ref[0], side) * count
            rows = pl.ds(pl.multiple_of(first, count), count)
            copies.append(pltpu.make_async_copy(source.at[rows, :], target.at[slot, part], sems.at[len(copies)]))
    for copy in copies:
        copy.start()
    for copy in copies:
        copy.wait()


def slices_of(probe_place, probe_groups, tokens, grads):
    tok_count, feature_width = tokens.shape
    size = tok_count // probe_groups
    return call(
        slices_kernel,
        inputs=[probe_place[None].astype(jnp.int32), far(tokens), far(grads)],
        in_specs=[SMEM, ANY, ANY],
        out_specs=[VMEM] * 2,
        out_shape=[shaped((count, 2, size, feature_width), BF) for count in (2, 1)],
        scratch_shapes=[pltpu.SemaphoreType.DMA((6,))],
        compiler_params=params(8),
        name="slices",
    )


def stack_kernel(plan, *refs):
    sources, targets = refs[: -len(plan)], refs[-len(plan) :]
    for parts, target in zip(plan, targets):
        number = 0
        for part in parts:
            count = sources[part].shape[0]
            target[number : number + count] = sources[part][...]
            number += count


def stack(sources, plan, after):
    heights = [sum(sources[part].shape[0] for part in parts) for parts in plan]
    return call(
        functools.partial(stack_kernel, plan),
        inputs=sources,
        after=after,
        in_specs=[VMEM] * len(sources),
        out_specs=[VMEM] * len(plan),
        out_shape=[shaped((n,) + sources[parts[0]].shape[1:], BF) for n, parts in zip(heights, plan)],
        compiler_params=params(8),
        name="stack",
    )


def vectors_kernel(groups, blocks, count, *refs):
    sources, vectors_ref, held, sems = refs[:count], refs[count], refs[count + 1 : -1], refs[-1]
    copies = [pltpu.make_async_copy(source, target, sems.at[k]) for k, (source, target) in enumerate(zip(sources, held))]
    for copy in copies:
        copy.start()
    vectors_ref[...] = jnp.zeros_like(vectors_ref)
    for copy in copies:
        copy.wait()
    *plain, first_bias, second_bias, qkv_bias, segments = held
    for number, source in enumerate(plain):
        vectors_ref[number : number + 1, :] = source[...].reshape(1, -1)
    total = first_bias[...].astype(F32) + second_bias[...].astype(F32)
    vectors_ref[len(plain) : len(plain) + 1, :] = total.reshape(1, -1)
    width = qkv_bias.shape[0] // groups
    bias = qkv_bias[...].astype(F32).reshape(1, -1)
    for number in range(groups):
        vectors_ref[8 + number : 9 + number, :width] = bias[:, number * width : (number + 1) * width]
    block = segments.shape[0] // blocks
    for number in range(blocks):
        row = segments[number * block : (number + 1) * block].astype(F32).reshape(1, -1)
        vectors_ref[16 + number : 17 + number, :block] = row


def vectors_of(groups, blocks, *sources):
    return call(
        functools.partial(vectors_kernel, groups, blocks, len(sources)),
        inputs=[far(source) for source in sources],
        in_specs=[ANY] * len(sources),
        out_specs=VMEM,
        out_shape=shaped((16 + blocks, sources[0].shape[0]), F32),
        scratch_shapes=[pltpu.VMEM(source.shape, source.dtype) for source in sources]
        + [pltpu.SemaphoreType.DMA((len(sources),))],
        compiler_params=params(4),
        name="vectors",
    )


def local_kernel(
    tokens_ref, grads_ref, up_ref, up_bias_ref, down_ref, vectors_ref,
    base_ref, rest_ref, small_ref, normed_s, branch_s, back_s,
):
    step = pl.program_id(0)
    gain, shift, out_bias = vectors_ref[2:3, :], vectors_ref[3:4, :], vectors_ref[4:5, :]

    @pl.when(step == 0)
    def _():
        unit = standardize(tokens_ref[...].astype(F32))
        normed_s[...] = (unit * gain + shift).astype(BF)
        branch_s[...] = jnp.zeros_like(branch_s)
        back_s[...] = jnp.zeros_like(back_s)

    bias = up_bias_ref[pl.ds(pl.multiple_of(step * up_ref.shape[1], LANES), up_ref.shape[1])]
    hidden = dot(normed_s[...], up_ref[...]) + bias.astype(F32).reshape(1, -1)
    upstream = dot_nt(grads_ref[...], down_ref[...])
    below, density = gelu_parts(hidden)
    branch_s[...] += dot((hidden * below).astype(BF), down_ref[...])
    hidden_grad = (upstream * (below + hidden * density)).astype(BF)
    back_s[...] += dot_nt(hidden_grad, up_ref[...])

    @pl.when(step == pl.num_programs(0) - 1)
    def _():
        inputs = tokens_ref[...].astype(F32)
        cot = grads_ref[...].astype(F32)
        centred, factor = spread_of(inputs)
        unit = centred * factor
        back = back_s[...]
        base_ref[...] = inputs + branch_s[...] + out_bias
        rest_ref[...] = cot + norm_input_term(back, gain, unit, factor)
        small_ref[...] = jnp.zeros_like(small_ref)
        small_ref[0:1, :] = jnp.sum(cot, axis=0, keepdims=True)
        small_ref[1:2, :] = jnp.sum(back * unit, axis=0, keepdims=True)
        small_ref[2:3, :] = jnp.sum(back, axis=0, keepdims=True)


def local_part(tokens, grads, up_weight, up_bias, down_weight, vectors):
    tok_count, feature_width = tokens.shape
    hidden_width = up_weight.shape[1]
    step = 512
    own = whole(tok_count, feature_width)
    return call(
        local_kernel,
        inputs=[tokens, grads, far(up_weight), up_bias, far(down_weight), vectors],
        grid=(hidden_width // step,),
        in_specs=[
            own, own,
            pl.BlockSpec((feature_width, step), lambda i: (0, i)),
            whole(hidden_width),
            pl.BlockSpec((step, feature_width), lambda i: (i, 0)),
            whole(8, feature_width),
        ],
        out_specs=[own, own, whole(8, feature_width)],
        out_shape=[
            shaped((tok_count, feature_width), F32),
            shaped((tok_count, feature_width), F32),
            shaped((8, feature_width), F32),
        ],
        scratch_shapes=[
            pltpu.VMEM((tok_count, feature_width), BF),
            pltpu.VMEM((tok_count, feature_width), F32),
            pltpu.VMEM((tok_count, feature_width), F32),
        ],
        compiler_params=params(24),
        name="local",
    )


def lanes(rows):
    return lax.broadcasted_iota(jnp.int32, (rows, 2 * HEAD_DIM), 1)


def flipped(tile):
    return pltpu.roll(tile, HEAD_DIM, 1)


def joined(left, right):
    return jnp.where(lanes(left.shape[0]) < HEAD_DIM, left, flipped(right))


def half_turned(tile):
    place_in = lanes(tile.shape[0]) % HEAD_DIM
    low = pltpu.roll(tile, 2 * HEAD_DIM - ROT // 2, 1)
    high = pltpu.roll(tile, ROT // 2, 1)
    return jnp.where(place_in < ROT // 2, -low, jnp.where(place_in < ROT, high, 0.0))


def with_column(tile, lane, column):
    first = column.astype(BF).astype(F32)
    number = lanes(tile.shape[0])
    return jnp.where(number == lane, first, jnp.where(number == lane + 1, column - first, tile))


def heads_joined(values):
    heads = len(values)
    values = [joined(values[k], values[k + 1]) if k + 1 < heads else values[k] for k in range(0, heads, 2)]
    if heads % 2:
        values[-1] = jnp.where(lanes(values[-1].shape[0]) < HEAD_DIM, values[-1], 0.0)
    return jnp.concatenate(values, axis=1)


def attention_kernel(heads, blocks, block, count, plan, *refs):
    sources, refs = refs[:count], refs[count:]
    (
        place_ref, weight_ref, vectors_ref, out_weight_ref, cos_in, sin_in,
        query_out, key_out, value_out, back_out, unit_out, cot_out, attended_out,
        cos_ref, sin_ref, query_s, key_s, value_s, back_s, unit_s, cot_s,
        window_s, weight_s, bias_s, out_weight_s, attended_s, query_code_s, key_code_s, sems,
        *array_refs,
    ) = refs
    place, probe_place = place_ref[0], place_ref[1]
    feature_width = unit_s.shape[1]
    pair = 2 * HEAD_DIM
    scale = HEAD_DIM ** (-0.5)
    gain, shift = vectors_ref[0:1, :], vectors_ref[1:2, :]
    own_rows = pl.ds(pl.multiple_of(place * block, block), block)
    head_width = heads * HEAD_DIM
    mixed_width = 3 * head_width

    first = probe_place * mixed_width // LANES * LANES
    columns = pl.ds(pl.multiple_of(first, LANES), window_s.shape[1])
    rows = pl.ds(pl.multiple_of(probe_place * head_width, HEAD_DIM), head_width)
    moves = [(weight_ref.at[:, columns], window_s), (out_weight_ref.at[rows, :], out_weight_s.at[:head_width, :])]
    moves += [(cos_in, cos_ref), (sin_in, sin_ref)] + list(zip(sources, array_refs))
    copies = [pltpu.make_async_copy(source, target, sems.at[k]) for k, (source, target) in enumerate(moves)]
    for copy in copies:
        copy.start()
    done = len(copies)

    def leave(number, source, target):
        return pltpu.make_async_copy(source, target, sems.at[done + number])

    def rows_of(number):
        return pl.ds(pl.multiple_of(number * block, block), block)

    def side_rows(distance, side, count):
        own = place_ref[1] % (block // count)
        first = jnp.bitwise_xor(place, distance) * block + jnp.bitwise_xor(own, side) * count
        return pl.ds(pl.multiple_of(first, count), count)

    def together(refs, slot, part):
        return jnp.concatenate([array_refs[ref][base + slot, part] for ref, base in refs], axis=0)

    def arrange(source, target):
        for head in range(heads):
            start = head * 3 * HEAD_DIM
            tile = source[:, start : start + pair]
            target[:, head * pair : (head + 1) * pair] = tile.astype(target.dtype)
        values = [source[:, (3 * head + 2) * HEAD_DIM : (3 * head + 3) * HEAD_DIM] for head in range(heads)]
        values.append(jnp.zeros((source.shape[0], -heads * HEAD_DIM % pair), source.dtype))
        target[:, heads * pair :] = jnp.concatenate(values, axis=1).astype(target.dtype)

    number = lanes(block)
    ones = (number >= HEAD_DIM + 16) & (number < HEAD_DIM + 18)
    coded = (number >= HEAD_DIM) & (number < HEAD_DIM + 16)
    for index in range(blocks):
        segment = jnp.broadcast_to(vectors_ref[16 + index : 17 + index, :block], (pair, block)).T
        segment = segment.astype(jnp.int32)
        match = (number == HEAD_DIM + segment // 8) | (number == HEAD_DIM + 8 + segment % 8)
        here = slice(index * block, (index + 1) * block)
        query_code_s[here, :] = jnp.where(coded & ~match, masked_score, 0.0)
        key_code_s[here, :] = jnp.where(match | ones, 1.0, 0.0)

    out_weight_s[head_width:, :] = jnp.zeros((out_weight_s.shape[0] - head_width, feature_width), BF)
    copies[0].wait()
    odd = probe_place * mixed_width % LANES != 0
    window = window_s[...]
    weight = jnp.where(odd, window[:, HEAD_DIM : HEAD_DIM + mixed_width], window[:, :mixed_width])
    arrange(weight, weight_s)
    bias = vectors_ref[pl.ds(8 + probe_place, 1), :mixed_width]
    arrange(jnp.broadcast_to(bias, (8, mixed_width)), bias_s)
    for copy in copies[1:4]:
        copy.wait()

    def project(sides, refs, slot, distance):
        unit = standardize(together(refs, slot, 0).astype(F32))
        normed = (unit * gain + shift).astype(BF)
        low = unit.astype(BF)
        whole_part = dot(normed, weight_s[...]) + bias_s[:1, :]
        cot = together(refs, slot, 1)
        whole_back = dot_nt(cot, out_weight_s[...])
        count = block // len(sides)
        for number, side in enumerate(sides):
            here = slice(number * count, (number + 1) * count)
            rows = side_rows(distance, side, count)
            unit_s[rows, :] = low[here]
            cot_s[rows, :] = cot[here]
            place_heads(rows, whole_part[here], whole_back[here])

    def place_heads(rows, part, back_part):
        cosine, sine = cos_ref[rows, :], sin_ref[rows, :]
        number = lanes(part.shape[0])
        query_code, key_code = query_code_s[rows, :], key_code_s[rows, :]
        value_code = jnp.where((number >= HEAD_DIM) & (number < HEAD_DIM + 2), 1.0, 0.0)
        first = number < HEAD_DIM
        for head in range(heads):
            plain = part[:, head * pair : (head + 1) * pair]
            both = plain * cosine + half_turned(plain) * sine
            query_s[head, rows, :] = jnp.where(first, both * scale, query_code).astype(BF)
            key_s[head, rows, :] = jnp.where(first, flipped(both), key_code).astype(BF)
            start = heads * pair + head // 2 * pair
            tile = part[:, start : start + pair]
            back_tile = back_part[:, head // 2 * pair : head // 2 * pair + pair]
            if head % 2:
                tile, back_tile = flipped(tile), flipped(back_tile)
            value_s[head, rows, :] = jnp.where(first, tile, value_code).astype(BF)
            back_s[head, rows, :] = jnp.where(first, back_tile, 0.0).astype(BF)

    here = set()
    for sides, distances, refs in plan:
        for number in sorted({ref for ref, _ in refs} - here):
            copies[4 + number].wait()
            here.add(number)
        for slot, distance in enumerate(distances):
            project(sides, refs, slot, distance)
    leaving = [leave(0, key_s, key_out), leave(1, value_s, value_out), leave(2, unit_s, unit_out)]
    leaving.append(leave(3, cot_s, cot_out))
    for copy in leaving:
        copy.start()

    square = (block, block)
    lower = lax.broadcasted_iota(jnp.int32, square, 1) <= lax.broadcasted_iota(jnp.int32, square, 0)

    def head_leaving(head):
        pairs = ((query_s, query_out), (back_s, back_out), (attended_s, attended_out))
        return [leave(4 + 3 * head + k, source.at[head], target.at[head]) for k, (source, target) in enumerate(pairs)]

    def attend(head, carry):
        def scores_of(number):
            start, stop = number * block, (number + 1) * block
            query = query_s[head, start:stop, :]
            near = jnp.where(lower, dot_nt(query, key_s[head, start:stop, :]), masked_score)
            return near, dot_nt(query, key_s[head, :start, :]) if number else None

        ahead = scores_of(0)
        for number in range(blocks):
            start, stop = number * block, (number + 1) * block
            near, far = ahead
            if number + 1 < blocks:
                ahead = scores_of(number + 1)
            top = jnp.max(near, axis=-1, keepdims=True)
            if number:
                top = jnp.maximum(top, jnp.max(far, axis=-1, keepdims=True))
            got = dot(jnp.exp(near - top).astype(BF), value_s[head, start:stop, :])
            if number:
                got = got + dot(jnp.exp(far - top).astype(BF), value_s[head, :start, :])
            total = got[:, HEAD_DIM : HEAD_DIM + 1]
            attended = got / total
            attended_s[head, start:stop, :] = attended.astype(BF)
            back = back_s[head, start:stop, :].astype(F32)
            delta = jnp.sum(attended * back, axis=-1, keepdims=True)
            log_total = top + jnp.log(total)
            query = query_s[head, start:stop, :].astype(F32)
            query_s[head, start:stop, :] = with_column(query, HEAD_DIM + 16, -log_total).astype(BF)
            back_s[head, start:stop, :] = with_column(back, HEAD_DIM, -delta).astype(BF)
        for copy in head_leaving(head):
            copy.start()
        return carry

    lax.fori_loop(0, heads, attend, 0)

    for copy in leaving:
        copy.wait()
    for head in range(heads):
        for copy in head_leaving(head):
            copy.wait()


def attention_back_kernel(
    heads, blocks, place_ref, query_in, key_in, value_in, back_in, unit_in, attended_ref, grad_out_ref, weight_ref,
    vectors_ref, cos_in, sin_in,
    keep_ref, send_ref,
    query_s, key_s, value_s, back_s, unit_ref, cos_ref, sin_ref,
    query_grad_s, key_grad_s, both_s, value_grad_s, mixed_s, total_s, small_s, window_s, sems,
):
    place, probe_place = place_ref[0], place_ref[1]
    block, head_width = attended_ref.shape
    feature_width = unit_ref.shape[1]
    mixed_width = 3 * head_width
    scale = HEAD_DIM ** (-0.5)
    first = probe_place * mixed_width // LANES * LANES
    columns = pl.ds(pl.multiple_of(first, LANES), window_s.shape[1])
    others = [(cos_in, cos_ref), (sin_in, sin_ref), (unit_in, unit_ref), (weight_ref.at[:, columns], window_s)]
    others = [pltpu.make_async_copy(source, target, sems.at[k]) for k, (source, target) in enumerate(others)]

    def arriving(head):
        pairs = ((key_in, key_s), (query_in, query_s), (value_in, value_s), (back_in, back_s))
        return [
            pltpu.make_async_copy(source.at[head], target.at[head], sems.at[4 + len(pairs) * head + k])
            for k, (source, target) in enumerate(pairs)
        ]

    for copy in arriving(0) + others[:2]:
        copy.start()
    for head in range(1, heads):
        for copy in arriving(head):
            copy.start()
    for copy in others[2:]:
        copy.start()
    for copy in others[:2]:
        copy.wait()
    square = (block, block)
    upper = lax.broadcasted_iota(jnp.int32, square, 0) <= lax.broadcasted_iota(jnp.int32, square, 1)

    def through(head, carry):
        for copy in arriving(head):
            copy.wait()
        query_grad_s[...] = jnp.zeros_like(query_grad_s)
        for number in range(blocks):
            start, stop = number * block, (number + 1) * block
            key, value = key_s[head, start:stop, :], value_s[head, start:stop, :]
            key_t = key.T
            key_grad = value_grad = None
            for rows, mask in ((slice(start, stop), upper), (slice(stop, blocks * block), None)):
                if rows.start == rows.stop:
                    continue
                query, back = query_s[head, rows, :], back_s[head, rows, :]
                scores = dot_nt(key, query)
                if mask is not None:
                    scores = jnp.where(mask, scores, masked_score)
                probs = jnp.exp(scores)
                score_grad = (probs * dot_nt(value, back)).astype(BF)
                value_term, key_term = dot(probs.astype(BF), back), dot(score_grad, query)
                value_grad = value_term if value_grad is None else value_grad + value_term
                key_grad = key_term if key_grad is None else key_grad + key_term
                query_grad_s[:, rows] += dot(key_t, score_grad)
            key_grad_s[start:stop, :] = key_grad
            value_grad_s[head, start:stop, :] = value_grad.astype(BF)
        for number in range(blocks):
            rows = slice(number * block, (number + 1) * block)
            both = joined(query_grad_s[:, rows].T * scale, key_grad_s[rows, :])
            both = both * cos_ref[rows, :] - half_turned(both * sin_ref[rows, :])
            both_s[head, rows, :] = both.astype(BF)
        return carry

    lax.fori_loop(0, heads, through, 0)

    for number in range(blocks):
        rows = slice(number * block, (number + 1) * block)
        tiles = []
        for head in range(heads):
            both, value = both_s[head, rows, :].astype(F32), value_grad_s[head, rows, :].astype(F32)
            if head % 2 == 0:
                tiles += [both, value]
            else:
                tiles[-1] = joined(tiles[-1], both)
                tiles.append(joined(flipped(both), value))
        if heads % 2:
            tiles[-1] = jnp.where(lanes(block) < HEAD_DIM, tiles[-1], 0.0)
        mixed_s[rows, :] = jnp.concatenate(tiles, axis=1).astype(BF)

    others[2].wait()
    total_s[...] = dot_tn(unit_ref[...], mixed_s[...])
    sums = jnp.sum(mixed_s[...].astype(F32), axis=0, keepdims=True)
    others[3].wait()
    odd = probe_place * mixed_width % LANES != 0
    window = window_s[...]
    weight = jnp.where(odd, window[:, HEAD_DIM : HEAD_DIM + mixed_width], window[:, :mixed_width])

    own_rows = pl.ds(pl.multiple_of(place * block, block), block)
    mixed_own = mixed_s[own_rows, :][:, :mixed_width]
    normed_back = dot_nt(mixed_own, weight).astype(BF)

    local_rows = grad_out_ref.shape[0]
    first = pl.multiple_of(place * local_rows, local_rows)
    pick = lax.broadcasted_iota(jnp.int32, (local_rows, feature_width), 1) == first + lax.broadcasted_iota(
        jnp.int32, (local_rows, feature_width), 0
    )
    gain, shift = [
        jnp.sum(jnp.where(pick, vectors_ref[k : k + 1, :], 0.0), axis=1, keepdims=True) for k in range(2)
    ]
    grad_qkv = (total_s[pl.ds(first, local_rows), :] * gain + sums * shift).astype(BF)

    wide = weight.astype(F32)
    columns = [
        jnp.sum(wide * total_s[:, :mixed_width], axis=1, keepdims=True),
        jnp.sum(wide * sums[:, :mixed_width], axis=1, keepdims=True),
    ]
    number = lax.broadcasted_iota(jnp.int32, (feature_width, LANES), 1)
    columns = jnp.where(number == 0, columns[0], jnp.where(number == 1, columns[1], 0.0)).T
    piece = feature_width // 2
    small_s[...] = jnp.zeros_like(small_s)
    for k in range(2):
        for part in range(2):
            here = slice(part * piece, (part + 1) * piece)
            small_s[2 * k + part : 2 * k + part + 1, :piece] = columns[k : k + 1, here]
    small_s[pl.ds(4 + 2 * probe_place, 1), :piece] = sums[:, :piece]
    small_s[pl.ds(5 + 2 * probe_place, 1), : mixed_width - piece] = sums[:, piece:mixed_width]
    half, few = block // 2, local_rows // 2
    third = head_width
    odd = probe_place % 2 == 1

    def halves(value):
        low, high = value[: value.shape[0] // 2], value[value.shape[0] // 2 :]
        return jnp.where(odd, high, low), jnp.where(odd, low, high)

    attended, grad_out = attended_ref[...], grad_out_ref[...]
    for number, target in enumerate((keep_ref, send_ref)):
        target[...] = jnp.zeros_like(target)
        target[:half, :feature_width] = halves(normed_back)[number]
        target[:half, feature_width:] = halves(attended)[number]
        target[half : half + few, :feature_width] = halves(grad_out)[number]
        part = halves(grad_qkv)[number]
        target[half : half + few, feature_width:] = part[:, :third]
        target[half + few : half + 2 * few, : 2 * third] = part[:, third : 3 * third]
        put_small(target, half + 2 * few, small_s[...])


def put_small(target, first, small):
    width = small.shape[1]
    high = small.astype(BF)
    target[first:, :width] = high
    target[first:, width : 2 * width] = (small - high.astype(F32)).astype(BF)


def get_small(source, first, width):
    return source[first:, :width].astype(F32) + source[first:, width : 2 * width].astype(F32)


def attention(heads, blocks, numbers, pieces, tokens, qkv_weight, vectors, out_weight, after):
    tok_count, feature_width = tokens.shape
    pair = 2 * HEAD_DIM
    head_width = heads * HEAD_DIM
    value_tiles = -(-heads // 2) * pair
    arrays, plan = [], []
    for refs, (sides, distances) in pieces:
        numbered = []
        for array, base in refs:
            if not any(array is other for other in arrays):
                arrays.append(array)
            numbered.append(([array is other for other in arrays].index(True), base))
        plan.append((sides, distances, numbered))
    cos_table, sin_table = rotary_tables(SEQ)
    per_head = shaped((heads, SEQ, pair), BF)
    window = -(-(3 * head_width) // LANES) * LANES
    return call(
        functools.partial(attention_kernel, heads, blocks, tok_count, len(arrays), plan),
        inputs=arrays + [numbers, far(qkv_weight), vectors, far(out_weight), far(jnp.asarray(cos_table)), far(jnp.asarray(sin_table))],
        after=after,
        in_specs=[ANY] * len(arrays) + [SMEM, ANY, VMEM, ANY, ANY, ANY],
        out_specs=[ANY] * 7,
        out_shape=[pltpu.HBM(per_head.shape, BF)] * 4
        + [pltpu.HBM((SEQ, feature_width), BF)] * 2
        + [pltpu.HBM(per_head.shape, BF)],
        scratch_shapes=[pltpu.VMEM((SEQ, pair), F32)] * 2
        + [pltpu.VMEM((heads, SEQ, pair), BF)] * 4
        + [pltpu.VMEM((SEQ, feature_width), BF)] * 2
        + [
            pltpu.VMEM((feature_width, window), BF),
            pltpu.VMEM((feature_width, heads * pair + value_tiles), BF),
            pltpu.VMEM((8, heads * pair + value_tiles), F32),
            pltpu.VMEM((value_tiles, feature_width), BF),
            pltpu.VMEM((heads, SEQ, pair), BF),
            pltpu.VMEM((SEQ, pair), F32),
            pltpu.VMEM((SEQ, pair), F32),
            pltpu.SemaphoreType.DMA((4 + len(arrays) + 4 + 3 * heads,)),
        ]
        + [pltpu.VMEM(array.shape, array.dtype) for array in arrays],
        compiler_params=params(44),
        name="attention",
    )


def attention_back(heads, blocks, numbers, parts, qkv_weight, vectors, after):
    *_, unit, attended, grad_out = parts
    (tok_count, head_width), (local_rows, feature_width) = attended.shape, grad_out.shape
    pair = 2 * HEAD_DIM
    width = -(-(3 * head_width) // LANES) * LANES
    small_rows = -(-(4 + 2 * HEADS // heads) // 16) * 16
    cos_table, sin_table = rotary_tables(SEQ)
    return call(
        functools.partial(attention_back_kernel, heads, blocks),
        inputs=[numbers, *[far(part) for part in parts[:5]], *parts[5:], far(qkv_weight), vectors, far(jnp.asarray(cos_table)), far(jnp.asarray(sin_table))],
        after=after,
        in_specs=[SMEM] + [ANY] * 5 + [VMEM] * 2 + [ANY, VMEM, ANY, ANY],
        out_specs=[VMEM] * 2,
        out_shape=[
            shaped((tok_count // 2 + local_rows + small_rows, feature_width + head_width), BF),
        ] * 2,
        scratch_shapes=[pltpu.VMEM((heads, SEQ, pair), BF)] * 4
        + [pltpu.VMEM((SEQ, feature_width), BF)]
        + [pltpu.VMEM((SEQ, pair), F32)] * 2
        + [
            pltpu.VMEM((pair, SEQ), F32),
            pltpu.VMEM((SEQ, pair), F32),
            pltpu.VMEM((heads, SEQ, pair), BF),
            pltpu.VMEM((heads, SEQ, pair), BF),
            pltpu.VMEM((SEQ, width), BF),
            pltpu.VMEM((feature_width, width), F32),
            pltpu.VMEM((small_rows, feature_width // 2), F32),
            pltpu.VMEM((feature_width, width), BF),
            pltpu.SemaphoreType.DMA((4 + 4 * heads,)),
        ],
        compiler_params=params(42),
        name="attention_back",
    )


def hidden_kernel(sides, first_call, *refs):
    place_ref, count = refs[0], len(sides)
    piece_refs, (up_ref, up_bias_ref, down_ref, vectors_ref) = refs[1 : count + 1], refs[count + 1 : count + 5]
    before_refs = [None, None] if first_call else refs[count + 5 : count + 7]
    normed_ref, turned_ref, curve_ref, grad_ref, active_ref, bias_grad_ref, cot_sum_ref = refs[-7:]
    cot = jnp.concatenate([ref[0, 1] for ref in piece_refs], axis=0)
    unit = standardize(jnp.concatenate([ref[0, 0] for ref in piece_refs], axis=0).astype(F32))
    normed = (unit * vectors_ref[2:3, :] + vectors_ref[3:4, :]).astype(BF)
    normed_ref[...] = normed
    turned_ref[...] = normed.T
    hidden = dot(normed, up_ref[...]) + up_bias_ref[...]
    upstream = dot_nt(cot, down_ref[...])
    below, density = gelu_parts(hidden)
    active = (hidden * below).astype(BF)
    hidden_grad = (upstream * (below + hidden * density)).astype(BF)
    grad_ref[...] = hidden_grad
    curve_ref[...] = upstream * density * (2.0 - hidden * hidden)
    size = active.shape[0] // count
    for number, side in enumerate(sides):
        rows = pl.ds(pl.multiple_of(jnp.bitwise_xor(place_ref[2], side) * size, size), size)
        active_ref[rows, :] = active[number * size : (number + 1) * size]

    @pl.when(pl.program_id(0) == 0)
    def _():
        for before, target in zip(before_refs, (bias_grad_ref, cot_sum_ref)):
            target[...] = jnp.zeros_like(target) if first_call else before[...]

    bias_grad_ref[...] += jnp.sum(hidden_grad.astype(F32), axis=0, keepdims=True)
    cot_sum_ref[...] += jnp.sum(cot.astype(F32), axis=0, keepdims=True)


def hidden_units(places, pieces, sides, first, distances, count, up_part, up_bias_part, down_part, vectors, before):
    arrays = [array for array, _ in pieces]
    feature_width, part_width = arrays[0].shape[3], up_bias_part.shape[1]
    tok_count = sum(array.shape[2] for array in arrays)

    def fixed(*shape):
        return pl.BlockSpec(shape, lambda i, place_ref: (0,) * len(shape))

    def piece(array, slot_of):
        return pl.BlockSpec((1,) + array.shape[1:], lambda i, place_ref: (slot_of(i), 0, 0, 0))

    def block_of(i, place_ref):
        distance = distances[0]
        for number in range(1, len(distances)):
            distance = jnp.where(i == number, distances[number], distance)
        return (jnp.bitwise_xor(place_ref[1], distance), 0)

    units = pl.BlockSpec((tok_count, part_width), lambda i, place_ref: (first + i, 0))
    sums = [fixed(1, part_width), fixed(1, feature_width)]
    inputs = [places, *arrays, far(up_part), up_bias_part, far(down_part), vectors]
    aliases = {}
    if before:
        aliases = {len(inputs) + 2 + k: k for k in range(5)}
        inputs += list(before[5:]) + [far(array) for array in before[:5]]

    def body(*refs):
        spare = 5 if before else 0
        kept = len(refs) - 7 - spare
        hidden_kernel(sides, before is None, *refs[:kept], *refs[kept + spare :])

    return pl.pallas_call(
        body,
        grid_spec=pltpu.PrefetchScalarGridSpec(
            num_scalar_prefetch=1,
            grid=(len(distances),),
            in_specs=[piece(array, slot_of) for array, slot_of in pieces] + [
                pl.BlockSpec((feature_width, part_width), lambda i, place_ref: (0, place_ref[0])),
                fixed(1, part_width),
                pl.BlockSpec((part_width, feature_width), lambda i, place_ref: (place_ref[0], 0)),
                fixed(8, feature_width),
            ] + (sums + [ANY] * 5 if before else []),
            out_specs=[
                pl.BlockSpec((tok_count, feature_width), lambda i, place_ref: (first + i, 0)),
                pl.BlockSpec((feature_width, tok_count), lambda i, place_ref: (0, first + i)),
                units, units, pl.BlockSpec((tok_count, part_width), block_of),
            ] + sums,
        ),
        out_shape=[
            pltpu.HBM((count, feature_width), BF),
            pltpu.HBM((feature_width, count), BF),
            pltpu.HBM((count, part_width), F32),
            pltpu.HBM((count, part_width), BF),
            pltpu.HBM((count, part_width), BF),
            shaped((1, part_width), F32),
            shaped((1, feature_width), F32),
        ],
        input_output_aliases=aliases,
        compiler_params=params(30),
        name="hidden_units",
        cost_estimate=LIGHT,
    )(*inputs)


def curvature_kernel(
    probes, steps, place_ref, dirs_in, local_ref, up_bias_ref, normed_in, turned_in, curve_in, grad_in,
    curvature_out, score_ref,
    curvature_ref, dirs_ref, normed_ref, turned_ref, curve_ref, score_s, spare_s, weighted_s, sems,
):
    feature_width, width = dirs_ref.shape
    part_width = width // probes
    half = part_width // 2
    size = normed_ref.shape[0] // steps

    def moves(step):
        rows = slice(step * size, (step + 1) * size)
        return [
            pltpu.make_async_copy(source.at[rows, :], target, sems.at[3 * step + k])
            for k, (source, target) in enumerate((
                (normed_in, normed_ref.at[rows, :]),
                (curve_in, curve_ref.at[rows, :]),
                (grad_in, weighted_s.at[rows, width:]),
            ))
        ]

    begin = pltpu.make_async_copy(dirs_in, dirs_ref, sems.at[3 * steps])
    last = pltpu.make_async_copy(turned_in, turned_ref, sems.at[3 * steps + 1])
    begin.start()
    for step in range(steps):
        for copy in moves(step):
            copy.start()
    last.start()
    score_s[...] = jnp.zeros_like(score_s)
    begin.wait()
    for step in range(steps):
        for copy in moves(step):
            copy.wait()
        rows = slice(step * size, (step + 1) * size)
        along = dot(normed_ref[rows, :], dirs_ref[...])
        curve, wide = curve_ref[rows, :], weighted_s[rows, width:].astype(F32)
        for k in range(probes):
            columns = slice(k * part_width, (k + 1) * part_width)
            part = along[:, columns]
            weighted_s[rows, columns] = (part * curve).astype(BF)
            score_s[k : k + 1, :] += jnp.sum(part * wide, axis=0, keepdims=True)
    last.wait()
    shape = curvature_ref.shape[:2]
    leaving = []
    for k in range(0, probes, 2):
        columns = slice(k * part_width, (k + 2) * part_width)
        total = dot(turned_ref[...], weighted_s[:, columns])
        curvature_ref[:, :, columns] = total.astype(BF).reshape(shape + (2 * part_width,))
        leaving.append((curvature_ref.at[:, :, columns], curvature_out.at[:, :, columns]))
        pltpu.make_async_copy(*leaving[-1], sems.at[3 * steps + 1 + len(leaving)]).start()
    final = dot(turned_ref[...], weighted_s[:, width:]).astype(BF)
    own = jnp.where(place_ref[0] == 1, final[:, half:], final[:, :half])
    scores = jnp.sum(score_s[...], axis=1, keepdims=True)
    score_ref[...] = jnp.broadcast_to(scores, score_ref.shape)

    spare_s[...] = jnp.zeros_like(spare_s)
    row = 0
    for values in (local_ref[1:2, :], local_ref[2:3, :], up_bias_ref[...]):
        high = values.astype(BF).astype(F32)
        for part in (high, values - high):
            for start in range(0, values.shape[1], HEAD_DIM):
                spare_s[row : row + 1, HEAD_DIM:] = part[:, start : start + HEAD_DIM]
                row += 1
    high = scores.astype(BF).astype(F32)
    for part in (high, scores - high):
        for k in range(probes):
            spare_s[row : row + 1, HEAD_DIM + k : HEAD_DIM + k + 1] = part[k : k + 1, :]
        row += 1
    tail = jnp.concatenate([own[:, LANES:], jnp.zeros((feature_width, HEAD_DIM), BF)], axis=1)
    tail = tail.reshape(shape + (LANES,)) + spare_s[...].astype(BF)[None]
    curvature_ref[:, :, width : width + LANES] = own[:, :LANES].reshape(shape + (LANES,))
    curvature_ref[:, :, width + LANES :] = tail
    leaving.append((curvature_ref.at[:, :, width:], curvature_out.at[:, :, width:]))
    pltpu.make_async_copy(*leaving[-1], sems.at[3 * steps + 1 + len(leaving)]).start()
    for number, move in enumerate(leaving):
        pltpu.make_async_copy(*move, sems.at[3 * steps + 2 + number]).wait()


def curvature_of(blocks, core, probes, units, dirs, local_small, up_bias_grad, after):
    (count, feature_width), part_width = units[0].shape, units[2].shape[1]
    width = probes * part_width
    steps = 4
    local_rows = feature_width // blocks
    out = (blocks, local_rows, width + 2 * LANES)
    return call(
        functools.partial(curvature_kernel, probes, steps),
        inputs=[core[None].astype(jnp.int32), far(dirs), local_small, up_bias_grad] + [far(array) for array in units],
        after=after,
        in_specs=[SMEM, ANY, VMEM, VMEM] + [ANY] * 4,
        out_specs=[ANY, VMEM],
        out_shape=[pltpu.HBM(out, BF), shaped((8, LANES), F32)],
        scratch_shapes=[
            pltpu.VMEM(out, BF),
            pltpu.VMEM((feature_width, width), BF),
            pltpu.VMEM((count, feature_width), BF),
            pltpu.VMEM((feature_width, count), BF),
            pltpu.VMEM((count, part_width), F32),
            pltpu.VMEM((8, part_width), F32),
            pltpu.VMEM((local_rows, LANES), F32),
            pltpu.VMEM((count, width + part_width), BF),
            pltpu.SemaphoreType.DMA((3 * steps + 3 + probes // 2,)),
        ],
        compiler_params=params(52),
        name="curvature",
    )


def weights_kernel(heads, place_ref, active_in, cot_in, attended_in, down_ref, attended_ref, out_ref, *scratch):
    active_s, cot_s, attended_s, joined_s, total_s, sems = scratch
    moves = [(cot_in, cot_s), (active_in, active_s), (attended_in, attended_s)]
    copies = [pltpu.make_async_copy(source, target, sems.at[k]) for k, (source, target) in enumerate(moves)]
    for copy in copies:
        copy.start()
    for copy in copies[:2]:
        copy.wait()
    down_ref[...] = dot_tn(active_s[...], cot_s[...])
    copies[2].wait()
    block = attended_ref.shape[0]
    for number in range(cot_s.shape[0] // block):
        rows = slice(number * block, (number + 1) * block)
        values = [attended_s[head, rows, :].astype(F32) for head in range(heads)]
        joined_s[rows, :] = heads_joined(values).astype(BF)
    own = pl.ds(pl.multiple_of(place_ref[0] * block, block), block)
    attended_ref[...] = joined_s[own, :][:, : attended_ref.shape[1]]
    total_s[...] = dot_tn(joined_s[...], cot_s[...])
    local_rows = out_ref.shape[0]
    rows = pl.ds(pl.multiple_of(place_ref[3], local_rows), local_rows)
    out_ref[...] = jnp.where(place_ref[2] == 1, total_s[rows, :], 0.0).astype(BF)


def weights_back(heads, blocks, numbers, active, cot, attended, after):
    (count, feature_width), part_width, pair = cot.shape, active.shape[1], 2 * HEAD_DIM
    value_tiles = -(-heads // 2) * pair
    return call(
        functools.partial(weights_kernel, heads),
        inputs=[numbers, far(active), far(cot), far(attended)],
        after=after,
        in_specs=[SMEM, ANY, ANY, ANY],
        out_specs=[VMEM] * 3,
        out_shape=[
            shaped((part_width, feature_width), F32),
            shaped((count // blocks, heads * HEAD_DIM), BF),
            shaped((feature_width // blocks, feature_width), BF),
        ],
        scratch_shapes=[
            pltpu.VMEM(active.shape, BF),
            pltpu.VMEM(cot.shape, BF),
            pltpu.VMEM(attended.shape, BF),
            pltpu.VMEM((count, value_tiles), BF),
            pltpu.VMEM((value_tiles, feature_width), F32),
            pltpu.SemaphoreType.DMA((3,)),
        ],
        compiler_params=params(32),
        name="weights_back",
    )


def unpack_kernel(got_in, curvature_out, got_s, curvature_s, sems):
    blocks, _, width = got_s.shape
    probes = curvature_s.shape[0]
    part_width = width // probes

    def arrive(k):
        columns = slice(k * part_width, (k + 1) * part_width)
        return pltpu.make_async_copy(got_in.at[:, :, columns], got_s.at[:, :, columns], sems.at[k])

    def leave(k):
        return pltpu.make_async_copy(curvature_s.at[k], curvature_out.at[k], sems.at[probes + k])

    for k in range(probes):
        arrive(k).start()
    for k in range(probes):
        arrive(k).wait()
        for block in range(blocks):
            part = got_s[block, :, k * part_width : (k + 1) * part_width]
            curvature_s[k, :, block * part_width : (block + 1) * part_width] = part.astype(F32)
        leave(k).start()
    for k in range(probes):
        leave(k).wait()


def unpack(got, probes, part_width, after):
    blocks, local_rows, _ = got.shape
    out = (probes, local_rows, blocks * part_width)
    return call(
        unpack_kernel,
        inputs=[far(got)],
        after=after,
        in_specs=[ANY],
        out_specs=ANY,
        out_shape=pltpu.HBM(out, F32),
        scratch_shapes=[
            pltpu.VMEM((blocks, local_rows, probes * part_width), BF),
            pltpu.VMEM(out, F32),
            pltpu.SemaphoreType.DMA((2 * probes,)),
        ],
        compiler_params=params(24),
        name="unpack",
    )


def peel_kernel(probes, got_ref, up_ref, gain_ref, shift_ref, up_bias_ref, score_ref):
    blocks, _, share = got_ref.shape
    part_width = up_bias_ref.shape[0] // blocks
    tails = []
    for block in range(blocks):
        up_ref[:, block * share : (block + 1) * share] = got_ref[block]
        tails.append(got_ref[block, :, share - LANES :].astype(F32))
    total = tails[0]
    for tail in tails[1:]:
        total = total + tail

    def vector(rows, first, length):
        count = length // HEAD_DIM
        parts = [
            rows[first + k : first + k + 1, HEAD_DIM:] + rows[first + count + k : first + count + k + 1, HEAD_DIM:]
            for k in range(count)
        ]
        return jnp.concatenate(parts, axis=1)

    length = gain_ref.shape[0]
    step = 2 * length // HEAD_DIM
    gain_ref[...] = vector(total, 0, length).reshape(gain_ref.shape)
    shift_ref[...] = vector(total, step, length).reshape(shift_ref.shape)
    biases = [vector(tail, 2 * step, part_width) for tail in tails]
    up_bias_ref[...] = jnp.concatenate(biases, axis=1).reshape(up_bias_ref.shape)
    row = 2 * step + 2 * part_width // HEAD_DIM
    scores = total[row : row + 1, HEAD_DIM : HEAD_DIM + probes] + total[row + 1 : row + 2, HEAD_DIM : HEAD_DIM + probes]
    score_ref[...] = scores.reshape(score_ref.shape)


def peel(got, probes, part_width, after):
    blocks, local_rows, width = got.shape
    share = width - probes * part_width
    feature_width = blocks * local_rows
    vector = shaped((feature_width,), F32)
    return call(
        functools.partial(peel_kernel, probes),
        inputs=[got],
        after=after,
        grid=(1,),
        in_specs=[pl.BlockSpec((blocks, local_rows, share), lambda i: (0, 0, width // share - 1))],
        out_specs=[
            whole(local_rows, blocks * share), whole(feature_width), whole(feature_width),
            whole(blocks * part_width), whole(probes),
        ],
        out_shape=[
            shaped((local_rows, blocks * share), BF),
            vector, vector, shaped((blocks * part_width,), F32), shaped((probes,), F32),
        ],
        compiler_params=params(BIG),
        name="peel",
    )


def spread_kernel(blocks, half, place_ref, mine_ref, got_ref, out_ref):
    odd = place_ref[0] == 1
    stride = mine_ref.shape[1] // blocks
    for block in range(blocks):
        here = slice(block * stride, block * stride + half)
        mine, got = mine_ref[:, here], got_ref[:, here]
        both = jnp.concatenate([jnp.where(odd, got, mine), jnp.where(odd, mine, got)], axis=1)
        out_ref[:, block * 2 * half : (block + 1) * 2 * half] = both.astype(F32)


def spread(core, mine, got, blocks, half, after):
    return call(
        functools.partial(spread_kernel, blocks, half),
        inputs=[core[None].astype(jnp.int32), mine, got],
        after=after,
        in_specs=[SMEM, VMEM, VMEM],
        out_specs=VMEM,
        out_shape=shaped((mine.shape[0], blocks * 2 * half), F32),
        compiler_params=params(12),
        name="spread",
    )


def merge_kernel(feature_width, half, few, place_ref, mine_ref, got_ref, merged_ref):
    odd = place_ref[0] == 1
    third = mine_ref.shape[1] - feature_width

    def ordered(rows, columns):
        mine, got = mine_ref[rows, columns], got_ref[rows, columns]
        return jnp.concatenate([jnp.where(odd, got, mine), jnp.where(odd, mine, got)], axis=1)

    main = slice(0, half + few)
    total = mine_ref[main, :feature_width].astype(F32) + got_ref[main, :feature_width].astype(F32)
    merged_ref[...] = jnp.zeros_like(merged_ref)
    merged_ref[main, :feature_width] = total.astype(BF)
    merged_ref[main, feature_width:] = ordered(main, slice(feature_width, feature_width + third))
    rows = slice(half + few, half + 2 * few)
    merged_ref[rows, : 4 * third] = ordered(rows, slice(0, 2 * third))
    first, width = half + 2 * few, feature_width // 2
    put_small(merged_ref, first, get_small(mine_ref, first, width) + get_small(got_ref, first, width))


def merge(core, mine, got, feature_width, half, few):
    count, width = mine.shape
    return call(
        functools.partial(merge_kernel, feature_width, half, few),
        inputs=[core[None].astype(jnp.int32), mine, got],
        in_specs=[SMEM, VMEM, VMEM],
        out_specs=VMEM,
        out_shape=shaped((count, 2 * width - feature_width), BF),
        compiler_params=params(12),
        name="merge",
    )


def finish_kernel(
    few, place_ref, mine_ref, got_ref, tokens_ref, base_ref, rest_ref, vectors_ref, out_weight_ref,
    final_ref, small_ref,
):
    tok_count, feature_width = tokens_ref.shape
    half = tok_count // 2
    third = (mine_ref.shape[1] - feature_width) // 2
    upper = place_ref[1] == 1
    own = pl.ds(pl.multiple_of(place_ref[0] * half, half), half)

    def ordered(rows, columns):
        mine, got = mine_ref[rows, columns], got_ref[rows, columns]
        return jnp.where(upper, got, mine), jnp.where(upper, mine, got)

    attended = jnp.concatenate(ordered(slice(0, half), slice(feature_width, None)), axis=1)
    layer_out = base_ref[own, :] + dot(attended, out_weight_ref[...])
    main = slice(0, half + few)
    total = mine_ref[main, :feature_width].astype(F32) + got_ref[main, :feature_width].astype(F32)
    centred, factor = spread_of(tokens_ref[own, :].astype(F32))
    term = norm_input_term(total[:half], vectors_ref[0:1, :], centred * factor, factor)
    final_ref[:half, :feature_width] = layer_out.astype(BF)
    final_ref[:half, feature_width:] = (rest_ref[own, :] + term).astype(BF)
    parts = []
    firsts = ordered(slice(half, half + few), slice(feature_width, None))
    others = ordered(slice(half + few, half + 2 * few), slice(0, 4 * third))
    for first, other in zip(firsts, others):
        for core in range(2):
            parts += [first[:, core * third : (core + 1) * third], other[:, 2 * core * third : 2 * (core + 1) * third]]
    grad_qkv = jnp.concatenate(parts, axis=1)
    final_ref[half : half + few, :feature_width] = total[half:].astype(BF)
    final_ref[half : half + few, feature_width:] = grad_qkv[:, :feature_width]
    final_ref[half + few :, :] = grad_qkv[:, feature_width:]
    first, width = half + 2 * few, feature_width // 2
    small_ref[...] = get_small(mine_ref, first, width) + get_small(got_ref, first, width)


def finish(places, mine, got, tokens, base, rest, vectors, out_weight, few):
    tok_count, feature_width = tokens.shape
    half = tok_count // 2
    return call(
        functools.partial(finish_kernel, few),
        inputs=[places, mine, got, tokens, far(base), far(rest), vectors, far(out_weight)],
        in_specs=[SMEM] + [VMEM] * 7,
        out_specs=[VMEM] * 2,
        out_shape=[
            shaped((half + 2 * few, 2 * feature_width), BF),
            shaped((mine.shape[0] - half - 2 * few, feature_width // 2), F32),
        ],
        compiler_params=params(20),
        name="finish",
    )


def join_kernel(
    few, mixed_width, place_ref, mine_ref, got_ref, small_ref, cot_ref,
    layer_out_ref, input_grad_ref, out_ref, qkv_ref, gain_ref, shift_ref, qkv_bias_ref, out_bias_ref, down_bias_ref,
):
    half = layer_out_ref.shape[0] // 2
    feature_width = layer_out_ref.shape[1]
    odd = place_ref[0] == 1
    mine, got = mine_ref[...], got_ref[...]
    for core, side in enumerate((jnp.where(odd, got, mine), jnp.where(odd, mine, got))):
        rows = slice(core * half, (core + 1) * half)
        layer_out_ref[rows, :] = side[:half, :feature_width]
        input_grad_ref[rows, :] = side[:half, feature_width:]
        rows = slice(core * few, (core + 1) * few)
        out_ref[rows, :] = side[half : half + few, :feature_width].astype(F32)
        qkv_ref[rows, :feature_width] = side[half : half + few, feature_width:].astype(F32)
        qkv_ref[rows, feature_width:] = side[half + few :, :].astype(F32)
    small = small_ref[...]

    def rows_of(first, total):
        return jnp.concatenate([small[first : first + 1, :], small[first + 1 : first + 2, :]], axis=1)[:, :total]

    gain_ref[...] = rows_of(0, feature_width).reshape(gain_ref.shape)
    shift_ref[...] = rows_of(2, feature_width).reshape(shift_ref.shape)
    groups = qkv_bias_ref.shape[0] // mixed_width
    bias = [rows_of(4 + 2 * number, mixed_width) for number in range(groups)]
    qkv_bias_ref[...] = jnp.concatenate(bias, axis=1).reshape(qkv_bias_ref.shape)
    for ref in (out_bias_ref, down_bias_ref):
        ref[...] = cot_ref[...].reshape(ref.shape)


def join(core, mine, got, small, cot, tok_count, few, mixed_width):
    feature_width = cot.shape[1]
    vector = shaped((feature_width,), F32)
    return call(
        functools.partial(join_kernel, few, mixed_width),
        inputs=[core[None].astype(jnp.int32), mine, got, small, cot],
        in_specs=[SMEM] + [VMEM] * 4,
        out_specs=[VMEM] * 9,
        out_shape=[shaped((tok_count, feature_width), BF)] * 2
        + [shaped((2 * few, feature_width), F32), shaped((2 * few, 3 * feature_width), F32), vector, vector]
        + [shaped((4 * mixed_width,), F32), vector, vector],
        compiler_params=params(16),
        name="join",
    )


def on_device(
    tokens,
    segment_ids,
    qkv_weight,
    qkv_bias,
    out_weight,
    out_bias,
    up_weight,
    up_bias,
    down_weight,
    down_bias,
    norm1_gain,
    norm1_bias,
    norm2_gain,
    norm2_bias,
    probe_dirs,
    out_grad,
):
    tok_count, feature_width = tokens.shape
    hidden_width = up_weight.shape[1]
    probe_count, local_rows = probe_dirs.shape[:2]
    groups = lax.axis_size("ex")
    probe_groups = lax.axis_size("probe")
    blocks = SEQ // tok_count
    rows = groups // blocks
    ex_place = lax.axis_index("ex")
    place = ex_place % blocks
    row_place = ex_place // blocks
    probe_place = lax.axis_index("probe")
    core, upper = probe_place % 2, probe_place // 2
    heads = HEADS // probe_groups
    head_width = heads * HEAD_DIM
    part_width = hidden_width // blocks
    fine = part_width // rows
    row_groups = None
    if rows > 1:
        row_groups = [[r * blocks + b for b in range(blocks)] for r in range(rows)]
    across = [[r * blocks + b for r in range(rows)] for b in range(blocks)]

    def swap(value, distance):
        return lax.ppermute(value, "ex", [(i, i ^ distance) for i in range(groups)])

    def swap_probe(value, distance):
        return lax.ppermute(value, "probe", [(i, i ^ distance) for i in range(probe_groups)])

    def over_rows(value):
        if rows > 1:
            return lax.psum_scatter(value, "ex", axis_index_groups=across, scatter_dimension=0, tiled=True)
        return value

    def my_part(value, axis):
        shape = value.shape
        split = shape[:axis] + (rows, blocks, fine) + shape[axis + 1 :]
        part = lax.dynamic_index_in_dim(value.reshape(split), place, axis + 1, keepdims=False)
        return part.reshape(shape[:axis] + (part_width,) + shape[axis + 1 :])

    mine, share = slices_of(probe_place, probe_groups, tokens, out_grad)
    aside = swap(mine, 1)
    near, diagonal, distant, farthest = [swap(share, distance) for distance in (2, 3, 4, 6)]

    segments = segment_ids
    if rows > 1:
        segments = lax.dynamic_slice_in_dim(segment_ids, row_place * SEQ, SEQ)
    vectors = vectors_of(
        probe_groups, blocks, norm1_gain, norm1_bias, norm2_gain, norm2_bias, out_bias, down_bias, qkv_bias, segments
    )
    base, rest, local_small = local_part(tokens, out_grad, up_weight, up_bias, down_weight, vectors)

    second, third = stack([near, diagonal, distant, farthest], [(0, 1), (2, 3)], [local_small])
    third_aside, third_over = swap(third, 1), swap_probe(third, 2)
    (quarters,) = stack([mine, aside, third, third_over], [(0, 1, 2, 3)], [])
    swapped = swap_probe(quarters, 1)
    up_bias_part = my_part(up_bias, 0).astype(F32)[None]
    up_part, down_part = up_weight, down_weight
    if rows > 1:
        up_part, down_part = my_part(up_weight, 1), my_part(down_weight, 0)

    def pieces_of(array, other, slots, distances):
        return [
            ([(side, slot) for side in (array, other) for slot in pair], ((0, 2, 1, 3), (distance,)))
            for pair, distance in zip(slots, distances)
        ]

    pieces = pieces_of(quarters, swapped, ((0, 1), (2, 3), (4, 6), (5, 7)), (0, 1, 4, 6))
    slots = [lambda i: jnp.where(i < 2, 2 * i, i + 2), lambda i: jnp.where(i < 2, 2 * i + 1, i + 4)]
    refs = [(array, slot_of) for array in (quarters, swapped) for slot_of in slots]
    unit_place = place if rows == 1 else place * 0
    places = jnp.stack([unit_place, place, probe_place]).astype(jnp.int32)
    fixed = (SEQ, up_part, up_bias_part, down_part, vectors)
    units = hidden_units(places, refs, (0, 2, 1, 3), 0, (0, 1, 4, 6), *fixed, None)
    second_over, third_across = swap_probe(second, 2), swap_probe(third_aside, 2)

    dirs = tie(pack(probe_dirs, blocks, rows, [local_small]), [third_aside, third_over, aside])
    dirs = lax.all_to_all(dirs, "ex", 0, 0, axis_index_groups=row_groups, tiled=True)
    dirs = dirs.reshape(blocks * local_rows, probe_count * part_width)
    if rows > 1:
        dirs = lax.all_gather(dirs, "ex", axis_index_groups=across, tiled=True)

    last = ((second, second_over, (2, 3)), (third_aside, third_across, (5, 7)))
    for number, (array, over, distances) in enumerate(last):
        (quarters,) = stack([array, over], [(0, 1)], [units[5]])
        swapped = swap_probe(quarters, 1)
        pieces += pieces_of(quarters, swapped, ((0, 2), (1, 3)), distances)
        refs = [(side, lambda i, k=k: i + 2 * k) for side in (quarters, swapped) for k in range(2)]
        units = hidden_units(places, refs, (0, 2, 1, 3), 4 + 2 * number, distances, *fixed, units)
    *units, active, grad_up_bias, cot_sum = units

    block_rows = feature_width // blocks
    offset = place * block_rows - probe_place * head_width
    holds = (offset >= 0) & (offset < head_width)
    numbers = jnp.stack([place, probe_place, holds, jnp.where(holds, offset, 0)]).astype(jnp.int32)
    *parts, cot, attended = attention(heads, blocks, numbers, pieces, tokens, qkv_weight, vectors, out_weight, [cot_sum])

    part, scores = curvature_of(
        blocks, core, probe_count, units, dirs, local_small, grad_up_bias, [far(attended)]
    )
    part = over_rows(part.reshape(feature_width, -1)).reshape(blocks, local_rows, -1)
    got = lax.all_to_all(part, "ex", 0, 0, axis_index_groups=row_groups, tiled=True)

    grad_down, attended, grad_out = weights_back(heads, blocks, numbers, active, cot, attended, [scores])
    parts += [attended, grad_out]
    keep, send = attention_back(heads, blocks, numbers, parts, qkv_weight, vectors, [scores])
    half, few = tok_count // 2, block_rows // 2
    merged = merge(core, keep, swap_probe(send, 1), feature_width, half, few)
    final, small = finish(
        jnp.stack([core, upper]).astype(jnp.int32), merged, swap_probe(merged, 2), tokens, base, rest, vectors,
        out_weight, few,
    )
    (
        layer_out, input_grad, grad_out_weight, grad_qkv_weight,
        grad_gain_one, grad_shift_one, grad_qkv_bias, grad_out_bias, grad_down_bias,
    ) = join(core, final, swap_probe(final, 1), small, cot_sum, tok_count, few, 3 * head_width)

    if rows == 1:
        up_half, grad_gain_two, grad_shift_two, grad_up_bias, scores = peel(
            got, probe_count, part_width, [layer_out]
        )
        other_half = swap_probe(up_half, 1)
        curvature = unpack(got, probe_count, part_width, [far(up_half)])
        scores = scores[:, None]
        grad_up_weight = spread(core, up_half, other_half, blocks, part_width // 2, [])
    else:
        start = probe_count * part_width
        units = got[:, :, :start].reshape(blocks, local_rows, probe_count, rows, fine)
        curvature = units.transpose(2, 1, 3, 0, 4).reshape(probe_count, local_rows, hidden_width)
        curvature = curvature.astype(F32)
        up_half = got[:, :, start : start + part_width // 2]
        both = lax.all_gather(up_half, "probe", axis_index_groups=[[0, 1], [2, 3]])
        both = both.transpose(2, 1, 0, 3).reshape(local_rows, blocks, rows, fine)
        grad_up_weight = both.transpose(0, 2, 1, 3).reshape(local_rows, hidden_width).astype(F32)
        grad_down = over_rows(grad_down)

        def over_groups(value):
            value = lax.all_gather(value, "ex", axis_index_groups=row_groups, tiled=True)
            return lax.dynamic_slice_in_dim(over_rows(value), place * local_rows, local_rows, 0)

        grad_qkv_weight, grad_out_weight = over_groups(grad_qkv_weight), over_groups(grad_out_weight)
        grad_gain_one, grad_shift_one, grad_qkv_bias, grad_out_bias, grad_up_bias = lax.psum(
            (grad_gain_one, grad_shift_one, grad_qkv_bias, grad_out_bias, grad_up_bias[0]),
            "ex",
            axis_index_groups=across,
        )
        grad_down_bias = grad_out_bias
        grad_up_bias = lax.all_gather(grad_up_bias, "ex", axis_index_groups=row_groups)
        grad_up_bias = grad_up_bias.reshape(blocks, rows, fine).transpose(1, 0, 2).reshape(-1)
        grad_gain_two, grad_shift_two = lax.psum((local_small[1], local_small[2]), "ex")
        scores = lax.psum(scores[:probe_count, :1], "ex", axis_index_groups=row_groups)
        scores = lax.all_gather(scores, "ex", axis_index_groups=across, axis=1, tiled=True)
    return (
        layer_out,
        input_grad,
        grad_qkv_weight,
        grad_qkv_bias,
        grad_out_weight,
        grad_out_bias,
        grad_up_weight,
        grad_up_bias,
        grad_down,
        grad_down_bias,
        grad_gain_one,
        grad_shift_one,
        grad_gain_two,
        grad_shift_two,
        curvature,
        scores,
    )


def solution(mesh):
    in_specs = (
        P("ex", None),
        P(),
        P(),
        P(),
        P(),
        P(),
        P(),
        P(),
        P(),
        P(),
        P(),
        P(),
        P(),
        P(),
        P("probe", "ex", None),
        P("ex", None),
    )
    out_specs = (
        P("ex", None),
        P("ex", None),
        P("ex", None),
        P(),
        P("ex", None),
        P(),
        P("ex", None),
        P(),
        P("ex", None),
        P(),
        P(),
        P(),
        P(),
        P(),
        P("probe", "ex", None),
        P("probe", None),
    )
    return jax.shard_map(
        on_device, mesh=mesh, in_specs=in_specs, out_specs=out_specs, check_vma=False
    )
```

```python
import functools

import jax
import jax.numpy as jnp
import numpy as np
from jax import lax
from jax.experimental import pallas as pl
from jax.experimental.pallas import tpu as pltpu
from jax.sharding import PartitionSpec as P

HEADS = 12
HEAD_DIM = 64
ROT = 16
SEQ = 2048

BF = jnp.bfloat16
F32 = jnp.float32
eps_norm = 1e-05
masked_score = -1e30
half_root = 0.7071067811865476
gauss_peak = 0.3989422804014327
MB = 1024 * 1024
LANES = 128
LIGHT = pl.CostEstimate(flops=1000, bytes_accessed=1000, transcendentals=0)
BIG = 58


def dot(a, b):
    return jnp.dot(a, b, preferred_element_type=F32)


def dot_nt(a, b):
    return lax.dot_general(a, b, (((1,), (1,)), ((), ())), preferred_element_type=F32)


def dot_tn(a, b):
    return lax.dot_general(a, b, (((0,), (0,)), ((), ())), preferred_element_type=F32)


def spread_of(features):
    center = jnp.mean(features, axis=-1, keepdims=True)
    centred = features - center
    spread = jnp.mean(centred * centred, axis=-1, keepdims=True)
    return centred, lax.rsqrt(spread + eps_norm)


def standardize(features):
    centred, factor = spread_of(features)
    return centred * factor


def norm_input_term(grad, gain_row, unit, factor):
    unit_grad = grad * gain_row
    inner = unit_grad - jnp.mean(unit_grad, -1, keepdims=True)
    return (inner - unit * jnp.mean(unit_grad * unit, -1, keepdims=True)) * factor


def gelu_parts(pre_act):
    below = 0.5 + 0.5 * lax.erf(pre_act * half_root)
    density = gauss_peak * jnp.exp(-0.5 * pre_act * pre_act)
    return below, density


def rotary_tables(count):
    steps = np.arange(ROT // 2, dtype=np.float32) * np.float32(2.0 / ROT)
    inverse = np.power(np.float32(10000.0), -steps).astype(np.float32)
    angles = np.arange(count, dtype=np.float32)[:, None] * inverse[None, :]
    angles = np.concatenate([angles, angles], axis=1)
    cosine = np.ones((count, HEAD_DIM), np.float32)
    sine = np.zeros((count, HEAD_DIM), np.float32)
    cosine[:, :ROT], sine[:, :ROT] = np.cos(angles), np.sin(angles)
    return np.concatenate([cosine, cosine], axis=1), np.concatenate([sine, sine], axis=1)


def params(limit_mb, **more):
    return pltpu.CompilerParams(vmem_limit_bytes=limit_mb * MB, **more)


def shaped(shape, dtype):
    return jax.ShapeDtypeStruct(shape, dtype)


def whole(*shape):
    return pl.BlockSpec(shape, lambda i: (0,) * len(shape))


VMEM = pl.BlockSpec(memory_space=pltpu.VMEM)
SMEM = pl.BlockSpec(memory_space=pltpu.SMEM)
ANY = pl.BlockSpec(memory_space=pl.ANY)


def far(array):
    return pltpu.with_memory_space_constraint(array, pltpu.HBM)


def call(kernel, *, inputs, in_specs, after=(), aliases=None, **more):
    spare = len(after)

    def body(*refs):
        kernel(*refs[: len(inputs)], *refs[len(inputs) + spare :])

    return pl.pallas_call(
        body, in_specs=list(in_specs) + [ANY] * spare, input_output_aliases=aliases or {},
        cost_estimate=LIGHT, **more,
    )(*inputs, *after)


def tie(value, after):
    return call(
        lambda value_ref, out_ref: None,
        inputs=[value],
        after=after,
        aliases={0: 0},
        in_specs=[ANY],
        out_specs=ANY,
        out_shape=shaped(value.shape, value.dtype),
        name="tie",
    )


def pack_kernel(dirs_ref, packed_ref, sems):
    probes = dirs_ref.shape[0]
    blocks, _, width = packed_ref.shape
    part_width = width // probes
    copies = []
    for block in range(blocks):
        for k in range(probes):
            source = dirs_ref.at[k, :, block * part_width : (block + 1) * part_width]
            target = packed_ref.at[block, :, k * part_width : (k + 1) * part_width]
            copies.append(pltpu.make_async_copy(source, target, sems.at[len(copies)]))
    for copy in copies:
        copy.start()
    for copy in copies:
        copy.wait()


def pack(dirs, blocks, rows, after):
    probes, local_rows, hidden_width = dirs.shape
    part_width = hidden_width // blocks
    if rows > 1:
        split = dirs.reshape(probes, local_rows, rows, blocks, part_width // rows)
        return split.transpose(3, 1, 0, 2, 4).reshape(blocks, local_rows, probes * part_width)
    return call(
        pack_kernel,
        inputs=[dirs],
        after=after,
        in_specs=[VMEM],
        out_specs=ANY,
        out_shape=pltpu.HBM((blocks, local_rows, probes * part_width), dirs.dtype),
        scratch_shapes=[pltpu.SemaphoreType.DMA((blocks * probes,))],
        compiler_params=params(8),
        name="pack",
    )


def slices_kernel(place_ref, tokens_ref, grads_ref, both_ref, first_ref, sems):
    count = both_ref.shape[2]
    copies = []
    for part, source in enumerate((tokens_ref, grads_ref)):
        for target, slot, side in ((both_ref, 0, 0), (both_ref, 1, 2), (first_ref, 0, 0)):
            first = jnp.bitwise_xor(place_ref[0], side) * count
            rows = pl.ds(pl.multiple_of(first, count), count)
            copies.append(pltpu.make_async_copy(source.at[rows, :], target.at[slot, part], sems.at[len(copies)]))
    for copy in copies:
        copy.start()
    for copy in copies:
        copy.wait()


def slices_of(probe_place, probe_groups, tokens, grads):
    tok_count, feature_width = tokens.shape
    size = tok_count // probe_groups
    return call(
        slices_kernel,
        inputs=[probe_place[None].astype(jnp.int32), far(tokens), far(grads)],
        in_specs=[SMEM, ANY, ANY],
        out_specs=[VMEM] * 2,
        out_shape=[shaped((count, 2, size, feature_width), BF) for count in (2, 1)],
        scratch_shapes=[pltpu.SemaphoreType.DMA((6,))],
        compiler_params=params(8),
        name="slices",
    )


def stack_kernel(plan, *refs):
    sources, targets = refs[: -len(plan)], refs[-len(plan) :]
    for parts, target in zip(plan, targets):
        number = 0
        for part in parts:
            count = sources[part].shape[0]
            target[number : number + count] = sources[part][...]
            number += count


def stack(sources, plan, after):
    heights = [sum(sources[part].shape[0] for part in parts) for parts in plan]
    return call(
        functools.partial(stack_kernel, plan),
        inputs=sources,
        after=after,
        in_specs=[VMEM] * len(sources),
        out_specs=[VMEM] * len(plan),
        out_shape=[shaped((n,) + sources[parts[0]].shape[1:], BF) for n, parts in zip(heights, plan)],
        compiler_params=params(8),
        name="stack",
    )


def vectors_kernel(groups, blocks, count, *refs):
    sources, vectors_ref, held, sems = refs[:count], refs[count], refs[count + 1 : -1], refs[-1]
    copies = [pltpu.make_async_copy(source, target, sems.at[k]) for k, (source, target) in enumerate(zip(sources, held))]
    for copy in copies:
        copy.start()
    vectors_ref[...] = jnp.zeros_like(vectors_ref)
    for copy in copies:
        copy.wait()
    *plain, first_bias, second_bias, qkv_bias, segments = held
    for number, source in enumerate(plain):
        vectors_ref[number : number + 1, :] = source[...].reshape(1, -1)
    total = first_bias[...].astype(F32) + second_bias[...].astype(F32)
    vectors_ref[len(plain) : len(plain) + 1, :] = total.reshape(1, -1)
    width = qkv_bias.shape[0] // groups
    bias = qkv_bias[...].astype(F32).reshape(1, -1)
    for number in range(groups):
        vectors_ref[8 + number : 9 + number, :width] = bias[:, number * width : (number + 1) * width]
    block = segments.shape[0] // blocks
    for number in range(blocks):
        row = segments[number * block : (number + 1) * block].astype(F32).reshape(1, -1)
        vectors_ref[16 + number : 17 + number, :block] = row


def vectors_of(groups, blocks, *sources):
    return call(
        functools.partial(vectors_kernel, groups, blocks, len(sources)),
        inputs=[far(source) for source in sources],
        in_specs=[ANY] * len(sources),
        out_specs=VMEM,
        out_shape=shaped((16 + blocks, sources[0].shape[0]), F32),
        scratch_shapes=[pltpu.VMEM(source.shape, source.dtype) for source in sources]
        + [pltpu.SemaphoreType.DMA((len(sources),))],
        compiler_params=params(4),
        name="vectors",
    )


def local_kernel(
    tokens_ref, grads_ref, up_ref, up_bias_ref, down_ref, vectors_ref,
    base_ref, rest_ref, small_ref, normed_s, branch_s, back_s,
):
    step = pl.program_id(0)
    gain, shift, out_bias = vectors_ref[2:3, :], vectors_ref[3:4, :], vectors_ref[4:5, :]

    @pl.when(step == 0)
    def _():
        unit = standardize(tokens_ref[...].astype(F32))
        normed_s[...] = (unit * gain + shift).astype(BF)
        branch_s[...] = jnp.zeros_like(branch_s)
        back_s[...] = jnp.zeros_like(back_s)

    bias = up_bias_ref[pl.ds(pl.multiple_of(step * up_ref.shape[1], LANES), up_ref.shape[1])]
    hidden = dot(normed_s[...], up_ref[...]) + bias.astype(F32).reshape(1, -1)
    upstream = dot_nt(grads_ref[...], down_ref[...])
    below, density = gelu_parts(hidden)
    branch_s[...] += dot((hidden * below).astype(BF), down_ref[...])
    hidden_grad = (upstream * (below + hidden * density)).astype(BF)
    back_s[...] += dot_nt(hidden_grad, up_ref[...])

    @pl.when(step == pl.num_programs(0) - 1)
    def _():
        inputs = tokens_ref[...].astype(F32)
        cot = grads_ref[...].astype(F32)
        centred, factor = spread_of(inputs)
        unit = centred * factor
        back = back_s[...]
        base_ref[...] = inputs + branch_s[...] + out_bias
        rest_ref[...] = cot + norm_input_term(back, gain, unit, factor)
        small_ref[...] = jnp.zeros_like(small_ref)
        small_ref[0:1, :] = jnp.sum(cot, axis=0, keepdims=True)
        small_ref[1:2, :] = jnp.sum(back * unit, axis=0, keepdims=True)
        small_ref[2:3, :] = jnp.sum(back, axis=0, keepdims=True)


def local_part(tokens, grads, up_weight, up_bias, down_weight, vectors):
    tok_count, feature_width = tokens.shape
    hidden_width = up_weight.shape[1]
    step = 512
    own = whole(tok_count, feature_width)
    return call(
        local_kernel,
        inputs=[tokens, grads, far(up_weight), up_bias, far(down_weight), vectors],
        grid=(hidden_width // step,),
        in_specs=[
            own, own,
            pl.BlockSpec((feature_width, step), lambda i: (0, i)),
            whole(hidden_width),
            pl.BlockSpec((step, feature_width), lambda i: (i, 0)),
            whole(8, feature_width),
        ],
        out_specs=[own, own, whole(8, feature_width)],
        out_shape=[
            shaped((tok_count, feature_width), F32),
            shaped((tok_count, feature_width), F32),
            shaped((8, feature_width), F32),
        ],
        scratch_shapes=[
            pltpu.VMEM((tok_count, feature_width), BF),
            pltpu.VMEM((tok_count, feature_width), F32),
            pltpu.VMEM((tok_count, feature_width), F32),
        ],
        compiler_params=params(24),
        name="local",
    )


def lanes(rows):
    return lax.broadcasted_iota(jnp.int32, (rows, 2 * HEAD_DIM), 1)


def flipped(tile):
    return pltpu.roll(tile, HEAD_DIM, 1)


def joined(left, right):
    return jnp.where(lanes(left.shape[0]) < HEAD_DIM, left, flipped(right))


def half_turned(tile):
    place_in = lanes(tile.shape[0]) % HEAD_DIM
    low = pltpu.roll(tile, 2 * HEAD_DIM - ROT // 2, 1)
    high = pltpu.roll(tile, ROT // 2, 1)
    return jnp.where(place_in < ROT // 2, -low, jnp.where(place_in < ROT, high, 0.0))


def with_column(tile, lane, column):
    first = column.astype(BF).astype(F32)
    number = lanes(tile.shape[0])
    return jnp.where(number == lane, first, jnp.where(number == lane + 1, column - first, tile))


def heads_joined(values):
    heads = len(values)
    values = [joined(values[k], values[k + 1]) if k + 1 < heads else values[k] for k in range(0, heads, 2)]
    if heads % 2:
        values[-1] = jnp.where(lanes(values[-1].shape[0]) < HEAD_DIM, values[-1], 0.0)
    return jnp.concatenate(values, axis=1)


def attention_kernel(heads, blocks, block, count, plan, *refs):
    sources, refs = refs[:count], refs[count:]
    (
        place_ref, weight_ref, vectors_ref, out_weight_ref, cos_in, sin_in,
        query_out, key_out, value_out, back_out, unit_out, cot_out, attended_out,
        cos_ref, sin_ref, query_s, key_s, value_s, back_s, unit_s, cot_s,
        window_s, weight_s, bias_s, out_weight_s, attended_s, query_code_s, key_code_s, sems,
        *array_refs,
    ) = refs
    place, probe_place = place_ref[0], place_ref[1]
    feature_width = unit_s.shape[1]
    pair = 2 * HEAD_DIM
    scale = HEAD_DIM ** (-0.5)
    gain, shift = vectors_ref[0:1, :], vectors_ref[1:2, :]
    own_rows = pl.ds(pl.multiple_of(place * block, block), block)
    head_width = heads * HEAD_DIM
    mixed_width = 3 * head_width

    first = probe_place * mixed_width // LANES * LANES
    columns = pl.ds(pl.multiple_of(first, LANES), window_s.shape[1])
    rows = pl.ds(pl.multiple_of(probe_place * head_width, HEAD_DIM), head_width)
    moves = [(weight_ref.at[:, columns], window_s), (out_weight_ref.at[rows, :], out_weight_s.at[:head_width, :])]
    moves += [(cos_in, cos_ref), (sin_in, sin_ref)] + list(zip(sources, array_refs))
    copies = [pltpu.make_async_copy(source, target, sems.at[k]) for k, (source, target) in enumerate(moves)]
    for copy in copies:
        copy.start()
    done = len(copies)

    def leave(number, source, target):
        return pltpu.make_async_copy(source, target, sems.at[done + number])

    def rows_of(number):
        return pl.ds(pl.multiple_of(number * block, block), block)

    def side_rows(distance, side, count):
        own = place_ref[1] % (block // count)
        first = jnp.bitwise_xor(place, distance) * block + jnp.bitwise_xor(own, side) * count
        return pl.ds(pl.multiple_of(first, count), count)

    def together(refs, slot, part):
        return jnp.concatenate([array_refs[ref][base + slot, part] for ref, base in refs], axis=0)

    def arrange(source, target):
        for head in range(heads):
            start = head * 3 * HEAD_DIM
            tile = source[:, start : start + pair]
            target[:, head * pair : (head + 1) * pair] = tile.astype(target.dtype)
        values = [source[:, (3 * head + 2) * HEAD_DIM : (3 * head + 3) * HEAD_DIM] for head in range(heads)]
        values.append(jnp.zeros((source.shape[0], -heads * HEAD_DIM % pair), source.dtype))
        target[:, heads * pair :] = jnp.concatenate(values, axis=1).astype(target.dtype)

    number = lanes(block)
    ones = (number >= HEAD_DIM + 16) & (number < HEAD_DIM + 18)
    coded = (number >= HEAD_DIM) & (number < HEAD_DIM + 16)
    for index in range(blocks):
        segment = jnp.broadcast_to(vectors_ref[16 + index : 17 + index, :block], (pair, block)).T
        segment = segment.astype(jnp.int32)
        match = (number == HEAD_DIM + segment // 8) | (number == HEAD_DIM + 8 + segment % 8)
        here = slice(index * block, (index + 1) * block)
        query_code_s[here, :] = jnp.where(coded & ~match, masked_score, 0.0)
        key_code_s[here, :] = jnp.where(match | ones, 1.0, 0.0)

    out_weight_s[head_width:, :] = jnp.zeros((out_weight_s.shape[0] - head_width, feature_width), BF)
    copies[0].wait()
    odd = probe_place * mixed_width % LANES != 0
    window = window_s[...]
    weight = jnp.where(odd, window[:, HEAD_DIM : HEAD_DIM + mixed_width], window[:, :mixed_width])
    arrange(weight, weight_s)
    bias = vectors_ref[pl.ds(8 + probe_place, 1), :mixed_width]
    arrange(jnp.broadcast_to(bias, (8, mixed_width)), bias_s)
    for copy in copies[1:4]:
        copy.wait()

    def project(sides, refs, slot, distance):
        unit = standardize(together(refs, slot, 0).astype(F32))
        normed = (unit * gain + shift).astype(BF)
        low = unit.astype(BF)
        whole_part = dot(normed, weight_s[...]) + bias_s[:1, :]
        cot = together(refs, slot, 1)
        whole_back = dot_nt(cot, out_weight_s[...])
        count = block // len(sides)
        for number, side in enumerate(sides):
            here = slice(number * count, (number + 1) * count)
            rows = side_rows(distance, side, count)
            unit_s[rows, :] = low[here]
            cot_s[rows, :] = cot[here]
            place_heads(rows, whole_part[here], whole_back[here])

    def place_heads(rows, part, back_part):
        cosine, sine = cos_ref[rows, :], sin_ref[rows, :]
        number = lanes(part.shape[0])
        query_code, key_code = query_code_s[rows, :], key_code_s[rows, :]
        value_code = jnp.where((number >= HEAD_DIM) & (number < HEAD_DIM + 2), 1.0, 0.0)
        first = number < HEAD_DIM
        for head in range(heads):
            plain = part[:, head * pair : (head + 1) * pair]
            both = plain * cosine + half_turned(plain) * sine
            query_s[head, rows, :] = jnp.where(first, both * scale, query_code).astype(BF)
            key_s[head, rows, :] = jnp.where(first, flipped(both), key_code).astype(BF)
            start = heads * pair + head // 2 * pair
            tile = part[:, start : start + pair]
            back_tile = back_part[:, head // 2 * pair : head // 2 * pair + pair]
            if head % 2:
                tile, back_tile = flipped(tile), flipped(back_tile)
            value_s[head, rows, :] = jnp.where(first, tile, value_code).astype(BF)
            back_s[head, rows, :] = jnp.where(first, back_tile, 0.0).astype(BF)

    here = set()
    for sides, distances, refs in plan:
        for number in sorted({ref for ref, _ in refs} - here):
            copies[4 + number].wait()
            here.add(number)
        for slot, distance in enumerate(distances):
            project(sides, refs, slot, distance)
    leaving = [leave(0, key_s, key_out), leave(1, value_s, value_out), leave(2, unit_s, unit_out)]
    leaving.append(leave(3, cot_s, cot_out))
    for copy in leaving:
        copy.start()

    square = (block, block)
    lower = lax.broadcasted_iota(jnp.int32, square, 1) <= lax.broadcasted_iota(jnp.int32, square, 0)

    def head_leaving(head):
        pairs = ((query_s, query_out), (back_s, back_out), (attended_s, attended_out))
        return [leave(4 + 3 * head + k, source.at[head], target.at[head]) for k, (source, target) in enumerate(pairs)]

    def attend(head, carry):
        def scores_of(number):
            start, stop = number * block, (number + 1) * block
            query = query_s[head, start:stop, :]
            near = jnp.where(lower, dot_nt(query, key_s[head, start:stop, :]), masked_score)
            return near, dot_nt(query, key_s[head, :start, :]) if number else None

        ahead = scores_of(0)
        for number in range(blocks):
            start, stop = number * block, (number + 1) * block
            near, far = ahead
            if number + 1 < blocks:
                ahead = scores_of(number + 1)
            top = jnp.max(near, axis=-1, keepdims=True)
            if number:
                top = jnp.maximum(top, jnp.max(far, axis=-1, keepdims=True))
            got = dot(jnp.exp(near - top).astype(BF), value_s[head, start:stop, :])
            if number:
                got = got + dot(jnp.exp(far - top).astype(BF), value_s[head, :start, :])
            total = got[:, HEAD_DIM : HEAD_DIM + 1]
            attended = got / total
            attended_s[head, start:stop, :] = attended.astype(BF)
            back = back_s[head, start:stop, :].astype(F32)
            delta = jnp.sum(attended * back, axis=-1, keepdims=True)
            log_total = top + jnp.log(total)
            query = query_s[head, start:stop, :].astype(F32)
            query_s[head, start:stop, :] = with_column(query, HEAD_DIM + 16, -log_total).astype(BF)
            back_s[head, start:stop, :] = with_column(back, HEAD_DIM, -delta).astype(BF)
        for copy in head_leaving(head):
            copy.start()
        return carry

    lax.fori_loop(0, heads, attend, 0)

    for copy in leaving:
        copy.wait()
    for head in range(heads):
        for copy in head_leaving(head):
            copy.wait()


def attention_back_kernel(
    heads, blocks, place_ref, query_in, key_in, value_in, back_in, unit_in, attended_ref, grad_out_ref, weight_ref,
    vectors_ref, cos_in, sin_in,
    keep_ref, send_ref,
    query_s, key_s, value_s, back_s, unit_ref, cos_ref, sin_ref,
    query_grad_s, key_grad_s, both_s, value_grad_s, mixed_s, total_s, small_s, window_s, sems,
):
    place, probe_place = place_ref[0], place_ref[1]
    block, head_width = attended_ref.shape
    feature_width = unit_ref.shape[1]
    mixed_width = 3 * head_width
    scale = HEAD_DIM ** (-0.5)
    first = probe_place * mixed_width // LANES * LANES
    columns = pl.ds(pl.multiple_of(first, LANES), window_s.shape[1])
    others = [(cos_in, cos_ref), (sin_in, sin_ref), (unit_in, unit_ref), (weight_ref.at[:, columns], window_s)]
    others = [pltpu.make_async_copy(source, target, sems.at[k]) for k, (source, target) in enumerate(others)]

    def arriving(head):
        pairs = ((key_in, key_s), (query_in, query_s), (value_in, value_s), (back_in, back_s))
        return [
            pltpu.make_async_copy(source.at[head], target.at[head], sems.at[4 + len(pairs) * head + k])
            for k, (source, target) in enumerate(pairs)
        ]

    for copy in arriving(0) + others[:2]:
        copy.start()
    for head in range(1, heads):
        for copy in arriving(head):
            copy.start()
    for copy in others[2:]:
        copy.start()
    for copy in others[:2]:
        copy.wait()
    square = (block, block)
    upper = lax.broadcasted_iota(jnp.int32, square, 0) <= lax.broadcasted_iota(jnp.int32, square, 1)

    def through(head, carry):
        for copy in arriving(head):
            copy.wait()
        query_grad_s[...] = jnp.zeros_like(query_grad_s)
        for number in range(blocks):
            start, stop = number * block, (number + 1) * block
            key, value = key_s[head, start:stop, :], value_s[head, start:stop, :]
            key_t = key.T
            key_grad = value_grad = None
            for rows, mask in ((slice(start, stop), upper), (slice(stop, blocks * block), None)):
                if rows.start == rows.stop:
                    continue
                query, back = query_s[head, rows, :], back_s[head, rows, :]
                scores = dot_nt(key, query)
                if mask is not None:
                    scores = jnp.where(mask, scores, masked_score)
                probs = jnp.exp(scores)
                score_grad = (probs * dot_nt(value, back)).astype(BF)
                value_term, key_term = dot(probs.astype(BF), back), dot(score_grad, query)
                value_grad = value_term if value_grad is None else value_grad + value_term
                key_grad = key_term if key_grad is None else key_grad + key_term
                query_grad_s[:, rows] += dot(key_t, score_grad)
            key_grad_s[start:stop, :] = key_grad
            value_grad_s[head, start:stop, :] = value_grad.astype(BF)
        for number in range(blocks):
            rows = slice(number * block, (number + 1) * block)
            both = joined(query_grad_s[:, rows].T * scale, key_grad_s[rows, :])
            both = both * cos_ref[rows, :] - half_turned(both * sin_ref[rows, :])
            both_s[head, rows, :] = both.astype(BF)
        return carry

    lax.fori_loop(0, heads, through, 0)

    for number in range(blocks):
        rows = slice(number * block, (number + 1) * block)
        tiles = []
        for head in range(heads):
            both, value = both_s[head, rows, :].astype(F32), value_grad_s[head, rows, :].astype(F32)
            if head % 2 == 0:
                tiles += [both, value]
            else:
                tiles[-1] = joined(tiles[-1], both)
                tiles.append(joined(flipped(both), value))
        if heads % 2:
            tiles[-1] = jnp.where(lanes(block) < HEAD_DIM, tiles[-1], 0.0)
        mixed_s[rows, :] = jnp.concatenate(tiles, axis=1).astype(BF)

    others[2].wait()
    total_s[...] = dot_tn(unit_ref[...], mixed_s[...])
    sums = jnp.sum(mixed_s[...].astype(F32), axis=0, keepdims=True)
    others[3].wait()
    odd = probe_place * mixed_width % LANES != 0
    window = window_s[...]
    weight = jnp.where(odd, window[:, HEAD_DIM : HEAD_DIM + mixed_width], window[:, :mixed_width])

    own_rows = pl.ds(pl.multiple_of(place * block, block), block)
    mixed_own = mixed_s[own_rows, :][:, :mixed_width]
    normed_back = dot_nt(mixed_own, weight).astype(BF)

    local_rows = grad_out_ref.shape[0]
    first = pl.multiple_of(place * local_rows, local_rows)
    pick = lax.broadcasted_iota(jnp.int32, (local_rows, feature_width), 1) == first + lax.broadcasted_iota(
        jnp.int32, (local_rows, feature_width), 0
    )
    gain, shift = [
        jnp.sum(jnp.where(pick, vectors_ref[k : k + 1, :], 0.0), axis=1, keepdims=True) for k in range(2)
    ]
    grad_qkv = (total_s[pl.ds(first, local_rows), :] * gain + sums * shift).astype(BF)

    wide = weight.astype(F32)
    columns = [
        jnp.sum(wide * total_s[:, :mixed_width], axis=1, keepdims=True),
        jnp.sum(wide * sums[:, :mixed_width], axis=1, keepdims=True),
    ]
    number = lax.broadcasted_iota(jnp.int32, (feature_width, LANES), 1)
    columns = jnp.where(number == 0, columns[0], jnp.where(number == 1, columns[1], 0.0)).T
    piece = feature_width // 2
    small_s[...] = jnp.zeros_like(small_s)
    for k in range(2):
        for part in range(2):
            here = slice(part * piece, (part + 1) * piece)
            small_s[2 * k + part : 2 * k + part + 1, :piece] = columns[k : k + 1, here]
    small_s[pl.ds(4 + 2 * probe_place, 1), :piece] = sums[:, :piece]
    small_s[pl.ds(5 + 2 * probe_place, 1), : mixed_width - piece] = sums[:, piece:mixed_width]
    half, few = block // 2, local_rows // 2
    third = head_width
    odd = probe_place % 2 == 1

    def halves(value):
        low, high = value[: value.shape[0] // 2], value[value.shape[0] // 2 :]
        return jnp.where(odd, high, low), jnp.where(odd, low, high)

    attended, grad_out = attended_ref[...], grad_out_ref[...]
    for number, target in enumerate((keep_ref, send_ref)):
        target[...] = jnp.zeros_like(target)
        target[:half, :feature_width] = halves(normed_back)[number]
        target[:half, feature_width:] = halves(attended)[number]
        target[half : half + few, :feature_width] = halves(grad_out)[number]
        part = halves(grad_qkv)[number]
        target[half : half + few, feature_width:] = part[:, :third]
        target[half + few : half + 2 * few, : 2 * third] = part[:, third : 3 * third]
        put_small(target, half + 2 * few, small_s[...])


def put_small(target, first, small):
    width = small.shape[1]
    high = small.astype(BF)
    target[first:, :width] = high
    target[first:, width : 2 * width] = (small - high.astype(F32)).astype(BF)


def get_small(source, first, width):
    return source[first:, :width].astype(F32) + source[first:, width : 2 * width].astype(F32)


def attention(heads, blocks, numbers, pieces, tokens, qkv_weight, vectors, out_weight, after):
    tok_count, feature_width = tokens.shape
    pair = 2 * HEAD_DIM
    head_width = heads * HEAD_DIM
    value_tiles = -(-heads // 2) * pair
    arrays, plan = [], []
    for refs, (sides, distances) in pieces:
        numbered = []
        for array, base in refs:
            if not any(array is other for other in arrays):
                arrays.append(array)
            numbered.append(([array is other for other in arrays].index(True), base))
        plan.append((sides, distances, numbered))
    cos_table, sin_table = rotary_tables(SEQ)
    per_head = shaped((heads, SEQ, pair), BF)
    window = -(-(3 * head_width) // LANES) * LANES
    return call(
        functools.partial(attention_kernel, heads, blocks, tok_count, len(arrays), plan),
        inputs=arrays + [numbers, far(qkv_weight), vectors, far(out_weight), far(jnp.asarray(cos_table)), far(jnp.asarray(sin_table))],
        after=after,
        in_specs=[ANY] * len(arrays) + [SMEM, ANY, VMEM, ANY, ANY, ANY],
        out_specs=[ANY] * 7,
        out_shape=[pltpu.HBM(per_head.shape, BF)] * 4
        + [pltpu.HBM((SEQ, feature_width), BF)] * 2
        + [pltpu.HBM(per_head.shape, BF)],
        scratch_shapes=[pltpu.VMEM((SEQ, pair), F32)] * 2
        + [pltpu.VMEM((heads, SEQ, pair), BF)] * 4
        + [pltpu.VMEM((SEQ, feature_width), BF)] * 2
        + [
            pltpu.VMEM((feature_width, window), BF),
            pltpu.VMEM((feature_width, heads * pair + value_tiles), BF),
            pltpu.VMEM((8, heads * pair + value_tiles), F32),
            pltpu.VMEM((value_tiles, feature_width), BF),
            pltpu.VMEM((heads, SEQ, pair), BF),
            pltpu.VMEM((SEQ, pair), F32),
            pltpu.VMEM((SEQ, pair), F32),
            pltpu.SemaphoreType.DMA((4 + len(arrays) + 4 + 3 * heads,)),
        ]
        + [pltpu.VMEM(array.shape, array.dtype) for array in arrays],
        compiler_params=params(44),
        name="attention",
    )


def attention_back(heads, blocks, numbers, parts, qkv_weight, vectors, after):
    *_, unit, attended, grad_out = parts
    (tok_count, head_width), (local_rows, feature_width) = attended.shape, grad_out.shape
    pair = 2 * HEAD_DIM
    width = -(-(3 * head_width) // LANES) * LANES
    small_rows = -(-(4 + 2 * HEADS // heads) // 16) * 16
    cos_table, sin_table = rotary_tables(SEQ)
    return call(
        functools.partial(attention_back_kernel, heads, blocks),
        inputs=[numbers, *[far(part) for part in parts[:5]], *parts[5:], far(qkv_weight), vectors, far(jnp.asarray(cos_table)), far(jnp.asarray(sin_table))],
        after=after,
        in_specs=[SMEM] + [ANY] * 5 + [VMEM] * 2 + [ANY, VMEM, ANY, ANY],
        out_specs=[VMEM] * 2,
        out_shape=[
            shaped((tok_count // 2 + local_rows + small_rows, feature_width + head_width), BF),
        ] * 2,
        scratch_shapes=[pltpu.VMEM((heads, SEQ, pair), BF)] * 4
        + [pltpu.VMEM((SEQ, feature_width), BF)]
        + [pltpu.VMEM((SEQ, pair), F32)] * 2
        + [
            pltpu.VMEM((pair, SEQ), F32),
            pltpu.VMEM((SEQ, pair), F32),
            pltpu.VMEM((heads, SEQ, pair), BF),
            pltpu.VMEM((heads, SEQ, pair), BF),
            pltpu.VMEM((SEQ, width), BF),
            pltpu.VMEM((feature_width, width), F32),
            pltpu.VMEM((small_rows, feature_width // 2), F32),
            pltpu.VMEM((feature_width, width), BF),
            pltpu.SemaphoreType.DMA((4 + 4 * heads,)),
        ],
        compiler_params=params(42),
        name="attention_back",
    )


def hidden_kernel(sides, first_call, *refs):
    place_ref, count = refs[0], len(sides)
    piece_refs, (up_ref, up_bias_ref, down_ref, vectors_ref) = refs[1 : count + 1], refs[count + 1 : count + 5]
    before_refs = [None, None] if first_call else refs[count + 5 : count + 7]
    normed_ref, turned_ref, curve_ref, grad_ref, active_ref, bias_grad_ref, cot_sum_ref = refs[-7:]
    cot = jnp.concatenate([ref[0, 1] for ref in piece_refs], axis=0)
    unit = standardize(jnp.concatenate([ref[0, 0] for ref in piece_refs], axis=0).astype(F32))
    normed = (unit * vectors_ref[2:3, :] + vectors_ref[3:4, :]).astype(BF)
    normed_ref[...] = normed
    turned_ref[...] = normed.T
    hidden = dot(normed, up_ref[...]) + up_bias_ref[...]
    upstream = dot_nt(cot, down_ref[...])
    below, density = gelu_parts(hidden)
    active = (hidden * below).astype(BF)
    hidden_grad = (upstream * (below + hidden * density)).astype(BF)
    grad_ref[...] = hidden_grad
    curve_ref[...] = upstream * density * (2.0 - hidden * hidden)
    size = active.shape[0] // count
    for number, side in enumerate(sides):
        rows = pl.ds(pl.multiple_of(jnp.bitwise_xor(place_ref[2], side) * size, size), size)
        active_ref[rows, :] = active[number * size : (number + 1) * size]

    @pl.when(pl.program_id(0) == 0)
    def _():
        for before, target in zip(before_refs, (bias_grad_ref, cot_sum_ref)):
            target[...] = jnp.zeros_like(target) if first_call else before[...]

    bias_grad_ref[...] += jnp.sum(hidden_grad.astype(F32), axis=0, keepdims=True)
    cot_sum_ref[...] += jnp.sum(cot.astype(F32), axis=0, keepdims=True)


def hidden_units(places, pieces, sides, first, distances, count, up_part, up_bias_part, down_part, vectors, before):
    arrays = [array for array, _ in pieces]
    feature_width, part_width = arrays[0].shape[3], up_bias_part.shape[1]
    tok_count = sum(array.shape[2] for array in arrays)

    def fixed(*shape):
        return pl.BlockSpec(shape, lambda i, place_ref: (0,) * len(shape))

    def piece(array, slot_of):
        return pl.BlockSpec((1,) + array.shape[1:], lambda i, place_ref: (slot_of(i), 0, 0, 0))

    def block_of(i, place_ref):
        distance = distances[0]
        for number in range(1, len(distances)):
            distance = jnp.where(i == number, distances[number], distance)
        return (jnp.bitwise_xor(place_ref[1], distance), 0)

    units = pl.BlockSpec((tok_count, part_width), lambda i, place_ref: (first + i, 0))
    sums = [fixed(1, part_width), fixed(1, feature_width)]
    inputs = [places, *arrays, far(up_part), up_bias_part, far(down_part), vectors]
    aliases = {}
    if before:
        aliases = {len(inputs) + 2 + k: k for k in range(5)}
        inputs += list(before[5:]) + [far(array) for array in before[:5]]

    def body(*refs):
        spare = 5 if before else 0
        kept = len(refs) - 7 - spare
        hidden_kernel(sides, before is None, *refs[:kept], *refs[kept + spare :])

    return pl.pallas_call(
        body,
        grid_spec=pltpu.PrefetchScalarGridSpec(
            num_scalar_prefetch=1,
            grid=(len(distances),),
            in_specs=[piece(array, slot_of) for array, slot_of in pieces] + [
                pl.BlockSpec((feature_width, part_width), lambda i, place_ref: (0, place_ref[0])),
                fixed(1, part_width),
                pl.BlockSpec((part_width, feature_width), lambda i, place_ref: (place_ref[0], 0)),
                fixed(8, feature_width),
            ] + (sums + [ANY] * 5 if before else []),
            out_specs=[
                pl.BlockSpec((tok_count, feature_width), lambda i, place_ref: (first + i, 0)),
                pl.BlockSpec((feature_width, tok_count), lambda i, place_ref: (0, first + i)),
                units, units, pl.BlockSpec((tok_count, part_width), block_of),
            ] + sums,
        ),
        out_shape=[
            pltpu.HBM((count, feature_width), BF),
            pltpu.HBM((feature_width, count), BF),
            pltpu.HBM((count, part_width), F32),
            pltpu.HBM((count, part_width), BF),
            pltpu.HBM((count, part_width), BF),
            shaped((1, part_width), F32),
            shaped((1, feature_width), F32),
        ],
        input_output_aliases=aliases,
        compiler_params=params(30),
        name="hidden_units",
        cost_estimate=LIGHT,
    )(*inputs)


def curvature_kernel(
    probes, steps, place_ref, dirs_in, local_ref, up_bias_ref, normed_in, turned_in, curve_in, grad_in,
    curvature_out, score_ref,
    curvature_ref, dirs_ref, normed_ref, turned_ref, curve_ref, score_s, spare_s, weighted_s, sems,
):
    feature_width, width = dirs_ref.shape
    part_width = width // probes
    half = part_width // 2
    size = normed_ref.shape[0] // steps

    def moves(step):
        rows = slice(step * size, (step + 1) * size)
        return [
            pltpu.make_async_copy(source.at[rows, :], target, sems.at[3 * step + k])
            for k, (source, target) in enumerate((
                (normed_in, normed_ref.at[rows, :]),
                (curve_in, curve_ref.at[rows, :]),
                (grad_in, weighted_s.at[rows, width:]),
            ))
        ]

    begin = pltpu.make_async_copy(dirs_in, dirs_ref, sems.at[3 * steps])
    last = pltpu.make_async_copy(turned_in, turned_ref, sems.at[3 * steps + 1])
    begin.start()
    for step in range(steps):
        for copy in moves(step):
            copy.start()
    last.start()
    score_s[...] = jnp.zeros_like(score_s)
    begin.wait()
    for step in range(steps):
        for copy in moves(step):
            copy.wait()
        rows = slice(step * size, (step + 1) * size)
        along = dot(normed_ref[rows, :], dirs_ref[...])
        curve, wide = curve_ref[rows, :], weighted_s[rows, width:].astype(F32)
        for k in range(probes):
            columns = slice(k * part_width, (k + 1) * part_width)
            part = along[:, columns]
            weighted_s[rows, columns] = (part * curve).astype(BF)
            score_s[k : k + 1, :] += jnp.sum(part * wide, axis=0, keepdims=True)
    last.wait()
    shape = curvature_ref.shape[:2]
    leaving = []
    for k in range(0, probes, 2):
        columns = slice(k * part_width, (k + 2) * part_width)
        total = dot(turned_ref[...], weighted_s[:, columns])
        curvature_ref[:, :, columns] = total.astype(BF).reshape(shape + (2 * part_width,))
        leaving.append((curvature_ref.at[:, :, columns], curvature_out.at[:, :, columns]))
        pltpu.make_async_copy(*leaving[-1], sems.at[3 * steps + 1 + len(leaving)]).start()
    final = dot(turned_ref[...], weighted_s[:, width:]).astype(BF)
    own = jnp.where(place_ref[0] == 1, final[:, half:], final[:, :half])
    scores = jnp.sum(score_s[...], axis=1, keepdims=True)
    score_ref[...] = jnp.broadcast_to(scores, score_ref.shape)

    spare_s[...] = jnp.zeros_like(spare_s)
    row = 0
    for values in (local_ref[1:2, :], local_ref[2:3, :], up_bias_ref[...]):
        high = values.astype(BF).astype(F32)
        for part in (high, values - high):
            for start in range(0, values.shape[1], HEAD_DIM):
                spare_s[row : row + 1, HEAD_DIM:] = part[:, start : start + HEAD_DIM]
                row += 1
    high = scores.astype(BF).astype(F32)
    for part in (high, scores - high):
        for k in range(probes):
            spare_s[row : row + 1, HEAD_DIM + k : HEAD_DIM + k + 1] = part[k : k + 1, :]
        row += 1
    tail = jnp.concatenate([own[:, LANES:], jnp.zeros((feature_width, HEAD_DIM), BF)], axis=1)
    tail = tail.reshape(shape + (LANES,)) + spare_s[...].astype(BF)[None]
    curvature_ref[:, :, width : width + LANES] = own[:, :LANES].reshape(shape + (LANES,))
    curvature_ref[:, :, width + LANES :] = tail
    leaving.append((curvature_ref.at[:, :, width:], curvature_out.at[:, :, width:]))
    pltpu.make_async_copy(*leaving[-1], sems.at[3 * steps + 1 + len(leaving)]).start()
    for number, move in enumerate(leaving):
        pltpu.make_async_copy(*move, sems.at[3 * steps + 2 + number]).wait()


def curvature_of(blocks, core, probes, units, dirs, local_small, up_bias_grad, after):
    (count, feature_width), part_width = units[0].shape, units[2].shape[1]
    width = probes * part_width
    steps = 4
    local_rows = feature_width // blocks
    out = (blocks, local_rows, width + 2 * LANES)
    return call(
        functools.partial(curvature_kernel, probes, steps),
        inputs=[core[None].astype(jnp.int32), far(dirs), local_small, up_bias_grad] + [far(array) for array in units],
        after=after,
        in_specs=[SMEM, ANY, VMEM, VMEM] + [ANY] * 4,
        out_specs=[ANY, VMEM],
        out_shape=[pltpu.HBM(out, BF), shaped((8, LANES), F32)],
        scratch_shapes=[
            pltpu.VMEM(out, BF),
            pltpu.VMEM((feature_width, width), BF),
            pltpu.VMEM((count, feature_width), BF),
            pltpu.VMEM((feature_width, count), BF),
            pltpu.VMEM((count, part_width), F32),
            pltpu.VMEM((8, part_width), F32),
            pltpu.VMEM((local_rows, LANES), F32),
            pltpu.VMEM((count, width + part_width), BF),
            pltpu.SemaphoreType.DMA((3 * steps + 3 + probes // 2,)),
        ],
        compiler_params=params(52),
        name="curvature",
    )


def weights_kernel(heads, place_ref, active_in, cot_in, attended_in, down_ref, attended_ref, out_ref, *scratch):
    active_s, cot_s, attended_s, joined_s, total_s, sems = scratch
    moves = [(cot_in, cot_s), (active_in, active_s), (attended_in, attended_s)]
    copies = [pltpu.make_async_copy(source, target, sems.at[k]) for k, (source, target) in enumerate(moves)]
    for copy in copies:
        copy.start()
    for copy in copies[:2]:
        copy.wait()
    down_ref[...] = dot_tn(active_s[...], cot_s[...])
    copies[2].wait()
    block = attended_ref.shape[0]
    for number in range(cot_s.shape[0] // block):
        rows = slice(number * block, (number + 1) * block)
        values = [attended_s[head, rows, :].astype(F32) for head in range(heads)]
        joined_s[rows, :] = heads_joined(values).astype(BF)
    own = pl.ds(pl.multiple_of(place_ref[0] * block, block), block)
    attended_ref[...] = joined_s[own, :][:, : attended_ref.shape[1]]
    total_s[...] = dot_tn(joined_s[...], cot_s[...])
    local_rows = out_ref.shape[0]
    rows = pl.ds(pl.multiple_of(place_ref[3], local_rows), local_rows)
    out_ref[...] = jnp.where(place_ref[2] == 1, total_s[rows, :], 0.0).astype(BF)


def weights_back(heads, blocks, numbers, active, cot, attended, after):
    (count, feature_width), part_width, pair = cot.shape, active.shape[1], 2 * HEAD_DIM
    value_tiles = -(-heads // 2) * pair
    return call(
        functools.partial(weights_kernel, heads),
        inputs=[numbers, far(active), far(cot), far(attended)],
        after=after,
        in_specs=[SMEM, ANY, ANY, ANY],
        out_specs=[VMEM] * 3,
        out_shape=[
            shaped((part_width, feature_width), F32),
            shaped((count // blocks, heads * HEAD_DIM), BF),
            shaped((feature_width // blocks, feature_width), BF),
        ],
        scratch_shapes=[
            pltpu.VMEM(active.shape, BF),
            pltpu.VMEM(cot.shape, BF),
            pltpu.VMEM(attended.shape, BF),
            pltpu.VMEM((count, value_tiles), BF),
            pltpu.VMEM((value_tiles, feature_width), F32),
            pltpu.SemaphoreType.DMA((3,)),
        ],
        compiler_params=params(32),
        name="weights_back",
    )


def unpack_kernel(got_in, curvature_out, got_s, curvature_s, sems):
    blocks, _, width = got_s.shape
    probes = curvature_s.shape[0]
    part_width = width // probes

    def arrive(k):
        columns = slice(k * part_width, (k + 1) * part_width)
        return pltpu.make_async_copy(got_in.at[:, :, columns], got_s.at[:, :, columns], sems.at[k])

    def leave(k):
        return pltpu.make_async_copy(curvature_s.at[k], curvature_out.at[k], sems.at[probes + k])

    for k in range(probes):
        arrive(k).start()
    for k in range(probes):
        arrive(k).wait()
        for block in range(blocks):
            part = got_s[block, :, k * part_width : (k + 1) * part_width]
            curvature_s[k, :, block * part_width : (block + 1) * part_width] = part.astype(F32)
        leave(k).start()
    for k in range(probes):
        leave(k).wait()


def unpack(got, probes, part_width, after):
    blocks, local_rows, _ = got.shape
    out = (probes, local_rows, blocks * part_width)
    return call(
        unpack_kernel,
        inputs=[far(got)],
        after=after,
        in_specs=[ANY],
        out_specs=ANY,
        out_shape=pltpu.HBM(out, F32),
        scratch_shapes=[
            pltpu.VMEM((blocks, local_rows, probes * part_width), BF),
            pltpu.VMEM(out, F32),
            pltpu.SemaphoreType.DMA((2 * probes,)),
        ],
        compiler_params=params(24),
        name="unpack",
    )


def peel_kernel(probes, got_ref, up_ref, gain_ref, shift_ref, up_bias_ref, score_ref):
    blocks, _, share = got_ref.shape
    part_width = up_bias_ref.shape[0] // blocks
    tails = []
    for block in range(blocks):
        up_ref[:, block * share : (block + 1) * share] = got_ref[block]
        tails.append(got_ref[block, :, share - LANES :].astype(F32))
    total = tails[0]
    for tail in tails[1:]:
        total = total + tail

    def vector(rows, first, length):
        count = length // HEAD_DIM
        parts = [
            rows[first + k : first + k + 1, HEAD_DIM:] + rows[first + count + k : first + count + k + 1, HEAD_DIM:]
            for k in range(count)
        ]
        return jnp.concatenate(parts, axis=1)

    length = gain_ref.shape[0]
    step = 2 * length // HEAD_DIM
    gain_ref[...] = vector(total, 0, length).reshape(gain_ref.shape)
    shift_ref[...] = vector(total, step, length).reshape(shift_ref.shape)
    biases = [vector(tail, 2 * step, part_width) for tail in tails]
    up_bias_ref[...] = jnp.concatenate(biases, axis=1).reshape(up_bias_ref.shape)
    row = 2 * step + 2 * part_width // HEAD_DIM
    scores = total[row : row + 1, HEAD_DIM : HEAD_DIM + probes] + total[row + 1 : row + 2, HEAD_DIM : HEAD_DIM + probes]
    score_ref[...] = scores.reshape(score_ref.shape)


def peel(got, probes, part_width, after):
    blocks, local_rows, width = got.shape
    share = width - probes * part_width
    feature_width = blocks * local_rows
    vector = shaped((feature_width,), F32)
    return call(
        functools.partial(peel_kernel, probes),
        inputs=[got],
        after=after,
        grid=(1,),
        in_specs=[pl.BlockSpec((blocks, local_rows, share), lambda i: (0, 0, width // share - 1))],
        out_specs=[
            whole(local_rows, blocks * share), whole(feature_width), whole(feature_width),
            whole(blocks * part_width), whole(probes),
        ],
        out_shape=[
            shaped((local_rows, blocks * share), BF),
            vector, vector, shaped((blocks * part_width,), F32), shaped((probes,), F32),
        ],
        compiler_params=params(BIG),
        name="peel",
    )


def spread_kernel(blocks, half, place_ref, mine_ref, got_ref, out_ref):
    odd = place_ref[0] == 1
    stride = mine_ref.shape[1] // blocks
    for block in range(blocks):
        here = slice(block * stride, block * stride + half)
        mine, got = mine_ref[:, here], got_ref[:, here]
        both = jnp.concatenate([jnp.where(odd, got, mine), jnp.where(odd, mine, got)], axis=1)
        out_ref[:, block * 2 * half : (block + 1) * 2 * half] = both.astype(F32)


def spread(core, mine, got, blocks, half, after):
    return call(
        functools.partial(spread_kernel, blocks, half),
        inputs=[core[None].astype(jnp.int32), mine, got],
        after=after,
        in_specs=[SMEM, VMEM, VMEM],
        out_specs=VMEM,
        out_shape=shaped((mine.shape[0], blocks * 2 * half), F32),
        compiler_params=params(12),
        name="spread",
    )


def merge_kernel(feature_width, half, few, place_ref, mine_ref, got_ref, merged_ref):
    odd = place_ref[0] == 1
    third = mine_ref.shape[1] - feature_width

    def ordered(rows, columns):
        mine, got = mine_ref[rows, columns], got_ref[rows, columns]
        return jnp.concatenate([jnp.where(odd, got, mine), jnp.where(odd, mine, got)], axis=1)

    main = slice(0, half + few)
    total = mine_ref[main, :feature_width].astype(F32) + got_ref[main, :feature_width].astype(F32)
    merged_ref[...] = jnp.zeros_like(merged_ref)
    merged_ref[main, :feature_width] = total.astype(BF)
    merged_ref[main, feature_width:] = ordered(main, slice(feature_width, feature_width + third))
    rows = slice(half + few, half + 2 * few)
    merged_ref[rows, : 4 * third] = ordered(rows, slice(0, 2 * third))
    first, width = half + 2 * few, feature_width // 2
    put_small(merged_ref, first, get_small(mine_ref, first, width) + get_small(got_ref, first, width))


def merge(core, mine, got, feature_width, half, few):
    count, width = mine.shape
    return call(
        functools.partial(merge_kernel, feature_width, half, few),
        inputs=[core[None].astype(jnp.int32), mine, got],
        in_specs=[SMEM, VMEM, VMEM],
        out_specs=VMEM,
        out_shape=shaped((count, 2 * width - feature_width), BF),
        compiler_params=params(12),
        name="merge",
    )


def finish_kernel(
    few, place_ref, mine_ref, got_ref, tokens_ref, base_ref, rest_ref, vectors_ref, out_weight_ref,
    final_ref, small_ref,
):
    tok_count, feature_width = tokens_ref.shape
    half = tok_count // 2
    third = (mine_ref.shape[1] - feature_width) // 2
    upper = place_ref[1] == 1
    own = pl.ds(pl.multiple_of(place_ref[0] * half, half), half)

    def ordered(rows, columns):
        mine, got = mine_ref[rows, columns], got_ref[rows, columns]
        return jnp.where(upper, got, mine), jnp.where(upper, mine, got)

    attended = jnp.concatenate(ordered(slice(0, half), slice(feature_width, None)), axis=1)
    layer_out = base_ref[own, :] + dot(attended, out_weight_ref[...])
    main = slice(0, half + few)
    total = mine_ref[main, :feature_width].astype(F32) + got_ref[main, :feature_width].astype(F32)
    centred, factor = spread_of(tokens_ref[own, :].astype(F32))
    term = norm_input_term(total[:half], vectors_ref[0:1, :], centred * factor, factor)
    final_ref[:half, :feature_width] = layer_out.astype(BF)
    final_ref[:half, feature_width:] = (rest_ref[own, :] + term).astype(BF)
    parts = []
    firsts = ordered(slice(half, half + few), slice(feature_width, None))
    others = ordered(slice(half + few, half + 2 * few), slice(0, 4 * third))
    for first, other in zip(firsts, others):
        for core in range(2):
            parts += [first[:, core * third : (core + 1) * third], other[:, 2 * core * third : 2 * (core + 1) * third]]
    grad_qkv = jnp.concatenate(parts, axis=1)
    final_ref[half : half + few, :feature_width] = total[half:].astype(BF)
    final_ref[half : half + few, feature_width:] = grad_qkv[:, :feature_width]
    final_ref[half + few :, :] = grad_qkv[:, feature_width:]
    first, width = half + 2 * few, feature_width // 2
    small_ref[...] = get_small(mine_ref, first, width) + get_small(got_ref, first, width)


def finish(places, mine, got, tokens, base, rest, vectors, out_weight, few):
    tok_count, feature_width = tokens.shape
    half = tok_count // 2
    return call(
        functools.partial(finish_kernel, few),
        inputs=[places, mine, got, tokens, far(base), far(rest), vectors, far(out_weight)],
        in_specs=[SMEM] + [VMEM] * 7,
        out_specs=[VMEM] * 2,
        out_shape=[
            shaped((half + 2 * few, 2 * feature_width), BF),
            shaped((mine.shape[0] - half - 2 * few, feature_width // 2), F32),
        ],
        compiler_params=params(20),
        name="finish",
    )


def join_kernel(
    few, mixed_width, place_ref, mine_ref, got_ref, small_ref, cot_ref,
    layer_out_ref, input_grad_ref, out_ref, qkv_ref, gain_ref, shift_ref, qkv_bias_ref, out_bias_ref, down_bias_ref,
):
    half = layer_out_ref.shape[0] // 2
    feature_width = layer_out_ref.shape[1]
    odd = place_ref[0] == 1
    mine, got = mine_ref[...], got_ref[...]
    for core, side in enumerate((jnp.where(odd, got, mine), jnp.where(odd, mine, got))):
        rows = slice(core * half, (core + 1) * half)
        layer_out_ref[rows, :] = side[:half, :feature_width]
        input_grad_ref[rows, :] = side[:half, feature_width:]
        rows = slice(core * few, (core + 1) * few)
        out_ref[rows, :] = side[half : half + few, :feature_width].astype(F32)
        qkv_ref[rows, :feature_width] = side[half : half + few, feature_width:].astype(F32)
        qkv_ref[rows, feature_width:] = side[half + few :, :].astype(F32)
    small = small_ref[...]

    def rows_of(first, total):
        return jnp.concatenate([small[first : first + 1, :], small[first + 1 : first + 2, :]], axis=1)[:, :total]

    gain_ref[...] = rows_of(0, feature_width).reshape(gain_ref.shape)
    shift_ref[...] = rows_of(2, feature_width).reshape(shift_ref.shape)
    groups = qkv_bias_ref.shape[0] // mixed_width
    bias = [rows_of(4 + 2 * number, mixed_width) for number in range(groups)]
    qkv_bias_ref[...] = jnp.concatenate(bias, axis=1).reshape(qkv_bias_ref.shape)
    for ref in (out_bias_ref, down_bias_ref):
        ref[...] = cot_ref[...].reshape(ref.shape)


def join(core, mine, got, small, cot, tok_count, few, mixed_width):
    feature_width = cot.shape[1]
    vector = shaped((feature_width,), F32)
    return call(
        functools.partial(join_kernel, few, mixed_width),
        inputs=[core[None].astype(jnp.int32), mine, got, small, cot],
        in_specs=[SMEM] + [VMEM] * 4,
        out_specs=[VMEM] * 9,
        out_shape=[shaped((tok_count, feature_width), BF)] * 2
        + [shaped((2 * few, feature_width), F32), shaped((2 * few, 3 * feature_width), F32), vector, vector]
        + [shaped((4 * mixed_width,), F32), vector, vector],
        compiler_params=params(16),
        name="join",
    )


def on_device(
    tokens,
    segment_ids,
    qkv_weight,
    qkv_bias,
    out_weight,
    out_bias,
    up_weight,
    up_bias,
    down_weight,
    down_bias,
    norm1_gain,
    norm1_bias,
    norm2_gain,
    norm2_bias,
    probe_dirs,
    out_grad,
):
    tok_count, feature_width = tokens.shape
    hidden_width = up_weight.shape[1]
    probe_count, local_rows = probe_dirs.shape[:2]
    groups = lax.axis_size("ex")
    probe_groups = lax.axis_size("probe")
    blocks = SEQ // tok_count
    rows = groups // blocks
    ex_place = lax.axis_index("ex")
    place = ex_place % blocks
    row_place = ex_place // blocks
    probe_place = lax.axis_index("probe")
    core, upper = probe_place % 2, probe_place // 2
    heads = HEADS // probe_groups
    head_width = heads * HEAD_DIM
    part_width = hidden_width // blocks
    fine = part_width // rows
    row_groups = None
    if rows > 1:
        row_groups = [[r * blocks + b for b in range(blocks)] for r in range(rows)]
    across = [[r * blocks + b for r in range(rows)] for b in range(blocks)]

    def swap(value, distance):
        return lax.ppermute(value, "ex", [(i, i ^ distance) for i in range(groups)])

    def swap_probe(value, distance):
        return lax.ppermute(value, "probe", [(i, i ^ distance) for i in range(probe_groups)])

    def over_rows(value):
        if rows > 1:
            return lax.psum_scatter(value, "ex", axis_index_groups=across, scatter_dimension=0, tiled=True)
        return value

    def my_part(value, axis):
        shape = value.shape
        split = shape[:axis] + (rows, blocks, fine) + shape[axis + 1 :]
        part = lax.dynamic_index_in_dim(value.reshape(split), place, axis + 1, keepdims=False)
        return part.reshape(shape[:axis] + (part_width,) + shape[axis + 1 :])

    mine, share = slices_of(probe_place, probe_groups, tokens, out_grad)
    aside = swap(mine, 1)
    near, diagonal, distant, farthest = [swap(share, distance) for distance in (2, 3, 4, 6)]

    segments = segment_ids
    if rows > 1:
        segments = lax.dynamic_slice_in_dim(segment_ids, row_place * SEQ, SEQ)
    vectors = vectors_of(
        probe_groups, blocks, norm1_gain, norm1_bias, norm2_gain, norm2_bias, out_bias, down_bias, qkv_bias, segments
    )
    base, rest, local_small = local_part(tokens, out_grad, up_weight, up_bias, down_weight, vectors)

    second, third = stack([near, diagonal, distant, farthest], [(0, 1), (2, 3)], [local_small])
    third_aside, third_over = swap(third, 1), swap_probe(third, 2)
    (quarters,) = stack([mine, aside, third, third_over], [(0, 1, 2, 3)], [])
    swapped = swap_probe(quarters, 1)
    up_bias_part = my_part(up_bias, 0).astype(F32)[None]
    up_part, down_part = up_weight, down_weight
    if rows > 1:
        up_part, down_part = my_part(up_weight, 1), my_part(down_weight, 0)

    def pieces_of(array, other, slots, distances):
        return [
            ([(side, slot) for side in (array, other) for slot in pair], ((0, 2, 1, 3), (distance,)))
            for pair, distance in zip(slots, distances)
        ]

    pieces = pieces_of(quarters, swapped, ((0, 1), (2, 3), (4, 6), (5, 7)), (0, 1, 4, 6))
    slots = [lambda i: jnp.where(i < 2, 2 * i, i + 2), lambda i: jnp.where(i < 2, 2 * i + 1, i + 4)]
    refs = [(array, slot_of) for array in (quarters, swapped) for slot_of in slots]
    unit_place = place if rows == 1 else place * 0
    places = jnp.stack([unit_place, place, probe_place]).astype(jnp.int32)
    fixed = (SEQ, up_part, up_bias_part, down_part, vectors)
    units = hidden_units(places, refs, (0, 2, 1, 3), 0, (0, 1, 4, 6), *fixed, None)
    second_over, third_across = swap_probe(second, 2), swap_probe(third_aside, 2)

    dirs = tie(pack(probe_dirs, blocks, rows, [local_small]), [third_aside, third_over, aside])
    dirs = lax.all_to_all(dirs, "ex", 0, 0, axis_index_groups=row_groups, tiled=True)
    dirs = dirs.reshape(blocks * local_rows, probe_count * part_width)
    if rows > 1:
        dirs = lax.all_gather(dirs, "ex", axis_index_groups=across, tiled=True)

    (near_quarters,) = stack([second, second_over], [(0, 1)], [units[5]])
    (far_quarters,) = stack([third_aside, third_across], [(0, 1)], [near_quarters])
    near_swapped = tie(swap_probe(near_quarters, 1), [far_quarters])
    last = ((near_quarters, near_swapped, (2, 3)), (far_quarters, swap_probe(far_quarters, 1), (5, 7)))
    for number, (array, swapped, distances) in enumerate(last):
        pieces += pieces_of(array, swapped, ((0, 2), (1, 3)), distances)
        refs = [(side, lambda i, k=k: i + 2 * k) for side in (array, swapped) for k in range(2)]
        units = hidden_units(places, refs, (0, 2, 1, 3), 4 + 2 * number, distances, *fixed, units)
    *units, active, grad_up_bias, cot_sum = units

    block_rows = feature_width // blocks
    offset = place * block_rows - probe_place * head_width
    holds = (offset >= 0) & (offset < head_width)
    numbers = jnp.stack([place, probe_place, holds, jnp.where(holds, offset, 0)]).astype(jnp.int32)
    *parts, cot, attended = attention(heads, blocks, numbers, pieces, tokens, qkv_weight, vectors, out_weight, [cot_sum])

    part, scores = curvature_of(
        blocks, core, probe_count, units, dirs, local_small, grad_up_bias, [far(attended)]
    )
    part = over_rows(part.reshape(feature_width, -1)).reshape(blocks, local_rows, -1)
    got = lax.all_to_all(part, "ex", 0, 0, axis_index_groups=row_groups, tiled=True)

    grad_down, attended, grad_out = weights_back(heads, blocks, numbers, active, cot, attended, [scores])
    parts += [attended, grad_out]
    keep, send = attention_back(heads, blocks, numbers, parts, qkv_weight, vectors, [scores])
    half, few = tok_count // 2, block_rows // 2
    merged = merge(core, keep, swap_probe(send, 1), feature_width, half, few)
    final, small = finish(
        jnp.stack([core, upper]).astype(jnp.int32), merged, swap_probe(merged, 2), tokens, base, rest, vectors,
        out_weight, few,
    )
    (
        layer_out, input_grad, grad_out_weight, grad_qkv_weight,
        grad_gain_one, grad_shift_one, grad_qkv_bias, grad_out_bias, grad_down_bias,
    ) = join(core, final, swap_probe(final, 1), small, cot_sum, tok_count, few, 3 * head_width)

    if rows == 1:
        up_half, grad_gain_two, grad_shift_two, grad_up_bias, scores = peel(
            got, probe_count, part_width, [layer_out]
        )
        other_half = swap_probe(up_half, 1)
        curvature = unpack(got, probe_count, part_width, [far(up_half)])
        scores = scores[:, None]
        grad_up_weight = spread(core, up_half, other_half, blocks, part_width // 2, [])
    else:
        start = probe_count * part_width
        units = got[:, :, :start].reshape(blocks, local_rows, probe_count, rows, fine)
        curvature = units.transpose(2, 1, 3, 0, 4).reshape(probe_count, local_rows, hidden_width)
        curvature = curvature.astype(F32)
        up_half = got[:, :, start : start + part_width // 2]
        both = lax.all_gather(up_half, "probe", axis_index_groups=[[0, 1], [2, 3]])
        both = both.transpose(2, 1, 0, 3).reshape(local_rows, blocks, rows, fine)
        grad_up_weight = both.transpose(0, 2, 1, 3).reshape(local_rows, hidden_width).astype(F32)
        grad_down = over_rows(grad_down)

        def over_groups(value):
            value = lax.all_gather(value, "ex", axis_index_groups=row_groups, tiled=True)
            return lax.dynamic_slice_in_dim(over_rows(value), place * local_rows, local_rows, 0)

        grad_qkv_weight, grad_out_weight = over_groups(grad_qkv_weight), over_groups(grad_out_weight)
        grad_gain_one, grad_shift_one, grad_qkv_bias, grad_out_bias, grad_up_bias = lax.psum(
            (grad_gain_one, grad_shift_one, grad_qkv_bias, grad_out_bias, grad_up_bias[0]),
            "ex",
            axis_index_groups=across,
        )
        grad_down_bias = grad_out_bias
        grad_up_bias = lax.all_gather(grad_up_bias, "ex", axis_index_groups=row_groups)
        grad_up_bias = grad_up_bias.reshape(blocks, rows, fine).transpose(1, 0, 2).reshape(-1)
        grad_gain_two, grad_shift_two = lax.psum((local_small[1], local_small[2]), "ex")
        scores = lax.psum(scores[:probe_count, :1], "ex", axis_index_groups=row_groups)
        scores = lax.all_gather(scores, "ex", axis_index_groups=across, axis=1, tiled=True)
    return (
        layer_out,
        input_grad,
        grad_qkv_weight,
        grad_qkv_bias,
        grad_out_weight,
        grad_out_bias,
        grad_up_weight,
        grad_up_bias,
        grad_down,
        grad_down_bias,
        grad_gain_one,
        grad_shift_one,
        grad_gain_two,
        grad_shift_two,
        curvature,
        scores,
    )


def solution(mesh):
    in_specs = (
        P("ex", None),
        P(),
        P(),
        P(),
        P(),
        P(),
        P(),
        P(),
        P(),
        P(),
        P(),
        P(),
        P(),
        P(),
        P("probe", "ex", None),
        P("ex", None),
    )
    out_specs = (
        P("ex", None),
        P("ex", None),
        P("ex", None),
        P(),
        P("ex", None),
        P(),
        P("ex", None),
        P(),
        P("ex", None),
        P(),
        P(),
        P(),
        P(),
        P(),
        P("probe", "ex", None),
        P("probe", None),
    )
    return jax.shard_map(
        on_device, mesh=mesh, in_specs=in_specs, out_specs=out_specs, check_vma=False
    )
```

```python
import functools

import jax
import jax.numpy as jnp
import numpy as np
from jax import lax
from jax.experimental import pallas as pl
from jax.experimental.pallas import tpu as pltpu
from jax.sharding import PartitionSpec as P

HEADS = 12
HEAD_DIM = 64
ROT = 16
SEQ = 2048

BF = jnp.bfloat16
F32 = jnp.float32
eps_norm = 1e-05
masked_score = -1e30
half_root = 0.7071067811865476
gauss_peak = 0.3989422804014327
MB = 1024 * 1024
LANES = 128
LIGHT = pl.CostEstimate(flops=1000, bytes_accessed=1000, transcendentals=0)
BIG = 58


def dot(a, b):
    return jnp.dot(a, b, preferred_element_type=F32)


def dot_nt(a, b):
    return lax.dot_general(a, b, (((1,), (1,)), ((), ())), preferred_element_type=F32)


def dot_tn(a, b):
    return lax.dot_general(a, b, (((0,), (0,)), ((), ())), preferred_element_type=F32)


def spread_of(features):
    center = jnp.mean(features, axis=-1, keepdims=True)
    centred = features - center
    spread = jnp.mean(centred * centred, axis=-1, keepdims=True)
    return centred, lax.rsqrt(spread + eps_norm)


def standardize(features):
    centred, factor = spread_of(features)
    return centred * factor


def norm_input_term(grad, gain_row, unit, factor):
    unit_grad = grad * gain_row
    inner = unit_grad - jnp.mean(unit_grad, -1, keepdims=True)
    return (inner - unit * jnp.mean(unit_grad * unit, -1, keepdims=True)) * factor


def gelu_parts(pre_act):
    below = 0.5 + 0.5 * lax.erf(pre_act * half_root)
    density = gauss_peak * jnp.exp(-0.5 * pre_act * pre_act)
    return below, density


def rotary_tables(count):
    steps = np.arange(ROT // 2, dtype=np.float32) * np.float32(2.0 / ROT)
    inverse = np.power(np.float32(10000.0), -steps).astype(np.float32)
    angles = np.arange(count, dtype=np.float32)[:, None] * inverse[None, :]
    angles = np.concatenate([angles, angles], axis=1)
    cosine = np.ones((count, HEAD_DIM), np.float32)
    sine = np.zeros((count, HEAD_DIM), np.float32)
    cosine[:, :ROT], sine[:, :ROT] = np.cos(angles), np.sin(angles)
    return np.concatenate([cosine, cosine], axis=1), np.concatenate([sine, sine], axis=1)


def params(limit_mb, **more):
    return pltpu.CompilerParams(vmem_limit_bytes=limit_mb * MB, **more)


def shaped(shape, dtype):
    return jax.ShapeDtypeStruct(shape, dtype)


def whole(*shape):
    return pl.BlockSpec(shape, lambda i: (0,) * len(shape))


VMEM = pl.BlockSpec(memory_space=pltpu.VMEM)
SMEM = pl.BlockSpec(memory_space=pltpu.SMEM)
ANY = pl.BlockSpec(memory_space=pl.ANY)


def far(array):
    return pltpu.with_memory_space_constraint(array, pltpu.HBM)


def call(kernel, *, inputs, in_specs, after=(), aliases=None, **more):
    spare = len(after)

    def body(*refs):
        kernel(*refs[: len(inputs)], *refs[len(inputs) + spare :])

    return pl.pallas_call(
        body, in_specs=list(in_specs) + [ANY] * spare, input_output_aliases=aliases or {},
        cost_estimate=LIGHT, **more,
    )(*inputs, *after)


def tie(value, after):
    return call(
        lambda value_ref, out_ref: None,
        inputs=[value],
        after=after,
        aliases={0: 0},
        in_specs=[ANY],
        out_specs=ANY,
        out_shape=shaped(value.shape, value.dtype),
        name="tie",
    )


def pack_kernel(dirs_ref, packed_ref, sems):
    probes = dirs_ref.shape[0]
    blocks, _, width = packed_ref.shape
    part_width = width // probes
    copies = []
    for block in range(blocks):
        for k in range(probes):
            source = dirs_ref.at[k, :, block * part_width : (block + 1) * part_width]
            target = packed_ref.at[block, :, k * part_width : (k + 1) * part_width]
            copies.append(pltpu.make_async_copy(source, target, sems.at[len(copies)]))
    for copy in copies:
        copy.start()
    for copy in copies:
        copy.wait()


def pack(dirs, blocks, rows, after):
    probes, local_rows, hidden_width = dirs.shape
    part_width = hidden_width // blocks
    if rows > 1:
        split = dirs.reshape(probes, local_rows, rows, blocks, part_width // rows)
        return split.transpose(3, 1, 0, 2, 4).reshape(blocks, local_rows, probes * part_width)
    return call(
        pack_kernel,
        inputs=[dirs],
        after=after,
        in_specs=[VMEM],
        out_specs=ANY,
        out_shape=pltpu.HBM((blocks, local_rows, probes * part_width), dirs.dtype),
        scratch_shapes=[pltpu.SemaphoreType.DMA((blocks * probes,))],
        compiler_params=params(8),
        name="pack",
    )


def slices_kernel(place_ref, tokens_ref, grads_ref, both_ref, first_ref, sems):
    count = both_ref.shape[2]
    copies = []
    for part, source in enumerate((tokens_ref, grads_ref)):
        for target, slot, side in ((both_ref, 0, 0), (both_ref, 1, 2), (first_ref, 0, 0)):
            first = jnp.bitwise_xor(place_ref[0], side) * count
            rows = pl.ds(pl.multiple_of(first, count), count)
            copies.append(pltpu.make_async_copy(source.at[rows, :], target.at[slot, part], sems.at[len(copies)]))
    for copy in copies:
        copy.start()
    for copy in copies:
        copy.wait()


def slices_of(probe_place, probe_groups, tokens, grads):
    tok_count, feature_width = tokens.shape
    size = tok_count // probe_groups
    return call(
        slices_kernel,
        inputs=[probe_place[None].astype(jnp.int32), far(tokens), far(grads)],
        in_specs=[SMEM, ANY, ANY],
        out_specs=[VMEM] * 2,
        out_shape=[shaped((count, 2, size, feature_width), BF) for count in (2, 1)],
        scratch_shapes=[pltpu.SemaphoreType.DMA((6,))],
        compiler_params=params(8),
        name="slices",
    )


def stack_kernel(plan, *refs):
    sources, targets = refs[: -len(plan)], refs[-len(plan) :]
    for parts, target in zip(plan, targets):
        number = 0
        for part in parts:
            count = sources[part].shape[0]
            target[number : number + count] = sources[part][...]
            number += count


def stack(sources, plan, after):
    heights = [sum(sources[part].shape[0] for part in parts) for parts in plan]
    return call(
        functools.partial(stack_kernel, plan),
        inputs=sources,
        after=after,
        in_specs=[VMEM] * len(sources),
        out_specs=[VMEM] * len(plan),
        out_shape=[shaped((n,) + sources[parts[0]].shape[1:], BF) for n, parts in zip(heights, plan)],
        compiler_params=params(8),
        name="stack",
    )


def vectors_kernel(groups, blocks, count, *refs):
    sources, vectors_ref, held, sems = refs[:count], refs[count], refs[count + 1 : -1], refs[-1]
    copies = [pltpu.make_async_copy(source, target, sems.at[k]) for k, (source, target) in enumerate(zip(sources, held))]
    for copy in copies:
        copy.start()
    vectors_ref[...] = jnp.zeros_like(vectors_ref)
    for copy in copies:
        copy.wait()
    *plain, first_bias, second_bias, qkv_bias, segments = held
    for number, source in enumerate(plain):
        vectors_ref[number : number + 1, :] = source[...].reshape(1, -1)
    total = first_bias[...].astype(F32) + second_bias[...].astype(F32)
    vectors_ref[len(plain) : len(plain) + 1, :] = total.reshape(1, -1)
    width = qkv_bias.shape[0] // groups
    bias = qkv_bias[...].astype(F32).reshape(1, -1)
    for number in range(groups):
        vectors_ref[8 + number : 9 + number, :width] = bias[:, number * width : (number + 1) * width]
    block = segments.shape[0] // blocks
    for number in range(blocks):
        row = segments[number * block : (number + 1) * block].astype(F32).reshape(1, -1)
        vectors_ref[16 + number : 17 + number, :block] = row


def vectors_of(groups, blocks, *sources):
    return call(
        functools.partial(vectors_kernel, groups, blocks, len(sources)),
        inputs=[far(source) for source in sources],
        in_specs=[ANY] * len(sources),
        out_specs=VMEM,
        out_shape=shaped((16 + blocks, sources[0].shape[0]), F32),
        scratch_shapes=[pltpu.VMEM(source.shape, source.dtype) for source in sources]
        + [pltpu.SemaphoreType.DMA((len(sources),))],
        compiler_params=params(4),
        name="vectors",
    )


def local_kernel(
    tokens_ref, grads_ref, up_ref, up_bias_ref, down_ref, vectors_ref,
    base_ref, rest_ref, small_ref, normed_s, branch_s, back_s,
):
    step = pl.program_id(0)
    gain, shift, out_bias = vectors_ref[2:3, :], vectors_ref[3:4, :], vectors_ref[4:5, :]

    @pl.when(step == 0)
    def _():
        unit = standardize(tokens_ref[...].astype(F32))
        normed_s[...] = (unit * gain + shift).astype(BF)
        branch_s[...] = jnp.zeros_like(branch_s)
        back_s[...] = jnp.zeros_like(back_s)

    bias = up_bias_ref[pl.ds(pl.multiple_of(step * up_ref.shape[1], LANES), up_ref.shape[1])]
    hidden = dot(normed_s[...], up_ref[...]) + bias.astype(F32).reshape(1, -1)
    upstream = dot_nt(grads_ref[...], down_ref[...])
    below, density = gelu_parts(hidden)
    branch_s[...] += dot((hidden * below).astype(BF), down_ref[...])
    hidden_grad = (upstream * (below + hidden * density)).astype(BF)
    back_s[...] += dot_nt(hidden_grad, up_ref[...])

    @pl.when(step == pl.num_programs(0) - 1)
    def _():
        inputs = tokens_ref[...].astype(F32)
        cot = grads_ref[...].astype(F32)
        centred, factor = spread_of(inputs)
        unit = centred * factor
        back = back_s[...]
        base_ref[...] = inputs + branch_s[...] + out_bias
        rest_ref[...] = cot + norm_input_term(back, gain, unit, factor)
        small_ref[...] = jnp.zeros_like(small_ref)
        small_ref[0:1, :] = jnp.sum(cot, axis=0, keepdims=True)
        small_ref[1:2, :] = jnp.sum(back * unit, axis=0, keepdims=True)
        small_ref[2:3, :] = jnp.sum(back, axis=0, keepdims=True)


def local_part(tokens, grads, up_weight, up_bias, down_weight, vectors):
    tok_count, feature_width = tokens.shape
    hidden_width = up_weight.shape[1]
    step = 512
    own = whole(tok_count, feature_width)
    return call(
        local_kernel,
        inputs=[tokens, grads, far(up_weight), up_bias, far(down_weight), vectors],
        grid=(hidden_width // step,),
        in_specs=[
            own, own,
            pl.BlockSpec((feature_width, step), lambda i: (0, i)),
            whole(hidden_width),
            pl.BlockSpec((step, feature_width), lambda i: (i, 0)),
            whole(8, feature_width),
        ],
        out_specs=[own, own, whole(8, feature_width)],
        out_shape=[
            shaped((tok_count, feature_width), F32),
            shaped((tok_count, feature_width), F32),
            shaped((8, feature_width), F32),
        ],
        scratch_shapes=[
            pltpu.VMEM((tok_count, feature_width), BF),
            pltpu.VMEM((tok_count, feature_width), F32),
            pltpu.VMEM((tok_count, feature_width), F32),
        ],
        compiler_params=params(24),
        name="local",
    )


def lanes(rows):
    return lax.broadcasted_iota(jnp.int32, (rows, 2 * HEAD_DIM), 1)


def flipped(tile):
    return pltpu.roll(tile, HEAD_DIM, 1)


def joined(left, right):
    return jnp.where(lanes(left.shape[0]) < HEAD_DIM, left, flipped(right))


def half_turned(tile):
    place_in = lanes(tile.shape[0]) % HEAD_DIM
    low = pltpu.roll(tile, 2 * HEAD_DIM - ROT // 2, 1)
    high = pltpu.roll(tile, ROT // 2, 1)
    return jnp.where(place_in < ROT // 2, -low, jnp.where(place_in < ROT, high, 0.0))


def with_column(tile, lane, column, parts):
    number = lanes(tile.shape[0])
    for k in range(parts):
        part = column.astype(BF).astype(F32) if k + 1 < parts else column
        tile = jnp.where(number == lane + k, part, tile)
        column = column - part
    return tile


def heads_joined(values):
    heads = len(values)
    values = [joined(values[k], values[k + 1]) if k + 1 < heads else values[k] for k in range(0, heads, 2)]
    if heads % 2:
        values[-1] = jnp.where(lanes(values[-1].shape[0]) < HEAD_DIM, values[-1], 0.0)
    return jnp.concatenate(values, axis=1)


def attention_kernel(heads, blocks, block, count, plan, *refs):
    sources, refs = refs[:count], refs[count:]
    (
        place_ref, weight_ref, vectors_ref, out_weight_ref, cos_in, sin_in,
        query_out, key_out, value_out, back_out, unit_out, cot_out, attended_out,
        cos_ref, sin_ref, query_s, key_s, value_s, back_s, unit_s, cot_s,
        window_s, weight_s, bias_s, out_weight_s, attended_s, query_code_s, key_code_s, sems,
        *array_refs,
    ) = refs
    place, probe_place = place_ref[0], place_ref[1]
    feature_width = unit_s.shape[1]
    pair = 2 * HEAD_DIM
    scale = HEAD_DIM ** (-0.5)
    gain, shift = vectors_ref[0:1, :], vectors_ref[1:2, :]
    own_rows = pl.ds(pl.multiple_of(place * block, block), block)
    head_width = heads * HEAD_DIM
    mixed_width = 3 * head_width

    first = probe_place * mixed_width // LANES * LANES
    columns = pl.ds(pl.multiple_of(first, LANES), window_s.shape[1])
    rows = pl.ds(pl.multiple_of(probe_place * head_width, HEAD_DIM), head_width)
    moves = [(weight_ref.at[:, columns], window_s), (out_weight_ref.at[rows, :], out_weight_s.at[:head_width, :])]
    moves += [(cos_in, cos_ref), (sin_in, sin_ref)] + list(zip(sources, array_refs))
    copies = [pltpu.make_async_copy(source, target, sems.at[k]) for k, (source, target) in enumerate(moves)]
    for copy in copies:
        copy.start()
    done = len(copies)

    def leave(number, source, target):
        return pltpu.make_async_copy(source, target, sems.at[done + number])

    def rows_of(number):
        return pl.ds(pl.multiple_of(number * block, block), block)

    def side_rows(distance, side, count):
        own = place_ref[1] % (block // count)
        first = jnp.bitwise_xor(place, distance) * block + jnp.bitwise_xor(own, side) * count
        return pl.ds(pl.multiple_of(first, count), count)

    def together(refs, slot, part):
        return jnp.concatenate([array_refs[ref][base + slot, part] for ref, base in refs], axis=0)

    def arrange(source, target):
        for head in range(heads):
            start = head * 3 * HEAD_DIM
            tile = source[:, start : start + pair]
            target[:, head * pair : (head + 1) * pair] = tile.astype(target.dtype)
        values = [source[:, (3 * head + 2) * HEAD_DIM : (3 * head + 3) * HEAD_DIM] for head in range(heads)]
        values.append(jnp.zeros((source.shape[0], -heads * HEAD_DIM % pair), source.dtype))
        target[:, heads * pair :] = jnp.concatenate(values, axis=1).astype(target.dtype)

    number = lanes(block)
    ones = (number >= HEAD_DIM + 16) & (number < HEAD_DIM + 19)
    coded = (number >= HEAD_DIM) & (number < HEAD_DIM + 16)
    for index in range(blocks):
        segment = jnp.broadcast_to(vectors_ref[16 + index : 17 + index, :block], (pair, block)).T
        segment = segment.astype(jnp.int32)
        match = (number == HEAD_DIM + segment // 8) | (number == HEAD_DIM + 8 + segment % 8)
        here = slice(index * block, (index + 1) * block)
        query_code_s[here, :] = jnp.where(coded & ~match, masked_score, 0.0)
        key_code_s[here, :] = jnp.where(match | ones, 1.0, 0.0)

    out_weight_s[head_width:, :] = jnp.zeros((out_weight_s.shape[0] - head_width, feature_width), BF)
    copies[0].wait()
    odd = probe_place * mixed_width % LANES != 0
    window = window_s[...]
    weight = jnp.where(odd, window[:, HEAD_DIM : HEAD_DIM + mixed_width], window[:, :mixed_width])
    arrange(weight, weight_s)
    bias = vectors_ref[pl.ds(8 + probe_place, 1), :mixed_width]
    arrange(jnp.broadcast_to(bias, (8, mixed_width)), bias_s)
    for copy in copies[1:4]:
        copy.wait()

    def project(sides, refs, slot, distance):
        unit = standardize(together(refs, slot, 0).astype(F32))
        normed = (unit * gain + shift).astype(BF)
        low = unit.astype(BF)
        whole_part = dot(normed, weight_s[...]) + bias_s[:1, :]
        cot = together(refs, slot, 1)
        whole_back = dot_nt(cot, out_weight_s[...])
        count = block // len(sides)
        for number, side in enumerate(sides):
            here = slice(number * count, (number + 1) * count)
            rows = side_rows(distance, side, count)
            unit_s[rows, :] = low[here]
            cot_s[rows, :] = cot[here]
            place_heads(rows, whole_part[here], whole_back[here])

    def place_heads(rows, part, back_part):
        cosine, sine = cos_ref[rows, :], sin_ref[rows, :]
        number = lanes(part.shape[0])
        query_code, key_code = query_code_s[rows, :], key_code_s[rows, :]
        value_code = jnp.where((number >= HEAD_DIM) & (number < HEAD_DIM + 2), 1.0, 0.0)
        first = number < HEAD_DIM
        for head in range(heads):
            plain = part[:, head * pair : (head + 1) * pair]
            both = plain * cosine + half_turned(plain) * sine
            query_s[head, rows, :] = jnp.where(first, both * scale, query_code).astype(BF)
            key_s[head, rows, :] = jnp.where(first, flipped(both), key_code).astype(BF)
            start = heads * pair + head // 2 * pair
            tile = part[:, start : start + pair]
            back_tile = back_part[:, head // 2 * pair : head // 2 * pair + pair]
            if head % 2:
                tile, back_tile = flipped(tile), flipped(back_tile)
            value_s[head, rows, :] = jnp.where(first, tile, value_code).astype(BF)
            back_s[head, rows, :] = jnp.where(first, back_tile, 0.0).astype(BF)

    here = set()
    for sides, distances, refs in plan:
        for number in sorted({ref for ref, _ in refs} - here):
            copies[4 + number].wait()
            here.add(number)
        for slot, distance in enumerate(distances):
            project(sides, refs, slot, distance)
    leaving = [leave(0, key_s, key_out), leave(1, value_s, value_out), leave(2, unit_s, unit_out)]
    leaving.append(leave(3, cot_s, cot_out))
    for copy in leaving:
        copy.start()

    square = (block, block)
    lower = lax.broadcasted_iota(jnp.int32, square, 1) <= lax.broadcasted_iota(jnp.int32, square, 0)

    def head_leaving(head):
        pairs = ((query_s, query_out), (back_s, back_out), (attended_s, attended_out))
        return [leave(4 + 3 * head + k, source.at[head], target.at[head]) for k, (source, target) in enumerate(pairs)]

    def attend(head, carry):
        def scores_of(number):
            start, stop = number * block, (number + 1) * block
            query = query_s[head, start:stop, :]
            near = jnp.where(lower, dot_nt(query, key_s[head, start:stop, :]), masked_score)
            return near, dot_nt(query, key_s[head, :start, :]) if number else None

        ahead = scores_of(0)
        for number in range(blocks):
            start, stop = number * block, (number + 1) * block
            near, far = ahead
            if number + 1 < blocks:
                ahead = scores_of(number + 1)
            top = jnp.max(near, axis=-1, keepdims=True)
            if number:
                top = jnp.maximum(top, jnp.max(far, axis=-1, keepdims=True))
            got = dot(jnp.exp(near - top).astype(BF), value_s[head, start:stop, :])
            if number:
                got = got + dot(jnp.exp(far - top).astype(BF), value_s[head, :start, :])
            total = got[:, HEAD_DIM : HEAD_DIM + 1]
            attended = got / total
            attended_s[head, start:stop, :] = attended.astype(BF)
            back = back_s[head, start:stop, :].astype(F32)
            delta = jnp.sum(attended * back, axis=-1, keepdims=True)
            log_total = top + jnp.log(total)
            query = query_s[head, start:stop, :].astype(F32)
            query_s[head, start:stop, :] = with_column(query, HEAD_DIM + 16, -log_total, 3).astype(BF)
            back_s[head, start:stop, :] = with_column(back, HEAD_DIM, -delta, 2).astype(BF)
        for copy in head_leaving(head):
            copy.start()
        return carry

    lax.fori_loop(0, heads, attend, 0)

    for copy in leaving:
        copy.wait()
    for head in range(heads):
        for copy in head_leaving(head):
            copy.wait()


def attention_back_kernel(
    heads, blocks, place_ref, query_in, key_in, value_in, back_in, unit_in, attended_ref, grad_out_ref, weight_ref,
    vectors_ref, cos_in, sin_in,
    keep_ref, send_ref,
    query_s, key_s, value_s, back_s, unit_ref, cos_ref, sin_ref,
    query_grad_s, key_grad_s, both_s, value_grad_s, mixed_s, total_s, small_s, window_s, sems,
):
    place, probe_place = place_ref[0], place_ref[1]
    block, head_width = attended_ref.shape
    feature_width = unit_ref.shape[1]
    mixed_width = 3 * head_width
    scale = HEAD_DIM ** (-0.5)
    first = probe_place * mixed_width // LANES * LANES
    columns = pl.ds(pl.multiple_of(first, LANES), window_s.shape[1])
    others = [(cos_in, cos_ref), (sin_in, sin_ref), (unit_in, unit_ref), (weight_ref.at[:, columns], window_s)]
    others = [pltpu.make_async_copy(source, target, sems.at[k]) for k, (source, target) in enumerate(others)]

    def arriving(head):
        pairs = ((key_in, key_s), (query_in, query_s), (value_in, value_s), (back_in, back_s))
        return [
            pltpu.make_async_copy(source.at[head], target.at[head], sems.at[4 + len(pairs) * head + k])
            for k, (source, target) in enumerate(pairs)
        ]

    for copy in arriving(0) + others[:2]:
        copy.start()
    for head in range(1, heads):
        for copy in arriving(head):
            copy.start()
    for copy in others[2:]:
        copy.start()
    for copy in others[:2]:
        copy.wait()
    square = (block, block)
    upper = lax.broadcasted_iota(jnp.int32, square, 0) <= lax.broadcasted_iota(jnp.int32, square, 1)

    def through(head, carry):
        for copy in arriving(head):
            copy.wait()
        query_grad_s[...] = jnp.zeros_like(query_grad_s)
        for number in range(blocks):
            start, stop = number * block, (number + 1) * block
            key, value = key_s[head, start:stop, :], value_s[head, start:stop, :]
            key_t = key.T
            key_grad = value_grad = None
            for rows, mask in ((slice(start, stop), upper), (slice(stop, blocks * block), None)):
                if rows.start == rows.stop:
                    continue
                query, back = query_s[head, rows, :], back_s[head, rows, :]
                scores = dot_nt(key, query)
                if mask is not None:
                    scores = jnp.where(mask, scores, masked_score)
                probs = jnp.exp(scores)
                score_grad = (probs * dot_nt(value, back)).astype(BF)
                value_term, key_term = dot(probs.astype(BF), back), dot(score_grad, query)
                value_grad = value_term if value_grad is None else value_grad + value_term
                key_grad = key_term if key_grad is None else key_grad + key_term
                query_grad_s[:, rows] += dot(key_t, score_grad)
            key_grad_s[start:stop, :] = key_grad
            value_grad_s[head, start:stop, :] = value_grad.astype(BF)
        for number in range(blocks):
            rows = slice(number * block, (number + 1) * block)
            both = joined(query_grad_s[:, rows].T * scale, key_grad_s[rows, :])
            both = both * cos_ref[rows, :] - half_turned(both * sin_ref[rows, :])
            both_s[head, rows, :] = both.astype(BF)
        return carry

    lax.fori_loop(0, heads, through, 0)

    for number in range(blocks):
        rows = slice(number * block, (number + 1) * block)
        tiles = []
        for head in range(heads):
            both, value = both_s[head, rows, :].astype(F32), value_grad_s[head, rows, :].astype(F32)
            if head % 2 == 0:
                tiles += [both, value]
            else:
                tiles[-1] = joined(tiles[-1], both)
                tiles.append(joined(flipped(both), value))
        if heads % 2:
            tiles[-1] = jnp.where(lanes(block) < HEAD_DIM, tiles[-1], 0.0)
        mixed_s[rows, :] = jnp.concatenate(tiles, axis=1).astype(BF)

    others[2].wait()
    total_s[...] = dot_tn(unit_ref[...], mixed_s[...])
    sums = jnp.sum(mixed_s[...].astype(F32), axis=0, keepdims=True)
    others[3].wait()
    odd = probe_place * mixed_width % LANES != 0
    window = window_s[...]
    weight = jnp.where(odd, window[:, HEAD_DIM : HEAD_DIM + mixed_width], window[:, :mixed_width])

    own_rows = pl.ds(pl.multiple_of(place * block, block), block)
    mixed_own = mixed_s[own_rows, :][:, :mixed_width]
    normed_back = dot_nt(mixed_own, weight).astype(BF)

    local_rows = grad_out_ref.shape[0]
    first = pl.multiple_of(place * local_rows, local_rows)
    pick = lax.broadcasted_iota(jnp.int32, (local_rows, feature_width), 1) == first + lax.broadcasted_iota(
        jnp.int32, (local_rows, feature_width), 0
    )
    gain, shift = [
        jnp.sum(jnp.where(pick, vectors_ref[k : k + 1, :], 0.0), axis=1, keepdims=True) for k in range(2)
    ]
    grad_qkv = (total_s[pl.ds(first, local_rows), :] * gain + sums * shift).astype(BF)

    wide = weight.astype(F32)
    columns = [
        jnp.sum(wide * total_s[:, :mixed_width], axis=1, keepdims=True),
        jnp.sum(wide * sums[:, :mixed_width], axis=1, keepdims=True),
    ]
    number = lax.broadcasted_iota(jnp.int32, (feature_width, LANES), 1)
    columns = jnp.where(number == 0, columns[0], jnp.where(number == 1, columns[1], 0.0)).T
    piece = feature_width // 2
    small_s[...] = jnp.zeros_like(small_s)
    for k in range(2):
        for part in range(2):
            here = slice(part * piece, (part + 1) * piece)
            small_s[2 * k + part : 2 * k + part + 1, :piece] = columns[k : k + 1, here]
    small_s[pl.ds(4 + 2 * probe_place, 1), :piece] = sums[:, :piece]
    small_s[pl.ds(5 + 2 * probe_place, 1), : mixed_width - piece] = sums[:, piece:mixed_width]
    half, few = block // 2, local_rows // 2
    third = head_width
    odd = probe_place % 2 == 1

    def halves(value):
        low, high = value[: value.shape[0] // 2], value[value.shape[0] // 2 :]
        return jnp.where(odd, high, low), jnp.where(odd, low, high)

    attended, grad_out = attended_ref[...], grad_out_ref[...]
    for number, target in enumerate((keep_ref, send_ref)):
        target[...] = jnp.zeros_like(target)
        target[:half, :feature_width] = halves(normed_back)[number]
        target[:half, feature_width:] = halves(attended)[number]
        target[half : half + few, :feature_width] = halves(grad_out)[number]
        part = halves(grad_qkv)[number]
        target[half : half + few, feature_width:] = part[:, :third]
        target[half + few : half + 2 * few, : 2 * third] = part[:, third : 3 * third]
        put_small(target, half + 2 * few, small_s[...])


def put_small(target, first, small):
    width = small.shape[1]
    high = small.astype(BF)
    target[first:, :width] = high
    target[first:, width : 2 * width] = (small - high.astype(F32)).astype(BF)


def get_small(source, first, width):
    return source[first:, :width].astype(F32) + source[first:, width : 2 * width].astype(F32)


def attention(heads, blocks, numbers, pieces, tokens, qkv_weight, vectors, out_weight, after):
    tok_count, feature_width = tokens.shape
    pair = 2 * HEAD_DIM
    head_width = heads * HEAD_DIM
    value_tiles = -(-heads // 2) * pair
    arrays, plan = [], []
    for refs, (sides, distances) in pieces:
        numbered = []
        for array, base in refs:
            if not any(array is other for other in arrays):
                arrays.append(array)
            numbered.append(([array is other for other in arrays].index(True), base))
        plan.append((sides, distances, numbered))
    cos_table, sin_table = rotary_tables(SEQ)
    per_head = shaped((heads, SEQ, pair), BF)
    window = -(-(3 * head_width) // LANES) * LANES
    return call(
        functools.partial(attention_kernel, heads, blocks, tok_count, len(arrays), plan),
        inputs=arrays + [numbers, far(qkv_weight), vectors, far(out_weight), far(jnp.asarray(cos_table)), far(jnp.asarray(sin_table))],
        after=after,
        in_specs=[ANY] * len(arrays) + [SMEM, ANY, VMEM, ANY, ANY, ANY],
        out_specs=[ANY] * 7,
        out_shape=[pltpu.HBM(per_head.shape, BF)] * 4
        + [pltpu.HBM((SEQ, feature_width), BF)] * 2
        + [pltpu.HBM(per_head.shape, BF)],
        scratch_shapes=[pltpu.VMEM((SEQ, pair), F32)] * 2
        + [pltpu.VMEM((heads, SEQ, pair), BF)] * 4
        + [pltpu.VMEM((SEQ, feature_width), BF)] * 2
        + [
            pltpu.VMEM((feature_width, window), BF),
            pltpu.VMEM((feature_width, heads * pair + value_tiles), BF),
            pltpu.VMEM((8, heads * pair + value_tiles), F32),
            pltpu.VMEM((value_tiles, feature_width), BF),
            pltpu.VMEM((heads, SEQ, pair), BF),
            pltpu.VMEM((SEQ, pair), F32),
            pltpu.VMEM((SEQ, pair), F32),
            pltpu.SemaphoreType.DMA((4 + len(arrays) + 4 + 3 * heads,)),
        ]
        + [pltpu.VMEM(array.shape, array.dtype) for array in arrays],
        compiler_params=params(44),
        name="attention",
    )


def attention_back(heads, blocks, numbers, parts, qkv_weight, vectors, after):
    *_, unit, attended, grad_out = parts
    (tok_count, head_width), (local_rows, feature_width) = attended.shape, grad_out.shape
    pair = 2 * HEAD_DIM
    width = -(-(3 * head_width) // LANES) * LANES
    small_rows = -(-(4 + 2 * HEADS // heads) // 16) * 16
    cos_table, sin_table = rotary_tables(SEQ)
    return call(
        functools.partial(attention_back_kernel, heads, blocks),
        inputs=[numbers, *[far(part) for part in parts[:5]], *parts[5:], far(qkv_weight), vectors, far(jnp.asarray(cos_table)), far(jnp.asarray(sin_table))],
        after=after,
        in_specs=[SMEM] + [ANY] * 5 + [VMEM] * 2 + [ANY, VMEM, ANY, ANY],
        out_specs=[VMEM] * 2,
        out_shape=[
            shaped((tok_count // 2 + local_rows + small_rows, feature_width + head_width), BF),
        ] * 2,
        scratch_shapes=[pltpu.VMEM((heads, SEQ, pair), BF)] * 4
        + [pltpu.VMEM((SEQ, feature_width), BF)]
        + [pltpu.VMEM((SEQ, pair), F32)] * 2
        + [
            pltpu.VMEM((pair, SEQ), F32),
            pltpu.VMEM((SEQ, pair), F32),
            pltpu.VMEM((heads, SEQ, pair), BF),
            pltpu.VMEM((heads, SEQ, pair), BF),
            pltpu.VMEM((SEQ, width), BF),
            pltpu.VMEM((feature_width, width), F32),
            pltpu.VMEM((small_rows, feature_width // 2), F32),
            pltpu.VMEM((feature_width, width), BF),
            pltpu.SemaphoreType.DMA((4 + 4 * heads,)),
        ],
        compiler_params=params(42),
        name="attention_back",
    )


def hidden_kernel(sides, first_call, *refs):
    place_ref, count = refs[0], len(sides)
    piece_refs, (up_ref, up_bias_ref, down_ref, vectors_ref) = refs[1 : count + 1], refs[count + 1 : count + 5]
    before_refs = [None, None] if first_call else refs[count + 5 : count + 7]
    normed_ref, turned_ref, curve_ref, grad_ref, active_ref, bias_grad_ref, cot_sum_ref = refs[-7:]
    cot = jnp.concatenate([ref[0, 1] for ref in piece_refs], axis=0)
    unit = standardize(jnp.concatenate([ref[0, 0] for ref in piece_refs], axis=0).astype(F32))
    normed = (unit * vectors_ref[2:3, :] + vectors_ref[3:4, :]).astype(BF)
    normed_ref[...] = normed
    turned_ref[...] = normed.T
    hidden = dot(normed, up_ref[...]) + up_bias_ref[...]
    upstream = dot_nt(cot, down_ref[...])
    below, density = gelu_parts(hidden)
    active = (hidden * below).astype(BF)
    hidden_grad = (upstream * (below + hidden * density)).astype(BF)
    grad_ref[...] = hidden_grad
    curve_ref[...] = upstream * density * (2.0 - hidden * hidden)
    size = active.shape[0] // count
    for number, side in enumerate(sides):
        rows = pl.ds(pl.multiple_of(jnp.bitwise_xor(place_ref[2], side) * size, size), size)
        active_ref[rows, :] = active[number * size : (number + 1) * size]

    @pl.when(pl.program_id(0) == 0)
    def _():
        for before, target in zip(before_refs, (bias_grad_ref, cot_sum_ref)):
            target[...] = jnp.zeros_like(target) if first_call else before[...]

    bias_grad_ref[...] += jnp.sum(hidden_grad.astype(F32), axis=0, keepdims=True)
    cot_sum_ref[...] += jnp.sum(cot.astype(F32), axis=0, keepdims=True)


def hidden_units(places, pieces, sides, first, distances, count, up_part, up_bias_part, down_part, vectors, before):
    arrays = [array for array, _ in pieces]
    feature_width, part_width = arrays[0].shape[3], up_bias_part.shape[1]
    tok_count = sum(array.shape[2] for array in arrays)

    def fixed(*shape):
        return pl.BlockSpec(shape, lambda i, place_ref: (0,) * len(shape))

    def piece(array, slot_of):
        return pl.BlockSpec((1,) + array.shape[1:], lambda i, place_ref: (slot_of(i), 0, 0, 0))

    def block_of(i, place_ref):
        distance = distances[0]
        for number in range(1, len(distances)):
            distance = jnp.where(i == number, distances[number], distance)
        return (jnp.bitwise_xor(place_ref[1], distance), 0)

    units = pl.BlockSpec((tok_count, part_width), lambda i, place_ref: (first + i, 0))
    sums = [fixed(1, part_width), fixed(1, feature_width)]
    inputs = [places, *arrays, far(up_part), up_bias_part, far(down_part), vectors]
    aliases = {}
    if before:
        aliases = {len(inputs) + 2 + k: k for k in range(5)}
        inputs += list(before[5:]) + [far(array) for array in before[:5]]

    def body(*refs):
        spare = 5 if before else 0
        kept = len(refs) - 7 - spare
        hidden_kernel(sides, before is None, *refs[:kept], *refs[kept + spare :])

    return pl.pallas_call(
        body,
        grid_spec=pltpu.PrefetchScalarGridSpec(
            num_scalar_prefetch=1,
            grid=(len(distances),),
            in_specs=[piece(array, slot_of) for array, slot_of in pieces] + [
                pl.BlockSpec((feature_width, part_width), lambda i, place_ref: (0, place_ref[0])),
                fixed(1, part_width),
                pl.BlockSpec((part_width, feature_width), lambda i, place_ref: (place_ref[0], 0)),
                fixed(8, feature_width),
            ] + (sums + [ANY] * 5 if before else []),
            out_specs=[
                pl.BlockSpec((tok_count, feature_width), lambda i, place_ref: (first + i, 0)),
                pl.BlockSpec((feature_width, tok_count), lambda i, place_ref: (0, first + i)),
                units, units, pl.BlockSpec((tok_count, part_width), block_of),
            ] + sums,
        ),
        out_shape=[
            pltpu.HBM((count, feature_width), BF),
            pltpu.HBM((feature_width, count), BF),
            pltpu.HBM((count, part_width), F32),
            pltpu.HBM((count, part_width), BF),
            pltpu.HBM((count, part_width), BF),
            shaped((1, part_width), F32),
            shaped((1, feature_width), F32),
        ],
        input_output_aliases=aliases,
        compiler_params=params(30),
        name="hidden_units",
        cost_estimate=LIGHT,
    )(*inputs)


def curvature_kernel(
    probes, steps, place_ref, dirs_in, local_ref, up_bias_ref, normed_in, turned_in, curve_in, grad_in,
    curvature_out, score_ref,
    curvature_ref, dirs_ref, normed_ref, turned_ref, curve_ref, score_s, spare_s, weighted_s, sems,
):
    feature_width, width = dirs_ref.shape
    part_width = width // probes
    half = part_width // 2
    size = normed_ref.shape[0] // steps

    def moves(step):
        rows = slice(step * size, (step + 1) * size)
        return [
            pltpu.make_async_copy(source.at[rows, :], target, sems.at[3 * step + k])
            for k, (source, target) in enumerate((
                (normed_in, normed_ref.at[rows, :]),
                (curve_in, curve_ref.at[rows, :]),
                (grad_in, weighted_s.at[rows, width:]),
            ))
        ]

    begin = pltpu.make_async_copy(dirs_in, dirs_ref, sems.at[3 * steps])
    last = pltpu.make_async_copy(turned_in, turned_ref, sems.at[3 * steps + 1])
    begin.start()
    for step in range(steps):
        for copy in moves(step):
            copy.start()
    last.start()
    score_s[...] = jnp.zeros_like(score_s)
    begin.wait()
    for step in range(steps):
        for copy in moves(step):
            copy.wait()
        rows = slice(step * size, (step + 1) * size)
        along = dot(normed_ref[rows, :], dirs_ref[...])
        curve, wide = curve_ref[rows, :], weighted_s[rows, width:].astype(F32)
        for k in range(probes):
            columns = slice(k * part_width, (k + 1) * part_width)
            part = along[:, columns]
            weighted_s[rows, columns] = (part * curve).astype(BF)
            score_s[k : k + 1, :] += jnp.sum(part * wide, axis=0, keepdims=True)
    last.wait()
    shape = curvature_ref.shape[:2]
    leaving = []
    for k in range(0, probes, 2):
        columns = slice(k * part_width, (k + 2) * part_width)
        total = dot(turned_ref[...], weighted_s[:, columns])
        curvature_ref[:, :, columns] = total.astype(BF).reshape(shape + (2 * part_width,))
        leaving.append((curvature_ref.at[:, :, columns], curvature_out.at[:, :, columns]))
        pltpu.make_async_copy(*leaving[-1], sems.at[3 * steps + 1 + len(leaving)]).start()
    final = dot(turned_ref[...], weighted_s[:, width:]).astype(BF)
    own = jnp.where(place_ref[0] == 1, final[:, half:], final[:, :half])
    scores = jnp.sum(score_s[...], axis=1, keepdims=True)
    score_ref[...] = jnp.broadcast_to(scores, score_ref.shape)

    spare_s[...] = jnp.zeros_like(spare_s)
    row = 0
    for values in (local_ref[1:2, :], local_ref[2:3, :], up_bias_ref[...]):
        high = values.astype(BF).astype(F32)
        for part in (high, values - high):
            for start in range(0, values.shape[1], HEAD_DIM):
                spare_s[row : row + 1, HEAD_DIM:] = part[:, start : start + HEAD_DIM]
                row += 1
    high = scores.astype(BF).astype(F32)
    for part in (high, scores - high):
        for k in range(probes):
            spare_s[row : row + 1, HEAD_DIM + k : HEAD_DIM + k + 1] = part[k : k + 1, :]
        row += 1
    tail = jnp.concatenate([own[:, LANES:], jnp.zeros((feature_width, HEAD_DIM), BF)], axis=1)
    tail = tail.reshape(shape + (LANES,)) + spare_s[...].astype(BF)[None]
    curvature_ref[:, :, width : width + LANES] = own[:, :LANES].reshape(shape + (LANES,))
    curvature_ref[:, :, width + LANES :] = tail
    leaving.append((curvature_ref.at[:, :, width:], curvature_out.at[:, :, width:]))
    pltpu.make_async_copy(*leaving[-1], sems.at[3 * steps + 1 + len(leaving)]).start()
    for number, move in enumerate(leaving):
        pltpu.make_async_copy(*move, sems.at[3 * steps + 2 + number]).wait()


def curvature_of(blocks, core, probes, units, dirs, local_small, up_bias_grad, after):
    (count, feature_width), part_width = units[0].shape, units[2].shape[1]
    width = probes * part_width
    steps = 4
    local_rows = feature_width // blocks
    out = (blocks, local_rows, width + 2 * LANES)
    return call(
        functools.partial(curvature_kernel, probes, steps),
        inputs=[core[None].astype(jnp.int32), far(dirs), local_small, up_bias_grad] + [far(array) for array in units],
        after=after,
        in_specs=[SMEM, ANY, VMEM, VMEM] + [ANY] * 4,
        out_specs=[ANY, VMEM],
        out_shape=[pltpu.HBM(out, BF), shaped((8, LANES), F32)],
        scratch_shapes=[
            pltpu.VMEM(out, BF),
            pltpu.VMEM((feature_width, width), BF),
            pltpu.VMEM((count, feature_width), BF),
            pltpu.VMEM((feature_width, count), BF),
            pltpu.VMEM((count, part_width), F32),
            pltpu.VMEM((8, part_width), F32),
            pltpu.VMEM((local_rows, LANES), F32),
            pltpu.VMEM((count, width + part_width), BF),
            pltpu.SemaphoreType.DMA((3 * steps + 3 + probes // 2,)),
        ],
        compiler_params=params(52),
        name="curvature",
    )


def weights_kernel(heads, place_ref, active_in, cot_in, attended_in, down_ref, attended_ref, out_ref, *scratch):
    active_s, cot_s, attended_s, joined_s, total_s, sems = scratch
    moves = [(cot_in, cot_s), (active_in, active_s), (attended_in, attended_s)]
    copies = [pltpu.make_async_copy(source, target, sems.at[k]) for k, (source, target) in enumerate(moves)]
    for copy in copies:
        copy.start()
    for copy in copies[:2]:
        copy.wait()
    down_ref[...] = dot_tn(active_s[...], cot_s[...])
    copies[2].wait()
    block = attended_ref.shape[0]
    for number in range(cot_s.shape[0] // block):
        rows = slice(number * block, (number + 1) * block)
        values = [attended_s[head, rows, :].astype(F32) for head in range(heads)]
        joined_s[rows, :] = heads_joined(values).astype(BF)
    own = pl.ds(pl.multiple_of(place_ref[0] * block, block), block)
    attended_ref[...] = joined_s[own, :][:, : attended_ref.shape[1]]
    total_s[...] = dot_tn(joined_s[...], cot_s[...])
    local_rows = out_ref.shape[0]
    rows = pl.ds(pl.multiple_of(place_ref[3], local_rows), local_rows)
    out_ref[...] = jnp.where(place_ref[2] == 1, total_s[rows, :], 0.0).astype(BF)


def weights_back(heads, blocks, numbers, active, cot, attended, after):
    (count, feature_width), part_width, pair = cot.shape, active.shape[1], 2 * HEAD_DIM
    value_tiles = -(-heads // 2) * pair
    return call(
        functools.partial(weights_kernel, heads),
        inputs=[numbers, far(active), far(cot), far(attended)],
        after=after,
        in_specs=[SMEM, ANY, ANY, ANY],
        out_specs=[VMEM] * 3,
        out_shape=[
            shaped((part_width, feature_width), F32),
            shaped((count // blocks, heads * HEAD_DIM), BF),
            shaped((feature_width // blocks, feature_width), BF),
        ],
        scratch_shapes=[
            pltpu.VMEM(active.shape, BF),
            pltpu.VMEM(cot.shape, BF),
            pltpu.VMEM(attended.shape, BF),
            pltpu.VMEM((count, value_tiles), BF),
            pltpu.VMEM((value_tiles, feature_width), F32),
            pltpu.SemaphoreType.DMA((3,)),
        ],
        compiler_params=params(32),
        name="weights_back",
    )


def unpack_kernel(got_in, curvature_out, got_s, curvature_s, sems):
    blocks, _, width = got_s.shape
    probes = curvature_s.shape[0]
    part_width = width // probes

    def arrive(k):
        columns = slice(k * part_width, (k + 1) * part_width)
        return pltpu.make_async_copy(got_in.at[:, :, columns], got_s.at[:, :, columns], sems.at[k])

    def leave(k):
        return pltpu.make_async_copy(curvature_s.at[k], curvature_out.at[k], sems.at[probes + k])

    for k in range(probes):
        arrive(k).start()
    for k in range(probes):
        arrive(k).wait()
        for block in range(blocks):
            part = got_s[block, :, k * part_width : (k + 1) * part_width]
            curvature_s[k, :, block * part_width : (block + 1) * part_width] = part.astype(F32)
        leave(k).start()
    for k in range(probes):
        leave(k).wait()


def unpack(got, probes, part_width, after):
    blocks, local_rows, _ = got.shape
    out = (probes, local_rows, blocks * part_width)
    return call(
        unpack_kernel,
        inputs=[far(got)],
        after=after,
        in_specs=[ANY],
        out_specs=ANY,
        out_shape=pltpu.HBM(out, F32),
        scratch_shapes=[
            pltpu.VMEM((blocks, local_rows, probes * part_width), BF),
            pltpu.VMEM(out, F32),
            pltpu.SemaphoreType.DMA((2 * probes,)),
        ],
        compiler_params=params(24),
        name="unpack",
    )


def peel_kernel(probes, got_ref, up_ref, gain_ref, shift_ref, up_bias_ref, score_ref):
    blocks, _, share = got_ref.shape
    part_width = up_bias_ref.shape[0] // blocks
    tails = []
    for block in range(blocks):
        up_ref[:, block * share : (block + 1) * share] = got_ref[block]
        tails.append(got_ref[block, :, share - LANES :].astype(F32))
    total = tails[0]
    for tail in tails[1:]:
        total = total + tail

    def vector(rows, first, length):
        count = length // HEAD_DIM
        parts = [
            rows[first + k : first + k + 1, HEAD_DIM:] + rows[first + count + k : first + count + k + 1, HEAD_DIM:]
            for k in range(count)
        ]
        return jnp.concatenate(parts, axis=1)

    length = gain_ref.shape[0]
    step = 2 * length // HEAD_DIM
    gain_ref[...] = vector(total, 0, length).reshape(gain_ref.shape)
    shift_ref[...] = vector(total, step, length).reshape(shift_ref.shape)
    biases = [vector(tail, 2 * step, part_width) for tail in tails]
    up_bias_ref[...] = jnp.concatenate(biases, axis=1).reshape(up_bias_ref.shape)
    row = 2 * step + 2 * part_width // HEAD_DIM
    scores = total[row : row + 1, HEAD_DIM : HEAD_DIM + probes] + total[row + 1 : row + 2, HEAD_DIM : HEAD_DIM + probes]
    score_ref[...] = scores.reshape(score_ref.shape)


def peel(got, probes, part_width, after):
    blocks, local_rows, width = got.shape
    share = width - probes * part_width
    feature_width = blocks * local_rows
    vector = shaped((feature_width,), F32)
    return call(
        functools.partial(peel_kernel, probes),
        inputs=[got],
        after=after,
        grid=(1,),
        in_specs=[pl.BlockSpec((blocks, local_rows, share), lambda i: (0, 0, width // share - 1))],
        out_specs=[
            whole(local_rows, blocks * share), whole(feature_width), whole(feature_width),
            whole(blocks * part_width), whole(probes),
        ],
        out_shape=[
            shaped((local_rows, blocks * share), BF),
            vector, vector, shaped((blocks * part_width,), F32), shaped((probes,), F32),
        ],
        compiler_params=params(BIG),
        name="peel",
    )


def spread_kernel(blocks, half, place_ref, mine_ref, got_ref, out_ref):
    odd = place_ref[0] == 1
    stride = mine_ref.shape[1] // blocks
    for block in range(blocks):
        here = slice(block * stride, block * stride + half)
        mine, got = mine_ref[:, here], got_ref[:, here]
        both = jnp.concatenate([jnp.where(odd, got, mine), jnp.where(odd, mine, got)], axis=1)
        out_ref[:, block * 2 * half : (block + 1) * 2 * half] = both.astype(F32)


def spread(core, mine, got, blocks, half, after):
    return call(
        functools.partial(spread_kernel, blocks, half),
        inputs=[core[None].astype(jnp.int32), mine, got],
        after=after,
        in_specs=[SMEM, VMEM, VMEM],
        out_specs=VMEM,
        out_shape=shaped((mine.shape[0], blocks * 2 * half), F32),
        compiler_params=params(12),
        name="spread",
    )


def merge_kernel(feature_width, half, few, place_ref, mine_ref, got_ref, merged_ref):
    odd = place_ref[0] == 1
    third = mine_ref.shape[1] - feature_width

    def ordered(rows, columns):
        mine, got = mine_ref[rows, columns], got_ref[rows, columns]
        return jnp.concatenate([jnp.where(odd, got, mine), jnp.where(odd, mine, got)], axis=1)

    main = slice(0, half + few)
    total = mine_ref[main, :feature_width].astype(F32) + got_ref[main, :feature_width].astype(F32)
    merged_ref[...] = jnp.zeros_like(merged_ref)
    merged_ref[main, :feature_width] = total.astype(BF)
    merged_ref[main, feature_width:] = ordered(main, slice(feature_width, feature_width + third))
    rows = slice(half + few, half + 2 * few)
    merged_ref[rows, : 4 * third] = ordered(rows, slice(0, 2 * third))
    first, width = half + 2 * few, feature_width // 2
    put_small(merged_ref, first, get_small(mine_ref, first, width) + get_small(got_ref, first, width))


def merge(core, mine, got, feature_width, half, few):
    count, width = mine.shape
    return call(
        functools.partial(merge_kernel, feature_width, half, few),
        inputs=[core[None].astype(jnp.int32), mine, got],
        in_specs=[SMEM, VMEM, VMEM],
        out_specs=VMEM,
        out_shape=shaped((count, 2 * width - feature_width), BF),
        compiler_params=params(12),
        name="merge",
    )


def finish_kernel(
    few, place_ref, mine_ref, got_ref, tokens_ref, base_ref, rest_ref, vectors_ref, out_weight_ref,
    final_ref, small_ref,
):
    tok_count, feature_width = tokens_ref.shape
    half = tok_count // 2
    third = (mine_ref.shape[1] - feature_width) // 2
    upper = place_ref[1] == 1
    own = pl.ds(pl.multiple_of(place_ref[0] * half, half), half)

    def ordered(rows, columns):
        mine, got = mine_ref[rows, columns], got_ref[rows, columns]
        return jnp.where(upper, got, mine), jnp.where(upper, mine, got)

    attended = jnp.concatenate(ordered(slice(0, half), slice(feature_width, None)), axis=1)
    layer_out = base_ref[own, :] + dot(attended, out_weight_ref[...])
    main = slice(0, half + few)
    total = mine_ref[main, :feature_width].astype(F32) + got_ref[main, :feature_width].astype(F32)
    centred, factor = spread_of(tokens_ref[own, :].astype(F32))
    term = norm_input_term(total[:half], vectors_ref[0:1, :], centred * factor, factor)
    final_ref[:half, :feature_width] = layer_out.astype(BF)
    final_ref[:half, feature_width:] = (rest_ref[own, :] + term).astype(BF)
    parts = []
    firsts = ordered(slice(half, half + few), slice(feature_width, None))
    others = ordered(slice(half + few, half + 2 * few), slice(0, 4 * third))
    for first, other in zip(firsts, others):
        for core in range(2):
            parts += [first[:, core * third : (core + 1) * third], other[:, 2 * core * third : 2 * (core + 1) * third]]
    grad_qkv = jnp.concatenate(parts, axis=1)
    final_ref[half : half + few, :feature_width] = total[half:].astype(BF)
    final_ref[half : half + few, feature_width:] = grad_qkv[:, :feature_width]
    final_ref[half + few :, :] = grad_qkv[:, feature_width:]
    first, width = half + 2 * few, feature_width // 2
    small_ref[...] = get_small(mine_ref, first, width) + get_small(got_ref, first, width)


def finish(places, mine, got, tokens, base, rest, vectors, out_weight, few):
    tok_count, feature_width = tokens.shape
    half = tok_count // 2
    return call(
        functools.partial(finish_kernel, few),
        inputs=[places, mine, got, tokens, far(base), far(rest), vectors, far(out_weight)],
        in_specs=[SMEM] + [VMEM] * 7,
        out_specs=[VMEM] * 2,
        out_shape=[
            shaped((half + 2 * few, 2 * feature_width), BF),
            shaped((mine.shape[0] - half - 2 * few, feature_width // 2), F32),
        ],
        compiler_params=params(20),
        name="finish",
    )


def join_kernel(
    few, mixed_width, place_ref, mine_ref, got_ref, small_ref, cot_ref,
    layer_out_ref, input_grad_ref, out_ref, qkv_ref, gain_ref, shift_ref, qkv_bias_ref, out_bias_ref, down_bias_ref,
):
    half = layer_out_ref.shape[0] // 2
    feature_width = layer_out_ref.shape[1]
    odd = place_ref[0] == 1
    mine, got = mine_ref[...], got_ref[...]
    for core, side in enumerate((jnp.where(odd, got, mine), jnp.where(odd, mine, got))):
        rows = slice(core * half, (core + 1) * half)
        layer_out_ref[rows, :] = side[:half, :feature_width]
        input_grad_ref[rows, :] = side[:half, feature_width:]
        rows = slice(core * few, (core + 1) * few)
        out_ref[rows, :] = side[half : half + few, :feature_width].astype(F32)
        qkv_ref[rows, :feature_width] = side[half : half + few, feature_width:].astype(F32)
        qkv_ref[rows, feature_width:] = side[half + few :, :].astype(F32)
    small = small_ref[...]

    def rows_of(first, total):
        return jnp.concatenate([small[first : first + 1, :], small[first + 1 : first + 2, :]], axis=1)[:, :total]

    gain_ref[...] = rows_of(0, feature_width).reshape(gain_ref.shape)
    shift_ref[...] = rows_of(2, feature_width).reshape(shift_ref.shape)
    groups = qkv_bias_ref.shape[0] // mixed_width
    bias = [rows_of(4 + 2 * number, mixed_width) for number in range(groups)]
    qkv_bias_ref[...] = jnp.concatenate(bias, axis=1).reshape(qkv_bias_ref.shape)
    for ref in (out_bias_ref, down_bias_ref):
        ref[...] = cot_ref[...].reshape(ref.shape)


def join(core, mine, got, small, cot, tok_count, few, mixed_width):
    feature_width = cot.shape[1]
    vector = shaped((feature_width,), F32)
    return call(
        functools.partial(join_kernel, few, mixed_width),
        inputs=[core[None].astype(jnp.int32), mine, got, small, cot],
        in_specs=[SMEM] + [VMEM] * 4,
        out_specs=[VMEM] * 9,
        out_shape=[shaped((tok_count, feature_width), BF)] * 2
        + [shaped((2 * few, feature_width), F32), shaped((2 * few, 3 * feature_width), F32), vector, vector]
        + [shaped((4 * mixed_width,), F32), vector, vector],
        compiler_params=params(16),
        name="join",
    )


def on_device(
    tokens,
    segment_ids,
    qkv_weight,
    qkv_bias,
    out_weight,
    out_bias,
    up_weight,
    up_bias,
    down_weight,
    down_bias,
    norm1_gain,
    norm1_bias,
    norm2_gain,
    norm2_bias,
    probe_dirs,
    out_grad,
):
    tok_count, feature_width = tokens.shape
    hidden_width = up_weight.shape[1]
    probe_count, local_rows = probe_dirs.shape[:2]
    groups = lax.axis_size("ex")
    probe_groups = lax.axis_size("probe")
    blocks = SEQ // tok_count
    rows = groups // blocks
    ex_place = lax.axis_index("ex")
    place = ex_place % blocks
    row_place = ex_place // blocks
    probe_place = lax.axis_index("probe")
    core, upper = probe_place % 2, probe_place // 2
    heads = HEADS // probe_groups
    head_width = heads * HEAD_DIM
    part_width = hidden_width // blocks
    fine = part_width // rows
    row_groups = None
    if rows > 1:
        row_groups = [[r * blocks + b for b in range(blocks)] for r in range(rows)]
    across = [[r * blocks + b for r in range(rows)] for b in range(blocks)]

    def swap(value, distance):
        return lax.ppermute(value, "ex", [(i, i ^ distance) for i in range(groups)])

    def swap_probe(value, distance):
        return lax.ppermute(value, "probe", [(i, i ^ distance) for i in range(probe_groups)])

    def over_rows(value):
        if rows > 1:
            return lax.psum_scatter(value, "ex", axis_index_groups=across, scatter_dimension=0, tiled=True)
        return value

    def my_part(value, axis):
        shape = value.shape
        split = shape[:axis] + (rows, blocks, fine) + shape[axis + 1 :]
        part = lax.dynamic_index_in_dim(value.reshape(split), place, axis + 1, keepdims=False)
        return part.reshape(shape[:axis] + (part_width,) + shape[axis + 1 :])

    mine, share = slices_of(probe_place, probe_groups, tokens, out_grad)
    aside = swap(mine, 1)
    near, diagonal, distant, farthest = [swap(share, distance) for distance in (2, 3, 4, 6)]

    segments = segment_ids
    if rows > 1:
        segments = lax.dynamic_slice_in_dim(segment_ids, row_place * SEQ, SEQ)
    vectors = vectors_of(
        probe_groups, blocks, norm1_gain, norm1_bias, norm2_gain, norm2_bias, out_bias, down_bias, qkv_bias, segments
    )
    base, rest, local_small = local_part(tokens, out_grad, up_weight, up_bias, down_weight, vectors)

    second, third = stack([near, diagonal, distant, farthest], [(0, 1), (2, 3)], [local_small])
    third_aside, third_over = swap(third, 1), swap_probe(third, 2)
    (quarters,) = stack([mine, aside, third, third_over], [(0, 1, 2, 3)], [])
    swapped = swap_probe(quarters, 1)
    up_bias_part = my_part(up_bias, 0).astype(F32)[None]
    up_part, down_part = up_weight, down_weight
    if rows > 1:
        up_part, down_part = my_part(up_weight, 1), my_part(down_weight, 0)

    def pieces_of(array, other, slots, distances):
        return [
            ([(side, slot) for side in (array, other) for slot in pair], ((0, 2, 1, 3), (distance,)))
            for pair, distance in zip(slots, distances)
        ]

    pieces = pieces_of(quarters, swapped, ((0, 1), (2, 3), (4, 6), (5, 7)), (0, 1, 4, 6))
    slots = [lambda i: jnp.where(i < 2, 2 * i, i + 2), lambda i: jnp.where(i < 2, 2 * i + 1, i + 4)]
    refs = [(array, slot_of) for array in (quarters, swapped) for slot_of in slots]
    unit_place = place if rows == 1 else place * 0
    places = jnp.stack([unit_place, place, probe_place]).astype(jnp.int32)
    fixed = (SEQ, up_part, up_bias_part, down_part, vectors)
    units = hidden_units(places, refs, (0, 2, 1, 3), 0, (0, 1, 4, 6), *fixed, None)
    second_over, third_across = swap_probe(second, 2), swap_probe(third_aside, 2)

    dirs = tie(pack(probe_dirs, blocks, rows, [local_small]), [third_aside, third_over, aside])
    dirs = lax.all_to_all(dirs, "ex", 0, 0, axis_index_groups=row_groups, tiled=True)
    dirs = dirs.reshape(blocks * local_rows, probe_count * part_width)
    if rows > 1:
        dirs = lax.all_gather(dirs, "ex", axis_index_groups=across, tiled=True)

    (near_quarters,) = stack([second, second_over], [(0, 1)], [units[5]])
    (far_quarters,) = stack([third_aside, third_across], [(0, 1)], [near_quarters])
    near_swapped = tie(swap_probe(near_quarters, 1), [far_quarters])
    last = ((near_quarters, near_swapped, (2, 3)), (far_quarters, swap_probe(far_quarters, 1), (5, 7)))
    for number, (array, swapped, distances) in enumerate(last):
        pieces += pieces_of(array, swapped, ((0, 2), (1, 3)), distances)
        refs = [(side, lambda i, k=k: i + 2 * k) for side in (array, swapped) for k in range(2)]
        units = hidden_units(places, refs, (0, 2, 1, 3), 4 + 2 * number, distances, *fixed, units)
    *units, active, grad_up_bias, cot_sum = units

    block_rows = feature_width // blocks
    offset = place * block_rows - probe_place * head_width
    holds = (offset >= 0) & (offset < head_width)
    numbers = jnp.stack([place, probe_place, holds, jnp.where(holds, offset, 0)]).astype(jnp.int32)
    *parts, cot, attended = attention(heads, blocks, numbers, pieces, tokens, qkv_weight, vectors, out_weight, [cot_sum])

    part, scores = curvature_of(
        blocks, core, probe_count, units, dirs, local_small, grad_up_bias, [far(attended)]
    )
    part = over_rows(part.reshape(feature_width, -1)).reshape(blocks, local_rows, -1)
    got = lax.all_to_all(part, "ex", 0, 0, axis_index_groups=row_groups, tiled=True)

    grad_down, attended, grad_out = weights_back(heads, blocks, numbers, active, cot, attended, [scores])
    parts += [attended, grad_out]
    keep, send = attention_back(heads, blocks, numbers, parts, qkv_weight, vectors, [scores])
    half, few = tok_count // 2, block_rows // 2
    merged = merge(core, keep, swap_probe(send, 1), feature_width, half, few)
    final, small = finish(
        jnp.stack([core, upper]).astype(jnp.int32), merged, swap_probe(merged, 2), tokens, base, rest, vectors,
        out_weight, few,
    )
    (
        layer_out, input_grad, grad_out_weight, grad_qkv_weight,
        grad_gain_one, grad_shift_one, grad_qkv_bias, grad_out_bias, grad_down_bias,
    ) = join(core, final, swap_probe(final, 1), small, cot_sum, tok_count, few, 3 * head_width)

    if rows == 1:
        up_half, grad_gain_two, grad_shift_two, grad_up_bias, scores = peel(
            got, probe_count, part_width, [layer_out]
        )
        other_half = swap_probe(up_half, 1)
        curvature = unpack(got, probe_count, part_width, [far(up_half)])
        scores = scores[:, None]
        grad_up_weight = spread(core, up_half, other_half, blocks, part_width // 2, [])
    else:
        start = probe_count * part_width
        units = got[:, :, :start].reshape(blocks, local_rows, probe_count, rows, fine)
        curvature = units.transpose(2, 1, 3, 0, 4).reshape(probe_count, local_rows, hidden_width)
        curvature = curvature.astype(F32)
        up_half = got[:, :, start : start + part_width // 2]
        both = lax.all_gather(up_half, "probe", axis_index_groups=[[0, 1], [2, 3]])
        both = both.transpose(2, 1, 0, 3).reshape(local_rows, blocks, rows, fine)
        grad_up_weight = both.transpose(0, 2, 1, 3).reshape(local_rows, hidden_width).astype(F32)
        grad_down = over_rows(grad_down)

        def over_groups(value):
            value = lax.all_gather(value, "ex", axis_index_groups=row_groups, tiled=True)
            return lax.dynamic_slice_in_dim(over_rows(value), place * local_rows, local_rows, 0)

        grad_qkv_weight, grad_out_weight = over_groups(grad_qkv_weight), over_groups(grad_out_weight)
        grad_gain_one, grad_shift_one, grad_qkv_bias, grad_out_bias, grad_up_bias = lax.psum(
            (grad_gain_one, grad_shift_one, grad_qkv_bias, grad_out_bias, grad_up_bias[0]),
            "ex",
            axis_index_groups=across,
        )
        grad_down_bias = grad_out_bias
        grad_up_bias = lax.all_gather(grad_up_bias, "ex", axis_index_groups=row_groups)
        grad_up_bias = grad_up_bias.reshape(blocks, rows, fine).transpose(1, 0, 2).reshape(-1)
        grad_gain_two, grad_shift_two = lax.psum((local_small[1], local_small[2]), "ex")
        scores = lax.psum(scores[:probe_count, :1], "ex", axis_index_groups=row_groups)
        scores = lax.all_gather(scores, "ex", axis_index_groups=across, axis=1, tiled=True)
    return (
        layer_out,
        input_grad,
        grad_qkv_weight,
        grad_qkv_bias,
        grad_out_weight,
        grad_out_bias,
        grad_up_weight,
        grad_up_bias,
        grad_down,
        grad_down_bias,
        grad_gain_one,
        grad_shift_one,
        grad_gain_two,
        grad_shift_two,
        curvature,
        scores,
    )


def solution(mesh):
    in_specs = (
        P("ex", None),
        P(),
        P(),
        P(),
        P(),
        P(),
        P(),
        P(),
        P(),
        P(),
        P(),
        P(),
        P(),
        P(),
        P("probe", "ex", None),
        P("ex", None),
    )
    out_specs = (
        P("ex", None),
        P("ex", None),
        P("ex", None),
        P(),
        P("ex", None),
        P(),
        P("ex", None),
        P(),
        P("ex", None),
        P(),
        P(),
        P(),
        P(),
        P(),
        P("probe", "ex", None),
        P("probe", None),
    )
    return jax.shard_map(
        on_device, mesh=mesh, in_specs=in_specs, out_specs=out_specs, check_vma=False
    )
```

```python
import functools

import jax
import jax.numpy as jnp
import numpy as np
from jax import lax
from jax.experimental import pallas as pl
from jax.experimental.pallas import tpu as pltpu
from jax.sharding import PartitionSpec as P

HEADS = 12
HEAD_DIM = 64
ROT = 16
SEQ = 2048

BF = jnp.bfloat16
F32 = jnp.float32
eps_norm = 1e-05
masked_score = -1e30
half_root = 0.7071067811865476
gauss_peak = 0.3989422804014327
MB = 1024 * 1024
LANES = 128
LIGHT = pl.CostEstimate(flops=1000, bytes_accessed=1000, transcendentals=0)
BIG = 58


def dot(a, b):
    return jnp.dot(a, b, preferred_element_type=F32)


def dot_nt(a, b):
    return lax.dot_general(a, b, (((1,), (1,)), ((), ())), preferred_element_type=F32)


def dot_tn(a, b):
    return lax.dot_general(a, b, (((0,), (0,)), ((), ())), preferred_element_type=F32)


def spread_of(features):
    center = jnp.mean(features, axis=-1, keepdims=True)
    centred = features - center
    spread = jnp.mean(centred * centred, axis=-1, keepdims=True)
    return centred, lax.rsqrt(spread + eps_norm)


def standardize(features):
    centred, factor = spread_of(features)
    return centred * factor


def norm_input_term(grad, gain_row, unit, factor):
    unit_grad = grad * gain_row
    inner = unit_grad - jnp.mean(unit_grad, -1, keepdims=True)
    return (inner - unit * jnp.mean(unit_grad * unit, -1, keepdims=True)) * factor


def gelu_parts(pre_act):
    below = 0.5 + 0.5 * lax.erf(pre_act * half_root)
    density = gauss_peak * jnp.exp(-0.5 * pre_act * pre_act)
    return below, density


def rotary_tables(count):
    steps = np.arange(ROT // 2, dtype=np.float32) * np.float32(2.0 / ROT)
    inverse = np.power(np.float32(10000.0), -steps).astype(np.float32)
    angles = np.arange(count, dtype=np.float32)[:, None] * inverse[None, :]
    angles = np.concatenate([angles, angles], axis=1)
    cosine = np.ones((count, HEAD_DIM), np.float32)
    sine = np.zeros((count, HEAD_DIM), np.float32)
    cosine[:, :ROT], sine[:, :ROT] = np.cos(angles), np.sin(angles)
    return np.concatenate([cosine, cosine], axis=1), np.concatenate([sine, sine], axis=1)


def params(limit_mb, **more):
    return pltpu.CompilerParams(vmem_limit_bytes=limit_mb * MB, **more)


def shaped(shape, dtype):
    return jax.ShapeDtypeStruct(shape, dtype)


def whole(*shape):
    return pl.BlockSpec(shape, lambda i: (0,) * len(shape))


VMEM = pl.BlockSpec(memory_space=pltpu.VMEM)
SMEM = pl.BlockSpec(memory_space=pltpu.SMEM)
ANY = pl.BlockSpec(memory_space=pl.ANY)


def far(array):
    return pltpu.with_memory_space_constraint(array, pltpu.HBM)


def call(kernel, *, inputs, in_specs, after=(), aliases=None, **more):
    spare = len(after)

    def body(*refs):
        kernel(*refs[: len(inputs)], *refs[len(inputs) + spare :])

    return pl.pallas_call(
        body, in_specs=list(in_specs) + [ANY] * spare, input_output_aliases=aliases or {},
        cost_estimate=LIGHT, **more,
    )(*inputs, *after)


def tie(value, after):
    return call(
        lambda value_ref, out_ref: None,
        inputs=[value],
        after=after,
        aliases={0: 0},
        in_specs=[ANY],
        out_specs=ANY,
        out_shape=shaped(value.shape, value.dtype),
        name="tie",
    )


def pack_kernel(dirs_ref, packed_ref, sems):
    probes = dirs_ref.shape[0]
    blocks, _, width = packed_ref.shape
    part_width = width // probes
    copies = []
    for block in range(blocks):
        for k in range(probes):
            source = dirs_ref.at[k, :, block * part_width : (block + 1) * part_width]
            target = packed_ref.at[block, :, k * part_width : (k + 1) * part_width]
            copies.append(pltpu.make_async_copy(source, target, sems.at[len(copies)]))
    for copy in copies:
        copy.start()
    for copy in copies:
        copy.wait()


def pack(dirs, blocks, rows, after):
    probes, local_rows, hidden_width = dirs.shape
    part_width = hidden_width // blocks
    if rows > 1:
        split = dirs.reshape(probes, local_rows, rows, blocks, part_width // rows)
        return split.transpose(3, 1, 0, 2, 4).reshape(blocks, local_rows, probes * part_width)
    return call(
        pack_kernel,
        inputs=[dirs],
        after=after,
        in_specs=[VMEM],
        out_specs=ANY,
        out_shape=pltpu.HBM((blocks, local_rows, probes * part_width), dirs.dtype),
        scratch_shapes=[pltpu.SemaphoreType.DMA((blocks * probes,))],
        compiler_params=params(8),
        name="pack",
    )


def slices_kernel(place_ref, tokens_ref, grads_ref, both_ref, first_ref, sems):
    count = both_ref.shape[2]
    copies = []
    for part, source in enumerate((tokens_ref, grads_ref)):
        for target, slot, side in ((both_ref, 0, 0), (both_ref, 1, 2), (first_ref, 0, 0)):
            first = jnp.bitwise_xor(place_ref[0], side) * count
            rows = pl.ds(pl.multiple_of(first, count), count)
            copies.append(pltpu.make_async_copy(source.at[rows, :], target.at[slot, part], sems.at[len(copies)]))
    for copy in copies:
        copy.start()
    for copy in copies:
        copy.wait()


def slices_of(probe_place, probe_groups, tokens, grads):
    tok_count, feature_width = tokens.shape
    size = tok_count // probe_groups
    return call(
        slices_kernel,
        inputs=[probe_place[None].astype(jnp.int32), far(tokens), far(grads)],
        in_specs=[SMEM, ANY, ANY],
        out_specs=[VMEM] * 2,
        out_shape=[shaped((count, 2, size, feature_width), BF) for count in (2, 1)],
        scratch_shapes=[pltpu.SemaphoreType.DMA((6,))],
        compiler_params=params(8),
        name="slices",
    )


def stack_kernel(plan, *refs):
    sources, targets = refs[: -len(plan)], refs[-len(plan) :]
    for parts, target in zip(plan, targets):
        number = 0
        for part in parts:
            count = sources[part].shape[0]
            target[number : number + count] = sources[part][...]
            number += count


def stack(sources, plan, after):
    heights = [sum(sources[part].shape[0] for part in parts) for parts in plan]
    return call(
        functools.partial(stack_kernel, plan),
        inputs=sources,
        after=after,
        in_specs=[VMEM] * len(sources),
        out_specs=[VMEM] * len(plan),
        out_shape=[shaped((n,) + sources[parts[0]].shape[1:], BF) for n, parts in zip(heights, plan)],
        compiler_params=params(8),
        name="stack",
    )


def vectors_kernel(groups, blocks, count, *refs):
    sources, vectors_ref, held, sems = refs[:count], refs[count], refs[count + 1 : -1], refs[-1]
    copies = [pltpu.make_async_copy(source, target, sems.at[k]) for k, (source, target) in enumerate(zip(sources, held))]
    for copy in copies:
        copy.start()
    vectors_ref[...] = jnp.zeros_like(vectors_ref)
    for copy in copies:
        copy.wait()
    *plain, first_bias, second_bias, qkv_bias, segments = held
    for number, source in enumerate(plain):
        vectors_ref[number : number + 1, :] = source[...].reshape(1, -1)
    total = first_bias[...].astype(F32) + second_bias[...].astype(F32)
    vectors_ref[len(plain) : len(plain) + 1, :] = total.reshape(1, -1)
    width = qkv_bias.shape[0] // groups
    bias = qkv_bias[...].astype(F32).reshape(1, -1)
    for number in range(groups):
        vectors_ref[8 + number : 9 + number, :width] = bias[:, number * width : (number + 1) * width]
    block = segments.shape[0] // blocks
    for number in range(blocks):
        row = segments[number * block : (number + 1) * block].astype(F32).reshape(1, -1)
        vectors_ref[16 + number : 17 + number, :block] = row


def vectors_of(groups, blocks, *sources):
    return call(
        functools.partial(vectors_kernel, groups, blocks, len(sources)),
        inputs=[far(source) for source in sources],
        in_specs=[ANY] * len(sources),
        out_specs=VMEM,
        out_shape=shaped((16 + blocks, sources[0].shape[0]), F32),
        scratch_shapes=[pltpu.VMEM(source.shape, source.dtype) for source in sources]
        + [pltpu.SemaphoreType.DMA((len(sources),))],
        compiler_params=params(4),
        name="vectors",
    )


def local_kernel(
    tokens_ref, grads_ref, up_ref, up_bias_ref, down_ref, vectors_ref,
    base_ref, rest_ref, small_ref, normed_s, branch_s, back_s,
):
    step = pl.program_id(0)
    gain, shift, out_bias = vectors_ref[2:3, :], vectors_ref[3:4, :], vectors_ref[4:5, :]

    @pl.when(step == 0)
    def _():
        unit = standardize(tokens_ref[...].astype(F32))
        normed_s[...] = (unit * gain + shift).astype(BF)
        branch_s[...] = jnp.zeros_like(branch_s)
        back_s[...] = jnp.zeros_like(back_s)

    bias = up_bias_ref[pl.ds(pl.multiple_of(step * up_ref.shape[1], LANES), up_ref.shape[1])]
    hidden = dot(normed_s[...], up_ref[...]) + bias.astype(F32).reshape(1, -1)
    upstream = dot_nt(grads_ref[...], down_ref[...])
    below, density = gelu_parts(hidden)
    branch_s[...] += dot((hidden * below).astype(BF), down_ref[...])
    hidden_grad = (upstream * (below + hidden * density)).astype(BF)
    back_s[...] += dot_nt(hidden_grad, up_ref[...])

    @pl.when(step == pl.num_programs(0) - 1)
    def _():
        inputs = tokens_ref[...].astype(F32)
        cot = grads_ref[...].astype(F32)
        centred, factor = spread_of(inputs)
        unit = centred * factor
        back = back_s[...]
        base_ref[...] = inputs + branch_s[...] + out_bias
        rest_ref[...] = cot + norm_input_term(back, gain, unit, factor)
        small_ref[...] = jnp.zeros_like(small_ref)
        small_ref[0:1, :] = jnp.sum(cot, axis=0, keepdims=True)
        small_ref[1:2, :] = jnp.sum(back * unit, axis=0, keepdims=True)
        small_ref[2:3, :] = jnp.sum(back, axis=0, keepdims=True)


def local_part(tokens, grads, up_weight, up_bias, down_weight, vectors):
    tok_count, feature_width = tokens.shape
    hidden_width = up_weight.shape[1]
    step = 512
    own = whole(tok_count, feature_width)
    return call(
        local_kernel,
        inputs=[tokens, grads, far(up_weight), up_bias, far(down_weight), vectors],
        grid=(hidden_width // step,),
        in_specs=[
            own, own,
            pl.BlockSpec((feature_width, step), lambda i: (0, i)),
            whole(hidden_width),
            pl.BlockSpec((step, feature_width), lambda i: (i, 0)),
            whole(8, feature_width),
        ],
        out_specs=[own, own, whole(8, feature_width)],
        out_shape=[
            shaped((tok_count, feature_width), F32),
            shaped((tok_count, feature_width), F32),
            shaped((8, feature_width), F32),
        ],
        scratch_shapes=[
            pltpu.VMEM((tok_count, feature_width), BF),
            pltpu.VMEM((tok_count, feature_width), F32),
            pltpu.VMEM((tok_count, feature_width), F32),
        ],
        compiler_params=params(24),
        name="local",
    )


def lanes(rows):
    return lax.broadcasted_iota(jnp.int32, (rows, 2 * HEAD_DIM), 1)


def flipped(tile):
    return pltpu.roll(tile, HEAD_DIM, 1)


def joined(left, right):
    return jnp.where(lanes(left.shape[0]) < HEAD_DIM, left, flipped(right))


def half_turned(tile):
    place_in = lanes(tile.shape[0]) % HEAD_DIM
    low = pltpu.roll(tile, 2 * HEAD_DIM - ROT // 2, 1)
    high = pltpu.roll(tile, ROT // 2, 1)
    return jnp.where(place_in < ROT // 2, -low, jnp.where(place_in < ROT, high, 0.0))


def with_column(tile, lane, column, parts):
    number = lanes(tile.shape[0])
    for k in range(parts):
        part = column.astype(BF).astype(F32) if k + 1 < parts else column
        tile = jnp.where(number == lane + k, part, tile)
        column = column - part
    return tile


def heads_joined(values):
    heads = len(values)
    values = [joined(values[k], values[k + 1]) if k + 1 < heads else values[k] for k in range(0, heads, 2)]
    if heads % 2:
        values[-1] = jnp.where(lanes(values[-1].shape[0]) < HEAD_DIM, values[-1], 0.0)
    return jnp.concatenate(values, axis=1)


def attention_kernel(heads, blocks, block, count, plan, *refs):
    sources, refs = refs[:count], refs[count:]
    (
        place_ref, weight_ref, vectors_ref, out_weight_ref, cos_in, sin_in,
        query_out, key_out, value_out, back_out, unit_out, cot_out, attended_out,
        cos_ref, sin_ref, query_s, key_s, value_s, back_s, unit_s, cot_s,
        window_s, weight_s, bias_s, out_weight_s, attended_s, query_code_s, key_code_s, sems,
        *array_refs,
    ) = refs
    place, probe_place = place_ref[0], place_ref[1]
    feature_width = unit_s.shape[1]
    pair = 2 * HEAD_DIM
    scale = HEAD_DIM ** (-0.5)
    gain, shift = vectors_ref[0:1, :], vectors_ref[1:2, :]
    own_rows = pl.ds(pl.multiple_of(place * block, block), block)
    head_width = heads * HEAD_DIM
    mixed_width = 3 * head_width

    first = probe_place * mixed_width // LANES * LANES
    columns = pl.ds(pl.multiple_of(first, LANES), window_s.shape[1])
    rows = pl.ds(pl.multiple_of(probe_place * head_width, HEAD_DIM), head_width)
    moves = [(weight_ref.at[:, columns], window_s), (out_weight_ref.at[rows, :], out_weight_s.at[:head_width, :])]
    moves += [(cos_in, cos_ref), (sin_in, sin_ref)] + list(zip(sources, array_refs))
    copies = [pltpu.make_async_copy(source, target, sems.at[k]) for k, (source, target) in enumerate(moves)]
    for copy in copies:
        copy.start()
    done = len(copies)

    def leave(number, source, target):
        return pltpu.make_async_copy(source, target, sems.at[done + number])

    def rows_of(number):
        return pl.ds(pl.multiple_of(number * block, block), block)

    def side_rows(distance, side, count):
        own = place_ref[1] % (block // count)
        first = jnp.bitwise_xor(place, distance) * block + jnp.bitwise_xor(own, side) * count
        return pl.ds(pl.multiple_of(first, count), count)

    def together(refs, slot, part):
        return jnp.concatenate([array_refs[ref][base + slot, part] for ref, base in refs], axis=0)

    def arrange(source, target):
        for head in range(heads):
            start = head * 3 * HEAD_DIM
            tile = source[:, start : start + pair]
            target[:, head * pair : (head + 1) * pair] = tile.astype(target.dtype)
        values = [source[:, (3 * head + 2) * HEAD_DIM : (3 * head + 3) * HEAD_DIM] for head in range(heads)]
        values.append(jnp.zeros((source.shape[0], -heads * HEAD_DIM % pair), source.dtype))
        target[:, heads * pair :] = jnp.concatenate(values, axis=1).astype(target.dtype)

    number = lanes(block)
    ones = (number >= HEAD_DIM + 16) & (number < HEAD_DIM + 19)
    coded = (number >= HEAD_DIM) & (number < HEAD_DIM + 16)
    for index in range(blocks):
        segment = jnp.broadcast_to(vectors_ref[16 + index : 17 + index, :block], (pair, block)).T
        segment = segment.astype(jnp.int32)
        match = (number == HEAD_DIM + segment // 8) | (number == HEAD_DIM + 8 + segment % 8)
        here = slice(index * block, (index + 1) * block)
        query_code_s[here, :] = jnp.where(coded & ~match, masked_score, 0.0)
        key_code_s[here, :] = jnp.where(match | ones, 1.0, 0.0)

    out_weight_s[head_width:, :] = jnp.zeros((out_weight_s.shape[0] - head_width, feature_width), BF)
    copies[0].wait()
    odd = probe_place * mixed_width % LANES != 0
    window = window_s[...]
    weight = jnp.where(odd, window[:, HEAD_DIM : HEAD_DIM + mixed_width], window[:, :mixed_width])
    arrange(weight, weight_s)
    bias = vectors_ref[pl.ds(8 + probe_place, 1), :mixed_width]
    arrange(jnp.broadcast_to(bias, (8, mixed_width)), bias_s)
    for copy in copies[1:4]:
        copy.wait()

    def project(sides, refs, slot, distance):
        unit = standardize(together(refs, slot, 0).astype(F32))
        normed = (unit * gain + shift).astype(BF)
        low = unit.astype(BF)
        whole_part = dot(normed, weight_s[...]) + bias_s[:1, :]
        cot = together(refs, slot, 1)
        whole_back = dot_nt(cot, out_weight_s[...])
        count = block // len(sides)
        for number, side in enumerate(sides):
            here = slice(number * count, (number + 1) * count)
            rows = side_rows(distance, side, count)
            unit_s[rows, :] = low[here]
            cot_s[rows, :] = cot[here]
            place_heads(rows, whole_part[here], whole_back[here])

    def place_heads(rows, part, back_part):
        cosine, sine = cos_ref[rows, :], sin_ref[rows, :]
        number = lanes(part.shape[0])
        query_code, key_code = query_code_s[rows, :], key_code_s[rows, :]
        value_code = jnp.where((number >= HEAD_DIM) & (number < HEAD_DIM + 2), 1.0, 0.0)
        first = number < HEAD_DIM
        for head in range(heads):
            plain = part[:, head * pair : (head + 1) * pair]
            both = plain * cosine + half_turned(plain) * sine
            query_s[head, rows, :] = jnp.where(first, both * scale, query_code).astype(BF)
            key_s[head, rows, :] = jnp.where(first, flipped(both), key_code).astype(BF)
            start = heads * pair + head // 2 * pair
            tile = part[:, start : start + pair]
            back_tile = back_part[:, head // 2 * pair : head // 2 * pair + pair]
            if head % 2:
                tile, back_tile = flipped(tile), flipped(back_tile)
            value_s[head, rows, :] = jnp.where(first, tile, value_code).astype(BF)
            back_s[head, rows, :] = jnp.where(first, back_tile, 0.0).astype(BF)

    here = set()
    for sides, distances, refs in plan:
        for number in sorted({ref for ref, _ in refs} - here):
            copies[4 + number].wait()
            here.add(number)
        for slot, distance in enumerate(distances):
            project(sides, refs, slot, distance)
    leaving = [leave(0, key_s, key_out), leave(1, value_s, value_out), leave(2, unit_s, unit_out)]
    leaving.append(leave(3, cot_s, cot_out))
    for copy in leaving:
        copy.start()

    square = (block, block)
    lower = lax.broadcasted_iota(jnp.int32, square, 1) <= lax.broadcasted_iota(jnp.int32, square, 0)

    def head_leaving(head):
        pairs = ((query_s, query_out), (back_s, back_out), (attended_s, attended_out))
        return [leave(4 + 3 * head + k, source.at[head], target.at[head]) for k, (source, target) in enumerate(pairs)]

    def attend(head, carry):
        def scores_of(number):
            start, stop = number * block, (number + 1) * block
            query = query_s[head, start:stop, :]
            near = jnp.where(lower, dot_nt(query, key_s[head, start:stop, :]), masked_score)
            return near, dot_nt(query, key_s[head, :start, :]) if number else None

        ahead = scores_of(0)
        for number in range(blocks):
            start, stop = number * block, (number + 1) * block
            near, far = ahead
            if number + 1 < blocks:
                ahead = scores_of(number + 1)
            top = jnp.max(near, axis=-1, keepdims=True)
            if number:
                top = jnp.maximum(top, jnp.max(far, axis=-1, keepdims=True))
            got = dot(jnp.exp(near - top).astype(BF), value_s[head, start:stop, :])
            if number:
                got = got + dot(jnp.exp(far - top).astype(BF), value_s[head, :start, :])
            total = got[:, HEAD_DIM : HEAD_DIM + 1]
            attended = got / total
            attended_s[head, start:stop, :] = attended.astype(BF)
            back = back_s[head, start:stop, :].astype(F32)
            delta = jnp.sum(attended * back, axis=-1, keepdims=True)
            log_total = top + jnp.log(total)
            query = query_s[head, start:stop, :].astype(F32)
            query_s[head, start:stop, :] = with_column(query, HEAD_DIM + 16, -log_total, 3).astype(BF)
            back_s[head, start:stop, :] = with_column(back, HEAD_DIM, -delta, 2).astype(BF)
        for copy in head_leaving(head):
            copy.start()
        return carry

    lax.fori_loop(0, heads, attend, 0)

    for copy in leaving:
        copy.wait()
    for head in range(heads):
        for copy in head_leaving(head):
            copy.wait()


def attention_back_kernel(
    heads, blocks, place_ref, query_in, key_in, value_in, back_in, unit_in, attended_ref, grad_out_ref, weight_ref,
    vectors_ref, cos_in, sin_in,
    keep_ref, send_ref,
    query_s, key_s, value_s, back_s, unit_ref, cos_ref, sin_ref,
    query_grad_s, key_grad_s, both_s, value_grad_s, mixed_s, total_s, small_s, window_s, sems,
):
    place, probe_place = place_ref[0], place_ref[1]
    block, head_width = attended_ref.shape
    feature_width = unit_ref.shape[1]
    mixed_width = 3 * head_width
    scale = HEAD_DIM ** (-0.5)
    first = probe_place * mixed_width // LANES * LANES
    columns = pl.ds(pl.multiple_of(first, LANES), window_s.shape[1])
    others = [(cos_in, cos_ref), (sin_in, sin_ref), (unit_in, unit_ref), (weight_ref.at[:, columns], window_s)]
    others = [pltpu.make_async_copy(source, target, sems.at[k]) for k, (source, target) in enumerate(others)]

    def arriving(head):
        pairs = ((key_in, key_s), (query_in, query_s), (value_in, value_s), (back_in, back_s))
        return [
            pltpu.make_async_copy(source.at[head], target.at[head], sems.at[4 + len(pairs) * head + k])
            for k, (source, target) in enumerate(pairs)
        ]

    for copy in arriving(0) + others[:2]:
        copy.start()
    for head in range(1, heads):
        for copy in arriving(head):
            copy.start()
    for copy in others[2:]:
        copy.start()
    for copy in others[:2]:
        copy.wait()
    square = (block, block)
    upper = lax.broadcasted_iota(jnp.int32, square, 0) <= lax.broadcasted_iota(jnp.int32, square, 1)

    def through(head, carry):
        for copy in arriving(head):
            copy.wait()
        query_grad_s[...] = jnp.zeros_like(query_grad_s)
        for number in range(blocks):
            start, stop = number * block, (number + 1) * block
            key, value = key_s[head, start:stop, :], value_s[head, start:stop, :]
            key_t = key.T
            key_grad = value_grad = None
            for rows, mask in ((slice(start, stop), upper), (slice(stop, blocks * block), None)):
                if rows.start == rows.stop:
                    continue
                query, back = query_s[head, rows, :], back_s[head, rows, :]
                scores = dot_nt(key, query)
                if mask is not None:
                    scores = jnp.where(mask, scores, masked_score)
                probs = jnp.exp(scores)
                score_grad = (probs * dot_nt(value, back)).astype(BF)
                value_term, key_term = dot(probs.astype(BF), back), dot(score_grad, query)
                value_grad = value_term if value_grad is None else value_grad + value_term
                key_grad = key_term if key_grad is None else key_grad + key_term
                query_grad_s[:, rows] += dot(key_t, score_grad)
            key_grad_s[start:stop, :] = key_grad
            value_grad_s[head, start:stop, :] = value_grad.astype(BF)
        for number in range(blocks):
            rows = slice(number * block, (number + 1) * block)
            both = joined(query_grad_s[:, rows].T * scale, key_grad_s[rows, :])
            both = both * cos_ref[rows, :] - half_turned(both * sin_ref[rows, :])
            both_s[head, rows, :] = both.astype(BF)
        return carry

    lax.fori_loop(0, heads, through, 0)

    for number in range(blocks):
        rows = slice(number * block, (number + 1) * block)
        tiles = []
        for head in range(heads):
            both, value = both_s[head, rows, :].astype(F32), value_grad_s[head, rows, :].astype(F32)
            if head % 2 == 0:
                tiles += [both, value]
            else:
                tiles[-1] = joined(tiles[-1], both)
                tiles.append(joined(flipped(both), value))
        if heads % 2:
            tiles[-1] = jnp.where(lanes(block) < HEAD_DIM, tiles[-1], 0.0)
        mixed_s[rows, :] = jnp.concatenate(tiles, axis=1).astype(BF)

    others[2].wait()
    total_s[...] = dot_tn(unit_ref[...], mixed_s[...])
    sums = jnp.sum(mixed_s[...].astype(F32), axis=0, keepdims=True)
    others[3].wait()
    odd = probe_place * mixed_width % LANES != 0
    window = window_s[...]
    weight = jnp.where(odd, window[:, HEAD_DIM : HEAD_DIM + mixed_width], window[:, :mixed_width])

    own_rows = pl.ds(pl.multiple_of(place * block, block), block)
    mixed_own = mixed_s[own_rows, :][:, :mixed_width]
    normed_back = dot_nt(mixed_own, weight).astype(BF)

    local_rows = grad_out_ref.shape[0]
    first = pl.multiple_of(place * local_rows, local_rows)
    pick = lax.broadcasted_iota(jnp.int32, (local_rows, feature_width), 1) == first + lax.broadcasted_iota(
        jnp.int32, (local_rows, feature_width), 0
    )
    gain, shift = [
        jnp.sum(jnp.where(pick, vectors_ref[k : k + 1, :], 0.0), axis=1, keepdims=True) for k in range(2)
    ]
    grad_qkv = (total_s[pl.ds(first, local_rows), :] * gain + sums * shift).astype(BF)

    wide = weight.astype(F32)
    columns = [
        jnp.sum(wide * total_s[:, :mixed_width], axis=1, keepdims=True),
        jnp.sum(wide * sums[:, :mixed_width], axis=1, keepdims=True),
    ]
    number = lax.broadcasted_iota(jnp.int32, (feature_width, LANES), 1)
    columns = jnp.where(number == 0, columns[0], jnp.where(number == 1, columns[1], 0.0)).T
    piece = feature_width // 2
    small_s[...] = jnp.zeros_like(small_s)
    for k in range(2):
        for part in range(2):
            here = slice(part * piece, (part + 1) * piece)
            small_s[2 * k + part : 2 * k + part + 1, :piece] = columns[k : k + 1, here]
    small_s[pl.ds(4 + 2 * probe_place, 1), :piece] = sums[:, :piece]
    small_s[pl.ds(5 + 2 * probe_place, 1), : mixed_width - piece] = sums[:, piece:mixed_width]
    half, few = block // 2, local_rows // 2
    third = head_width
    odd = probe_place % 2 == 1

    def halves(value):
        low, high = value[: value.shape[0] // 2], value[value.shape[0] // 2 :]
        return jnp.where(odd, high, low), jnp.where(odd, low, high)

    attended, grad_out = attended_ref[...], grad_out_ref[...]
    for number, target in enumerate((keep_ref, send_ref)):
        target[...] = jnp.zeros_like(target)
        target[:half, :feature_width] = halves(normed_back)[number]
        target[:half, feature_width:] = halves(attended)[number]
        target[half : half + few, :feature_width] = halves(grad_out)[number]
        part = halves(grad_qkv)[number]
        target[half : half + few, feature_width:] = part[:, :third]
        target[half + few : half + 2 * few, : 2 * third] = part[:, third : 3 * third]
        put_small(target, half + 2 * few, small_s[...])


def put_small(target, first, small):
    width = small.shape[1]
    high = small.astype(BF)
    target[first:, :width] = high
    target[first:, width : 2 * width] = (small - high.astype(F32)).astype(BF)


def get_small(source, first, width):
    return source[first:, :width].astype(F32) + source[first:, width : 2 * width].astype(F32)


def attention(heads, blocks, numbers, pieces, tokens, qkv_weight, vectors, out_weight, after):
    tok_count, feature_width = tokens.shape
    pair = 2 * HEAD_DIM
    head_width = heads * HEAD_DIM
    value_tiles = -(-heads // 2) * pair
    arrays, plan = [], []
    for refs, (sides, distances) in pieces:
        numbered = []
        for array, base in refs:
            if not any(array is other for other in arrays):
                arrays.append(array)
            numbered.append(([array is other for other in arrays].index(True), base))
        plan.append((sides, distances, numbered))
    cos_table, sin_table = rotary_tables(SEQ)
    per_head = shaped((heads, SEQ, pair), BF)
    window = -(-(3 * head_width) // LANES) * LANES
    return call(
        functools.partial(attention_kernel, heads, blocks, tok_count, len(arrays), plan),
        inputs=arrays + [numbers, far(qkv_weight), vectors, far(out_weight), far(jnp.asarray(cos_table)), far(jnp.asarray(sin_table))],
        after=after,
        in_specs=[ANY] * len(arrays) + [SMEM, ANY, VMEM, ANY, ANY, ANY],
        out_specs=[ANY] * 7,
        out_shape=[pltpu.HBM(per_head.shape, BF)] * 4
        + [pltpu.HBM((SEQ, feature_width), BF)] * 2
        + [pltpu.HBM(per_head.shape, BF)],
        scratch_shapes=[pltpu.VMEM((SEQ, pair), F32)] * 2
        + [pltpu.VMEM((heads, SEQ, pair), BF)] * 4
        + [pltpu.VMEM((SEQ, feature_width), BF)] * 2
        + [
            pltpu.VMEM((feature_width, window), BF),
            pltpu.VMEM((feature_width, heads * pair + value_tiles), BF),
            pltpu.VMEM((8, heads * pair + value_tiles), F32),
            pltpu.VMEM((value_tiles, feature_width), BF),
            pltpu.VMEM((heads, SEQ, pair), BF),
            pltpu.VMEM((SEQ, pair), F32),
            pltpu.VMEM((SEQ, pair), F32),
            pltpu.SemaphoreType.DMA((4 + len(arrays) + 4 + 3 * heads,)),
        ]
        + [pltpu.VMEM(array.shape, array.dtype) for array in arrays],
        compiler_params=params(44),
        name="attention",
    )


def attention_back(heads, blocks, numbers, parts, qkv_weight, vectors, after):
    *_, unit, attended, grad_out = parts
    (tok_count, head_width), (local_rows, feature_width) = attended.shape, grad_out.shape
    pair = 2 * HEAD_DIM
    width = -(-(3 * head_width) // LANES) * LANES
    small_rows = -(-(4 + 2 * HEADS // heads) // 16) * 16
    cos_table, sin_table = rotary_tables(SEQ)
    return call(
        functools.partial(attention_back_kernel, heads, blocks),
        inputs=[numbers, *[far(part) for part in parts[:5]], *parts[5:], far(qkv_weight), vectors, far(jnp.asarray(cos_table)), far(jnp.asarray(sin_table))],
        after=after,
        in_specs=[SMEM] + [ANY] * 5 + [VMEM] * 2 + [ANY, VMEM, ANY, ANY],
        out_specs=[VMEM] * 2,
        out_shape=[
            shaped((tok_count // 2 + local_rows + small_rows, feature_width + head_width), BF),
        ] * 2,
        scratch_shapes=[pltpu.VMEM((heads, SEQ, pair), BF)] * 4
        + [pltpu.VMEM((SEQ, feature_width), BF)]
        + [pltpu.VMEM((SEQ, pair), F32)] * 2
        + [
            pltpu.VMEM((pair, SEQ), F32),
            pltpu.VMEM((SEQ, pair), F32),
            pltpu.VMEM((heads, SEQ, pair), BF),
            pltpu.VMEM((heads, SEQ, pair), BF),
            pltpu.VMEM((SEQ, width), BF),
            pltpu.VMEM((feature_width, width), F32),
            pltpu.VMEM((small_rows, feature_width // 2), F32),
            pltpu.VMEM((feature_width, width), BF),
            pltpu.SemaphoreType.DMA((4 + 4 * heads,)),
        ],
        compiler_params=params(42),
        name="attention_back",
    )


def hidden_kernel(sides, first_call, *refs):
    place_ref, count = refs[0], len(sides)
    piece_refs, (up_ref, up_bias_ref, down_ref, vectors_ref) = refs[1 : count + 1], refs[count + 1 : count + 5]
    before_refs = [None, None] if first_call else refs[count + 5 : count + 7]
    normed_ref, turned_ref, curve_ref, grad_ref, active_ref, bias_grad_ref, cot_sum_ref = refs[-7:]
    cot = jnp.concatenate([ref[0, 1] for ref in piece_refs], axis=0)
    unit = standardize(jnp.concatenate([ref[0, 0] for ref in piece_refs], axis=0).astype(F32))
    normed = (unit * vectors_ref[2:3, :] + vectors_ref[3:4, :]).astype(BF)
    normed_ref[...] = normed
    turned_ref[...] = normed.T
    hidden = dot(normed, up_ref[...]) + up_bias_ref[...]
    upstream = dot_nt(cot, down_ref[...])
    below, density = gelu_parts(hidden)
    active = (hidden * below).astype(BF)
    hidden_grad = (upstream * (below + hidden * density)).astype(BF)
    grad_ref[...] = hidden_grad
    curve_ref[...] = upstream * density * (2.0 - hidden * hidden)
    size = active.shape[0] // count
    for number, side in enumerate(sides):
        rows = pl.ds(pl.multiple_of(jnp.bitwise_xor(place_ref[2], side) * size, size), size)
        active_ref[rows, :] = active[number * size : (number + 1) * size]

    @pl.when(pl.program_id(0) == 0)
    def _():
        for before, target in zip(before_refs, (bias_grad_ref, cot_sum_ref)):
            target[...] = jnp.zeros_like(target) if first_call else before[...]

    bias_grad_ref[...] += jnp.sum(hidden_grad.astype(F32), axis=0, keepdims=True)
    cot_sum_ref[...] += jnp.sum(cot.astype(F32), axis=0, keepdims=True)


def hidden_units(places, pieces, sides, first, distances, count, up_part, up_bias_part, down_part, vectors, before):
    arrays = [array for array, _ in pieces]
    feature_width, part_width = arrays[0].shape[3], up_bias_part.shape[1]
    tok_count = sum(array.shape[2] for array in arrays)

    def fixed(*shape):
        return pl.BlockSpec(shape, lambda i, place_ref: (0,) * len(shape))

    def piece(array, slot_of):
        return pl.BlockSpec((1,) + array.shape[1:], lambda i, place_ref: (slot_of(i), 0, 0, 0))

    def block_of(i, place_ref):
        distance = distances[0]
        for number in range(1, len(distances)):
            distance = jnp.where(i == number, distances[number], distance)
        return (jnp.bitwise_xor(place_ref[1], distance), 0)

    units = pl.BlockSpec((tok_count, part_width), lambda i, place_ref: (first + i, 0))
    sums = [fixed(1, part_width), fixed(1, feature_width)]
    inputs = [places, *arrays, far(up_part), up_bias_part, far(down_part), vectors]
    aliases = {}
    if before:
        aliases = {len(inputs) + 2 + k: k for k in range(5)}
        inputs += list(before[5:]) + [far(array) for array in before[:5]]

    def body(*refs):
        spare = 5 if before else 0
        kept = len(refs) - 7 - spare
        hidden_kernel(sides, before is None, *refs[:kept], *refs[kept + spare :])

    return pl.pallas_call(
        body,
        grid_spec=pltpu.PrefetchScalarGridSpec(
            num_scalar_prefetch=1,
            grid=(len(distances),),
            in_specs=[piece(array, slot_of) for array, slot_of in pieces] + [
                pl.BlockSpec((feature_width, part_width), lambda i, place_ref: (0, place_ref[0])),
                fixed(1, part_width),
                pl.BlockSpec((part_width, feature_width), lambda i, place_ref: (place_ref[0], 0)),
                fixed(8, feature_width),
            ] + (sums + [ANY] * 5 if before else []),
            out_specs=[
                pl.BlockSpec((tok_count, feature_width), lambda i, place_ref: (first + i, 0)),
                pl.BlockSpec((feature_width, tok_count), lambda i, place_ref: (0, first + i)),
                units, units, pl.BlockSpec((tok_count, part_width), block_of),
            ] + sums,
        ),
        out_shape=[
            pltpu.HBM((count, feature_width), BF),
            pltpu.HBM((feature_width, count), BF),
            pltpu.HBM((count, part_width), F32),
            pltpu.HBM((count, part_width), BF),
            pltpu.HBM((count, part_width), BF),
            shaped((1, part_width), F32),
            shaped((1, feature_width), F32),
        ],
        input_output_aliases=aliases,
        compiler_params=params(30),
        name="hidden_units",
        cost_estimate=LIGHT,
    )(*inputs)


def curvature_kernel(
    probes, steps, place_ref, dirs_in, local_ref, up_bias_ref, normed_in, turned_in, curve_in, grad_in,
    curvature_out, score_ref,
    curvature_ref, dirs_ref, normed_ref, turned_ref, curve_ref, score_s, spare_s, weighted_s, sems,
):
    feature_width, width = dirs_ref.shape
    part_width = width // probes
    half = part_width // 2
    size = normed_ref.shape[0] // steps

    def moves(step):
        rows = slice(step * size, (step + 1) * size)
        return [
            pltpu.make_async_copy(source.at[rows, :], target, sems.at[3 * step + k])
            for k, (source, target) in enumerate((
                (normed_in, normed_ref.at[rows, :]),
                (curve_in, curve_ref.at[rows, :]),
                (grad_in, weighted_s.at[rows, width:]),
            ))
        ]

    begin = pltpu.make_async_copy(dirs_in, dirs_ref, sems.at[3 * steps])
    last = pltpu.make_async_copy(turned_in, turned_ref, sems.at[3 * steps + 1])
    begin.start()
    for step in range(steps):
        for copy in moves(step):
            copy.start()
    last.start()
    score_s[...] = jnp.zeros_like(score_s)
    begin.wait()
    for step in range(steps):
        for copy in moves(step):
            copy.wait()
        rows = slice(step * size, (step + 1) * size)
        along = dot(normed_ref[rows, :], dirs_ref[...])
        curve, wide = curve_ref[rows, :], weighted_s[rows, width:].astype(F32)
        for k in range(probes):
            columns = slice(k * part_width, (k + 1) * part_width)
            part = along[:, columns]
            weighted_s[rows, columns] = (part * curve).astype(BF)
            score_s[k : k + 1, :] += jnp.sum(part * wide, axis=0, keepdims=True)
    last.wait()
    shape = curvature_ref.shape[:2]
    leaving = []
    final = dot(turned_ref[...], weighted_s[:, width:]).astype(BF)
    own = jnp.where(place_ref[0] == 1, final[:, half:], final[:, :half])
    scores = jnp.sum(score_s[...], axis=1, keepdims=True)
    score_ref[...] = jnp.broadcast_to(scores, score_ref.shape)

    spare_s[...] = jnp.zeros_like(spare_s)
    row = 0
    for values in (local_ref[1:2, :], local_ref[2:3, :], up_bias_ref[...]):
        high = values.astype(BF).astype(F32)
        for part in (high, values - high):
            for start in range(0, values.shape[1], HEAD_DIM):
                spare_s[row : row + 1, HEAD_DIM:] = part[:, start : start + HEAD_DIM]
                row += 1
    high = scores.astype(BF).astype(F32)
    for part in (high, scores - high):
        for k in range(probes):
            spare_s[row : row + 1, HEAD_DIM + k : HEAD_DIM + k + 1] = part[k : k + 1, :]
        row += 1
    tail = jnp.concatenate([own[:, LANES:], jnp.zeros((feature_width, HEAD_DIM), BF)], axis=1)
    tail = tail.reshape(shape + (LANES,)) + spare_s[...].astype(BF)[None]
    curvature_ref[:, :, width : width + LANES] = own[:, :LANES].reshape(shape + (LANES,))
    curvature_ref[:, :, width + LANES :] = tail
    leaving.append((curvature_ref.at[:, :, width:], curvature_out.at[:, :, width:]))
    pltpu.make_async_copy(*leaving[-1], sems.at[3 * steps + 1 + len(leaving)]).start()
    for k in range(0, probes, 2):
        columns = slice(k * part_width, (k + 2) * part_width)
        total = dot(turned_ref[...], weighted_s[:, columns])
        curvature_ref[:, :, columns] = total.astype(BF).reshape(shape + (2 * part_width,))
        leaving.append((curvature_ref.at[:, :, columns], curvature_out.at[:, :, columns]))
        pltpu.make_async_copy(*leaving[-1], sems.at[3 * steps + 1 + len(leaving)]).start()
    for number, move in enumerate(leaving):
        pltpu.make_async_copy(*move, sems.at[3 * steps + 2 + number]).wait()


def curvature_of(blocks, core, probes, units, dirs, local_small, up_bias_grad, after):
    (count, feature_width), part_width = units[0].shape, units[2].shape[1]
    width = probes * part_width
    steps = 4
    local_rows = feature_width // blocks
    out = (blocks, local_rows, width + 2 * LANES)
    return call(
        functools.partial(curvature_kernel, probes, steps),
        inputs=[core[None].astype(jnp.int32), far(dirs), local_small, up_bias_grad] + [far(array) for array in units],
        after=after,
        in_specs=[SMEM, ANY, VMEM, VMEM] + [ANY] * 4,
        out_specs=[ANY, VMEM],
        out_shape=[pltpu.HBM(out, BF), shaped((8, LANES), F32)],
        scratch_shapes=[
            pltpu.VMEM(out, BF),
            pltpu.VMEM((feature_width, width), BF),
            pltpu.VMEM((count, feature_width), BF),
            pltpu.VMEM((feature_width, count), BF),
            pltpu.VMEM((count, part_width), F32),
            pltpu.VMEM((8, part_width), F32),
            pltpu.VMEM((local_rows, LANES), F32),
            pltpu.VMEM((count, width + part_width), BF),
            pltpu.SemaphoreType.DMA((3 * steps + 3 + probes // 2,)),
        ],
        compiler_params=params(52),
        name="curvature",
    )


def weights_kernel(heads, place_ref, active_in, cot_in, attended_in, down_ref, attended_ref, out_ref, *scratch):
    active_s, cot_s, attended_s, joined_s, total_s, sems = scratch
    moves = [(cot_in, cot_s), (active_in, active_s), (attended_in, attended_s)]
    copies = [pltpu.make_async_copy(source, target, sems.at[k]) for k, (source, target) in enumerate(moves)]
    for copy in copies:
        copy.start()
    for copy in copies[:2]:
        copy.wait()
    down_ref[...] = dot_tn(active_s[...], cot_s[...])
    copies[2].wait()
    block = attended_ref.shape[0]
    for number in range(cot_s.shape[0] // block):
        rows = slice(number * block, (number + 1) * block)
        values = [attended_s[head, rows, :].astype(F32) for head in range(heads)]
        joined_s[rows, :] = heads_joined(values).astype(BF)
    own = pl.ds(pl.multiple_of(place_ref[0] * block, block), block)
    attended_ref[...] = joined_s[own, :][:, : attended_ref.shape[1]]
    total_s[...] = dot_tn(joined_s[...], cot_s[...])
    local_rows = out_ref.shape[0]
    rows = pl.ds(pl.multiple_of(place_ref[3], local_rows), local_rows)
    out_ref[...] = jnp.where(place_ref[2] == 1, total_s[rows, :], 0.0).astype(BF)


def weights_back(heads, blocks, numbers, active, cot, attended, after):
    (count, feature_width), part_width, pair = cot.shape, active.shape[1], 2 * HEAD_DIM
    value_tiles = -(-heads // 2) * pair
    return call(
        functools.partial(weights_kernel, heads),
        inputs=[numbers, far(active), far(cot), far(attended)],
        after=after,
        in_specs=[SMEM, ANY, ANY, ANY],
        out_specs=[VMEM] * 3,
        out_shape=[
            shaped((part_width, feature_width), F32),
            shaped((count // blocks, heads * HEAD_DIM), BF),
            shaped((feature_width // blocks, feature_width), BF),
        ],
        scratch_shapes=[
            pltpu.VMEM(active.shape, BF),
            pltpu.VMEM(cot.shape, BF),
            pltpu.VMEM(attended.shape, BF),
            pltpu.VMEM((count, value_tiles), BF),
            pltpu.VMEM((value_tiles, feature_width), F32),
            pltpu.SemaphoreType.DMA((3,)),
        ],
        compiler_params=params(32),
        name="weights_back",
    )


def unpack_kernel(got_in, curvature_out, got_s, curvature_s, sems):
    blocks, _, width = got_s.shape
    probes = curvature_s.shape[0]
    part_width = width // probes

    def arrive(k):
        columns = slice(k * part_width, (k + 1) * part_width)
        return pltpu.make_async_copy(got_in.at[:, :, columns], got_s.at[:, :, columns], sems.at[k])

    def leave(k):
        return pltpu.make_async_copy(curvature_s.at[k], curvature_out.at[k], sems.at[probes + k])

    for k in range(probes):
        arrive(k).start()
    for k in range(probes):
        arrive(k).wait()
        for block in range(blocks):
            part = got_s[block, :, k * part_width : (k + 1) * part_width]
            curvature_s[k, :, block * part_width : (block + 1) * part_width] = part.astype(F32)
        leave(k).start()
    for k in range(probes):
        leave(k).wait()


def unpack(got, probes, part_width, after):
    blocks, local_rows, _ = got.shape
    out = (probes, local_rows, blocks * part_width)
    return call(
        unpack_kernel,
        inputs=[far(got)],
        after=after,
        in_specs=[ANY],
        out_specs=ANY,
        out_shape=pltpu.HBM(out, F32),
        scratch_shapes=[
            pltpu.VMEM((blocks, local_rows, probes * part_width), BF),
            pltpu.VMEM(out, F32),
            pltpu.SemaphoreType.DMA((2 * probes,)),
        ],
        compiler_params=params(24),
        name="unpack",
    )


def peel_kernel(probes, got_ref, up_ref, gain_ref, shift_ref, up_bias_ref, score_ref):
    blocks, _, share = got_ref.shape
    part_width = up_bias_ref.shape[0] // blocks
    tails = []
    for block in range(blocks):
        up_ref[:, block * share : (block + 1) * share] = got_ref[block]
        tails.append(got_ref[block, :, share - LANES :].astype(F32))
    total = tails[0]
    for tail in tails[1:]:
        total = total + tail

    def vector(rows, first, length):
        count = length // HEAD_DIM
        parts = [
            rows[first + k : first + k + 1, HEAD_DIM:] + rows[first + count + k : first + count + k + 1, HEAD_DIM:]
            for k in range(count)
        ]
        return jnp.concatenate(parts, axis=1)

    length = gain_ref.shape[0]
    step = 2 * length // HEAD_DIM
    gain_ref[...] = vector(total, 0, length).reshape(gain_ref.shape)
    shift_ref[...] = vector(total, step, length).reshape(shift_ref.shape)
    biases = [vector(tail, 2 * step, part_width) for tail in tails]
    up_bias_ref[...] = jnp.concatenate(biases, axis=1).reshape(up_bias_ref.shape)
    row = 2 * step + 2 * part_width // HEAD_DIM
    scores = total[row : row + 1, HEAD_DIM : HEAD_DIM + probes] + total[row + 1 : row + 2, HEAD_DIM : HEAD_DIM + probes]
    score_ref[...] = scores.reshape(score_ref.shape)


def peel(got, probes, part_width, after):
    blocks, local_rows, width = got.shape
    share = width - probes * part_width
    feature_width = blocks * local_rows
    vector = shaped((feature_width,), F32)
    return call(
        functools.partial(peel_kernel, probes),
        inputs=[got],
        after=after,
        grid=(1,),
        in_specs=[pl.BlockSpec((blocks, local_rows, share), lambda i: (0, 0, width // share - 1))],
        out_specs=[
            whole(local_rows, blocks * share), whole(feature_width), whole(feature_width),
            whole(blocks * part_width), whole(probes),
        ],
        out_shape=[
            shaped((local_rows, blocks * share), BF),
            vector, vector, shaped((blocks * part_width,), F32), shaped((probes,), F32),
        ],
        compiler_params=params(BIG),
        name="peel",
    )


def spread_kernel(blocks, half, place_ref, mine_ref, got_ref, out_ref):
    odd = place_ref[0] == 1
    stride = mine_ref.shape[1] // blocks
    for block in range(blocks):
        here = slice(block * stride, block * stride + half)
        mine, got = mine_ref[:, here], got_ref[:, here]
        both = jnp.concatenate([jnp.where(odd, got, mine), jnp.where(odd, mine, got)], axis=1)
        out_ref[:, block * 2 * half : (block + 1) * 2 * half] = both.astype(F32)


def spread(core, mine, got, blocks, half, after):
    return call(
        functools.partial(spread_kernel, blocks, half),
        inputs=[core[None].astype(jnp.int32), mine, got],
        after=after,
        in_specs=[SMEM, VMEM, VMEM],
        out_specs=VMEM,
        out_shape=shaped((mine.shape[0], blocks * 2 * half), F32),
        compiler_params=params(12),
        name="spread",
    )


def merge_kernel(feature_width, half, few, place_ref, mine_ref, got_ref, merged_ref):
    odd = place_ref[0] == 1
    third = mine_ref.shape[1] - feature_width

    def ordered(rows, columns):
        mine, got = mine_ref[rows, columns], got_ref[rows, columns]
        return jnp.concatenate([jnp.where(odd, got, mine), jnp.where(odd, mine, got)], axis=1)

    main = slice(0, half + few)
    total = mine_ref[main, :feature_width].astype(F32) + got_ref[main, :feature_width].astype(F32)
    merged_ref[...] = jnp.zeros_like(merged_ref)
    merged_ref[main, :feature_width] = total.astype(BF)
    merged_ref[main, feature_width:] = ordered(main, slice(feature_width, feature_width + third))
    rows = slice(half + few, half + 2 * few)
    merged_ref[rows, : 4 * third] = ordered(rows, slice(0, 2 * third))
    first, width = half + 2 * few, feature_width // 2
    put_small(merged_ref, first, get_small(mine_ref, first, width) + get_small(got_ref, first, width))


def merge(core, mine, got, feature_width, half, few):
    count, width = mine.shape
    return call(
        functools.partial(merge_kernel, feature_width, half, few),
        inputs=[core[None].astype(jnp.int32), mine, got],
        in_specs=[SMEM, VMEM, VMEM],
        out_specs=VMEM,
        out_shape=shaped((count, 2 * width - feature_width), BF),
        compiler_params=params(12),
        name="merge",
    )


def finish_kernel(
    few, place_ref, mine_ref, got_ref, tokens_ref, base_ref, rest_ref, vectors_ref, out_weight_ref,
    final_ref, small_ref,
):
    tok_count, feature_width = tokens_ref.shape
    half = tok_count // 2
    third = (mine_ref.shape[1] - feature_width) // 2
    upper = place_ref[1] == 1
    own = pl.ds(pl.multiple_of(place_ref[0] * half, half), half)

    def ordered(rows, columns):
        mine, got = mine_ref[rows, columns], got_ref[rows, columns]
        return jnp.where(upper, got, mine), jnp.where(upper, mine, got)

    attended = jnp.concatenate(ordered(slice(0, half), slice(feature_width, None)), axis=1)
    layer_out = base_ref[own, :] + dot(attended, out_weight_ref[...])
    main = slice(0, half + few)
    total = mine_ref[main, :feature_width].astype(F32) + got_ref[main, :feature_width].astype(F32)
    centred, factor = spread_of(tokens_ref[own, :].astype(F32))
    term = norm_input_term(total[:half], vectors_ref[0:1, :], centred * factor, factor)
    final_ref[:half, :feature_width] = layer_out.astype(BF)
    final_ref[:half, feature_width:] = (rest_ref[own, :] + term).astype(BF)
    parts = []
    firsts = ordered(slice(half, half + few), slice(feature_width, None))
    others = ordered(slice(half + few, half + 2 * few), slice(0, 4 * third))
    for first, other in zip(firsts, others):
        for core in range(2):
            parts += [first[:, core * third : (core + 1) * third], other[:, 2 * core * third : 2 * (core + 1) * third]]
    grad_qkv = jnp.concatenate(parts, axis=1)
    final_ref[half : half + few, :feature_width] = total[half:].astype(BF)
    final_ref[half : half + few, feature_width:] = grad_qkv[:, :feature_width]
    final_ref[half + few :, :] = grad_qkv[:, feature_width:]
    first, width = half + 2 * few, feature_width // 2
    small_ref[...] = get_small(mine_ref, first, width) + get_small(got_ref, first, width)


def finish(places, mine, got, tokens, base, rest, vectors, out_weight, few):
    tok_count, feature_width = tokens.shape
    half = tok_count // 2
    return call(
        functools.partial(finish_kernel, few),
        inputs=[places, mine, got, tokens, far(base), far(rest), vectors, far(out_weight)],
        in_specs=[SMEM] + [VMEM] * 7,
        out_specs=[VMEM] * 2,
        out_shape=[
            shaped((half + 2 * few, 2 * feature_width), BF),
            shaped((mine.shape[0] - half - 2 * few, feature_width // 2), F32),
        ],
        compiler_params=params(20),
        name="finish",
    )


def join_kernel(
    few, mixed_width, place_ref, mine_ref, got_ref, small_ref, cot_ref,
    layer_out_ref, input_grad_ref, out_ref, qkv_ref, gain_ref, shift_ref, qkv_bias_ref, out_bias_ref, down_bias_ref,
):
    half = layer_out_ref.shape[0] // 2
    feature_width = layer_out_ref.shape[1]
    odd = place_ref[0] == 1
    mine, got = mine_ref[...], got_ref[...]
    for core, side in enumerate((jnp.where(odd, got, mine), jnp.where(odd, mine, got))):
        rows = slice(core * half, (core + 1) * half)
        layer_out_ref[rows, :] = side[:half, :feature_width]
        input_grad_ref[rows, :] = side[:half, feature_width:]
        rows = slice(core * few, (core + 1) * few)
        out_ref[rows, :] = side[half : half + few, :feature_width].astype(F32)
        qkv_ref[rows, :feature_width] = side[half : half + few, feature_width:].astype(F32)
        qkv_ref[rows, feature_width:] = side[half + few :, :].astype(F32)
    small = small_ref[...]

    def rows_of(first, total):
        return jnp.concatenate([small[first : first + 1, :], small[first + 1 : first + 2, :]], axis=1)[:, :total]

    gain_ref[...] = rows_of(0, feature_width).reshape(gain_ref.shape)
    shift_ref[...] = rows_of(2, feature_width).reshape(shift_ref.shape)
    groups = qkv_bias_ref.shape[0] // mixed_width
    bias = [rows_of(4 + 2 * number, mixed_width) for number in range(groups)]
    qkv_bias_ref[...] = jnp.concatenate(bias, axis=1).reshape(qkv_bias_ref.shape)
    for ref in (out_bias_ref, down_bias_ref):
        ref[...] = cot_ref[...].reshape(ref.shape)


def join(core, mine, got, small, cot, tok_count, few, mixed_width):
    feature_width = cot.shape[1]
    vector = shaped((feature_width,), F32)
    return call(
        functools.partial(join_kernel, few, mixed_width),
        inputs=[core[None].astype(jnp.int32), mine, got, small, cot],
        in_specs=[SMEM] + [VMEM] * 4,
        out_specs=[VMEM] * 9,
        out_shape=[shaped((tok_count, feature_width), BF)] * 2
        + [shaped((2 * few, feature_width), F32), shaped((2 * few, 3 * feature_width), F32), vector, vector]
        + [shaped((4 * mixed_width,), F32), vector, vector],
        compiler_params=params(16),
        name="join",
    )


def on_device(
    tokens,
    segment_ids,
    qkv_weight,
    qkv_bias,
    out_weight,
    out_bias,
    up_weight,
    up_bias,
    down_weight,
    down_bias,
    norm1_gain,
    norm1_bias,
    norm2_gain,
    norm2_bias,
    probe_dirs,
    out_grad,
):
    tok_count, feature_width = tokens.shape
    hidden_width = up_weight.shape[1]
    probe_count, local_rows = probe_dirs.shape[:2]
    groups = lax.axis_size("ex")
    probe_groups = lax.axis_size("probe")
    blocks = SEQ // tok_count
    rows = groups // blocks
    ex_place = lax.axis_index("ex")
    place = ex_place % blocks
    row_place = ex_place // blocks
    probe_place = lax.axis_index("probe")
    core, upper = probe_place % 2, probe_place // 2
    heads = HEADS // probe_groups
    head_width = heads * HEAD_DIM
    part_width = hidden_width // blocks
    fine = part_width // rows
    row_groups = None
    if rows > 1:
        row_groups = [[r * blocks + b for b in range(blocks)] for r in range(rows)]
    across = [[r * blocks + b for r in range(rows)] for b in range(blocks)]

    def swap(value, distance):
        return lax.ppermute(value, "ex", [(i, i ^ distance) for i in range(groups)])

    def swap_probe(value, distance):
        return lax.ppermute(value, "probe", [(i, i ^ distance) for i in range(probe_groups)])

    def over_rows(value):
        if rows > 1:
            return lax.psum_scatter(value, "ex", axis_index_groups=across, scatter_dimension=0, tiled=True)
        return value

    def my_part(value, axis):
        shape = value.shape
        split = shape[:axis] + (rows, blocks, fine) + shape[axis + 1 :]
        part = lax.dynamic_index_in_dim(value.reshape(split), place, axis + 1, keepdims=False)
        return part.reshape(shape[:axis] + (part_width,) + shape[axis + 1 :])

    mine, share = slices_of(probe_place, probe_groups, tokens, out_grad)
    aside = swap(mine, 1)
    near, diagonal, distant, farthest = [swap(share, distance) for distance in (2, 3, 4, 6)]

    segments = segment_ids
    if rows > 1:
        segments = lax.dynamic_slice_in_dim(segment_ids, row_place * SEQ, SEQ)
    vectors = vectors_of(
        probe_groups, blocks, norm1_gain, norm1_bias, norm2_gain, norm2_bias, out_bias, down_bias, qkv_bias, segments
    )
    base, rest, local_small = local_part(tokens, out_grad, up_weight, up_bias, down_weight, vectors)

    second, third = stack([near, diagonal, distant, farthest], [(0, 1), (2, 3)], [local_small])
    third_aside, third_over = swap(third, 1), swap_probe(third, 2)
    (quarters,) = stack([mine, aside, third, third_over], [(0, 1, 2, 3)], [])
    swapped = swap_probe(quarters, 1)
    up_bias_part = my_part(up_bias, 0).astype(F32)[None]
    up_part, down_part = up_weight, down_weight
    if rows > 1:
        up_part, down_part = my_part(up_weight, 1), my_part(down_weight, 0)

    def pieces_of(array, other, slots, distances):
        return [
            ([(side, slot) for side in (array, other) for slot in pair], ((0, 2, 1, 3), (distance,)))
            for pair, distance in zip(slots, distances)
        ]

    pieces = pieces_of(quarters, swapped, ((0, 1), (2, 3), (4, 6), (5, 7)), (0, 1, 4, 6))
    slots = [lambda i: jnp.where(i < 2, 2 * i, i + 2), lambda i: jnp.where(i < 2, 2 * i + 1, i + 4)]
    refs = [(array, slot_of) for array in (quarters, swapped) for slot_of in slots]
    unit_place = place if rows == 1 else place * 0
    places = jnp.stack([unit_place, place, probe_place]).astype(jnp.int32)
    fixed = (SEQ, up_part, up_bias_part, down_part, vectors)
    units = hidden_units(places, refs, (0, 2, 1, 3), 0, (0, 1, 4, 6), *fixed, None)
    second_over, third_across = swap_probe(second, 2), swap_probe(third_aside, 2)

    dirs = tie(pack(probe_dirs, blocks, rows, [local_small]), [third_aside, third_over, aside])
    dirs = lax.all_to_all(dirs, "ex", 0, 0, axis_index_groups=row_groups, tiled=True)
    dirs = dirs.reshape(blocks * local_rows, probe_count * part_width)
    if rows > 1:
        dirs = lax.all_gather(dirs, "ex", axis_index_groups=across, tiled=True)

    (near_quarters,) = stack([second, second_over], [(0, 1)], [units[5]])
    (far_quarters,) = stack([third_aside, third_across], [(0, 1)], [near_quarters])
    near_swapped = tie(swap_probe(near_quarters, 1), [far_quarters])
    last = ((near_quarters, near_swapped, (2, 3)), (far_quarters, swap_probe(far_quarters, 1), (5, 7)))
    for number, (array, swapped, distances) in enumerate(last):
        pieces += pieces_of(array, swapped, ((0, 2), (1, 3)), distances)
        refs = [(side, lambda i, k=k: i + 2 * k) for side in (array, swapped) for k in range(2)]
        units = hidden_units(places, refs, (0, 2, 1, 3), 4 + 2 * number, distances, *fixed, units)
    *units, active, grad_up_bias, cot_sum = units

    block_rows = feature_width // blocks
    offset = place * block_rows - probe_place * head_width
    holds = (offset >= 0) & (offset < head_width)
    numbers = jnp.stack([place, probe_place, holds, jnp.where(holds, offset, 0)]).astype(jnp.int32)
    *parts, cot, attended = attention(heads, blocks, numbers, pieces, tokens, qkv_weight, vectors, out_weight, [cot_sum])

    part, scores = curvature_of(
        blocks, core, probe_count, units, dirs, local_small, grad_up_bias, [far(attended)]
    )
    part = over_rows(part.reshape(feature_width, -1)).reshape(blocks, local_rows, -1)
    got = lax.all_to_all(part, "ex", 0, 0, axis_index_groups=row_groups, tiled=True)

    grad_down, attended, grad_out = weights_back(heads, blocks, numbers, active, cot, attended, [scores])
    parts += [attended, grad_out]
    keep, send = attention_back(heads, blocks, numbers, parts, qkv_weight, vectors, [scores])
    half, few = tok_count // 2, block_rows // 2
    merged = merge(core, keep, swap_probe(send, 1), feature_width, half, few)
    final, small = finish(
        jnp.stack([core, upper]).astype(jnp.int32), merged, swap_probe(merged, 2), tokens, base, rest, vectors,
        out_weight, few,
    )
    (
        layer_out, input_grad, grad_out_weight, grad_qkv_weight,
        grad_gain_one, grad_shift_one, grad_qkv_bias, grad_out_bias, grad_down_bias,
    ) = join(core, final, swap_probe(final, 1), small, cot_sum, tok_count, few, 3 * head_width)

    if rows == 1:
        up_half, grad_gain_two, grad_shift_two, grad_up_bias, scores = peel(
            got, probe_count, part_width, [layer_out]
        )
        other_half = swap_probe(up_half, 1)
        curvature = unpack(got, probe_count, part_width, [far(up_half)])
        scores = scores[:, None]
        grad_up_weight = spread(core, up_half, other_half, blocks, part_width // 2, [])
    else:
        start = probe_count * part_width
        units = got[:, :, :start].reshape(blocks, local_rows, probe_count, rows, fine)
        curvature = units.transpose(2, 1, 3, 0, 4).reshape(probe_count, local_rows, hidden_width)
        curvature = curvature.astype(F32)
        up_half = got[:, :, start : start + part_width // 2]
        both = lax.all_gather(up_half, "probe", axis_index_groups=[[0, 1], [2, 3]])
        both = both.transpose(2, 1, 0, 3).reshape(local_rows, blocks, rows, fine)
        grad_up_weight = both.transpose(0, 2, 1, 3).reshape(local_rows, hidden_width).astype(F32)
        grad_down = over_rows(grad_down)

        def over_groups(value):
            value = lax.all_gather(value, "ex", axis_index_groups=row_groups, tiled=True)
            return lax.dynamic_slice_in_dim(over_rows(value), place * local_rows, local_rows, 0)

        grad_qkv_weight, grad_out_weight = over_groups(grad_qkv_weight), over_groups(grad_out_weight)
        grad_gain_one, grad_shift_one, grad_qkv_bias, grad_out_bias, grad_up_bias = lax.psum(
            (grad_gain_one, grad_shift_one, grad_qkv_bias, grad_out_bias, grad_up_bias[0]),
            "ex",
            axis_index_groups=across,
        )
        grad_down_bias = grad_out_bias
        grad_up_bias = lax.all_gather(grad_up_bias, "ex", axis_index_groups=row_groups)
        grad_up_bias = grad_up_bias.reshape(blocks, rows, fine).transpose(1, 0, 2).reshape(-1)
        grad_gain_two, grad_shift_two = lax.psum((local_small[1], local_small[2]), "ex")
        scores = lax.psum(scores[:probe_count, :1], "ex", axis_index_groups=row_groups)
        scores = lax.all_gather(scores, "ex", axis_index_groups=across, axis=1, tiled=True)
    return (
        layer_out,
        input_grad,
        grad_qkv_weight,
        grad_qkv_bias,
        grad_out_weight,
        grad_out_bias,
        grad_up_weight,
        grad_up_bias,
        grad_down,
        grad_down_bias,
        grad_gain_one,
        grad_shift_one,
        grad_gain_two,
        grad_shift_two,
        curvature,
        scores,
    )


def solution(mesh):
    in_specs = (
        P("ex", None),
        P(),
        P(),
        P(),
        P(),
        P(),
        P(),
        P(),
        P(),
        P(),
        P(),
        P(),
        P(),
        P(),
        P("probe", "ex", None),
        P("ex", None),
    )
    out_specs = (
        P("ex", None),
        P("ex", None),
        P("ex", None),
        P(),
        P("ex", None),
        P(),
        P("ex", None),
        P(),
        P("ex", None),
        P(),
        P(),
        P(),
        P(),
        P(),
        P("probe", "ex", None),
        P("probe", None),
    )
    return jax.shard_map(
        on_device, mesh=mesh, in_specs=in_specs, out_specs=out_specs, check_vma=False
    )
```
